32 devices in a mesh: dp: 8 (over y, x, core), blk: 4 (over z).
Axes of the slice: x: 2, y: 2, z: 4, core: 2. Of those that a mesh axis runs over, the one named last changes fastest.
Arguments:
- inputs: float32 [24576, 768], P(('dp', 'blk')), may hold values from -6 to 6
- positions: int32 [24576], P(('dp', 'blk')), may hold values from 0 to 1535
- segments: int32 [24576], P('dp'), may hold values from 0 to 24575, as said below
- gain_attn: float32 [768], replicated, may hold values from 0.1 to 1.9
- w_qkv: bfloat16 [768, 2304], replicated, may hold values from -0.21875 to 0.21875
- w_out: bfloat16 [768, 768], replicated, may hold values from -0.875 to 0.875
- gain_mlp: float32 [768], replicated, may hold values from 0.1 to 1.9
- w_up: bfloat16 [768, 3072], replicated, may hold values from -0.21875 to 0.21875
- b_up: float32 [3072], replicated, may hold values from -3 to 3
- w_down: bfloat16 [3072, 768], replicated, may hold values from -0.109375 to 0.109375
- cotangent: float32 [24576, 768], P(('dp', 'blk')), may hold values from -6 to 6
Outputs:
- outputs: float32 [24576, 768], P(('dp', 'blk'))
- input_grad: float32 [24576, 768], P(('dp', 'blk'))
- grad_gain_attn: float32 [768], replicated
- grad_qkv: float32 [768, 2304], replicated
- grad_out: float32 [768, 768], replicated
- grad_gain_mlp: float32 [768], replicated
- grad_up: float32 [768, 3072], replicated
- grad_bias_up: float32 [3072], replicated
- grad_down: float32 [3072, 768], replicated
The draws below stay inside these ranges and needn't reach their ends.
Inputs may be any that keep to these rules, and one draw needn't show every extreme that they name: `segments`: ids never fall along the rows of one index of dp, and rows of different indices of dp have different ids; one clip of each index of dp covers rows of all its 4 devices along blk.
All inputs are finite; a program needn't handle non-finite values.
Results may differ from the reference program's by a relative error of at most 0.0095.
Values may be sent and summed in bfloat16 or wider, within the bound.
A program may use at most 256 MiB of HBM per device.

```python
import math
import jax
import jax.numpy as jnp
from jax import lax

D = 768
HEADS = 12
HEAD = 64
FF = 3072
ROWS_DEV = 768
GROUP_ROWS = 3072
TOKENS = 24576


def draw_segments(key, part):
    key = jax.random.fold_in(key, 11)
    key_start, key_extra, key_breaks = jax.random.split(key, 3)
    groups = TOKENS // GROUP_ROWS
    reach_most = max(ROWS_DEV // 2, 2)
    long_start = jax.random.randint(key_start, (groups, 1), 1, reach_most)
    long_extra = jax.random.randint(key_extra, (groups, 1), 1, reach_most)
    long_finish = 3 * ROWS_DEV + long_extra
    row_place = jnp.arange(GROUP_ROWS, dtype=jnp.int32)[None, :]
    breaks = jax.random.randint(key_breaks, (groups, GROUP_ROWS), 0, 100) == 0
    inside = (row_place > long_start) & (row_place < long_finish)
    breaks = breaks & jnp.logical_not(inside) | (row_place == long_start) | (row_place == long_finish)
    breaks = breaks | (row_place == 0) | (row_place == GROUP_ROWS - 1)
    starts = jnp.where(breaks, row_place, jnp.zeros_like(row_place)).astype(jnp.int32)
    starts = lax.cummax(starts, axis=1)
    segment_ids = starts + jnp.arange(groups, dtype=jnp.int32)[:, None] * GROUP_ROWS
    return segment_ids.reshape(-1).astype(jnp.int32)


def with_ends(array, rng, low, high):
    extent = array.shape
    spot = [jax.random.randint(jax.random.fold_in(rng, axis), (), 0, extent[axis]) for axis in range(len(extent))]
    array = array.at[tuple(spot)].set(low)
    longest = extent.index(max(extent))
    spot[longest] = (spot[longest] + 1) % extent[longest]
    return array.at[tuple(spot)].set(high)


def shard_levels(stream_key, extent, cuts, low, top_value):
    gain, own = 1.0, jax.random.fold_in(stream_key, 6)
    for position, parts in cuts:
        draws = jnp.exp(jax.random.uniform(jax.random.fold_in(own, position), (parts,), jnp.float32, low / len(cuts), top_value / len(cuts)))
        gain = gain * jnp.repeat(draws, extent[position] // parts).reshape([-1 if axis == position else 1 for axis in range(len(extent))])
    return gain


def bell_draw(key, extent, width, reach, pieces=(), kind=jnp.bfloat16):
    entries = width * jax.random.normal(key, extent, jnp.float32)
    if pieces:
        entries = entries * shard_levels(key, extent, pieces, -0.22, 0.18)
    return jnp.clip(entries, -reach, reach).astype(kind)


def setup_inputs(seed: int = 0) -> dict:
    splits = jax.random.split(jax.random.key(seed), 12)
    return {
        "inputs": bell_draw(splits[0], (TOKENS, D), 1.0, 6.0, ((0, 32),), jnp.float32),
        "positions": with_ends(jax.random.randint(splits[1], (TOKENS,), 0, 1536), jax.random.fold_in(splits[1], 1), 0, 1535).astype(jnp.int32),
        "segments": draw_segments(jax.random.fold_in(splits[11], 71), 0),
        "gain_attn": jnp.clip(1.0 + 0.18 * jax.random.normal(splits[3], (D,), jnp.float32), 0.1, 1.9),
        "w_qkv": bell_draw(splits[4], (D, 3 * D), D ** -0.5, 0.21875),
        "w_out": bell_draw(splits[5], (D, D), (D // 16) ** -0.5, 0.875),
        "gain_mlp": jnp.clip(1.0 + 0.18 * jax.random.normal(splits[6], (D,), jnp.float32), 0.1, 1.9),
        "w_up": bell_draw(splits[7], (D, FF), D ** -0.5, 0.21875),
        "b_up": bell_draw(splits[8], (FF,), 0.5, 3.0, (), jnp.float32),
        "w_down": bell_draw(splits[9], (FF, D), FF ** -0.5, 0.109375),
        "cotangent": bell_draw(splits[10], (TOKENS, D), 1.0, 6.0, ((0, 32),), jnp.float32),
    }


@jax.custom_vjp
def low(v):
    return lax.optimization_barrier(v.astype(jnp.bfloat16)).astype(jnp.float32)

@jax.custom_vjp
def low_back(v):
    return v

def low_keep(v):
    return (low(v), None)

def low_pass(kept, grad):
    return (grad,)

def back_keep(v):
    return (v, None)

def back_low(kept, grad):
    return (low(grad),)
low.defvjp(low_keep, low_pass)
low_back.defvjp(back_keep, back_low)
eps_norm = 1e-06
mask_fill = -1000000000.0

def position_table(positions, model_width):
    half_width = model_width // 2
    freqs = jnp.exp(jnp.arange(half_width, dtype=jnp.float32) * (-math.log(10000.0) / half_width))
    angles = positions.astype(jnp.float32)[:, None] * freqs[None, :]
    return jnp.concatenate([jnp.sin(angles), jnp.cos(angles)], axis=1)

def normalize(values):
    center = values - lax.optimization_barrier(jnp.mean(values, axis=-1, keepdims=True))
    return center * lax.rsqrt(lax.optimization_barrier(jnp.mean(center * center, axis=-1, keepdims=True)) + eps_norm)

def encoder_layer(inputs, positions, segments, gain_attn, w_qkv, w_out, gain_mlp, w_up, b_up, w_down):
    highest = lax.Precision.HIGHEST
    row_count, model_width = inputs.shape
    hidden = inputs + position_table(positions, model_width)
    a_low = low(normalize(hidden) * gain_attn)
    qkv = low(low_back(jnp.dot(a_low, w_qkv, precision=highest)))
    queries = qkv[:, :model_width].reshape(row_count, HEADS, HEAD).transpose(1, 0, 2)
    keys = qkv[:, model_width:2 * model_width].reshape(row_count, HEADS, HEAD).transpose(1, 0, 2)
    values = qkv[:, 2 * model_width:].reshape(row_count, HEADS, HEAD).transpose(1, 0, 2)
    same_clip = segments[:, None] == segments[None, :]
    score_scale = HEAD ** (-0.5)

    def one_head(items):
        query_head, key_head, value_head = items
        scores = jnp.dot(query_head, key_head.T, precision=highest) * score_scale
        scores = low_back(jnp.where(same_clip, scores, mask_fill))
        probs = low(jax.nn.softmax(scores, axis=-1))
        return jnp.dot(probs, value_head, precision=highest)
    attended = lax.map(jax.checkpoint(one_head), (queries, keys, values))
    attn_low = low(low_back(attended.transpose(1, 0, 2).reshape(row_count, model_width)))
    resid = hidden + low_back(jnp.dot(attn_low, w_out, precision=highest))
    b_low = low(normalize(resid) * gain_mlp)
    pre_act = low_back(jnp.dot(b_low, w_up, precision=highest) + b_up)
    z_low = low(jax.nn.gelu(pre_act, approximate=False))
    return resid + low_back(jnp.dot(z_low, w_down, precision=highest))

def reference(inputs, positions, segments, gain_attn, w_qkv, w_out, gain_mlp, w_up, b_up, w_down, cotangent):
    group_count = TOKENS // GROUP_ROWS
    params = (gain_attn.astype(jnp.float32), w_qkv.astype(jnp.float32), w_out.astype(jnp.float32), gain_mlp.astype(jnp.float32), w_up.astype(jnp.float32), b_up.astype(jnp.float32), w_down.astype(jnp.float32))
    inputs_grouped = inputs.reshape(group_count, GROUP_ROWS, D)
    positions_grouped = positions.reshape(group_count, GROUP_ROWS)
    segments_grouped = segments.reshape(group_count, GROUP_ROWS)
    cotangent_grouped = cotangent.reshape(group_count, GROUP_ROWS, D)

    def group_step(totals, items):
        group_inputs, group_positions, group_segments, group_cotangent = items

        def forward(x_rows, g_attn, wq, wo, g_mlp, wu, bu, wd):
            return encoder_layer(x_rows, group_positions, group_segments, g_attn, wq, wo, g_mlp, wu, bu, wd)
        result, pullback = jax.vjp(forward, group_inputs, *params)
        gradients = pullback(group_cotangent)
        totals = tuple((total + grad for total, grad in zip(totals, gradients[1:])))
        return (totals, (result, gradients[0]))
    zero_grads = tuple((jnp.zeros(param.shape, jnp.float32) for param in params))
    totals, (results, input_grads) = lax.scan(group_step, zero_grads, (inputs_grouped, positions_grouped, segments_grouped, cotangent_grouped))
    return (results.reshape(TOKENS, D), input_grads.reshape(TOKENS, D), totals[0], totals[1], totals[2], totals[3], totals[4], totals[5], totals[6])
```

```python
import functools
import math

import jax
import jax.numpy as jnp
from jax import lax
from jax.experimental import pallas as pl
from jax.experimental.pallas import tpu as pltpu
from jax.sharding import PartitionSpec as P

HEADS = 12
HEAD = 64
PAIR = 2 * HEAD
SCALE = HEAD**-0.5
LOG2E = 1.4426950408889634
MASKED = -1.0e9
QUERY_BLOCK = 384
EPS_NORM = 1e-06
LOW = jnp.bfloat16
WIDE = jnp.float32

NN = (((1,), (0,)), ((), ()))
NT = (((1,), (1,)), ((), ()))
TN = (((0,), (0,)), ((), ()))


def dot(left, right, dims):
    return lax.dot_general(left, right, dims, preferred_element_type=WIDE)


def position_table(positions, model_width):
    half_width = model_width // 2
    freqs = jnp.exp(jnp.arange(half_width, dtype=WIDE) * (-math.log(10000.0) / half_width))
    angles = positions.astype(WIDE)[:, None] * freqs[None, :]
    return jnp.concatenate([jnp.sin(angles), jnp.cos(angles)], axis=1)


def normalize(values):
    center = values - jnp.mean(values, axis=-1, keepdims=True)
    inverse = lax.rsqrt(jnp.mean(center * center, axis=-1, keepdims=True) + EPS_NORM)
    return center * inverse, inverse


def norm_back(grad_norm, normed, inverse):
    first = jnp.mean(grad_norm, axis=-1, keepdims=True)
    second = jnp.mean(grad_norm * normed, axis=-1, keepdims=True)
    return inverse * (grad_norm - first - normed * second)


def in_head(values, head):
    lanes = lax.broadcasted_iota(jnp.int32, values.shape, 1)
    return (lanes < HEAD) == (head == 0)


def only_head(values, head, other=None):
    other = jnp.zeros_like(values) if other is None else other
    return jnp.where(in_head(values, head), values, other)


def split_scaled(query):
    scaled = query.astype(WIDE) * (SCALE * LOG2E)
    high = scaled.astype(LOW)
    return high, (scaled - high.astype(WIDE)).astype(LOW)


def extra_columns(own, key_keep, query_keep, rows):
    if own:
        zeros = jnp.zeros((rows, PAIR), LOW)
        return zeros, zeros
    lanes = lax.broadcasted_iota(jnp.int32, (rows, PAIR), 1) % HEAD
    key_fill = jnp.where(key_keep == 0, MASKED, 0.0)
    query_fill = jnp.where(query_keep == 0, MASKED, 0.0)
    one, zero = jnp.ones((rows, PAIR), WIDE), jnp.zeros((rows, PAIR), WIDE)
    key_extra = jnp.where(lanes == 0, key_fill, jnp.where(lanes == 1, one, zero))
    query_extra = jnp.where(lanes == 0, one, jnp.where(lanes == 1, query_fill, zero))
    return key_extra.astype(LOW), query_extra.astype(LOW)


def score_sides(key, query, key_extra, query_extra):
    high, low = split_scaled(query)
    key_side = [
        jnp.concatenate([only_head(key, head, key_extra), only_head(key, head)], axis=1)
        for head in range(2)
    ]
    query_side = [
        jnp.concatenate([only_head(high, head, query_extra), only_head(low, head)], axis=1)
        for head in range(2)
    ]
    return key_side, query_side


def work_items(rows):
    return [(start, head) for start in range(0, rows, QUERY_BLOCK) for head in range(2)]


def forward_kernel(own, last, *refs):
    a_ref, w_ref, q_ref, key_mark, query_mark = refs[:5]
    refs = refs[5:]
    if not own:
        acc_in, top_in, total_in = refs[:3]
        refs = refs[3:]
    kv_ref, acc_ref, top_ref, total_ref = refs[:4]
    refs = refs[4:]
    if last:
        attn_ref = refs[0]
    rows = q_ref.shape[0]
    kv = dot(a_ref[...], w_ref[...], NN).astype(LOW)
    kv_ref[...] = kv
    key, value = kv[:, :PAIR], kv[:, PAIR:]
    value_t = value.T
    ones = jnp.ones((16, rows), LOW)
    value_rows = [
        jnp.concatenate([value_t[head * HEAD : (head + 1) * HEAD], ones], axis=0) for head in range(2)
    ]
    marks = (None, None) if own else (key_mark[...], query_mark[...])
    key_extra, query_extra = extra_columns(own, *marks, rows)
    key_side, query_side = score_sides(key, q_ref[...], key_extra, query_extra)

    def scores(start, head):
        stop = start + QUERY_BLOCK
        result = dot(key_side[head], query_side[head][start:stop], NT)
        if own:
            result = jnp.where(key_mark[...] == query_mark[:, start:stop], result, MASKED)
        return result

    def weights(start, head, result):
        stop = start + QUERY_BLOCK
        top = jnp.max(result, axis=0, keepdims=True)
        if not own:
            top = jnp.maximum(top, top_in[head : head + 1, start:stop])
        return jnp.exp2(result - top).astype(LOW), top

    def attend(start, head, expd, top):
        stop = start + QUERY_BLOCK
        lanes, row = slice(head * HEAD, (head + 1) * HEAD), slice(head, head + 1)
        result = dot(value_rows[head], expd, NN)
        acc, total = result[:HEAD], result[HEAD : HEAD + 1]
        if not own:
            shrink = jnp.exp2(top_in[row, start:stop] - top)
            acc = acc_in[lanes, start:stop] * shrink + acc
            total = total_in[row, start:stop] * shrink + total
        if last:
            acc = acc * (1.0 / total)
            top = top + jnp.log(total) * LOG2E
        acc_ref[lanes, start:stop] = acc
        top_ref[row, start:stop] = top
        total_ref[row, start:stop] = total

    items = work_items(rows)
    result = scores(*items[0])
    before = None
    for index, item in enumerate(items):
        following = scores(*items[index + 1]) if index + 1 < len(items) else None
        done = weights(*item, result)
        if before is not None:
            attend(*before)
        before = (*item, *done)
        result = following
    attend(*before)
    if last:
        attn_ref[...] = acc_ref[...].T.astype(LOW)


def forward_call(own, last, a_shard, w_kv, query, key_mark, query_mark, state):
    rows, width = query.shape
    pairs = width // PAIR
    whole = lambda shape: pl.BlockSpec(shape, lambda pair: (0,) * len(shape))
    columns = pl.BlockSpec((rows, PAIR), lambda pair: (0, pair))
    across = pl.BlockSpec((PAIR, rows), lambda pair: (pair, 0))
    line = pl.BlockSpec((None, 2, rows), lambda pair: (pair, 0, 0))
    state_specs = [across, line, line]
    state_shapes = [
        jax.ShapeDtypeStruct((width, rows), WIDE),
        jax.ShapeDtypeStruct((pairs, 2, rows), WIDE),
        jax.ShapeDtypeStruct((pairs, 2, rows), WIDE),
    ]
    in_specs = [
        whole((rows, width)),
        pl.BlockSpec((width, 2 * PAIR), lambda pair: (0, pair)),
        columns,
        whole(key_mark.shape),
        whole(query_mark.shape),
    ]
    operands = [a_shard, w_kv, query, key_mark, query_mark]
    if not own:
        in_specs += state_specs
        operands += list(state)
    out_specs = [pl.BlockSpec((rows, 2 * PAIR), lambda pair: (0, pair)), *state_specs]
    out_shape = [jax.ShapeDtypeStruct((rows, 2 * width), LOW), *state_shapes]
    if last:
        out_specs.append(columns)
        out_shape.append(jax.ShapeDtypeStruct((rows, width), LOW))
    return pl.pallas_call(
        functools.partial(forward_kernel, own, last),
        grid=(pairs,),
        in_specs=in_specs,
        out_specs=out_specs,
        out_shape=out_shape,
        name="attend_own" if own else "attend_shard",
        cost_estimate=pl.CostEstimate(
            flops=14 * rows * rows * width, bytes_accessed=24 * rows * width, transcendentals=0
        ),
        compiler_params=pltpu.CompilerParams(vmem_limit_bytes=48 * 2**20),
    )(*operands)


def backward_kernel(own, first, *refs):
    kv_ref, q_ref, da_ref, lse_ref, attn_ref, key_mark, query_mark = refs[:7]
    refs = refs[7:]
    if not first:
        dq_in = refs[0]
        refs = refs[1:]
    dkv_ref, dq_ref, dk_sum, dv_sum = refs
    rows = q_ref.shape[0]
    key, value = kv_ref[:, :PAIR], kv_ref[:, PAIR:]
    query, grad = q_ref[...], da_ref[...]
    key_t, query_t, grad_t = key.T, query.T, grad.T
    marks = (None, None) if own else (key_mark[...], query_mark[...])
    key_extra, query_extra = extra_columns(own, *marks, rows)
    key_side, query_side = score_sides(key, query, key_extra, query_extra)
    grad_side = [only_head(grad, head) for head in range(2)]
    product = grad_t.astype(WIDE) * attn_ref[...]
    row_dots = [
        jnp.sum(product[head * HEAD : (head + 1) * HEAD], axis=0, keepdims=True) for head in range(2)
    ]
    dq_all = []
    for start, head in work_items(rows):
        stop = start + QUERY_BLOCK
        lanes, row = slice(head * HEAD, (head + 1) * HEAD), slice(head, head + 1)
        score = dot(key_side[head], query_side[head][start:stop], NT)
        if own:
            score = jnp.where(key_mark[...] == query_mark[:, start:stop], score, MASKED)
        probs = jnp.exp2(score - lse_ref[row, start:stop])
        d_probs = dot(value, grad_side[head][start:stop], NT)
        d_scores = (probs * (d_probs - row_dots[head][:, start:stop])).astype(LOW)
        probs = probs.astype(LOW)
        dv = dot(grad_t[lanes, start:stop], probs, NT)
        dk = dot(query_t[lanes, start:stop], d_scores, NT)
        dq = dot(key_t[lanes], d_scores, NN)
        if start == 0:
            dv_sum[lanes], dk_sum[lanes] = dv, dk
        else:
            dv_sum[lanes] += dv
            dk_sum[lanes] += dk
        if not first:
            dq = dq + dq_in[lanes, start:stop]
        if own:
            dq_all.append((start, head, dq))
        else:
            dq_ref[lanes, start:stop] = dq
    if own:
        for start in range(0, rows, QUERY_BLOCK):
            both = jnp.concatenate([dq for at, head, dq in dq_all if at == start], axis=0)
            dq_ref[start : start + QUERY_BLOCK] = (both * SCALE).T.astype(LOW)
    dkv_ref[:, :PAIR] = (dk_sum[...] * SCALE).T.astype(LOW)
    dkv_ref[:, PAIR:] = dv_sum[...].T.astype(LOW)


def backward_call(own, first, kv, query, d_attn, lse, attended, key_mark, query_mark, dq):
    rows, width = query.shape
    pairs = width // PAIR
    whole = lambda shape: pl.BlockSpec(shape, lambda pair: (0,) * len(shape))
    columns = pl.BlockSpec((rows, PAIR), lambda pair: (0, pair))
    across = pl.BlockSpec((PAIR, rows), lambda pair: (pair, 0))
    line = pl.BlockSpec((None, 2, rows), lambda pair: (pair, 0, 0))
    double = pl.BlockSpec((rows, 2 * PAIR), lambda pair: (0, pair))
    in_specs = [double, columns, columns, line, across, whole(key_mark.shape), whole(query_mark.shape)]
    operands = [kv, query, d_attn, lse, attended, key_mark, query_mark]
    if not first:
        in_specs.append(across)
        operands.append(dq)
    dq_shape = jax.ShapeDtypeStruct((rows, width), LOW) if own else jax.ShapeDtypeStruct((width, rows), WIDE)
    return pl.pallas_call(
        functools.partial(backward_kernel, own, first),
        grid=(pairs,),
        in_specs=in_specs,
        out_specs=[double, columns if own else across],
        out_shape=[jax.ShapeDtypeStruct((rows, 2 * width), LOW), dq_shape],
        scratch_shapes=[pltpu.VMEM((PAIR, rows), WIDE), pltpu.VMEM((PAIR, rows), WIDE)],
        name="back_own" if own else "back_shard",
        cost_estimate=pl.CostEstimate(
            flops=26 * rows * rows * width, bytes_accessed=24 * rows * width, transcendentals=0
        ),
        compiler_params=pltpu.CompilerParams(vmem_limit_bytes=48 * 2**20),
    )(*operands)


def on_device(
    inputs, positions, segments, gain_attn, w_qkv, w_out, gain_mlp, w_up, b_up, w_down, cotangent
):
    rows, width = inputs.shape
    pairs = width // PAIR
    place = lax.axis_index("blk")
    w_query = w_qkv[:, :width]
    w_kv = (
        w_qkv[:, width:].reshape(width, 2, pairs, PAIR).swapaxes(1, 2).reshape(width, 2 * width)
    )

    def send(value, pairs_of_places):
        return lax.ppermute(value, "blk", pairs_of_places)

    hidden = inputs + position_table(positions, width)
    normed_attn, inverse_attn = normalize(hidden)
    a_low = (normed_attn * gain_attn).astype(LOW)

    near = [(0, 1), (1, 0), (2, 3), (3, 2)]
    middle = [(1, 2), (2, 1)]
    outward = [(1, 0), (2, 3)]
    inward = [(0, 1), (3, 2)]
    table = jnp.array([[0, 1, 2, 3], [1, 0, 2, 3], [2, 3, 1, 0], [3, 2, 1, 0]], jnp.int32)
    shard_1 = send(a_low, near)
    shard_2_middle = send(a_low, middle)
    shard_2 = shard_2_middle + send(shard_2_middle, outward)
    shard_3_middle = send(shard_1, middle)
    shard_3 = shard_3_middle + send(shard_3_middle, outward)
    shards = [a_low, shard_1, shard_2, shard_3]

    seg_query = lax.dynamic_slice_in_dim(segments, place * rows, rows)
    marks = [(seg_query[:, None], seg_query[None, :])]
    for index in range(1, 4):
        other = lax.dynamic_index_in_dim(table[:, index], place, keepdims=False)
        seg_key = lax.dynamic_slice_in_dim(segments, other * rows, rows)
        later_first = jnp.where(other > place, seg_key[0], seg_query[0])
        earlier_last = jnp.where(other > place, seg_query[-1], seg_key[-1])
        clip = jnp.where(later_first == earlier_last, later_first, -1)
        marks.append(
            ((seg_key == clip).astype(jnp.int32)[:, None], (seg_query == clip).astype(jnp.int32)[:, None])
        )

    query = dot(a_low, w_query, NN).astype(LOW)
    kvs, state = [], None
    for index in range(4):
        kv, *state = forward_call(
            index == 0, index == 3, shards[index], w_kv, query, *marks[index], state
        )
        kvs.append(kv)
    attended, lse, _, attn_low = state

    resid = hidden + dot(attn_low, w_out, NN)
    normed_mlp, inverse_mlp = normalize(resid)
    b_low = (normed_mlp * gain_mlp).astype(LOW)
    pre_act = dot(b_low, w_up, NN) + b_up
    cumulative = 0.5 * (1.0 + lax.erf(pre_act * 0.7071067811865476))
    density = jnp.exp(-0.5 * pre_act * pre_act) * 0.3989422804014327
    z_low = (pre_act * cumulative).astype(LOW)
    outputs = resid + dot(z_low, w_down, NN)
    dy_low = cotangent.astype(LOW)
    grad_down = dot(z_low, dy_low, TN)
    d_gelu = dot(dy_low, w_down, NT)
    d_pre = (d_gelu * (cumulative + pre_act * density)).astype(LOW)
    grad_up = dot(b_low, d_pre, TN)
    grad_bias_up = jnp.sum(d_pre.astype(WIDE), axis=0)
    d_normed = dot(d_pre, w_up, NT)
    grad_gain_mlp = jnp.sum(d_normed * normed_mlp, axis=0)
    d_resid = cotangent + norm_back(d_normed * gain_mlp, normed_mlp, inverse_mlp)
    dr_low = d_resid.astype(LOW)
    grad_out = dot(attn_low, dr_low, TN)
    d_attn = dot(dr_low, w_out, NT).astype(LOW)

    everywhere = ("dp", "blk")
    sum_down, sum_up, sum_out = lax.psum(
        (grad_down.astype(LOW), grad_up.astype(LOW), grad_out.astype(LOW)), everywhere
    )

    dq = None
    parts, grad_kv = [None] * 4, 0.0
    for index in (3, 2, 1, 0):
        dkv, dq = backward_call(
            index == 0, index == 3, kvs[index], query, d_attn, lse, attended, *marks[index], dq
        )
        parts[index] = dot(dkv, w_kv, NT)
        grad_kv = grad_kv + dot(shards[index], dkv, TN)
    far = send(parts[3].astype(LOW), inward)
    mid_3 = send((parts[3] + far.astype(WIDE)).astype(LOW), middle)
    mid_2 = send(parts[2].astype(LOW), inward)
    last_1 = send((parts[2] + mid_2.astype(WIDE)).astype(LOW), middle)
    last_2 = send((parts[1] + mid_3.astype(WIDE)).astype(LOW), outward)
    last_3 = send(parts[1].astype(LOW), inward)
    d_normed_attn = (
        parts[0]
        + dot(dq, w_query, NT)
        + last_1.astype(WIDE)
        + last_2.astype(WIDE)
        + last_3.astype(WIDE)
    )
    grad_query = dot(a_low, dq, TN)
    grad_gain_attn = jnp.sum(d_normed_attn * normed_attn, axis=0)
    input_grad = d_resid + norm_back(d_normed_attn * gain_attn, normed_attn, inverse_attn)
    grad_kv = (
        grad_kv.astype(LOW).reshape(width, pairs, 2, PAIR).swapaxes(1, 2).reshape(width, 2 * width)
    )
    grad_qkv = jnp.concatenate([grad_query.astype(LOW), grad_kv], axis=1)
    small = jnp.concatenate([grad_gain_attn, grad_gain_mlp, grad_bias_up])
    sum_qkv, sum_small = lax.psum((grad_qkv, small), everywhere)
    return (
        outputs,
        input_grad,
        sum_small[:width],
        sum_qkv.astype(WIDE),
        sum_out.astype(WIDE),
        sum_small[width : 2 * width],
        sum_up.astype(WIDE),
        sum_small[2 * width :],
        sum_down.astype(WIDE),
    )


def solution(mesh):
    rows = P(("dp", "blk"), None)
    placed = (rows, P(("dp", "blk")), P("dp"), P(), P(), P(), P(), P(), P(), P(), rows)
    return jax.shard_map(
        on_device,
        mesh=mesh,
        in_specs=placed,
        out_specs=(rows, rows, P(), P(), P(), P(), P(), P(), P()),
        check_vma=False,
    )
```

```python
import functools
import math

import jax
import jax.numpy as jnp
from jax import lax
from jax.experimental import pallas as pl
from jax.experimental.pallas import tpu as pltpu
from jax.sharding import PartitionSpec as P

HEADS = 12
HEAD = 64
PAIR = 2 * HEAD
SCALE = HEAD**-0.5
LOG2E = 1.4426950408889634
MASKED = -1.0e9
QUERY_BLOCK = 384
EPS_NORM = 1e-06
LOW = jnp.bfloat16
WIDE = jnp.float32

NN = (((1,), (0,)), ((), ()))
NT = (((1,), (1,)), ((), ()))
TN = (((0,), (0,)), ((), ()))


def dot(left, right, dims):
    return lax.dot_general(left, right, dims, preferred_element_type=WIDE)


def position_table(positions, model_width):
    half_width = model_width // 2
    freqs = jnp.exp(jnp.arange(half_width, dtype=WIDE) * (-math.log(10000.0) / half_width))
    angles = positions.astype(WIDE)[:, None] * freqs[None, :]
    return jnp.concatenate([jnp.sin(angles), jnp.cos(angles)], axis=1)


def normalize(values):
    center = values - jnp.mean(values, axis=-1, keepdims=True)
    inverse = lax.rsqrt(jnp.mean(center * center, axis=-1, keepdims=True) + EPS_NORM)
    return center * inverse, inverse


def norm_back(grad_norm, normed, inverse):
    first = jnp.mean(grad_norm, axis=-1, keepdims=True)
    second = jnp.mean(grad_norm * normed, axis=-1, keepdims=True)
    return inverse * (grad_norm - first - normed * second)


def in_head(values, head):
    lanes = lax.broadcasted_iota(jnp.int32, values.shape, 1)
    return (lanes < HEAD) == (head == 0)


def only_head(values, head, other=None):
    other = jnp.zeros_like(values) if other is None else other
    return jnp.where(in_head(values, head), values, other)


def split_scaled(query):
    scaled = query.astype(WIDE) * (SCALE * LOG2E)
    high = scaled.astype(LOW)
    return high, (scaled - high.astype(WIDE)).astype(LOW)


def score_sides(key, query):
    high, low = split_scaled(query)
    key_side = jnp.concatenate([key, key], axis=1)
    query_side = [
        jnp.concatenate([only_head(high, head), only_head(low, head)], axis=1) for head in range(2)
    ]
    return key_side, query_side


def work_items(rows):
    return [(start, head) for start in range(0, rows, QUERY_BLOCK) for head in range(2)]


def whole(*shape):
    return pl.BlockSpec(shape, lambda pair: (0,) * len(shape))


def columns_of(rows, first=0):
    return pl.BlockSpec((rows, PAIR), lambda pair: (0, pair + first))


def forward_kernel(first, last, *refs):
    a_ref, wk_ref, wv_ref, q_ref, key_clip, query_clip = refs[:6]
    refs = refs[6:]
    if not first:
        acc_in, top_in, total_in = refs[:3]
        refs = refs[3:]
    k_ref, v_ref, acc_ref, top_ref, total_ref = refs[:5]
    attn_ref = refs[5] if last else None
    rows = q_ref.shape[0]
    kv = dot(a_ref[...], jnp.concatenate([wk_ref[...], wv_ref[...]], axis=1), NN).astype(LOW)
    key, value = kv[:, :PAIR], kv[:, PAIR:]
    k_ref[...] = key
    v_ref[...] = value
    value_t = value.T
    ones = jnp.ones((16, rows), LOW)
    value_rows = [
        jnp.concatenate([value_t[head * HEAD : (head + 1) * HEAD], ones], axis=0) for head in range(2)
    ]
    key_side, query_side = score_sides(key, q_ref[...])

    def scores(start, head):
        stop = start + QUERY_BLOCK
        result = dot(key_side, query_side[head][start:stop], NT)
        return jnp.where(key_clip[...] == query_clip[:, start:stop], result, MASKED)

    def weights(start, head, result):
        stop = start + QUERY_BLOCK
        top = jnp.max(result, axis=0, keepdims=True)
        if not first:
            top = jnp.maximum(top, top_in[head : head + 1, start:stop])
        return jnp.exp2(result - top).astype(LOW), top

    def attend(start, head, expd, top):
        stop = start + QUERY_BLOCK
        lanes, row = slice(head * HEAD, (head + 1) * HEAD), slice(head, head + 1)
        result = dot(value_rows[head], expd, NN)
        acc, total = result[:HEAD], result[HEAD : HEAD + 1]
        if not first:
            shrink = jnp.exp2(top_in[row, start:stop] - top)
            acc = acc_in[lanes, start:stop] * shrink + acc
            total = total_in[row, start:stop] * shrink + total
        if last:
            acc = acc * (1.0 / total)
            top = top + jnp.log(total) * LOG2E
        acc_ref[lanes, start:stop] = acc
        top_ref[row, start:stop] = top
        total_ref[row, start:stop] = total

    items = work_items(rows)
    result = scores(*items[0])
    before = None
    for index, item in enumerate(items):
        following = scores(*items[index + 1]) if index + 1 < len(items) else None
        done = weights(*item, result)
        if before is not None:
            attend(*before)
        before = (*item, *done)
        result = following
    attend(*before)
    if last:
        attn_ref[...] = acc_ref[...].T.astype(LOW)


def forward_call(first, last, a_shard, w_qkv, query, key_clip, query_clip, state):
    rows, width = query.shape
    pairs = width // PAIR
    across = pl.BlockSpec((PAIR, rows), lambda pair: (pair, 0))
    line = pl.BlockSpec((None, 2, rows), lambda pair: (pair, 0, 0))
    state_specs = [across, line, line]
    state_shapes = [
        jax.ShapeDtypeStruct((width, rows), WIDE),
        jax.ShapeDtypeStruct((pairs, 2, rows), WIDE),
        jax.ShapeDtypeStruct((pairs, 2, rows), WIDE),
    ]
    in_specs = [
        whole(rows, width),
        columns_of(width, pairs),
        columns_of(width, 2 * pairs),
        columns_of(rows),
        whole(rows, 1),
        whole(1, rows),
    ]
    operands = [a_shard, w_qkv, w_qkv, query, key_clip, query_clip]
    if not first:
        in_specs += state_specs
        operands += list(state)
    low_rows = jax.ShapeDtypeStruct((rows, width), LOW)
    out_specs = [columns_of(rows), columns_of(rows), *state_specs]
    out_shape = [low_rows, low_rows, *state_shapes]
    if last:
        out_specs.append(columns_of(rows))
        out_shape.append(low_rows)
    return pl.pallas_call(
        functools.partial(forward_kernel, first, last),
        grid=(pairs,),
        in_specs=in_specs,
        out_specs=out_specs,
        out_shape=out_shape,
        name="attend",
        cost_estimate=pl.CostEstimate(
            flops=20 * rows * rows * width, bytes_accessed=24 * rows * width, transcendentals=0
        ),
        compiler_params=pltpu.CompilerParams(vmem_limit_bytes=48 * 2**20),
    )(*operands)


def backward_pair(key, value, query, grad_t, lse, row_dots, key_clip, query_clip, add):
    rows = query.shape[0]
    grad = grad_t.T
    key_t, query_t = key.T, query.T
    key_side, query_side = score_sides(key, query)
    grad_side = [only_head(grad, head) for head in range(2)]
    for start, head in work_items(rows):
        stop = start + QUERY_BLOCK
        lanes, row = slice(head * HEAD, (head + 1) * HEAD), slice(head, head + 1)
        score = dot(key_side, query_side[head][start:stop], NT)
        score = jnp.where(key_clip == query_clip[:, start:stop], score, MASKED)
        probs = jnp.exp2(score - lse[row, start:stop])
        d_probs = dot(value, grad_side[head][start:stop], NT)
        d_scores = (probs * (d_probs - row_dots[row, start:stop])).astype(LOW)
        probs = probs.astype(LOW)
        dv = dot(grad_t[lanes, start:stop], probs, NT)
        dk = dot(query_t[lanes, start:stop], d_scores, NT)
        dq = dot(key_t[lanes], d_scores, NN)
        add(head, start, stop, dq, dk, dv)


def backward_kernel(first, last, *refs):
    k_ref, v_ref, q_ref, grad_ref, lse_ref, dots_ref, key_clip, query_clip, wk_ref, wv_ref = refs[:10]
    refs = refs[10:]
    if not first:
        dq_in = refs[0]
        refs = refs[1:]
    dk_ref, dv_ref, dq_ref, part_ref, dk_sum, dv_sum, dq_sum, dk_all, dv_all = refs
    pair = pl.program_id(0)
    rows = q_ref.shape[0]

    def add(head, start, stop, dq, dk, dv):
        lanes = slice(head * HEAD, (head + 1) * HEAD)
        if start == 0:
            dv_sum[lanes], dk_sum[lanes] = dv, dk
        else:
            dv_sum[lanes] += dv
            dk_sum[lanes] += dk
        if not first:
            dq = dq + dq_in[lanes, start:stop]
        if last:
            dq_sum[lanes, start:stop] = dq
        else:
            dq_ref[lanes, start:stop] = dq

    backward_pair(
        k_ref[...],
        v_ref[...],
        q_ref[...],
        grad_ref[...],
        lse_ref,
        dots_ref,
        key_clip[...],
        query_clip[...],
        add,
    )
    if last:
        dq_ref[...] = (dq_sum[...] * SCALE).T.astype(LOW)
    dk = (dk_sum[...] * SCALE).T.astype(LOW)
    dv = dv_sum[...].T.astype(LOW)
    dk_ref[...] = dk
    dv_ref[...] = dv
    dk_all[pair] = dk
    dv_all[pair] = dv

    @pl.when(pair == pl.num_programs(0) - 1)
    def _():
        pairs = dk_all.shape[0]
        dk_rows = jnp.concatenate([dk_all[index] for index in range(pairs)], axis=1)
        dv_rows = jnp.concatenate([dv_all[index] for index in range(pairs)], axis=1)
        part = dot(dk_rows, wk_ref[...], NT) + dot(dv_rows, wv_ref[...], NT)
        part_ref[...] = part.astype(part_ref.dtype)


def backward_call(first, last, key, value, query, grad_t, lse, row_dots, key_clip, query_clip, w_qkv, dq):
    rows, width = query.shape
    pairs = width // PAIR
    across = pl.BlockSpec((PAIR, rows), lambda pair: (pair, 0))
    line = pl.BlockSpec((None, 2, rows), lambda pair: (pair, 0, 0))
    columns = columns_of(rows)
    in_specs = [columns, columns, columns, across, line, line, whole(rows, 1), whole(1, rows)]
    in_specs += [
        pl.BlockSpec((width, width), lambda pair: (0, 1)),
        pl.BlockSpec((width, width), lambda pair: (0, 2)),
    ]
    operands = [key, value, query, grad_t, lse, row_dots, key_clip, query_clip, w_qkv, w_qkv]
    if not first:
        in_specs.append(across)
        operands.append(dq)
    low_rows = jax.ShapeDtypeStruct((rows, width), LOW)
    tall = pltpu.VMEM((PAIR, rows), WIDE)
    parts = pltpu.VMEM((pairs, rows, PAIR), LOW)
    return pl.pallas_call(
        functools.partial(backward_kernel, first, last),
        grid=(pairs,),
        in_specs=in_specs,
        out_specs=[columns, columns, columns if last else across, whole(rows, width)],
        out_shape=[
            low_rows,
            low_rows,
            low_rows if last else jax.ShapeDtypeStruct((width, rows), WIDE),
            jax.ShapeDtypeStruct((rows, width), WIDE if last else LOW),
        ],
        scratch_shapes=[tall, tall, tall, parts, parts],
        name="attend_back",
        cost_estimate=pl.CostEstimate(
            flops=40 * rows * rows * width, bytes_accessed=24 * rows * width, transcendentals=0
        ),
        compiler_params=pltpu.CompilerParams(vmem_limit_bytes=48 * 2**20),
    )(*operands)


MESH = pl.DeviceIdType.MESH
TURNS = ((0, 1, 2), (0, 2, 1))


def place_bits(turn):
    group, place = lax.axis_index("dp"), lax.axis_index("blk")
    steps = []
    for bit in TURNS[turn]:
        mine = group // (1 << bit) % 2
        steps.append((mine, (group + (1 - 2 * mine) * (1 << bit), place)))
    for bit in range(2):
        mine = place // (1 << bit) % 2
        steps.append((mine, (group, place + (1 - 2 * mine) * (1 << bit))))
    return steps


def remote(source, target, sems, index, device):
    return pltpu.make_async_remote_copy(
        src_ref=source,
        dst_ref=target,
        send_sem=sems[0].at[index],
        recv_sem=sems[1].at[index],
        device_id=device,
        device_id_type=MESH,
    )


def add_rows(total, start, term, rows, step):
    @pl.loop(0, rows // step)
    def _(index):
        here = pl.ds(pl.multiple_of(start + index * step, 16), step)
        there = pl.ds(pl.multiple_of(index * step, 16), step)
        total[here] = (total[here].astype(WIDE) + term[there].astype(WIDE)).astype(total.dtype)


class Sum:
    def __init__(self, turn, term, result, total, arrived, sems, local_sems):
        self.term, self.result, self.total, self.arrived = term, result, total, arrived
        self.sems, self.local_sems = sems, local_sems
        self.steps = place_bits(turn)
        self.count = len(self.steps)
        rows = total.shape[0]
        self.first = self.steps[0][0] * rows
        self.keep = [(0, rows)]
        for mine, _ in self.steps[1:]:
            start, size = self.keep[-1]
            self.keep.append((start + mine * (size // 2), size // 2))
        self.block = min(rows, self.keep[-1][1])
        self.pending = {}

    def _rows(self, ref, start, size):
        return ref.at[pl.ds(pl.multiple_of(start, 16), size)]

    def load(self):
        source = self._rows(self.term, self.first, self.total.shape[0])
        return pltpu.make_async_copy(source, self.total, self.local_sems.at[0])

    def store(self):
        start, size = self.keep[-1]
        source = self._rows(self.total, start, size)
        target = self._rows(self.result, self.first + start, size)
        return pltpu.make_async_copy(source, target, self.local_sems.at[1])

    def gather(self, step):
        mine, device = self.steps[step]
        start, size = self.keep[step]
        if step == 0:
            rows = self.total.shape[0]
            source = self._rows(self.term, (1 - mine) * rows, rows)
        else:
            upper, _ = self.keep[step - 1]
            source = self._rows(self.total, upper + (1 - mine) * size, size)
        return remote(source, self.arrived[step], self.sems, step, device)

    def start_sum(self, step):
        if step == 0:
            self.load().start()
        self.gather(step).start()

    def finish_sum(self, step):
        if step == 0:
            self.load().wait()
        self.gather(step).wait()
        start, size = self.keep[step]
        add_rows(self.total, start, self.arrived[step], size, self.block)

    def spread(self, step):
        start, size = self.keep[step]
        here = self._rows(self.result, self.first + start, size)
        return remote(here, here, self.sems, self.count + step, self.steps[step][1])

    def start_spread(self, step):
        if step == self.count - 1:
            self.store().start()
            self.store().wait()
        self.spread(step).start()

    def finish_spread(self, step):
        self.spread(step).wait()


def greet():
    group, place = lax.axis_index("dp"), lax.axis_index("blk")
    devices = [device for _, device in place_bits(0)]
    devices.append((group, 3 - place))
    barrier = pltpu.get_barrier_semaphore()
    for device in devices:
        pl.semaphore_signal(barrier, inc=1, device_id=device, device_id_type=MESH)
    pl.semaphore_wait(barrier, len(devices))


def arrivals(rows, lanes, steps=5):
    return [pltpu.VMEM((rows >> (step + 1), lanes), LOW) for step in range(steps)]


def sum_kernel(shapes, *refs):
    count = len(shapes)
    terms, small_in = refs[:count], refs[count]
    results, small_out = refs[count + 1 : 2 * count + 1], refs[2 * count + 1]
    refs = refs[2 * count + 2 :]
    totals = refs[:count]
    arrived = [refs[count + 5 * index : count + 5 * index + 5] for index in range(count)]
    small_arrived, sends, receives, locals_, small_sends, small_receives = refs[6 * count :]
    greet()
    sums = [
        Sum(
            index % 2,
            terms[index],
            results[index],
            totals[index],
            arrived[index],
            (sends.at[index], receives.at[index]),
            locals_.at[index],
        )
        for index in range(count)
    ]
    small_out[...] = small_in[...]
    small_steps = place_bits(0)

    def small(step):
        return remote(
            small_out, small_arrived.at[step], (small_sends, small_receives), step, small_steps[step][1]
        )

    for each in sums:
        each.start_sum(0)
    for step in range(5):
        small(step).start()
        for each in sums:
            each.finish_sum(step)
            if step < 4:
                each.start_sum(step + 1)
            else:
                each.start_spread(step)
        small(step).wait()
        small_out[...] += small_arrived[step]
    for step in reversed(range(5)):
        for each in sums:
            each.finish_spread(step)
            if step:
                each.start_spread(step - 1)


def sum_call(terms, small):
    shapes = [term.shape for term in terms]
    count = len(shapes)
    anywhere = pl.BlockSpec(memory_space=pl.ANY)
    inside = pl.BlockSpec(memory_space=pltpu.VMEM)
    scratch = [pltpu.VMEM((rows // 2, lanes), LOW) for rows, lanes in shapes]
    for rows, lanes in shapes:
        scratch += arrivals(rows, lanes)
    scratch += [
        pltpu.VMEM((5, *small.shape), WIDE),
        pltpu.SemaphoreType.DMA((count, 10)),
        pltpu.SemaphoreType.DMA((count, 10)),
        pltpu.SemaphoreType.DMA((count, 2)),
        pltpu.SemaphoreType.DMA((5,)),
        pltpu.SemaphoreType.DMA((5,)),
    ]
    return pl.pallas_call(
        functools.partial(sum_kernel, shapes),
        in_specs=[anywhere] * count + [inside],
        out_specs=[anywhere] * count + [inside],
        out_shape=[jax.ShapeDtypeStruct(shape, LOW) for shape in shapes]
        + [jax.ShapeDtypeStruct(small.shape, WIDE)],
        scratch_shapes=scratch,
        name="sum_gradients",
        compiler_params=pltpu.CompilerParams(
            collective_id=1, has_side_effects=True, vmem_limit_bytes=60 * 2**20
        ),
    )(*terms, small)


def on_device(
    groups, inputs, positions, segments, gain_attn, w_qkv, w_out, gain_mlp, w_up, b_up, w_down, cotangent
):
    rows, width = inputs.shape
    pairs = width // PAIR
    place = lax.axis_index("blk")
    w_query = w_qkv[:, :width]

    def send(value, pairs_of_places):
        return lax.ppermute(value, "blk", pairs_of_places)

    hidden = inputs + position_table(positions, width)
    normed_attn, inverse_attn = normalize(hidden)
    a_low = (normed_attn * gain_attn).astype(LOW)

    near = [(0, 1), (1, 0), (2, 3), (3, 2)]
    middle = [(1, 2), (2, 1)]
    outward = [(1, 0), (2, 3)]
    inward = [(0, 1), (3, 2)]
    table = jnp.array([[0, 1, 2, 3], [1, 0, 2, 3], [2, 3, 1, 0], [3, 2, 1, 0]], jnp.int32)
    shard_1 = send(a_low, near)
    shard_2_middle = send(a_low, middle)
    shard_2 = shard_2_middle + send(shard_2_middle, outward)
    shard_3_middle = send(shard_1, middle)
    shard_3 = shard_3_middle + send(shard_3_middle, outward)
    shards = [a_low, shard_1, shard_2, shard_3]

    def clips_of(index):
        other = lax.dynamic_index_in_dim(table[:, index], place, keepdims=False)
        return lax.dynamic_slice_in_dim(segments, other * rows, rows)

    clips = [clips_of(index)[:, None] for index in range(4)]
    query_clip = lax.dynamic_slice_in_dim(segments, place * rows, rows)[None, :]

    query = dot(a_low, w_query, NN).astype(LOW)
    keys, values, state = [], [], None
    for index in range(4):
        key, value, *state = forward_call(
            index == 0, index == 3, shards[index], w_qkv, query, clips[index], query_clip, state
        )
        keys.append(key)
        values.append(value)
    attended, lse, _, attn_low = state

    resid = hidden + dot(attn_low, w_out, NN)
    normed_mlp, inverse_mlp = normalize(resid)
    b_low = (normed_mlp * gain_mlp).astype(LOW)
    pre_act = dot(b_low, w_up, NN) + b_up
    cumulative = 0.5 * (1.0 + lax.erf(pre_act * 0.7071067811865476))
    density = jnp.exp(-0.5 * pre_act * pre_act) * 0.3989422804014327
    z_low = (pre_act * cumulative).astype(LOW)
    outputs = resid + dot(z_low, w_down, NN)
    dy_low = cotangent.astype(LOW)
    grad_down = dot(z_low, dy_low, TN).astype(LOW)
    d_gelu = dot(dy_low, w_down, NT)
    d_pre = (d_gelu * (cumulative + pre_act * density)).astype(LOW)
    grad_up_t = dot(d_pre, b_low, TN).astype(LOW)
    grad_bias_up = jnp.sum(d_pre.astype(WIDE), axis=0)
    d_normed = dot(d_pre, w_up, NT)
    grad_gain_mlp = jnp.sum(d_normed * normed_mlp, axis=0)
    d_resid = cotangent + norm_back(d_normed * gain_mlp, normed_mlp, inverse_mlp)
    dr_low = d_resid.astype(LOW)
    grad_out = dot(attn_low, dr_low, TN).astype(LOW)
    d_attn_t = dot(w_out, dr_low, NT).astype(LOW)
    row_dots = jnp.sum(
        (d_attn_t.astype(WIDE) * attended).reshape(pairs, 2, HEAD, rows), axis=2
    )

    everywhere = ("dp", "blk")

    def back(index, dq):
        return backward_call(
            index == 3,
            index == 0,
            keys[index],
            values[index],
            query,
            d_attn_t,
            lse,
            row_dots,
            clips[index],
            query_clip,
            w_qkv,
            dq,
        )

    dk_3, dv_3, dq, part_3 = back(3, None)
    far = send(part_3, inward)
    dk_2, dv_2, dq, part_2 = back(2, dq)
    far, part_2, dq = lax.optimization_barrier((far, part_2, dq))
    onward = (part_3.astype(WIDE) + far.astype(WIDE)).astype(LOW)
    mid_3 = send(onward, middle)
    mid_2 = send(part_2, inward)
    dq, onward = lax.optimization_barrier((dq, onward))
    dk_1, dv_1, dq, part_1 = back(1, dq)
    mid_3, mid_2, part_1, dq = lax.optimization_barrier((mid_3, mid_2, part_1, dq))
    onward_1 = (part_2.astype(WIDE) + mid_2.astype(WIDE)).astype(LOW)
    onward_2 = (part_1.astype(WIDE) + mid_3.astype(WIDE)).astype(LOW)
    last_1 = send(onward_1, middle)
    last_2 = send(onward_2, outward)
    last_3 = send(part_1, inward)
    dq, onward_1, onward_2 = lax.optimization_barrier((dq, onward_1, onward_2))
    dk_0, dv_0, dq, part_0 = back(0, dq)
    grad_query = dot(a_low, dq, TN).astype(LOW)
    d_keys, d_values = (dk_0, dk_1, dk_2, dk_3), (dv_0, dv_1, dv_2, dv_3)
    grad_key = sum(dot(shard, term, TN) for shard, term in zip(shards, d_keys)).astype(LOW)
    grad_value = sum(dot(shard, term, TN) for shard, term in zip(shards, d_values)).astype(LOW)
    d_normed_attn = (
        part_0
        + dot(dq, w_query, NT)
        + last_1.astype(WIDE)
        + last_2.astype(WIDE)
        + last_3.astype(WIDE)
    )
    grad_gain_attn = jnp.sum(d_normed_attn * normed_attn, axis=0)
    input_grad = d_resid + norm_back(d_normed_attn * gain_attn, normed_attn, inverse_attn)
    small = jnp.concatenate([grad_gain_attn, grad_gain_mlp, grad_bias_up])
    if groups == 8:
        stack = lambda matrix: matrix.reshape(width, pairs, PAIR).swapaxes(0, 1).reshape(-1, PAIR)
        unstack = lambda matrix: matrix.reshape(pairs, width, PAIR).swapaxes(0, 1).reshape(width, width)
        half = grad_down.shape[0] // 2
        terms = [grad_down[:half], grad_down[half:], grad_up_t[:half], grad_up_t[half:]]
        terms += [stack(matrix) for matrix in (grad_out, grad_query, grad_key, grad_value)]
        *sums, sum_small = sum_call(terms, jnp.pad(small.reshape(6, width), ((0, 2), (0, 0))))
        sum_down = jnp.concatenate(sums[:2], axis=0)
        sum_up_t = jnp.concatenate(sums[2:4], axis=0)
        sum_out, *sum_qkv = [unstack(matrix) for matrix in sums[4:]]
        sum_small = sum_small[:6].reshape(-1)
    else:
        sums = lax.psum(
            (grad_down, grad_up_t, grad_out, grad_query, grad_key, grad_value), everywhere
        )
        sum_small = lax.psum(small, everywhere)
        sum_down, sum_up_t, sum_out, *sum_qkv = sums
    return (
        outputs,
        input_grad,
        sum_small[:width],
        jnp.concatenate(sum_qkv, axis=1).astype(WIDE),
        sum_out.astype(WIDE),
        sum_small[width : 2 * width],
        sum_up_t.T.astype(WIDE),
        sum_small[2 * width :],
        sum_down.astype(WIDE),
    )


def solution(mesh):
    rows = P(("dp", "blk"), None)
    placed = (rows, P(("dp", "blk")), P("dp"), P(), P(), P(), P(), P(), P(), P(), rows)
    return jax.shard_map(
        functools.partial(on_device, mesh.shape["dp"]),
        mesh=mesh,
        in_specs=placed,
        out_specs=(rows, rows, P(), P(), P(), P(), P(), P(), P()),
        check_vma=False,
    )
```

```python
import functools
import math

import jax
import jax.numpy as jnp
from jax import lax
from jax.experimental import pallas as pl
from jax.experimental.pallas import tpu as pltpu
from jax.sharding import PartitionSpec as P

HEADS = 12
HEAD = 64
PAIR = 2 * HEAD
SCALE = HEAD**-0.5
LOG2E = 1.4426950408889634
MASKED = -1.0e9
QUERY_BLOCK = 384
EPS_NORM = 1e-06
LOW = jnp.bfloat16
WIDE = jnp.float32

NN = (((1,), (0,)), ((), ()))
NT = (((1,), (1,)), ((), ()))
TN = (((0,), (0,)), ((), ()))


def dot(left, right, dims):
    return lax.dot_general(left, right, dims, preferred_element_type=WIDE)


def position_table(positions, model_width):
    half_width = model_width // 2
    freqs = jnp.exp(jnp.arange(half_width, dtype=WIDE) * (-math.log(10000.0) / half_width))
    angles = positions.astype(WIDE)[:, None] * freqs[None, :]
    return jnp.concatenate([jnp.sin(angles), jnp.cos(angles)], axis=1)


def normalize(values):
    center = values - jnp.mean(values, axis=-1, keepdims=True)
    inverse = lax.rsqrt(jnp.mean(center * center, axis=-1, keepdims=True) + EPS_NORM)
    return center * inverse, inverse


def norm_back(grad_norm, normed, inverse):
    first = jnp.mean(grad_norm, axis=-1, keepdims=True)
    second = jnp.mean(grad_norm * normed, axis=-1, keepdims=True)
    return inverse * (grad_norm - first - normed * second)


def in_head(values, head):
    lanes = lax.broadcasted_iota(jnp.int32, values.shape, 1)
    return (lanes < HEAD) == (head == 0)


def only_head(values, head, other=None):
    other = jnp.zeros_like(values) if other is None else other
    return jnp.where(in_head(values, head), values, other)


def split_scaled(query):
    scaled = query.astype(WIDE) * (SCALE * LOG2E)
    high = scaled.astype(LOW)
    return high, (scaled - high.astype(WIDE)).astype(LOW)


def score_sides(key, query):
    high, low = split_scaled(query)
    key_side = jnp.concatenate([key, key], axis=1)
    query_side = [
        jnp.concatenate([only_head(high, head), only_head(low, head)], axis=1) for head in range(2)
    ]
    return key_side, query_side


def work_items(rows):
    return [(start, head) for start in range(0, rows, QUERY_BLOCK) for head in range(2)]


def whole(*shape):
    return pl.BlockSpec(shape, lambda pair: (0,) * len(shape))


def columns_of(rows, first=0):
    return pl.BlockSpec((rows, PAIR), lambda pair: (0, pair + first))


def forward_kernel(first, last, *refs):
    a_ref, wk_ref, wv_ref, q_ref, key_clip, query_clip = refs[:6]
    refs = refs[6:]
    if not first:
        acc_in, top_in, total_in = refs[:3]
        refs = refs[3:]
    k_ref, v_ref, acc_ref, top_ref, total_ref = refs[:5]
    attn_ref = refs[5] if last else None
    rows = q_ref.shape[0]
    kv = dot(a_ref[...], jnp.concatenate([wk_ref[...], wv_ref[...]], axis=1), NN).astype(LOW)
    key, value = kv[:, :PAIR], kv[:, PAIR:]
    k_ref[...] = key
    v_ref[...] = value
    value_t = value.T
    ones = jnp.ones((16, rows), LOW)
    value_rows = [
        jnp.concatenate([value_t[head * HEAD : (head + 1) * HEAD], ones], axis=0) for head in range(2)
    ]
    key_side, query_side = score_sides(key, q_ref[...])

    def scores(start, head):
        stop = start + QUERY_BLOCK
        result = dot(key_side, query_side[head][start:stop], NT)
        return jnp.where(key_clip[...] == query_clip[:, start:stop], result, MASKED)

    def weights(start, head, result):
        stop = start + QUERY_BLOCK
        top = jnp.max(result, axis=0, keepdims=True)
        if not first:
            top = jnp.maximum(top, top_in[head : head + 1, start:stop])
        return jnp.exp2(result - top).astype(LOW), top

    def attend(start, head, expd, top):
        stop = start + QUERY_BLOCK
        lanes, row = slice(head * HEAD, (head + 1) * HEAD), slice(head, head + 1)
        result = dot(value_rows[head], expd, NN)
        acc, total = result[:HEAD], result[HEAD : HEAD + 1]
        if not first:
            shrink = jnp.exp2(top_in[row, start:stop] - top)
            acc = acc_in[lanes, start:stop] * shrink + acc
            total = total_in[row, start:stop] * shrink + total
        if last:
            acc = acc * (1.0 / total)
            top = top + jnp.log(total) * LOG2E
        acc_ref[lanes, start:stop] = acc
        top_ref[row, start:stop] = top
        total_ref[row, start:stop] = total

    items = work_items(rows)
    result = scores(*items[0])
    before = None
    for index, item in enumerate(items):
        following = scores(*items[index + 1]) if index + 1 < len(items) else None
        done = weights(*item, result)
        if before is not None:
            attend(*before)
        before = (*item, *done)
        result = following
    attend(*before)
    if last:
        attn_ref[...] = acc_ref[...].T.astype(LOW)


def forward_call(first, last, a_shard, w_qkv, query, key_clip, query_clip, state):
    rows, width = query.shape
    pairs = width // PAIR
    across = pl.BlockSpec((PAIR, rows), lambda pair: (pair, 0))
    line = pl.BlockSpec((None, 2, rows), lambda pair: (pair, 0, 0))
    state_specs = [across, line, line]
    state_shapes = [
        jax.ShapeDtypeStruct((width, rows), WIDE),
        jax.ShapeDtypeStruct((pairs, 2, rows), WIDE),
        jax.ShapeDtypeStruct((pairs, 2, rows), WIDE),
    ]
    in_specs = [
        whole(rows, width),
        columns_of(width, pairs),
        columns_of(width, 2 * pairs),
        columns_of(rows),
        whole(rows, 1),
        whole(1, rows),
    ]
    operands = [a_shard, w_qkv, w_qkv, query, key_clip, query_clip]
    if not first:
        in_specs += state_specs
        operands += list(state)
    low_rows = jax.ShapeDtypeStruct((rows, width), LOW)
    out_specs = [columns_of(rows), columns_of(rows), *state_specs]
    out_shape = [low_rows, low_rows, *state_shapes]
    if last:
        out_specs.append(columns_of(rows))
        out_shape.append(low_rows)
    return pl.pallas_call(
        functools.partial(forward_kernel, first, last),
        grid=(pairs,),
        in_specs=in_specs,
        out_specs=out_specs,
        out_shape=out_shape,
        name="attend",
        cost_estimate=pl.CostEstimate(
            flops=20 * rows * rows * width, bytes_accessed=24 * rows * width, transcendentals=0
        ),
        compiler_params=pltpu.CompilerParams(vmem_limit_bytes=48 * 2**20),
    )(*operands)


def backward_pair(key, value, query, grad_t, lse, row_dots, key_clip, query_clip, add):
    rows = query.shape[0]
    grad = grad_t.T
    key_t, query_t = key.T, query.T
    key_side, query_side = score_sides(key, query)
    grad_side = [only_head(grad, head) for head in range(2)]
    for start, head in work_items(rows):
        stop = start + QUERY_BLOCK
        lanes, row = slice(head * HEAD, (head + 1) * HEAD), slice(head, head + 1)
        score = dot(key_side, query_side[head][start:stop], NT)
        score = jnp.where(key_clip == query_clip[:, start:stop], score, MASKED)
        probs = jnp.exp2(score - lse[row, start:stop])
        d_probs = dot(value, grad_side[head][start:stop], NT)
        d_scores = (probs * (d_probs - row_dots[row, start:stop])).astype(LOW)
        probs = probs.astype(LOW)
        dv = dot(grad_t[lanes, start:stop], probs, NT)
        dk = dot(query_t[lanes, start:stop], d_scores, NT)
        dq = dot(key_t[lanes], d_scores, NN)
        add(head, start, stop, dq, dk, dv)


def backward_kernel(first, last, *refs):
    k_ref, v_ref, q_ref, grad_ref, lse_ref, dots_ref, key_clip, query_clip, wk_ref, wv_ref = refs[:10]
    refs = refs[10:]
    if not first:
        dq_in = refs[0]
        refs = refs[1:]
    dk_ref, dv_ref, dq_ref, part_ref, dk_sum, dv_sum, dq_sum, dk_all, dv_all = refs
    pair = pl.program_id(0)
    rows = q_ref.shape[0]

    def add(head, start, stop, dq, dk, dv):
        lanes = slice(head * HEAD, (head + 1) * HEAD)
        if start == 0:
            dv_sum[lanes], dk_sum[lanes] = dv, dk
        else:
            dv_sum[lanes] += dv
            dk_sum[lanes] += dk
        if not first:
            dq = dq + dq_in[lanes, start:stop]
        if last:
            dq_sum[lanes, start:stop] = dq
        else:
            dq_ref[lanes, start:stop] = dq

    backward_pair(
        k_ref[...],
        v_ref[...],
        q_ref[...],
        grad_ref[...],
        lse_ref,
        dots_ref,
        key_clip[...],
        query_clip[...],
        add,
    )
    if last:
        dq_ref[...] = (dq_sum[...] * SCALE).T.astype(LOW)
    dk = (dk_sum[...] * SCALE).T.astype(LOW)
    dv = dv_sum[...].T.astype(LOW)
    dk_ref[...] = dk
    dv_ref[...] = dv
    dk_all[pair] = dk
    dv_all[pair] = dv

    @pl.when(pair == pl.num_programs(0) - 1)
    def _():
        pairs = dk_all.shape[0]
        dk_rows = jnp.concatenate([dk_all[index] for index in range(pairs)], axis=1)
        dv_rows = jnp.concatenate([dv_all[index] for index in range(pairs)], axis=1)
        part = dot(dk_rows, wk_ref[...], NT) + dot(dv_rows, wv_ref[...], NT)
        part_ref[...] = part.astype(part_ref.dtype)


def backward_call(first, last, key, value, query, grad_t, lse, row_dots, key_clip, query_clip, w_qkv, dq):
    rows, width = query.shape
    pairs = width // PAIR
    across = pl.BlockSpec((PAIR, rows), lambda pair: (pair, 0))
    line = pl.BlockSpec((None, 2, rows), lambda pair: (pair, 0, 0))
    columns = columns_of(rows)
    in_specs = [columns, columns, columns, across, line, line, whole(rows, 1), whole(1, rows)]
    in_specs += [
        pl.BlockSpec((width, width), lambda pair: (0, 1)),
        pl.BlockSpec((width, width), lambda pair: (0, 2)),
    ]
    operands = [key, value, query, grad_t, lse, row_dots, key_clip, query_clip, w_qkv, w_qkv]
    if not first:
        in_specs.append(across)
        operands.append(dq)
    low_rows = jax.ShapeDtypeStruct((rows, width), LOW)
    tall = pltpu.VMEM((PAIR, rows), WIDE)
    parts = pltpu.VMEM((pairs, rows, PAIR), LOW)
    return pl.pallas_call(
        functools.partial(backward_kernel, first, last),
        grid=(pairs,),
        in_specs=in_specs,
        out_specs=[columns, columns, columns if last else across, whole(rows, width)],
        out_shape=[
            low_rows,
            low_rows,
            low_rows if last else jax.ShapeDtypeStruct((width, rows), WIDE),
            jax.ShapeDtypeStruct((rows, width), WIDE if last else LOW),
        ],
        scratch_shapes=[tall, tall, tall, parts, parts],
        name="attend_back",
        cost_estimate=pl.CostEstimate(
            flops=40 * rows * rows * width, bytes_accessed=24 * rows * width, transcendentals=0
        ),
        compiler_params=pltpu.CompilerParams(vmem_limit_bytes=48 * 2**20),
    )(*operands)


MESH = pl.DeviceIdType.MESH
TURNS = ((0, 1, 2), (0, 2, 1))
STEPS = 5
ADD_ROWS = 48


def place_bits(turn):
    group, place = lax.axis_index("dp"), lax.axis_index("blk")
    steps = []
    for bit in TURNS[turn]:
        mine = group // (1 << bit) % 2
        steps.append((mine, (group + (1 - 2 * mine) * (1 << bit), place)))
    for bit in range(2):
        mine = place // (1 << bit) % 2
        steps.append((mine, (group, place + (1 - 2 * mine) * (1 << bit))))
    return steps


def remote(source, target, sems, index, device):
    return pltpu.make_async_remote_copy(
        src_ref=source,
        dst_ref=target,
        send_sem=sems[0].at[index],
        recv_sem=sems[1].at[index],
        device_id=device,
        device_id_type=MESH,
    )


def part_of(row, rows, column, columns):
    row = row if isinstance(row, int) else pl.multiple_of(row, 16)
    column = column if isinstance(column, int) else pl.multiple_of(column, PAIR)
    return pl.ds(row, rows), pl.ds(column, columns)


def add_block(total, term, row=0, column=0):
    rows, columns = term.shape

    @pl.loop(0, rows // ADD_ROWS)
    def _(index):
        here = part_of(row + index * ADD_ROWS, ADD_ROWS, column, columns)
        there = part_of(index * ADD_ROWS, ADD_ROWS, 0, columns)
        total[here] = (total[here].astype(WIDE) + term[there].astype(WIDE)).astype(total.dtype)


def halves(shape, axes):
    shapes = []
    for axis in axes:
        shape = (shape[0] // 2, shape[1]) if axis == "r" else (shape[0], shape[1] // 2)
        shapes.append(shape)
    return shapes


class Sum:
    def __init__(self, turn, axes, corner, shape, term, result, total, arrived, sems, local_sems):
        self.term, self.result, self.total, self.arrived = term, result, total, arrived
        self.sems, self.local_sems = sems, local_sems
        self.steps = place_bits(turn)
        self.shapes = halves(shape, axes)
        self.kept, self.left = [], []
        row, column = corner
        for axis, (rows, columns), (mine, _) in zip(axes, self.shapes, self.steps):
            down, across = (rows, 0) if axis == "r" else (0, columns)
            self.left.append((row + (1 - mine) * down, rows, column + (1 - mine) * across, columns))
            row, column = row + mine * down, column + mine * across
            self.kept.append((row, rows, column, columns))

    def inside(self, place):
        row, rows, column, columns = place
        return part_of(row - self.kept[0][0], rows, column - self.kept[0][2], columns)

    def load(self):
        return pltpu.make_async_copy(
            self.term.at[part_of(*self.kept[0])], self.total, self.local_sems.at[0]
        )

    def store(self):
        return pltpu.make_async_copy(
            self.total.at[self.inside(self.kept[-1])],
            self.result.at[part_of(*self.kept[-1])],
            self.local_sems.at[1],
        )

    def gather(self, step):
        place = self.left[step]
        source = self.term.at[part_of(*place)] if step == 0 else self.total.at[self.inside(place)]
        return remote(source, self.arrived[step], self.sems, step, self.steps[step][1])

    def spread(self, step):
        here = self.result.at[part_of(*self.kept[step])]
        return remote(here, here, self.sems, STEPS + step, self.steps[step][1])

    def start(self):
        self.load().start()
        self.gather(0).start()

    def turn(self, tick):
        if tick < STEPS:
            if tick == 0:
                self.load().wait()
            self.gather(tick).wait()
            row, _, column, _ = self.kept[tick]
            add_block(self.total, self.arrived[tick], row - self.kept[0][0], column - self.kept[0][2])
            if tick + 1 < STEPS:
                self.gather(tick + 1).start()
            else:
                self.store().start()
                self.store().wait()
                self.spread(STEPS - 1).start()
        else:
            step = 2 * STEPS - 1 - tick
            self.spread(step).wait()
            if step:
                self.spread(step - 1).start()


def greet():
    group, place = lax.axis_index("dp"), lax.axis_index("blk")
    devices = [device for _, device in place_bits(0)]
    devices.append((group, 3 - place))
    barrier = pltpu.get_barrier_semaphore()
    for device in devices:
        pl.semaphore_signal(barrier, inc=1, device_id=device, device_id_type=MESH)
    pl.semaphore_wait(barrier, len(devices))


PARTS = (
    ("down", (0, 0), (1536, 768), "rrrrr", 0, (2, 6, 9, 12, 14, 16, 18, 20, 22, 23)),
    ("down", (1536, 0), (1536, 768), "rrrrr", 1, (2, 6, 9, 12, 14, 16, 18, 20, 22, 23)),
    ("up", (0, 0), (768, 1536), "rrrcc", 0, (3, 8, 11, 13, 15, 17, 19, 21, 24, 24)),
    ("up", (0, 1536), (768, 1536), "rrrcc", 1, (3, 8, 11, 13, 15, 17, 19, 21, 24, 24)),
    ("out", (0, 0), (768, 768), "rrrrc", 0, (4, 9, 11, 13, 15, 17, 19, 21, 23, 24)),
    ("qkv", (0, 0), (768, 512), "rrrrc", 0, None),
    ("qkv", (0, 512), (768, 512), "rrrrc", 1, None),
    ("qkv", (0, 1024), (768, 512), "rrrrc", 0, None),
    ("qkv", (0, 1536), (768, 768), "rrrrc", 1, None),
)


def gradient_kernel(*refs):
    keys, values, shards = refs[:4], refs[4:8], refs[8:12]
    q_ref, grad_ref, lse_ref, dots_ref, clips, query_clip, w_ref = refs[12:19]
    down_in, up_in, out_in, small_in = refs[19:23]
    down_out, up_out, out_out, qkv_out, small_out, input_out = refs[23:29]
    refs = refs[29:]
    kv_slot, a_slot, dq_sum, dk_sum, dv_sum, dk_all, dv_all, grad_k, grad_v, parts = refs[:10]
    far, mid_2, mid_3, last_1, last_3, qkv_term, clip_slot, small_arrived = refs[10:18]
    input_sum = dq_sum
    kv_sems, a_sem, line_sends, line_receives, sends, receives, locals_ = refs[18:25]
    small_sends, small_receives, out_sem, clip_sem = refs[25:29]
    refs = refs[29:]
    rows, width = q_ref.shape
    pairs = width // PAIR
    pieces = 4 * pairs
    group, place = lax.axis_index("dp"), lax.axis_index("blk")
    near = (group, place + 1 - 2 * (place % 2))
    across = (group, 3 - place)
    at_end = place % 3 == 0

    arrays = {
        "down": (down_in, down_out),
        "up": (up_in, up_out),
        "out": (out_in, out_out),
        "qkv": (qkv_term, qkv_out),
    }
    sums = []
    for index, (name, corner, shape, axes, turn, _) in enumerate(PARTS):
        total, arrived = refs[0], refs[1:STEPS]
        refs = refs[STEPS:]
        if name == "down":
            arrived = (qkv_term.at[:, pl.ds(index * width, width)], *arrived)
        else:
            arrived, refs = (refs[0], *arrived), refs[1:]
        sums.append(
            Sum(
                turn,
                axes,
                corner,
                shape,
                *arrays[name],
                total,
                arrived,
                (sends.at[index], receives.at[index]),
                locals_.at[index],
            )
        )
    early = [(each, part[5]) for each, part in zip(sums, PARTS) if part[5] is not None]
    late = [each for each, part in zip(sums, PARTS) if part[5] is None]

    line_sems = (line_sends, line_receives)
    send_far = remote(parts.at[0], far, line_sems, 0, near)
    send_mid_2 = remote(parts.at[1], mid_2, line_sems, 1, near)
    send_mid_3 = remote(parts.at[0], mid_3, line_sems, 2, across)
    send_last_1 = remote(parts.at[1], last_1, line_sems, 3, across)
    send_last_2 = remote(parts.at[2], far, line_sems, 4, near)
    send_last_3 = remote(parts.at[2], last_3, line_sems, 5, near)

    def pair_columns(pair):
        return pl.ds(pl.multiple_of(pair * PAIR, PAIR), PAIR)

    def kv_copies(shard, pair, slot):
        return [
            pltpu.make_async_copy(
                source[shard].at[:, pair_columns(pair)], kv_slot.at[slot, side], kv_sems.at[slot, side]
            )
            for side, source in enumerate((keys, values))
        ]

    def a_copy(shard):
        return pltpu.make_async_copy(shards[shard], a_slot, a_sem)

    def clip_copy(turn):
        source = clips.at[pl.ds(pl.multiple_of(turn * rows, 8), rows)]
        return pltpu.make_async_copy(source, clip_slot, clip_sem)

    def of_pairs(stack):
        return jnp.concatenate([stack[pair] for pair in range(pairs)], axis=1)

    for copy in kv_copies(3, 0, 0):
        copy.start()
    greet()
    for each, _ in early:
        each.start()
    dq_sum[...] = jnp.zeros_like(dq_sum)
    grad_k[...] = jnp.zeros_like(grad_k)
    grad_v[...] = jnp.zeros_like(grad_v)
    small_out[...] = small_in[...]

    def weight_terms(d_query):
        a_copy(0).wait()
        d_key, d_value = of_pairs(dk_all), of_pairs(dv_all)
        part = dot(d_key, w_ref[:, width : 2 * width], NT) + dot(d_value, w_ref[:, 2 * width :], NT)
        if d_query is not None:
            part = part + dot(d_query, w_ref[:, :width], NT)
        small_out[:1] += jnp.sum(part * a_slot[...].astype(WIDE), axis=0, keepdims=True)
        grad_k[...] += dot(a_slot[...], d_key, TN)
        grad_v[...] += dot(a_slot[...], d_value, TN)
        return part

    @pl.loop(0, pieces)
    def _(piece):
        turn, pair, slot = piece // pairs, piece % pairs, piece % 2

        def at(when, *actions, also=None):
            @pl.when(piece == when if also is None else jnp.logical_and(piece == when, also))
            def _():
                for action in actions:
                    action()

        for shard in range(4):
            following = piece + 1

            @pl.when(jnp.logical_and(following // pairs == 3 - shard, following < pieces))
            def _():
                for copy in kv_copies(shard, following % pairs, following % 2):
                    copy.start()

            at((3 - shard) * pairs + 1, lambda: a_copy(shard).start())
        for when in range(pieces):
            ends = [
                functools.partial(each.turn, tick)
                for tick in range(2 * STEPS)
                for each, ticks in early
                if ticks[tick] == when
            ]
            if ends:
                at(when, *ends)
        at_middle = jnp.logical_not(at_end)
        at(pairs, send_far.start, also=at_end)
        at(2 * pairs, send_far.wait_send, send_mid_2.start, also=at_end)
        at(
            2 * pairs + 1,
            send_far.wait_recv,
            lambda: add_block(parts.at[0], far),
            send_mid_3.start,
            also=at_middle,
        )
        at(3 * pairs, send_mid_2.wait_send, send_last_3.start, also=at_end)
        at(
            3 * pairs + 2,
            send_mid_2.wait_recv,
            lambda: add_block(parts.at[1], mid_2),
            send_last_1.start,
            send_mid_3.wait,
            lambda: add_block(parts.at[2], mid_3),
            send_last_2.start,
            also=at_middle,
        )

        @pl.when(pair == 0)
        def _():
            clip_copy(turn).start()
            clip_copy(turn).wait()

        for copy in kv_copies(0, pair, slot):
            copy.wait()
        columns = pair_columns(pair)

        def add(head, start, stop, dq, dk, dv):
            lanes = slice(head * HEAD, (head + 1) * HEAD)
            if start == 0:
                dv_sum[lanes], dk_sum[lanes] = dv, dk
            else:
                dv_sum[lanes] += dv
                dk_sum[lanes] += dk
            at_lanes = pl.ds(pl.multiple_of(pair * PAIR + head * HEAD, HEAD), HEAD)
            dq_sum[at_lanes, start:stop] += dq

        backward_pair(
            kv_slot[slot, 0],
            kv_slot[slot, 1],
            q_ref[:, columns],
            grad_ref[columns, :],
            lse_ref.at[pair],
            dots_ref.at[pair],
            clip_slot[...],
            query_clip[...],
            add,
        )
        dk_all[pair] = (dk_sum[...] * SCALE).T.astype(LOW)
        dv_all[pair] = dv_sum[...].T.astype(LOW)

        @pl.when(jnp.logical_and(pair == pairs - 1, turn < 3))
        def _():
            parts[turn] = weight_terms(None).astype(LOW)

    d_query = (dq_sum[...] * SCALE).T.astype(LOW)
    input_sum[...] = weight_terms(d_query)
    qkv_term[:, :width] = dot(a_slot[...], d_query, TN).astype(LOW)
    qkv_term[:, width : 2 * width] = grad_k[...].astype(LOW)
    qkv_term[:, 2 * width :] = grad_v[...].astype(LOW)

    small_steps = place_bits(0)

    def small(step):
        return remote(
            small_out, small_arrived.at[step], (small_sends, small_receives), step, small_steps[step][1]
        )

    for each in late:
        each.start()
    for each, ticks in early:
        for tick in range(2 * STEPS):
            if ticks[tick] == pieces:
                each.turn(tick)

    @pl.when(at_end)
    def _():
        send_last_3.wait_send()
        send_last_2.wait_recv()
        add_block(input_sum, far)

    @pl.when(jnp.logical_not(at_end))
    def _():
        send_last_1.wait()
        send_last_2.wait_send()
        send_last_3.wait_recv()
        add_block(input_sum, last_1)
        add_block(input_sum, last_3)

    store = pltpu.make_async_copy(input_sum, input_out, out_sem)
    store.start()
    for tick in range(2 * STEPS):
        if tick < STEPS:
            small(tick).start()
        for each in late:
            each.turn(tick)
        if tick < STEPS:
            small(tick).wait()
            small_out[...] += small_arrived[tick]
    store.wait()


def gradient_call(
    keys, values, shards, query, grad_t, lse, row_dots, clips, query_clip, w_qkv, grad_down, grad_up, grad_out, small
):
    rows, width = query.shape
    pairs = width // PAIR
    anywhere = pl.BlockSpec(memory_space=pl.ANY)
    inside = pl.BlockSpec(memory_space=pltpu.VMEM)
    square = (rows, width)
    scratch = [
        pltpu.VMEM((2, 2, rows, PAIR), LOW),
        pltpu.VMEM(square, LOW),
        pltpu.VMEM((width, rows), WIDE),
        pltpu.VMEM((PAIR, rows), WIDE),
        pltpu.VMEM((PAIR, rows), WIDE),
        pltpu.VMEM((pairs, rows, PAIR), LOW),
        pltpu.VMEM((pairs, rows, PAIR), LOW),
        pltpu.VMEM((width, width), WIDE),
        pltpu.VMEM((width, width), WIDE),
        pltpu.VMEM((3, *square), LOW),
    ]
    scratch += [pltpu.VMEM(square, LOW)] * 5
    scratch += [
        pltpu.VMEM((width, 3 * width), LOW),
        pltpu.VMEM((rows, 1), clips.dtype),
        pltpu.VMEM((STEPS, *small.shape), WIDE),
        pltpu.SemaphoreType.DMA((2, 2)),
        pltpu.SemaphoreType.DMA,
        pltpu.SemaphoreType.DMA((6,)),
        pltpu.SemaphoreType.DMA((6,)),
        pltpu.SemaphoreType.DMA((len(PARTS), 2 * STEPS)),
        pltpu.SemaphoreType.DMA((len(PARTS), 2 * STEPS)),
        pltpu.SemaphoreType.DMA((len(PARTS), 2)),
        pltpu.SemaphoreType.DMA((STEPS,)),
        pltpu.SemaphoreType.DMA((STEPS,)),
        pltpu.SemaphoreType.DMA,
        pltpu.SemaphoreType.DMA,
    ]
    for name, _, shape, axes, _, _ in PARTS:
        shapes = halves(shape, axes)
        scratch += [pltpu.VMEM(each, LOW) for each in (shapes[0], *shapes[1:])]
        if name != "down":
            scratch.append(pltpu.VMEM(shapes[0], LOW))
    like = lambda array: jax.ShapeDtypeStruct(array.shape, array.dtype)
    return pl.pallas_call(
        gradient_kernel,
        in_specs=[anywhere] * 12 + [inside] * 4 + [anywhere] + [inside] * 2 + [anywhere] * 3 + [inside],
        out_specs=[anywhere] * 4 + [inside, anywhere],
        out_shape=[
            like(grad_down),
            like(grad_up),
            like(grad_out),
            jax.ShapeDtypeStruct((width, 3 * width), LOW),
            like(small),
            jax.ShapeDtypeStruct(square, WIDE),
        ],
        scratch_shapes=scratch,
        name="gradients",
        compiler_params=pltpu.CompilerParams(
            collective_id=1, has_side_effects=True, vmem_limit_bytes=62 * 2**20
        ),
    )(
        *keys, *values, *shards, query, grad_t, lse, row_dots, clips, query_clip, w_qkv,
        grad_down, grad_up, grad_out, small,
    )


def on_device(
    groups, inputs, positions, segments, gain_attn, w_qkv, w_out, gain_mlp, w_up, b_up, w_down, cotangent
):
    rows, width = inputs.shape
    pairs = width // PAIR
    place = lax.axis_index("blk")
    w_query = w_qkv[:, :width]

    def send(value, pairs_of_places):
        return lax.ppermute(value, "blk", pairs_of_places)

    hidden = inputs + position_table(positions, width)
    normed_attn, inverse_attn = normalize(hidden)
    a_low = (normed_attn * gain_attn).astype(LOW)

    near = [(0, 1), (1, 0), (2, 3), (3, 2)]
    middle = [(1, 2), (2, 1)]
    outward = [(1, 0), (2, 3)]
    inward = [(0, 1), (3, 2)]
    table = jnp.array([[0, 1, 2, 3], [1, 0, 2, 3], [2, 3, 1, 0], [3, 2, 1, 0]], jnp.int32)
    shard_1 = send(a_low, near)
    shard_2_middle = send(a_low, middle)
    shard_2 = shard_2_middle + send(shard_2_middle, outward)
    shard_3_middle = send(shard_1, middle)
    shard_3 = shard_3_middle + send(shard_3_middle, outward)
    shards = [a_low, shard_1, shard_2, shard_3]

    def clips_of(index):
        other = lax.dynamic_index_in_dim(table[:, index], place, keepdims=False)
        return lax.dynamic_slice_in_dim(segments, other * rows, rows)

    clips = [clips_of(index)[:, None] for index in range(4)]
    query_clip = lax.dynamic_slice_in_dim(segments, place * rows, rows)[None, :]

    query = dot(a_low, w_query, NN).astype(LOW)
    keys, values, state = [], [], None
    for index in range(4):
        key, value, *state = forward_call(
            index == 0, index == 3, shards[index], w_qkv, query, clips[index], query_clip, state
        )
        keys.append(key)
        values.append(value)
    attended, lse, _, attn_low = state

    resid = hidden + dot(attn_low, w_out, NN)
    normed_mlp, inverse_mlp = normalize(resid)
    b_low = (normed_mlp * gain_mlp).astype(LOW)
    pre_act = dot(b_low, w_up, NN) + b_up
    cumulative = 0.5 * (1.0 + lax.erf(pre_act * 0.7071067811865476))
    density = jnp.exp(-0.5 * pre_act * pre_act) * 0.3989422804014327
    z_low = (pre_act * cumulative).astype(LOW)
    outputs = resid + dot(z_low, w_down, NN)
    dy_low = cotangent.astype(LOW)
    grad_down = dot(z_low, dy_low, TN).astype(LOW)
    d_gelu = dot(dy_low, w_down, NT)
    d_pre = (d_gelu * (cumulative + pre_act * density)).astype(LOW)
    grad_up = dot(b_low, d_pre, TN).astype(LOW)
    grad_bias_up = jnp.sum(d_pre.astype(WIDE), axis=0)
    d_normed = dot(d_pre, w_up, NT)
    grad_gain_mlp = jnp.sum(d_normed * normed_mlp, axis=0)
    d_resid = cotangent + norm_back(d_normed * gain_mlp, normed_mlp, inverse_mlp)
    dr_low = d_resid.astype(LOW)
    grad_out = dot(attn_low, dr_low, TN).astype(LOW)
    d_attn_t = dot(w_out, dr_low, NT).astype(LOW)
    row_dots = jnp.sum(
        (d_attn_t.astype(WIDE) * attended).reshape(pairs, 2, HEAD, rows), axis=2
    )

    if groups == 8 and rows == width:
        small = jnp.concatenate([jnp.zeros_like(gain_attn), grad_gain_mlp, grad_bias_up])
        sum_down, sum_up, sum_out, sum_qkv, sum_small, d_normed_attn = gradient_call(
            keys,
            values,
            shards,
            query,
            d_attn_t,
            lse,
            row_dots,
            jnp.concatenate(clips[::-1], axis=0),
            query_clip,
            w_qkv,
            grad_down,
            grad_up,
            grad_out,
            jnp.pad(small.reshape(6, width), ((0, 2), (0, 0))),
        )
        input_grad = d_resid + norm_back(d_normed_attn * gain_attn, normed_attn, inverse_attn)
        return (
            outputs,
            input_grad,
            sum_small[0] / gain_attn,
            sum_qkv.astype(WIDE),
            sum_out.astype(WIDE),
            sum_small[1],
            sum_up.astype(WIDE),
            sum_small[2:6].reshape(-1),
            sum_down.astype(WIDE),
        )

    everywhere = ("dp", "blk")

    def back(index, dq):
        return backward_call(
            index == 3,
            index == 0,
            keys[index],
            values[index],
            query,
            d_attn_t,
            lse,
            row_dots,
            clips[index],
            query_clip,
            w_qkv,
            dq,
        )

    dk_3, dv_3, dq, part_3 = back(3, None)
    far = send(part_3, inward)
    dk_2, dv_2, dq, part_2 = back(2, dq)
    far, part_2, dq = lax.optimization_barrier((far, part_2, dq))
    onward = (part_3.astype(WIDE) + far.astype(WIDE)).astype(LOW)
    mid_3 = send(onward, middle)
    mid_2 = send(part_2, inward)
    dq, onward = lax.optimization_barrier((dq, onward))
    dk_1, dv_1, dq, part_1 = back(1, dq)
    mid_3, mid_2, part_1, dq = lax.optimization_barrier((mid_3, mid_2, part_1, dq))
    onward_1 = (part_2.astype(WIDE) + mid_2.astype(WIDE)).astype(LOW)
    onward_2 = (part_1.astype(WIDE) + mid_3.astype(WIDE)).astype(LOW)
    last_1 = send(onward_1, middle)
    last_2 = send(onward_2, outward)
    last_3 = send(part_1, inward)
    dq, onward_1, onward_2 = lax.optimization_barrier((dq, onward_1, onward_2))
    dk_0, dv_0, dq, part_0 = back(0, dq)
    grad_query = dot(a_low, dq, TN).astype(LOW)
    d_keys, d_values = (dk_0, dk_1, dk_2, dk_3), (dv_0, dv_1, dv_2, dv_3)
    grad_key = sum(dot(shard, term, TN) for shard, term in zip(shards, d_keys)).astype(LOW)
    grad_value = sum(dot(shard, term, TN) for shard, term in zip(shards, d_values)).astype(LOW)
    d_normed_attn = (
        part_0
        + dot(dq, w_query, NT)
        + last_1.astype(WIDE)
        + last_2.astype(WIDE)
        + last_3.astype(WIDE)
    )
    grad_gain_attn = jnp.sum(d_normed_attn * normed_attn, axis=0)
    input_grad = d_resid + norm_back(d_normed_attn * gain_attn, normed_attn, inverse_attn)
    small = jnp.concatenate([grad_gain_attn, grad_gain_mlp, grad_bias_up])
    sums = lax.psum((grad_down, grad_up, grad_out, grad_query, grad_key, grad_value), everywhere)
    sum_small = lax.psum(small, everywhere)
    sum_down, sum_up, sum_out, *sum_qkv = sums
    return (
        outputs,
        input_grad,
        sum_small[:width],
        jnp.concatenate(sum_qkv, axis=1).astype(WIDE),
        sum_out.astype(WIDE),
        sum_small[width : 2 * width],
        sum_up.astype(WIDE),
        sum_small[2 * width :],
        sum_down.astype(WIDE),
    )


def solution(mesh):
    rows = P(("dp", "blk"), None)
    placed = (rows, P(("dp", "blk")), P("dp"), P(), P(), P(), P(), P(), P(), P(), rows)
    return jax.shard_map(
        functools.partial(on_device, mesh.shape["dp"]),
        mesh=mesh,
        in_specs=placed,
        out_specs=(rows, rows, P(), P(), P(), P(), P(), P(), P()),
        check_vma=False,
    )
```

```python
import functools
import math

import jax
import jax.numpy as jnp
from jax import lax
from jax.experimental import pallas as pl
from jax.experimental.pallas import tpu as pltpu
from jax.sharding import PartitionSpec as P

HEADS = 12
HEAD = 64
PAIR = 2 * HEAD
SCALE = HEAD**-0.5
LOG2E = 1.4426950408889634
MASKED = -1.0e9
QUERY_BLOCK = 384
EPS_NORM = 1e-06
LOW = jnp.bfloat16
WIDE = jnp.float32

NN = (((1,), (0,)), ((), ()))
NT = (((1,), (1,)), ((), ()))
TN = (((0,), (0,)), ((), ()))


def dot(left, right, dims):
    return lax.dot_general(left, right, dims, preferred_element_type=WIDE)


def position_table(positions, model_width):
    half_width = model_width // 2
    freqs = jnp.exp(jnp.arange(half_width, dtype=WIDE) * (-math.log(10000.0) / half_width))
    angles = positions.astype(WIDE)[:, None] * freqs[None, :]
    return jnp.concatenate([jnp.sin(angles), jnp.cos(angles)], axis=1)


def normalize(values):
    center = values - jnp.mean(values, axis=-1, keepdims=True)
    inverse = lax.rsqrt(jnp.mean(center * center, axis=-1, keepdims=True) + EPS_NORM)
    return center * inverse, inverse


def norm_back(grad_norm, normed, inverse):
    first = jnp.mean(grad_norm, axis=-1, keepdims=True)
    second = jnp.mean(grad_norm * normed, axis=-1, keepdims=True)
    return inverse * (grad_norm - first - normed * second)


def in_head(values, head):
    lanes = lax.broadcasted_iota(jnp.int32, values.shape, 1)
    return (lanes < HEAD) == (head == 0)


def only_head(values, head, other=None):
    other = jnp.zeros_like(values) if other is None else other
    return jnp.where(in_head(values, head), values, other)


def split_scaled(query):
    scaled = query.astype(WIDE) * (SCALE * LOG2E)
    high = scaled.astype(LOW)
    return high, (scaled - high.astype(WIDE)).astype(LOW)


def score_sides(key, query):
    high, low = split_scaled(query)
    key_side = jnp.concatenate([key, key], axis=1)
    query_side = [
        jnp.concatenate([only_head(high, head), only_head(low, head)], axis=1) for head in range(2)
    ]
    return key_side, query_side


def work_items(rows):
    return [(start, head) for start in range(0, rows, QUERY_BLOCK) for head in range(2)]


def whole(*shape):
    return pl.BlockSpec(shape, lambda pair: (0,) * len(shape))


def columns_of(rows, first=0):
    return pl.BlockSpec((rows, PAIR), lambda pair: (0, pair + first))


def forward_kernel(first, last, *refs):
    a_ref, wk_ref, wv_ref, q_ref, key_clip, query_clip = refs[:6]
    refs = refs[6:]
    if not first:
        acc_in, top_in, total_in = refs[:3]
        refs = refs[3:]
    k_ref, v_ref, acc_ref, top_ref, total_ref = refs[:5]
    attn_ref = refs[5] if last else None
    rows = q_ref.shape[0]
    kv = dot(a_ref[...], jnp.concatenate([wk_ref[...], wv_ref[...]], axis=1), NN).astype(LOW)
    key, value = kv[:, :PAIR], kv[:, PAIR:]
    k_ref[...] = key
    v_ref[...] = value
    value_t = value.T
    ones = jnp.ones((16, rows), LOW)
    value_rows = [
        jnp.concatenate([value_t[head * HEAD : (head + 1) * HEAD], ones], axis=0) for head in range(2)
    ]
    key_side, query_side = score_sides(key, q_ref[...])

    def scores(start, head):
        stop = start + QUERY_BLOCK
        result = dot(key_side, query_side[head][start:stop], NT)
        return jnp.where(key_clip[...] == query_clip[:, start:stop], result, MASKED)

    def weights(start, head, result):
        stop = start + QUERY_BLOCK
        top = jnp.max(result, axis=0, keepdims=True)
        if not first:
            top = jnp.maximum(top, top_in[head : head + 1, start:stop])
        return jnp.exp2(result - top).astype(LOW), top

    def attend(start, head, expd, top):
        stop = start + QUERY_BLOCK
        lanes, row = slice(head * HEAD, (head + 1) * HEAD), slice(head, head + 1)
        result = dot(value_rows[head], expd, NN)
        acc, total = result[:HEAD], result[HEAD : HEAD + 1]
        if not first:
            shrink = jnp.exp2(top_in[row, start:stop] - top)
            acc = acc_in[lanes, start:stop] * shrink + acc
            total = total_in[row, start:stop] * shrink + total
        if last:
            acc = acc * (1.0 / total)
            top = top + jnp.log(total) * LOG2E
        acc_ref[lanes, start:stop] = acc
        top_ref[row, start:stop] = top
        total_ref[row, start:stop] = total

    items = work_items(rows)
    result = scores(*items[0])
    before = None
    for index, item in enumerate(items):
        following = scores(*items[index + 1]) if index + 1 < len(items) else None
        done = weights(*item, result)
        if before is not None:
            attend(*before)
        before = (*item, *done)
        result = following
    attend(*before)
    if last:
        attn_ref[...] = acc_ref[...].T.astype(LOW)


def forward_call(first, last, a_shard, w_qkv, query, key_clip, query_clip, state):
    rows, width = query.shape
    pairs = width // PAIR
    across = pl.BlockSpec((PAIR, rows), lambda pair: (pair, 0))
    line = pl.BlockSpec((None, 2, rows), lambda pair: (pair, 0, 0))
    state_specs = [across, line, line]
    state_shapes = [
        jax.ShapeDtypeStruct((width, rows), WIDE),
        jax.ShapeDtypeStruct((pairs, 2, rows), WIDE),
        jax.ShapeDtypeStruct((pairs, 2, rows), WIDE),
    ]
    in_specs = [
        whole(rows, width),
        columns_of(width, pairs),
        columns_of(width, 2 * pairs),
        columns_of(rows),
        whole(rows, 1),
        whole(1, rows),
    ]
    operands = [a_shard, w_qkv, w_qkv, query, key_clip, query_clip]
    if not first:
        in_specs += state_specs
        operands += list(state)
    low_rows = jax.ShapeDtypeStruct((rows, width), LOW)
    out_specs = [columns_of(rows), columns_of(rows), *state_specs]
    out_shape = [low_rows, low_rows, *state_shapes]
    if last:
        out_specs.append(columns_of(rows))
        out_shape.append(low_rows)
    return pl.pallas_call(
        functools.partial(forward_kernel, first, last),
        grid=(pairs,),
        in_specs=in_specs,
        out_specs=out_specs,
        out_shape=out_shape,
        name="attend",
        cost_estimate=pl.CostEstimate(
            flops=20 * rows * rows * width, bytes_accessed=24 * rows * width, transcendentals=0
        ),
        compiler_params=pltpu.CompilerParams(vmem_limit_bytes=48 * 2**20),
    )(*operands)


def backward_pair(key, value, query, grad_t, lse, row_dots, key_clip, query_clip, add):
    rows = query.shape[0]
    grad = grad_t.T
    key_t, query_t = key.T, query.T
    key_side, query_side = score_sides(key, query)
    grad_side = [only_head(grad, head) for head in range(2)]
    for start, head in work_items(rows):
        stop = start + QUERY_BLOCK
        lanes, row = slice(head * HEAD, (head + 1) * HEAD), slice(head, head + 1)
        score = dot(key_side, query_side[head][start:stop], NT)
        score = jnp.where(key_clip == query_clip[:, start:stop], score, MASKED)
        probs = jnp.exp2(score - lse[row, start:stop])
        d_probs = dot(value, grad_side[head][start:stop], NT)
        d_scores = (probs * (d_probs - row_dots[row, start:stop])).astype(LOW)
        probs = probs.astype(LOW)
        dv = dot(grad_t[lanes, start:stop], probs, NT)
        dk = dot(query_t[lanes, start:stop], d_scores, NT)
        dq = dot(key_t[lanes], d_scores, NN)
        add(head, start, stop, dq, dk, dv)


def backward_kernel(first, last, *refs):
    k_ref, v_ref, q_ref, grad_ref, lse_ref, dots_ref, key_clip, query_clip, wk_ref, wv_ref = refs[:10]
    refs = refs[10:]
    if not first:
        dq_in = refs[0]
        refs = refs[1:]
    dk_ref, dv_ref, dq_ref, part_ref, dk_sum, dv_sum, dq_sum, dk_all, dv_all = refs
    pair = pl.program_id(0)
    rows = q_ref.shape[0]

    def add(head, start, stop, dq, dk, dv):
        lanes = slice(head * HEAD, (head + 1) * HEAD)
        if start == 0:
            dv_sum[lanes], dk_sum[lanes] = dv, dk
        else:
            dv_sum[lanes] += dv
            dk_sum[lanes] += dk
        if not first:
            dq = dq + dq_in[lanes, start:stop]
        if last:
            dq_sum[lanes, start:stop] = dq
        else:
            dq_ref[lanes, start:stop] = dq

    backward_pair(
        k_ref[...],
        v_ref[...],
        q_ref[...],
        grad_ref[...],
        lse_ref,
        dots_ref,
        key_clip[...],
        query_clip[...],
        add,
    )
    if last:
        dq_ref[...] = (dq_sum[...] * SCALE).T.astype(LOW)
    dk = (dk_sum[...] * SCALE).T.astype(LOW)
    dv = dv_sum[...].T.astype(LOW)
    dk_ref[...] = dk
    dv_ref[...] = dv
    dk_all[pair] = dk
    dv_all[pair] = dv

    @pl.when(pair == pl.num_programs(0) - 1)
    def _():
        pairs = dk_all.shape[0]
        dk_rows = jnp.concatenate([dk_all[index] for index in range(pairs)], axis=1)
        dv_rows = jnp.concatenate([dv_all[index] for index in range(pairs)], axis=1)
        part = dot(dk_rows, wk_ref[...], NT) + dot(dv_rows, wv_ref[...], NT)
        part_ref[...] = part.astype(part_ref.dtype)


def backward_call(first, last, key, value, query, grad_t, lse, row_dots, key_clip, query_clip, w_qkv, dq):
    rows, width = query.shape
    pairs = width // PAIR
    across = pl.BlockSpec((PAIR, rows), lambda pair: (pair, 0))
    line = pl.BlockSpec((None, 2, rows), lambda pair: (pair, 0, 0))
    columns = columns_of(rows)
    in_specs = [columns, columns, columns, across, line, line, whole(rows, 1), whole(1, rows)]
    in_specs += [
        pl.BlockSpec((width, width), lambda pair: (0, 1)),
        pl.BlockSpec((width, width), lambda pair: (0, 2)),
    ]
    operands = [key, value, query, grad_t, lse, row_dots, key_clip, query_clip, w_qkv, w_qkv]
    if not first:
        in_specs.append(across)
        operands.append(dq)
    low_rows = jax.ShapeDtypeStruct((rows, width), LOW)
    tall = pltpu.VMEM((PAIR, rows), WIDE)
    parts = pltpu.VMEM((pairs, rows, PAIR), LOW)
    return pl.pallas_call(
        functools.partial(backward_kernel, first, last),
        grid=(pairs,),
        in_specs=in_specs,
        out_specs=[columns, columns, columns if last else across, whole(rows, width)],
        out_shape=[
            low_rows,
            low_rows,
            low_rows if last else jax.ShapeDtypeStruct((width, rows), WIDE),
            jax.ShapeDtypeStruct((rows, width), WIDE if last else LOW),
        ],
        scratch_shapes=[tall, tall, tall, parts, parts],
        name="attend_back",
        cost_estimate=pl.CostEstimate(
            flops=40 * rows * rows * width, bytes_accessed=24 * rows * width, transcendentals=0
        ),
        compiler_params=pltpu.CompilerParams(vmem_limit_bytes=48 * 2**20),
    )(*operands)


MESH = pl.DeviceIdType.MESH
TURNS = ((0, 1, 2), (0, 2, 1))
STEPS = 5
ADD_ROWS = 48
FORWARD = 8


def place_bits(turn):
    group, place = lax.axis_index("dp"), lax.axis_index("blk")
    steps = []
    for bit in TURNS[turn]:
        mine = group // (1 << bit) % 2
        steps.append((mine, (group + (1 - 2 * mine) * (1 << bit), place)))
    for bit in range(2):
        mine = place // (1 << bit) % 2
        steps.append((mine, (group, place + (1 - 2 * mine) * (1 << bit))))
    return steps


def remote(source, target, sems, index, device):
    return pltpu.make_async_remote_copy(
        src_ref=source,
        dst_ref=target,
        send_sem=sems[0].at[index],
        recv_sem=sems[1].at[index],
        device_id=device,
        device_id_type=MESH,
    )


def part_of(row, rows, column, columns):
    row = row if isinstance(row, int) else pl.multiple_of(row, 16)
    column = column if isinstance(column, int) else pl.multiple_of(column, PAIR)
    return pl.ds(row, rows), pl.ds(column, columns)


def add_block(total, term, row=0, column=0):
    rows, columns = term.shape

    @pl.loop(0, rows // ADD_ROWS)
    def _(index):
        here = part_of(row + index * ADD_ROWS, ADD_ROWS, column, columns)
        there = part_of(index * ADD_ROWS, ADD_ROWS, 0, columns)
        total[here] = (total[here].astype(WIDE) + term[there].astype(WIDE)).astype(total.dtype)


def halves(shape, axes):
    shapes = []
    for axis in axes:
        shape = (shape[0] // 2, shape[1]) if axis == "r" else (shape[0], shape[1] // 2)
        shapes.append(shape)
    return shapes


class Sum:
    def __init__(self, turn, axes, corner, shape, term, result, total, arrived, sems, local_sems):
        self.term, self.result, self.total, self.arrived = term, result, total, arrived
        self.sems, self.local_sems = sems, local_sems
        self.steps = place_bits(turn)
        self.shapes = halves(shape, axes)
        self.kept, self.left = [], []
        row, column = corner
        for axis, (rows, columns), (mine, _) in zip(axes, self.shapes, self.steps):
            down, across = (rows, 0) if axis == "r" else (0, columns)
            self.left.append((row + (1 - mine) * down, rows, column + (1 - mine) * across, columns))
            row, column = row + mine * down, column + mine * across
            self.kept.append((row, rows, column, columns))

    def inside(self, place):
        row, rows, column, columns = place
        return part_of(row - self.kept[0][0], rows, column - self.kept[0][2], columns)

    def load(self):
        return pltpu.make_async_copy(
            self.term.at[part_of(*self.kept[0])], self.total, self.local_sems.at[0]
        )

    def store(self):
        return pltpu.make_async_copy(
            self.total.at[self.inside(self.kept[-1])],
            self.result.at[part_of(*self.kept[-1])],
            self.local_sems.at[1],
        )

    def gather(self, step):
        place = self.left[step]
        source = self.term.at[part_of(*place)] if step == 0 else self.total.at[self.inside(place)]
        return remote(source, self.arrived[step], self.sems, step, self.steps[step][1])

    def spread(self, step):
        here = self.result.at[part_of(*self.kept[step])]
        return remote(here, here, self.sems, STEPS + step, self.steps[step][1])

    def start(self):
        self.load().start()
        self.gather(0).start()

    def turn(self, tick):
        if tick < STEPS:
            if tick == 0:
                self.load().wait()
            self.gather(tick).wait()
            row, _, column, _ = self.kept[tick]
            add_block(self.total, self.arrived[tick], row - self.kept[0][0], column - self.kept[0][2])
            if tick + 1 < STEPS:
                self.gather(tick + 1).start()
            else:
                self.store().start()
                self.store().wait()
                self.spread(STEPS - 1).start()
        else:
            step = 2 * STEPS - 1 - tick
            self.spread(step).wait()
            if step:
                self.spread(step - 1).start()


def greet():
    group, place = lax.axis_index("dp"), lax.axis_index("blk")
    devices = [device for _, device in place_bits(0)]
    devices.append((group, 3 - place))
    barrier = pltpu.get_barrier_semaphore()
    for device in devices:
        pl.semaphore_signal(barrier, inc=1, device_id=device, device_id_type=MESH)
    pl.semaphore_wait(barrier, len(devices))


PARTS = (
    ("down", (0, 0), (1536, 384), "rrrrr", 0, (1, 3, 7, 9, 10, 12, 14, 15, 17, 18)),
    ("down", (0, 384), (1536, 384), "rrrrr", 1, (1, 3, 7, 8, 9, 11, 12, 14, 17, 18)),
    ("down", (1536, 0), (1536, 384), "rrrrr", 1, (2, 5, 10, 11, 13, 15, 17, 18, 21, 22)),
    ("down", (1536, 384), (1536, 384), "rrrrr", 0, (2, 5, 8, 9, 11, 12, 15, 18, 20, 21)),
    ("up", (0, 0), (768, 768), "rrrrc", 0, (2, 6, 9, 10, 12, 14, 16, 18, 23, 24)),
    ("up", (0, 768), (768, 768), "rrrrc", 1, (3, 6, 10, 12, 14, 17, 18, 21, 23, 24)),
    ("up", (0, 1536), (768, 768), "rrrrc", 0, (3, 7, 10, 12, 13, 16, 18, 20, 24, 24)),
    ("up", (0, 2304), (768, 768), "rrrrc", 1, (3, 7, 11, 13, 16, 18, 19, 23, 24, 24)),
    ("out", (0, 0), (768, 768), "rrrrc", 0, (3, 9, 10, 12, 15, 17, 18, 22, 24, 24)),
    ("qkv", (0, 0), (768, 512), "rrrrc", 0, None),
    ("qkv", (0, 512), (768, 512), "rrrrc", 1, None),
    ("qkv", (0, 1024), (768, 512), "rrrrc", 0, None),
    ("qkv", (0, 1536), (768, 768), "rrrrc", 1, None),
)


def gradient_kernel(*refs):
    keys, values, shards = refs[:4], refs[4:8], refs[8:12]
    q_ref, grad_ref, lse_ref, dots_ref, clips, query_clip, w_ref = refs[12:19]
    down_in, up_in, out_in, small_in = refs[19:23]
    down_out, up_out, out_out, qkv_out, small_out, input_out = refs[23:29]
    refs = refs[29:]
    kv_slot, a_slot, dq_sum, dk_sum, dv_sum, dk_all, dv_all, grad_k, grad_v, parts = refs[:10]
    from_near, from_across, qkv_term, clip_slot, small_arrived = refs[10:15]
    input_sum = dq_sum
    kv_sems, a_sem, line_sends, line_receives, sends, receives, locals_ = refs[15:22]
    small_sends, small_receives, out_sem, clip_sem = refs[22:26]
    refs = refs[26:]
    rows, width = q_ref.shape
    pairs = width // PAIR
    pieces = 4 * pairs
    group, place = lax.axis_index("dp"), lax.axis_index("blk")
    near = (group, place + 1 - 2 * (place % 2))
    across = (group, 3 - place)
    at_end = place % 3 == 0

    arrays = {
        "down": (down_in, down_out),
        "up": (up_in, up_out),
        "out": (out_in, out_out),
        "qkv": (qkv_term, qkv_out),
    }
    sums = []
    for index, (name, corner, shape, axes, turn, _) in enumerate(PARTS):
        total, arrived = refs[0], refs[1:STEPS]
        refs = refs[STEPS:]
        if name == "down":
            arrived = (qkv_term.at[:, pl.ds(index * shape[1], shape[1])], *arrived)
        else:
            arrived, refs = (refs[0], *arrived), refs[1:]
        sums.append(
            Sum(
                turn,
                axes,
                corner,
                shape,
                *arrays[name],
                total,
                arrived,
                (sends.at[index], receives.at[index]),
                locals_.at[index],
            )
        )
    early = [(each, part[5]) for each, part in zip(sums, PARTS) if part[5] is not None]
    late = [each for each, part in zip(sums, PARTS) if part[5] is None]

    chunk_rows = rows // pairs

    def chunk_of(chunk):
        return pl.ds(pl.multiple_of(chunk * chunk_rows, chunk_rows), chunk_rows)

    def line_copy(channel, chunk, source, target, device):
        return pltpu.make_async_remote_copy(
            src_ref=parts.at[source, chunk_of(chunk)],
            dst_ref=target.at[chunk_of(chunk)],
            send_sem=line_sends.at[channel, chunk],
            recv_sem=line_receives.at[channel, chunk],
            device_id=device,
            device_id_type=MESH,
        )

    def inward(source, chunk):
        return line_copy(source, chunk, source, from_near.at[source], near)

    def middle(source, chunk):
        return line_copy(3 + source, chunk, source, from_across.at[source], across)

    def outward(chunk):
        return line_copy(5, chunk, 2, from_near.at[0], near)

    def add_chunk(total, term, chunk):
        here = chunk_of(chunk)
        total[here] = (total[here].astype(WIDE) + term[here].astype(WIDE)).astype(total.dtype)

    def pair_columns(pair):
        return pl.ds(pl.multiple_of(pair * PAIR, PAIR), PAIR)

    def kv_copies(shard, pair, slot):
        return [
            pltpu.make_async_copy(
                source[shard].at[:, pair_columns(pair)], kv_slot.at[slot, side], kv_sems.at[slot, side]
            )
            for side, source in enumerate((keys, values))
        ]

    def a_copy(shard):
        return pltpu.make_async_copy(shards[shard], a_slot, a_sem)

    def clip_copy(turn):
        source = clips.at[pl.ds(pl.multiple_of(turn * rows, 8), rows)]
        return pltpu.make_async_copy(source, clip_slot, clip_sem)

    def of_pairs(stack):
        return jnp.concatenate([stack[pair] for pair in range(pairs)], axis=1)

    for copy in kv_copies(3, 0, 0):
        copy.start()
    greet()
    for each, _ in early:
        each.start()
    dq_sum[...] = jnp.zeros_like(dq_sum)
    grad_k[...] = jnp.zeros_like(grad_k)
    grad_v[...] = jnp.zeros_like(grad_v)
    small_out[...] = small_in[...]

    def weight_terms(d_query):
        a_copy(0).wait()
        d_key, d_value = of_pairs(dk_all), of_pairs(dv_all)
        part = dot(d_key, w_ref[:, width : 2 * width], NT) + dot(d_value, w_ref[:, 2 * width :], NT)
        if d_query is not None:
            part = part + dot(d_query, w_ref[:, :width], NT)
        small_out[:1] += jnp.sum(part * a_slot[...].astype(WIDE), axis=0, keepdims=True)
        grad_k[...] += dot(a_slot[...], d_key, TN)
        grad_v[...] += dot(a_slot[...], d_value, TN)
        return part

    @pl.loop(0, pieces)
    def _(piece):
        turn, pair, slot = piece // pairs, piece % pairs, piece % 2

        def at(when, *actions, also=None):
            @pl.when(piece == when if also is None else jnp.logical_and(piece == when, also))
            def _():
                for action in actions:
                    action()

        for shard in range(4):
            following = piece + 1

            @pl.when(jnp.logical_and(following // pairs == 3 - shard, following < pieces))
            def _():
                for copy in kv_copies(shard, following % pairs, following % 2):
                    copy.start()

            at((3 - shard) * pairs + 1, lambda: a_copy(shard).start())
        for when in range(pieces):
            ends = [
                functools.partial(each.turn, tick)
                for tick in range(2 * STEPS)
                for each, ticks in early
                if ticks[tick] == when
            ]
            if ends:
                at(when, *ends)
        at_middle = jnp.logical_not(at_end)

        @pl.when(jnp.logical_and(turn > 0, at_end))
        def _():
            inward(turn - 1, pair).start()

        @pl.when(jnp.logical_and(at_middle, jnp.logical_and(piece >= FORWARD, piece < FORWARD + 2 * pairs)))
        def _():
            source, chunk = (piece - FORWARD) // pairs, (piece - FORWARD) % pairs
            inward(source, chunk).wait_recv()
            add_chunk(parts.at[source], from_near.at[source], chunk)
            middle(source, chunk).start()

        @pl.when(jnp.logical_and(at_middle, turn == 3))
        def _():
            middle(0, pair).wait_recv()
            add_chunk(parts.at[2], from_across.at[0], pair)
            outward(pair).start()

        @pl.when(pair == 0)
        def _():
            clip_copy(turn).start()
            clip_copy(turn).wait()

        for copy in kv_copies(0, pair, slot):
            copy.wait()
        columns = pair_columns(pair)

        def add(head, start, stop, dq, dk, dv):
            lanes = slice(head * HEAD, (head + 1) * HEAD)
            if start == 0:
                dv_sum[lanes], dk_sum[lanes] = dv, dk
            else:
                dv_sum[lanes] += dv
                dk_sum[lanes] += dk
            at_lanes = pl.ds(pl.multiple_of(pair * PAIR + head * HEAD, HEAD), HEAD)
            dq_sum[at_lanes, start:stop] += dq

        backward_pair(
            kv_slot[slot, 0],
            kv_slot[slot, 1],
            q_ref[:, columns],
            grad_ref[columns, :],
            lse_ref.at[pair],
            dots_ref.at[pair],
            clip_slot[...],
            query_clip[...],
            add,
        )
        dk_all[pair] = (dk_sum[...] * SCALE).T.astype(LOW)
        dv_all[pair] = dv_sum[...].T.astype(LOW)

        @pl.when(jnp.logical_and(pair == pairs - 1, turn < 3))
        def _():
            parts[turn] = weight_terms(None).astype(LOW)

    d_query = (dq_sum[...] * SCALE).T.astype(LOW)
    input_sum[...] = weight_terms(d_query)
    qkv_term[:, :width] = dot(a_slot[...], d_query, TN).astype(LOW)
    qkv_term[:, width : 2 * width] = grad_k[...].astype(LOW)
    qkv_term[:, 2 * width :] = grad_v[...].astype(LOW)

    small_steps = place_bits(0)

    def small(step):
        return remote(
            small_out, small_arrived.at[step], (small_sends, small_receives), step, small_steps[step][1]
        )

    for each in late:
        each.start()
    open_sums = [(each, [tick for tick in range(2 * STEPS) if ticks[tick] == pieces]) for each, ticks in early]
    open_sums += [(each, list(range(2 * STEPS))) for each in late]

    @pl.when(at_end)
    def _():
        @pl.loop(0, pairs)
        def _(chunk):
            for source in range(3):
                inward(source, chunk).wait_send()
            outward(chunk).wait_recv()
            add_chunk(input_sum, from_near.at[0], chunk)

    @pl.when(jnp.logical_not(at_end))
    def _():
        @pl.loop(0, pairs)
        def _(chunk):
            outward(chunk).wait_send()
            for source in range(2):
                middle(source, chunk).wait_send()
            middle(1, chunk).wait_recv()
            add_chunk(input_sum, from_across.at[1], chunk)
            inward(2, chunk).wait_recv()
            add_chunk(input_sum, from_near.at[2], chunk)

    store = pltpu.make_async_copy(input_sum, input_out, out_sem)
    store.start()
    for tick in range(2 * STEPS):
        if tick < STEPS:
            small(tick).start()
        for each, ticks in open_sums:
            if ticks:
                each.turn(ticks.pop(0))
        if tick < STEPS:
            small(tick).wait()
            small_out[...] += small_arrived[tick]
    store.wait()


def gradient_call(
    keys, values, shards, query, grad_t, lse, row_dots, clips, query_clip, w_qkv, grad_down, grad_up, grad_out, small
):
    rows, width = query.shape
    pairs = width // PAIR
    anywhere = pl.BlockSpec(memory_space=pl.ANY)
    inside = pl.BlockSpec(memory_space=pltpu.VMEM)
    square = (rows, width)
    scratch = [
        pltpu.VMEM((2, 2, rows, PAIR), LOW),
        pltpu.VMEM(square, LOW),
        pltpu.VMEM((width, rows), WIDE),
        pltpu.VMEM((PAIR, rows), WIDE),
        pltpu.VMEM((PAIR, rows), WIDE),
        pltpu.VMEM((pairs, rows, PAIR), LOW),
        pltpu.VMEM((pairs, rows, PAIR), LOW),
        pltpu.VMEM((width, width), WIDE),
        pltpu.VMEM((width, width), WIDE),
        pltpu.VMEM((3, *square), LOW),
    ]
    scratch += [pltpu.VMEM((3, *square), LOW), pltpu.VMEM((2, *square), LOW)]
    scratch += [
        pltpu.VMEM((width, 3 * width), LOW),
        pltpu.VMEM((rows, 1), clips.dtype),
        pltpu.VMEM((STEPS, *small.shape), WIDE),
        pltpu.SemaphoreType.DMA((2, 2)),
        pltpu.SemaphoreType.DMA,
        pltpu.SemaphoreType.DMA((6, pairs)),
        pltpu.SemaphoreType.DMA((6, pairs)),
        pltpu.SemaphoreType.DMA((len(PARTS), 2 * STEPS)),
        pltpu.SemaphoreType.DMA((len(PARTS), 2 * STEPS)),
        pltpu.SemaphoreType.DMA((len(PARTS), 2)),
        pltpu.SemaphoreType.DMA((STEPS,)),
        pltpu.SemaphoreType.DMA((STEPS,)),
        pltpu.SemaphoreType.DMA,
        pltpu.SemaphoreType.DMA,
    ]
    for name, _, shape, axes, _, _ in PARTS:
        shapes = halves(shape, axes)
        scratch += [pltpu.VMEM(each, LOW) for each in (shapes[0], *shapes[1:])]
        if name != "down":
            scratch.append(pltpu.VMEM(shapes[0], LOW))
    like = lambda array: jax.ShapeDtypeStruct(array.shape, array.dtype)
    return pl.pallas_call(
        gradient_kernel,
        in_specs=[anywhere] * 12 + [inside] * 4 + [anywhere] + [inside] * 2 + [anywhere] * 3 + [inside],
        out_specs=[anywhere] * 4 + [inside, anywhere],
        out_shape=[
            like(grad_down),
            like(grad_up),
            like(grad_out),
            jax.ShapeDtypeStruct((width, 3 * width), LOW),
            like(small),
            jax.ShapeDtypeStruct(square, WIDE),
        ],
        scratch_shapes=scratch,
        name="gradients",
        compiler_params=pltpu.CompilerParams(
            collective_id=1, has_side_effects=True, vmem_limit_bytes=62 * 2**20
        ),
    )(
        *keys, *values, *shards, query, grad_t, lse, row_dots, clips, query_clip, w_qkv,
        grad_down, grad_up, grad_out, small,
    )


def on_device(
    groups, inputs, positions, segments, gain_attn, w_qkv, w_out, gain_mlp, w_up, b_up, w_down, cotangent
):
    rows, width = inputs.shape
    pairs = width // PAIR
    place = lax.axis_index("blk")
    w_query = w_qkv[:, :width]

    def send(value, pairs_of_places):
        return lax.ppermute(value, "blk", pairs_of_places)

    hidden = inputs + position_table(positions, width)
    normed_attn, inverse_attn = normalize(hidden)
    a_low = (normed_attn * gain_attn).astype(LOW)

    near = [(0, 1), (1, 0), (2, 3), (3, 2)]
    middle = [(1, 2), (2, 1)]
    outward = [(1, 0), (2, 3)]
    inward = [(0, 1), (3, 2)]
    table = jnp.array([[0, 1, 2, 3], [1, 0, 2, 3], [2, 3, 1, 0], [3, 2, 1, 0]], jnp.int32)
    shard_1 = send(a_low, near)
    shard_2_middle = send(a_low, middle)
    shard_2 = shard_2_middle + send(shard_2_middle, outward)
    shard_3_middle = send(shard_1, middle)
    shard_3 = shard_3_middle + send(shard_3_middle, outward)
    shards = [a_low, shard_1, shard_2, shard_3]

    def clips_of(index):
        other = lax.dynamic_index_in_dim(table[:, index], place, keepdims=False)
        return lax.dynamic_slice_in_dim(segments, other * rows, rows)

    clips = [clips_of(index)[:, None] for index in range(4)]
    query_clip = lax.dynamic_slice_in_dim(segments, place * rows, rows)[None, :]

    query = dot(a_low, w_query, NN).astype(LOW)
    keys, values, state = [], [], None
    for index in range(4):
        key, value, *state = forward_call(
            index == 0, index == 3, shards[index], w_qkv, query, clips[index], query_clip, state
        )
        keys.append(key)
        values.append(value)
    attended, lse, _, attn_low = state

    resid = hidden + dot(attn_low, w_out, NN)
    normed_mlp, inverse_mlp = normalize(resid)
    b_low = (normed_mlp * gain_mlp).astype(LOW)
    pre_act = dot(b_low, w_up, NN) + b_up
    cumulative = 0.5 * (1.0 + lax.erf(pre_act * 0.7071067811865476))
    density = jnp.exp(-0.5 * pre_act * pre_act) * 0.3989422804014327
    z_low = (pre_act * cumulative).astype(LOW)
    outputs = resid + dot(z_low, w_down, NN)
    dy_low = cotangent.astype(LOW)
    grad_down = dot(z_low, dy_low, TN).astype(LOW)
    d_gelu = dot(dy_low, w_down, NT)
    d_pre = (d_gelu * (cumulative + pre_act * density)).astype(LOW)
    grad_up = dot(b_low, d_pre, TN).astype(LOW)
    grad_bias_up = jnp.sum(d_pre.astype(WIDE), axis=0)
    d_normed = dot(d_pre, w_up, NT)
    grad_gain_mlp = jnp.sum(d_normed * normed_mlp, axis=0)
    d_resid = cotangent + norm_back(d_normed * gain_mlp, normed_mlp, inverse_mlp)
    dr_low = d_resid.astype(LOW)
    grad_out = dot(attn_low, dr_low, TN).astype(LOW)
    d_attn_t = dot(w_out, dr_low, NT).astype(LOW)
    row_dots = jnp.sum(
        (d_attn_t.astype(WIDE) * attended).reshape(pairs, 2, HEAD, rows), axis=2
    )

    if groups == 8 and rows == width:
        small = jnp.concatenate([jnp.zeros_like(gain_attn), grad_gain_mlp, grad_bias_up])
        sum_down, sum_up, sum_out, sum_qkv, sum_small, d_normed_attn = gradient_call(
            keys,
            values,
            shards,
            query,
            d_attn_t,
            lse,
            row_dots,
            jnp.concatenate(clips[::-1], axis=0),
            query_clip,
            w_qkv,
            grad_down,
            grad_up,
            grad_out,
            jnp.pad(small.reshape(6, width), ((0, 2), (0, 0))),
        )
        input_grad = d_resid + norm_back(d_normed_attn * gain_attn, normed_attn, inverse_attn)
        return (
            outputs,
            input_grad,
            sum_small[0] / gain_attn,
            sum_qkv.astype(WIDE),
            sum_out.astype(WIDE),
            sum_small[1],
            sum_up.astype(WIDE),
            sum_small[2:6].reshape(-1),
            sum_down.astype(WIDE),
        )

    everywhere = ("dp", "blk")

    def back(index, dq):
        return backward_call(
            index == 3,
            index == 0,
            keys[index],
            values[index],
            query,
            d_attn_t,
            lse,
            row_dots,
            clips[index],
            query_clip,
            w_qkv,
            dq,
        )

    dk_3, dv_3, dq, part_3 = back(3, None)
    far = send(part_3, inward)
    dk_2, dv_2, dq, part_2 = back(2, dq)
    far, part_2, dq = lax.optimization_barrier((far, part_2, dq))
    onward = (part_3.astype(WIDE) + far.astype(WIDE)).astype(LOW)
    mid_3 = send(onward, middle)
    mid_2 = send(part_2, inward)
    dq, onward = lax.optimization_barrier((dq, onward))
    dk_1, dv_1, dq, part_1 = back(1, dq)
    mid_3, mid_2, part_1, dq = lax.optimization_barrier((mid_3, mid_2, part_1, dq))
    onward_1 = (part_2.astype(WIDE) + mid_2.astype(WIDE)).astype(LOW)
    onward_2 = (part_1.astype(WIDE) + mid_3.astype(WIDE)).astype(LOW)
    last_1 = send(onward_1, middle)
    last_2 = send(onward_2, outward)
    last_3 = send(part_1, inward)
    dq, onward_1, onward_2 = lax.optimization_barrier((dq, onward_1, onward_2))
    dk_0, dv_0, dq, part_0 = back(0, dq)
    grad_query = dot(a_low, dq, TN).astype(LOW)
    d_keys, d_values = (dk_0, dk_1, dk_2, dk_3), (dv_0, dv_1, dv_2, dv_3)
    grad_key = sum(dot(shard, term, TN) for shard, term in zip(shards, d_keys)).astype(LOW)
    grad_value = sum(dot(shard, term, TN) for shard, term in zip(shards, d_values)).astype(LOW)
    d_normed_attn = (
        part_0
        + dot(dq, w_query, NT)
        + last_1.astype(WIDE)
        + last_2.astype(WIDE)
        + last_3.astype(WIDE)
    )
    grad_gain_attn = jnp.sum(d_normed_attn * normed_attn, axis=0)
    input_grad = d_resid + norm_back(d_normed_attn * gain_attn, normed_attn, inverse_attn)
    small = jnp.concatenate([grad_gain_attn, grad_gain_mlp, grad_bias_up])
    sums = lax.psum((grad_down, grad_up, grad_out, grad_query, grad_key, grad_value), everywhere)
    sum_small = lax.psum(small, everywhere)
    sum_down, sum_up, sum_out, *sum_qkv = sums
    return (
        outputs,
        input_grad,
        sum_small[:width],
        jnp.concatenate(sum_qkv, axis=1).astype(WIDE),
        sum_out.astype(WIDE),
        sum_small[width : 2 * width],
        sum_up.astype(WIDE),
        sum_small[2 * width :],
        sum_down.astype(WIDE),
    )


def solution(mesh):
    rows = P(("dp", "blk"), None)
    placed = (rows, P(("dp", "blk")), P("dp"), P(), P(), P(), P(), P(), P(), P(), rows)
    return jax.shard_map(
        functools.partial(on_device, mesh.shape["dp"]),
        mesh=mesh,
        in_specs=placed,
        out_specs=(rows, rows, P(), P(), P(), P(), P(), P(), P()),
        check_vma=False,
    )
```

```python
import functools
import math

import jax
import jax.numpy as jnp
from jax import lax
from jax.experimental import pallas as pl
from jax.experimental.pallas import tpu as pltpu
from jax.sharding import PartitionSpec as P

HEADS = 12
HEAD = 64
PAIR = 2 * HEAD
SCALE = HEAD**-0.5
LOG2E = 1.4426950408889634
MASKED = -1.0e9
QUERY_BLOCK = 384
EPS_NORM = 1e-06
LOW = jnp.bfloat16
WIDE = jnp.float32

NN = (((1,), (0,)), ((), ()))
NT = (((1,), (1,)), ((), ()))
TN = (((0,), (0,)), ((), ()))


def dot(left, right, dims):
    return lax.dot_general(left, right, dims, preferred_element_type=WIDE)


def position_table(positions, model_width):
    half_width = model_width // 2
    freqs = jnp.exp(jnp.arange(half_width, dtype=WIDE) * (-math.log(10000.0) / half_width))
    angles = positions.astype(WIDE)[:, None] * freqs[None, :]
    return jnp.concatenate([jnp.sin(angles), jnp.cos(angles)], axis=1)


def normalize(values):
    center = values - jnp.mean(values, axis=-1, keepdims=True)
    inverse = lax.rsqrt(jnp.mean(center * center, axis=-1, keepdims=True) + EPS_NORM)
    return center * inverse, inverse


def norm_back(grad_norm, normed, inverse):
    first = jnp.mean(grad_norm, axis=-1, keepdims=True)
    second = jnp.mean(grad_norm * normed, axis=-1, keepdims=True)
    return inverse * (grad_norm - first - normed * second)


def in_head(values, head):
    lanes = lax.broadcasted_iota(jnp.int32, values.shape, 1)
    return (lanes < HEAD) == (head == 0)


def only_head(values, head, other=None):
    other = jnp.zeros_like(values) if other is None else other
    return jnp.where(in_head(values, head), values, other)


def split_scaled(query):
    scaled = query.astype(WIDE) * (SCALE * LOG2E)
    high = scaled.astype(LOW)
    return high, (scaled - high.astype(WIDE)).astype(LOW)


def score_sides(key, query):
    high, low = split_scaled(query)
    key_side = jnp.concatenate([key, key], axis=1)
    query_side = [
        jnp.concatenate([only_head(high, head), only_head(low, head)], axis=1) for head in range(2)
    ]
    return key_side, query_side


def work_items(rows):
    return [(start, head) for start in range(0, rows, QUERY_BLOCK) for head in range(2)]


def whole(*shape):
    return pl.BlockSpec(shape, lambda pair: (0,) * len(shape))


def columns_of(rows, first=0):
    return pl.BlockSpec((rows, PAIR), lambda pair: (0, pair + first))


def backward_pair(key, value, query, grad_t, lse, row_dots, key_clip, query_clip, add):
    rows = query.shape[0]
    grad = grad_t.T
    key_t, query_t = key.T, query.T
    key_side, query_side = score_sides(key, query)
    grad_side = [only_head(grad, head) for head in range(2)]
    for start, head in work_items(rows):
        stop = start + QUERY_BLOCK
        lanes, row = slice(head * HEAD, (head + 1) * HEAD), slice(head, head + 1)
        score = dot(key_side, query_side[head][start:stop], NT)
        score = jnp.where(key_clip == query_clip[:, start:stop], score, MASKED)
        probs = jnp.exp2(score - lse[row, start:stop])
        d_probs = dot(value, grad_side[head][start:stop], NT)
        d_scores = (probs * (d_probs - row_dots[row, start:stop])).astype(LOW)
        probs = probs.astype(LOW)
        dv = dot(grad_t[lanes, start:stop], probs, NT)
        dk = dot(query_t[lanes, start:stop], d_scores, NT)
        dq = dot(key_t[lanes], d_scores, NN)
        add(head, start, stop, dq, dk, dv)


def backward_kernel(first, last, *refs):
    k_ref, v_ref, q_ref, grad_ref, lse_ref, dots_ref, key_clip, query_clip, wk_ref, wv_ref = refs[:10]
    refs = refs[10:]
    if not first:
        dq_in = refs[0]
        refs = refs[1:]
    dk_ref, dv_ref, dq_ref, part_ref, dk_sum, dv_sum, dq_sum, dk_all, dv_all = refs
    pair = pl.program_id(0)
    rows = q_ref.shape[0]

    def add(head, start, stop, dq, dk, dv):
        lanes = slice(head * HEAD, (head + 1) * HEAD)
        if start == 0:
            dv_sum[lanes], dk_sum[lanes] = dv, dk
        else:
            dv_sum[lanes] += dv
            dk_sum[lanes] += dk
        if not first:
            dq = dq + dq_in[lanes, start:stop]
        if last:
            dq_sum[lanes, start:stop] = dq
        else:
            dq_ref[lanes, start:stop] = dq

    backward_pair(
        k_ref[...],
        v_ref[...],
        q_ref[...],
        grad_ref[...],
        lse_ref,
        dots_ref,
        key_clip[...],
        query_clip[...],
        add,
    )
    if last:
        dq_ref[...] = (dq_sum[...] * SCALE).T.astype(LOW)
    dk = (dk_sum[...] * SCALE).T.astype(LOW)
    dv = dv_sum[...].T.astype(LOW)
    dk_ref[...] = dk
    dv_ref[...] = dv
    dk_all[pair] = dk
    dv_all[pair] = dv

    @pl.when(pair == pl.num_programs(0) - 1)
    def _():
        pairs = dk_all.shape[0]
        dk_rows = jnp.concatenate([dk_all[index] for index in range(pairs)], axis=1)
        dv_rows = jnp.concatenate([dv_all[index] for index in range(pairs)], axis=1)
        part = dot(dk_rows, wk_ref[...], NT) + dot(dv_rows, wv_ref[...], NT)
        part_ref[...] = part.astype(part_ref.dtype)


def backward_call(first, last, key, value, query, grad_t, lse, row_dots, key_clip, query_clip, w_qkv, dq):
    rows, width = query.shape
    pairs = width // PAIR
    across = pl.BlockSpec((PAIR, rows), lambda pair: (pair, 0))
    line = pl.BlockSpec((None, 2, rows), lambda pair: (pair, 0, 0))
    columns = columns_of(rows)
    in_specs = [columns, columns, columns, across, line, line, whole(rows, 1), whole(1, rows)]
    in_specs += [
        pl.BlockSpec((width, width), lambda pair: (0, 1)),
        pl.BlockSpec((width, width), lambda pair: (0, 2)),
    ]
    operands = [key, value, query, grad_t, lse, row_dots, key_clip, query_clip, w_qkv, w_qkv]
    if not first:
        in_specs.append(across)
        operands.append(dq)
    low_rows = jax.ShapeDtypeStruct((rows, width), LOW)
    tall = pltpu.VMEM((PAIR, rows), WIDE)
    parts = pltpu.VMEM((pairs, rows, PAIR), LOW)
    return pl.pallas_call(
        functools.partial(backward_kernel, first, last),
        grid=(pairs,),
        in_specs=in_specs,
        out_specs=[columns, columns, columns if last else across, whole(rows, width)],
        out_shape=[
            low_rows,
            low_rows,
            low_rows if last else jax.ShapeDtypeStruct((width, rows), WIDE),
            jax.ShapeDtypeStruct((rows, width), WIDE if last else LOW),
        ],
        scratch_shapes=[tall, tall, tall, parts, parts],
        name="attend_back",
        cost_estimate=pl.CostEstimate(
            flops=40 * rows * rows * width, bytes_accessed=24 * rows * width, transcendentals=0
        ),
        compiler_params=pltpu.CompilerParams(vmem_limit_bytes=48 * 2**20),
    )(*operands)


MESH = pl.DeviceIdType.MESH
TURNS = ((0, 1, 2), (0, 2, 1))
STEPS = 5
ADD_ROWS = 48
FORWARD = 8


def place_bits(turn):
    group, place = lax.axis_index("dp"), lax.axis_index("blk")
    steps = []
    for bit in TURNS[turn]:
        mine = group // (1 << bit) % 2
        steps.append((mine, (group + (1 - 2 * mine) * (1 << bit), place)))
    for bit in range(2):
        mine = place // (1 << bit) % 2
        steps.append((mine, (group, place + (1 - 2 * mine) * (1 << bit))))
    return steps


def remote(source, target, sems, index, device):
    return pltpu.make_async_remote_copy(
        src_ref=source,
        dst_ref=target,
        send_sem=sems[0].at[index],
        recv_sem=sems[1].at[index],
        device_id=device,
        device_id_type=MESH,
    )


def part_of(row, rows, column, columns):
    row = row if isinstance(row, int) else pl.multiple_of(row, 16)
    column = column if isinstance(column, int) else pl.multiple_of(column, PAIR)
    return pl.ds(row, rows), pl.ds(column, columns)


def add_block(total, term, row=0, column=0):
    rows, columns = term.shape

    @pl.loop(0, rows // ADD_ROWS)
    def _(index):
        here = part_of(row + index * ADD_ROWS, ADD_ROWS, column, columns)
        there = part_of(index * ADD_ROWS, ADD_ROWS, 0, columns)
        total[here] = (total[here].astype(WIDE) + term[there].astype(WIDE)).astype(total.dtype)


def halves(shape, axes):
    shapes = []
    for axis in axes:
        shape = (shape[0] // 2, shape[1]) if axis == "r" else (shape[0], shape[1] // 2)
        shapes.append(shape)
    return shapes


class Sum:
    def __init__(self, turn, axes, corner, shape, term, result, total, arrived, sems, local_sems):
        self.term, self.result, self.total, self.arrived = term, result, total, arrived
        self.sems, self.local_sems = sems, local_sems
        self.steps = place_bits(turn)
        self.shapes = halves(shape, axes)
        self.kept, self.left = [], []
        row, column = corner
        for axis, (rows, columns), (mine, _) in zip(axes, self.shapes, self.steps):
            down, across = (rows, 0) if axis == "r" else (0, columns)
            self.left.append((row + (1 - mine) * down, rows, column + (1 - mine) * across, columns))
            row, column = row + mine * down, column + mine * across
            self.kept.append((row, rows, column, columns))

    def inside(self, place):
        row, rows, column, columns = place
        return part_of(row - self.kept[0][0], rows, column - self.kept[0][2], columns)

    def load(self):
        return pltpu.make_async_copy(
            self.term.at[part_of(*self.kept[0])], self.total, self.local_sems.at[0]
        )

    def store(self):
        return pltpu.make_async_copy(
            self.total.at[self.inside(self.kept[-1])],
            self.result.at[part_of(*self.kept[-1])],
            self.local_sems.at[1],
        )

    def gather(self, step):
        place = self.left[step]
        source = self.term.at[part_of(*place)] if step == 0 else self.total.at[self.inside(place)]
        return remote(source, self.arrived[step], self.sems, step, self.steps[step][1])

    def spread(self, step):
        here = self.result.at[part_of(*self.kept[step])]
        return remote(here, here, self.sems, STEPS + step, self.steps[step][1])

    def start(self):
        self.load().start()
        self.gather(0).start()

    def turn(self, tick):
        if tick < STEPS:
            if tick == 0:
                self.load().wait()
            self.gather(tick).wait()
            row, _, column, _ = self.kept[tick]
            add_block(self.total, self.arrived[tick], row - self.kept[0][0], column - self.kept[0][2])
            if tick + 1 < STEPS:
                self.gather(tick + 1).start()
            else:
                self.store().start()
                self.store().wait()
                self.spread(STEPS - 1).start()
        else:
            step = 2 * STEPS - 1 - tick
            self.spread(step).wait()
            if step:
                self.spread(step - 1).start()


def greet():
    group, place = lax.axis_index("dp"), lax.axis_index("blk")
    devices = [device for _, device in place_bits(0)]
    devices.append((group, 3 - place))
    barrier = pltpu.get_barrier_semaphore()
    for device in devices:
        pl.semaphore_signal(barrier, inc=1, device_id=device, device_id_type=MESH)
    pl.semaphore_wait(barrier, len(devices))


PASS_NEAR = (2, 4, 5, 6, 6, 6)
PASS_FAR = (10, 11, 12, 13, 15, 16)


def attention_kernel(*refs):
    a_in, w_ref, clips, query_clip = refs[:4]
    a_out, k_out, v_out, q_ref, acc_ref, lse_ref, attn_ref = refs[4:11]
    a_all, top_all, total_all, kv_slot, clip_slot = refs[11:16]
    a_sems, kv_sems, clip_sem, line_sends, line_receives = refs[16:]
    rows, width = q_ref.shape
    pairs = width // PAIR
    pieces = 4 * pairs
    chunk_rows = rows // pairs
    group, place = lax.axis_index("dp"), lax.axis_index("blk")
    near = (group, place + 1 - 2 * (place % 2))
    across = (group, 3 - place)
    at_end = place % 3 == 0
    at_middle = jnp.logical_not(at_end)

    def line_copy(channel, chunk, source, target, device):
        here = pl.ds(pl.multiple_of(chunk * chunk_rows, chunk_rows), chunk_rows)
        return pltpu.make_async_remote_copy(
            src_ref=source.at[here],
            dst_ref=a_all.at[target, here],
            send_sem=line_sends.at[channel, chunk],
            recv_sem=line_receives.at[channel, chunk],
            device_id=device,
            device_id_type=MESH,
        )

    channels = (
        lambda chunk: line_copy(0, chunk, a_in, 1, near),
        lambda chunk: line_copy(1, chunk, a_in, 2, across),
        lambda chunk: line_copy(2, chunk, a_all.at[2], 2, near),
        lambda chunk: line_copy(3, chunk, a_all.at[1], 3, across),
        lambda chunk: line_copy(4, chunk, a_all.at[3], 3, near),
    )
    load = pltpu.make_async_copy(a_in, a_all.at[0], a_sems.at[4])
    load.start()
    barrier = pltpu.get_barrier_semaphore()
    for device in (near, across):
        pl.semaphore_signal(barrier, inc=1, device_id=device, device_id_type=MESH)
    pl.semaphore_wait(barrier, 2)
    for chunk in range(pairs):
        channels[0](chunk).start()

    @pl.when(at_middle)
    def _():
        for chunk in range(pairs):
            channels[1](chunk).start()

    top_all[...] = jnp.full_like(top_all, -1.0e30)
    total_all[...] = jnp.zeros_like(total_all)
    acc_ref[...] = jnp.zeros_like(acc_ref)

    def keep(shard):
        return pltpu.make_async_copy(a_all.at[shard], a_out.at[shard], a_sems.at[shard])

    def clip_copy(turn):
        source = clips.at[pl.ds(pl.multiple_of(turn * rows, 8), rows)]
        return pltpu.make_async_copy(source, clip_slot, clip_sem)

    def pair_columns(pair):
        return pl.ds(pl.multiple_of(pair * PAIR, PAIR), PAIR)

    def kv_copies(turn, pair, slot):
        return [
            pltpu.make_async_copy(
                kv_slot.at[slot, side], target.at[turn, :, pair_columns(pair)], kv_sems.at[slot, side]
            )
            for side, target in enumerate((k_out, v_out))
        ]

    load.wait()
    keep(0).start()

    @pl.loop(0, pieces)
    def _(piece):
        turn, pair, slot = piece // pairs, piece % pairs, piece % 2
        for chunk, when in enumerate(PASS_NEAR):

            @pl.when(jnp.logical_and(piece == when, at_middle))
            def _():
                channels[0](chunk).wait_recv()
                channels[3](chunk).start()
                channels[1](chunk).wait_recv()
                channels[2](chunk).start()

        for chunk, when in enumerate(PASS_FAR):

            @pl.when(jnp.logical_and(piece == when, at_middle))
            def _():
                channels[3](chunk).wait_recv()
                channels[4](chunk).start()

        for shard, channel in ((1, 0), (2, 2), (3, 4)):

            @pl.when(jnp.logical_and(piece == shard * pairs, at_end))
            def _():
                for chunk in range(pairs):
                    channels[channel](chunk).wait_recv()

            @pl.when(piece == shard * pairs)
            def _():
                keep(shard).start()

        @pl.when(pair == 0)
        def _():
            clip_copy(turn).start()
            clip_copy(turn).wait()

        @pl.when(piece >= 2)
        def _():
            for copy in kv_copies(turn, pair, slot):
                copy.wait()

        columns = pair_columns(pair)

        @pl.when(turn == 0)
        def _():
            q_ref[:, columns] = dot(a_all[0], w_ref[:, columns], NN).astype(LOW)

        w_pair = jnp.concatenate(
            [w_ref[:, pair_columns(pair + pairs)], w_ref[:, pair_columns(pair + 2 * pairs)]], axis=1
        )
        kv = dot(a_all[turn], w_pair, NN).astype(LOW)
        key, value = kv[:, :PAIR], kv[:, PAIR:]
        kv_slot[slot, 0] = key
        kv_slot[slot, 1] = value
        for copy in kv_copies(turn, pair, slot):
            copy.start()
        value_t = value.T
        ones = jnp.ones((16, rows), LOW)
        value_rows = [
            jnp.concatenate([value_t[head * HEAD : (head + 1) * HEAD], ones], axis=0)
            for head in range(2)
        ]
        key_side, query_side = score_sides(key, q_ref[:, columns])
        key_clip = clip_slot[...]

        def scores(start, head):
            stop = start + QUERY_BLOCK
            result = dot(key_side, query_side[head][start:stop], NT)
            return jnp.where(key_clip == query_clip[:, start:stop], result, MASKED)

        def weights(start, head, result):
            here = slice(start, start + QUERY_BLOCK)
            before = top_all[pair, head : head + 1, here]
            top = jnp.maximum(before, jnp.max(result, axis=0, keepdims=True))
            top_all[pair, head : head + 1, here] = top
            return jnp.exp2(result - top).astype(LOW), jnp.exp2(before - top)

        def attend(start, head, expd, shrink):
            here, row = slice(start, start + QUERY_BLOCK), slice(head, head + 1)
            lanes = pl.ds(pl.multiple_of(pair * PAIR + head * HEAD, HEAD), HEAD)
            result = dot(value_rows[head], expd, NN)
            acc_ref[lanes, here] = acc_ref[lanes, here] * shrink + result[:HEAD]
            total_all[pair, row, here] = total_all[pair, row, here] * shrink + result[HEAD : HEAD + 1]

        items = work_items(rows)
        result = scores(*items[0])
        before = None
        for index, item in enumerate(items):
            following = scores(*items[index + 1]) if index + 1 < len(items) else None
            done = weights(*item, result)
            if before is not None:
                attend(*before)
            before = (*item, *done)
            result = following
        attend(*before)

        @pl.when(turn == 3)
        def _():
            for head in range(2):
                lanes = pl.ds(pl.multiple_of(pair * PAIR + head * HEAD, HEAD), HEAD)
                total = total_all[pair, head : head + 1]
                acc_ref[lanes] = acc_ref[lanes] * (1.0 / total)
                lse_ref[pair, head : head + 1] = top_all[pair, head : head + 1] + jnp.log(total) * LOG2E
            attn_ref[:, columns] = acc_ref[columns].T.astype(LOW)

    for slot in range(2):
        for copy in kv_copies(3, pairs - 2 + slot, slot):
            copy.wait()
    for shard in range(4):
        keep(shard).wait()
    for chunk in range(pairs):
        channels[0](chunk).wait_send()

    @pl.when(at_middle)
    def _():
        for channel in channels[1:]:
            for chunk in range(pairs):
                channel(chunk).wait_send()


def attention_call(a_low, w_qkv, clips, query_clip):
    rows, width = a_low.shape
    pairs = width // PAIR
    anywhere = pl.BlockSpec(memory_space=pl.ANY)
    inside = pl.BlockSpec(memory_space=pltpu.VMEM)
    four = jax.ShapeDtypeStruct((4, rows, width), LOW)
    square = jax.ShapeDtypeStruct((rows, width), LOW)
    lines = jax.ShapeDtypeStruct((pairs, 2, rows), WIDE)
    return pl.pallas_call(
        attention_kernel,
        in_specs=[anywhere, inside, anywhere, inside],
        out_specs=[anywhere] * 3 + [inside] * 4,
        out_shape=[four, four, four, square, jax.ShapeDtypeStruct((width, rows), WIDE), lines, square],
        scratch_shapes=[
            pltpu.VMEM((4, rows, width), LOW),
            pltpu.VMEM((pairs, 2, rows), WIDE),
            pltpu.VMEM((pairs, 2, rows), WIDE),
            pltpu.VMEM((2, 2, rows, PAIR), LOW),
            pltpu.VMEM((rows, 1), clips.dtype),
            pltpu.SemaphoreType.DMA((5,)),
            pltpu.SemaphoreType.DMA((2, 2)),
            pltpu.SemaphoreType.DMA,
            pltpu.SemaphoreType.DMA((5, pairs)),
            pltpu.SemaphoreType.DMA((5, pairs)),
        ],
        name="attention",
        compiler_params=pltpu.CompilerParams(
            collective_id=2, has_side_effects=True, vmem_limit_bytes=48 * 2**20
        ),
    )(a_low, w_qkv, clips, query_clip)


PARTS = (
    ("down", (0, 0), (1536, 384), "rrrrr", 0, (1, 3, 7, 9, 10, 12, 14, 15, 17, 18)),
    ("down", (0, 384), (1536, 384), "rrrrr", 1, (1, 3, 7, 8, 9, 11, 12, 14, 17, 18)),
    ("down", (1536, 0), (1536, 384), "rrrrr", 1, (2, 5, 10, 11, 13, 15, 17, 18, 21, 22)),
    ("down", (1536, 384), (1536, 384), "rrrrr", 0, (2, 5, 8, 9, 11, 12, 15, 18, 20, 21)),
    ("up", (0, 0), (768, 768), "rrrrc", 0, (2, 6, 9, 10, 12, 14, 16, 18, 23, 24)),
    ("up", (0, 768), (768, 768), "rrrrc", 1, (3, 6, 10, 12, 14, 17, 18, 21, 23, 24)),
    ("up", (0, 1536), (768, 768), "rrrrc", 0, (3, 7, 10, 12, 13, 16, 18, 20, 24, 24)),
    ("up", (0, 2304), (768, 768), "rrrrc", 1, (3, 7, 11, 13, 16, 18, 19, 23, 24, 24)),
    ("out", (0, 0), (768, 768), "rrrrc", 0, (3, 9, 10, 12, 15, 17, 18, 22, 24, 24)),
    ("qkv", (0, 0), (768, 512), "rrrrc", 0, None),
    ("qkv", (0, 512), (768, 512), "rrrrc", 1, None),
    ("qkv", (0, 1024), (768, 512), "rrrrc", 0, None),
    ("qkv", (0, 1536), (768, 768), "rrrrc", 1, None),
)


def gradient_kernel(*refs):
    keys, values, shards = refs[:3]
    q_ref, grad_ref, lse_ref, dots_ref, clips, query_clip, w_ref = refs[3:10]
    down_in, up_in, out_in, small_in = refs[10:14]
    down_out, up_out, out_out, qkv_out, small_out, input_out = refs[14:20]
    refs = refs[20:]
    kv_slot, a_slot, dq_sum, dk_sum, dv_sum, dk_all, dv_all, grad_k, grad_v, parts = refs[:10]
    from_near, from_across, qkv_term, clip_slot, small_arrived = refs[10:15]
    input_sum = dq_sum
    kv_sems, a_sem, line_sends, line_receives, sends, receives, locals_ = refs[15:22]
    small_sends, small_receives, out_sem, clip_sem = refs[22:26]
    refs = refs[26:]
    rows, width = q_ref.shape
    pairs = width // PAIR
    pieces = 4 * pairs
    group, place = lax.axis_index("dp"), lax.axis_index("blk")
    near = (group, place + 1 - 2 * (place % 2))
    across = (group, 3 - place)
    at_end = place % 3 == 0

    arrays = {
        "down": (down_in, down_out),
        "up": (up_in, up_out),
        "out": (out_in, out_out),
        "qkv": (qkv_term, qkv_out),
    }
    sums = []
    for index, (name, corner, shape, axes, turn, _) in enumerate(PARTS):
        total, arrived = refs[0], refs[1:STEPS]
        refs = refs[STEPS:]
        if name == "down":
            arrived = (qkv_term.at[:, pl.ds(index * shape[1], shape[1])], *arrived)
        else:
            arrived, refs = (refs[0], *arrived), refs[1:]
        sums.append(
            Sum(
                turn,
                axes,
                corner,
                shape,
                *arrays[name],
                total,
                arrived,
                (sends.at[index], receives.at[index]),
                locals_.at[index],
            )
        )
    early = [(each, part[5]) for each, part in zip(sums, PARTS) if part[5] is not None]
    late = [each for each, part in zip(sums, PARTS) if part[5] is None]

    chunk_rows = rows // pairs

    def chunk_of(chunk):
        return pl.ds(pl.multiple_of(chunk * chunk_rows, chunk_rows), chunk_rows)

    def line_copy(channel, chunk, source, target, device):
        return pltpu.make_async_remote_copy(
            src_ref=parts.at[source, chunk_of(chunk)],
            dst_ref=target.at[chunk_of(chunk)],
            send_sem=line_sends.at[channel, chunk],
            recv_sem=line_receives.at[channel, chunk],
            device_id=device,
            device_id_type=MESH,
        )

    def inward(source, chunk):
        return line_copy(source, chunk, source, from_near.at[source], near)

    def middle(source, chunk):
        return line_copy(3 + source, chunk, source, from_across.at[source], across)

    def outward(chunk):
        return line_copy(5, chunk, 2, from_near.at[0], near)

    def add_chunk(total, term, chunk):
        here = chunk_of(chunk)
        total[here] = (total[here].astype(WIDE) + term[here].astype(WIDE)).astype(total.dtype)

    def pair_columns(pair):
        return pl.ds(pl.multiple_of(pair * PAIR, PAIR), PAIR)

    def kv_copies(shard, pair, slot):
        return [
            pltpu.make_async_copy(
                source.at[shard, :, pair_columns(pair)], kv_slot.at[slot, side], kv_sems.at[slot, side]
            )
            for side, source in enumerate((keys, values))
        ]

    def a_copy(shard):
        return pltpu.make_async_copy(shards.at[shard], a_slot, a_sem)

    def clip_copy(turn):
        source = clips.at[pl.ds(pl.multiple_of((3 - turn) * rows, 8), rows)]
        return pltpu.make_async_copy(source, clip_slot, clip_sem)

    def of_pairs(stack):
        return jnp.concatenate([stack[pair] for pair in range(pairs)], axis=1)

    for copy in kv_copies(3, 0, 0):
        copy.start()
    greet()
    for each, _ in early:
        each.start()
    dq_sum[...] = jnp.zeros_like(dq_sum)
    grad_k[...] = jnp.zeros_like(grad_k)
    grad_v[...] = jnp.zeros_like(grad_v)
    small_out[...] = small_in[...]

    def weight_terms(d_query):
        a_copy(0).wait()
        d_key, d_value = of_pairs(dk_all), of_pairs(dv_all)
        part = dot(d_key, w_ref[:, width : 2 * width], NT) + dot(d_value, w_ref[:, 2 * width :], NT)
        if d_query is not None:
            part = part + dot(d_query, w_ref[:, :width], NT)
        small_out[:1] += jnp.sum(part * a_slot[...].astype(WIDE), axis=0, keepdims=True)
        grad_k[...] += dot(a_slot[...], d_key, TN)
        grad_v[...] += dot(a_slot[...], d_value, TN)
        return part

    @pl.loop(0, pieces)
    def _(piece):
        turn, pair, slot = piece // pairs, piece % pairs, piece % 2

        def at(when, *actions):
            @pl.when(piece == when)
            def _():
                for action in actions:
                    action()

        following = piece + 1

        @pl.when(following < pieces)
        def _():
            for copy in kv_copies(3 - following // pairs, following % pairs, following % 2):
                copy.start()

        @pl.when(pair == 1)
        def _():
            a_copy(3 - turn).start()

        for when in range(pieces):
            ends = [
                functools.partial(each.turn, tick)
                for tick in range(2 * STEPS)
                for each, ticks in early
                if ticks[tick] == when
            ]
            if ends:
                at(when, *ends)
        at_middle = jnp.logical_not(at_end)

        @pl.when(jnp.logical_and(turn > 0, at_end))
        def _():
            inward(turn - 1, pair).start()

        @pl.when(jnp.logical_and(at_middle, jnp.logical_and(piece >= FORWARD, piece < FORWARD + 2 * pairs)))
        def _():
            source, chunk = (piece - FORWARD) // pairs, (piece - FORWARD) % pairs
            inward(source, chunk).wait_recv()
            add_chunk(parts.at[source], from_near.at[source], chunk)
            middle(source, chunk).start()

        @pl.when(jnp.logical_and(at_middle, turn == 3))
        def _():
            middle(0, pair).wait_recv()
            add_chunk(parts.at[2], from_across.at[0], pair)
            outward(pair).start()

        @pl.when(pair == 0)
        def _():
            clip_copy(turn).start()
            clip_copy(turn).wait()

        for copy in kv_copies(0, pair, slot):
            copy.wait()
        columns = pair_columns(pair)

        def add(head, start, stop, dq, dk, dv):
            lanes = slice(head * HEAD, (head + 1) * HEAD)
            if start == 0:
                dv_sum[lanes], dk_sum[lanes] = dv, dk
            else:
                dv_sum[lanes] += dv
                dk_sum[lanes] += dk
            at_lanes = pl.ds(pl.multiple_of(pair * PAIR + head * HEAD, HEAD), HEAD)
            dq_sum[at_lanes, start:stop] += dq

        backward_pair(
            kv_slot[slot, 0],
            kv_slot[slot, 1],
            q_ref[:, columns],
            grad_ref[columns, :],
            lse_ref.at[pair],
            dots_ref.at[pair],
            clip_slot[...],
            query_clip[...],
            add,
        )
        dk_all[pair] = (dk_sum[...] * SCALE).T.astype(LOW)
        dv_all[pair] = dv_sum[...].T.astype(LOW)

        @pl.when(jnp.logical_and(pair == pairs - 1, turn < 3))
        def _():
            parts[turn] = weight_terms(None).astype(LOW)

    d_query = (dq_sum[...] * SCALE).T.astype(LOW)
    input_sum[...] = weight_terms(d_query)
    qkv_term[:, :width] = dot(a_slot[...], d_query, TN).astype(LOW)
    qkv_term[:, width : 2 * width] = grad_k[...].astype(LOW)
    qkv_term[:, 2 * width :] = grad_v[...].astype(LOW)

    small_steps = place_bits(0)

    def small(step):
        return remote(
            small_out, small_arrived.at[step], (small_sends, small_receives), step, small_steps[step][1]
        )

    for each in late:
        each.start()
    open_sums = [(each, [tick for tick in range(2 * STEPS) if ticks[tick] == pieces]) for each, ticks in early]
    open_sums += [(each, list(range(2 * STEPS))) for each in late]

    @pl.when(at_end)
    def _():
        @pl.loop(0, pairs)
        def _(chunk):
            for source in range(3):
                inward(source, chunk).wait_send()
            outward(chunk).wait_recv()
            add_chunk(input_sum, from_near.at[0], chunk)

    @pl.when(jnp.logical_not(at_end))
    def _():
        @pl.loop(0, pairs)
        def _(chunk):
            outward(chunk).wait_send()
            for source in range(2):
                middle(source, chunk).wait_send()
            middle(1, chunk).wait_recv()
            add_chunk(input_sum, from_across.at[1], chunk)
            inward(2, chunk).wait_recv()
            add_chunk(input_sum, from_near.at[2], chunk)

    store = pltpu.make_async_copy(input_sum, input_out, out_sem)
    store.start()
    for tick in range(2 * STEPS):
        if tick < STEPS:
            small(tick).start()
        for each, ticks in open_sums:
            if ticks:
                each.turn(ticks.pop(0))
        if tick < STEPS:
            small(tick).wait()
            small_out[...] += small_arrived[tick]
    store.wait()


def gradient_call(
    keys, values, shards, query, grad_t, lse, row_dots, clips, query_clip, w_qkv, grad_down, grad_up, grad_out, small
):
    rows, width = query.shape
    pairs = width // PAIR
    anywhere = pl.BlockSpec(memory_space=pl.ANY)
    inside = pl.BlockSpec(memory_space=pltpu.VMEM)
    square = (rows, width)
    scratch = [
        pltpu.VMEM((2, 2, rows, PAIR), LOW),
        pltpu.VMEM(square, LOW),
        pltpu.VMEM((width, rows), WIDE),
        pltpu.VMEM((PAIR, rows), WIDE),
        pltpu.VMEM((PAIR, rows), WIDE),
        pltpu.VMEM((pairs, rows, PAIR), LOW),
        pltpu.VMEM((pairs, rows, PAIR), LOW),
        pltpu.VMEM((width, width), WIDE),
        pltpu.VMEM((width, width), WIDE),
        pltpu.VMEM((3, *square), LOW),
    ]
    scratch += [pltpu.VMEM((3, *square), LOW), pltpu.VMEM((2, *square), LOW)]
    scratch += [
        pltpu.VMEM((width, 3 * width), LOW),
        pltpu.VMEM((rows, 1), clips.dtype),
        pltpu.VMEM((STEPS, *small.shape), WIDE),
        pltpu.SemaphoreType.DMA((2, 2)),
        pltpu.SemaphoreType.DMA,
        pltpu.SemaphoreType.DMA((6, pairs)),
        pltpu.SemaphoreType.DMA((6, pairs)),
        pltpu.SemaphoreType.DMA((len(PARTS), 2 * STEPS)),
        pltpu.SemaphoreType.DMA((len(PARTS), 2 * STEPS)),
        pltpu.SemaphoreType.DMA((len(PARTS), 2)),
        pltpu.SemaphoreType.DMA((STEPS,)),
        pltpu.SemaphoreType.DMA((STEPS,)),
        pltpu.SemaphoreType.DMA,
        pltpu.SemaphoreType.DMA,
    ]
    for name, _, shape, axes, _, _ in PARTS:
        shapes = halves(shape, axes)
        scratch += [pltpu.VMEM(each, LOW) for each in (shapes[0], *shapes[1:])]
        if name != "down":
            scratch.append(pltpu.VMEM(shapes[0], LOW))
    like = lambda array: jax.ShapeDtypeStruct(array.shape, array.dtype)
    return pl.pallas_call(
        gradient_kernel,
        in_specs=[anywhere] * 3 + [inside] * 4 + [anywhere] + [inside] * 2 + [anywhere] * 3 + [inside],
        out_specs=[anywhere] * 4 + [inside, anywhere],
        out_shape=[
            like(grad_down),
            like(grad_up),
            like(grad_out),
            jax.ShapeDtypeStruct((width, 3 * width), LOW),
            like(small),
            jax.ShapeDtypeStruct(square, WIDE),
        ],
        scratch_shapes=scratch,
        name="gradients",
        compiler_params=pltpu.CompilerParams(
            collective_id=1, has_side_effects=True, vmem_limit_bytes=62 * 2**20
        ),
    )(
        keys, values, shards, query, grad_t, lse, row_dots, clips, query_clip, w_qkv,
        grad_down, grad_up, grad_out, small,
    )


def on_device(
    groups, inputs, positions, segments, gain_attn, w_qkv, w_out, gain_mlp, w_up, b_up, w_down, cotangent
):
    rows, width = inputs.shape
    pairs = width // PAIR
    place = lax.axis_index("blk")
    w_query = w_qkv[:, :width]

    def send(value, pairs_of_places):
        return lax.ppermute(value, "blk", pairs_of_places)

    hidden = inputs + position_table(positions, width)
    normed_attn, inverse_attn = normalize(hidden)
    a_low = (normed_attn * gain_attn).astype(LOW)

    table = jnp.array([[0, 1, 2, 3], [1, 0, 2, 3], [2, 3, 1, 0], [3, 2, 1, 0]], jnp.int32)
    order = lax.dynamic_index_in_dim(table, place, keepdims=False)
    clips = jnp.concatenate(
        [lax.dynamic_slice_in_dim(segments, order[index] * rows, rows) for index in range(4)]
    )[:, None]
    query_clip = lax.dynamic_slice_in_dim(segments, place * rows, rows)[None, :]
    shards, keys, values, query, attended, lse, attn_low = attention_call(
        a_low, w_qkv, clips, query_clip
    )

    resid = hidden + dot(attn_low, w_out, NN)
    normed_mlp, inverse_mlp = normalize(resid)
    b_low = (normed_mlp * gain_mlp).astype(LOW)
    pre_act = dot(b_low, w_up, NN) + b_up
    cumulative = 0.5 * (1.0 + lax.erf(pre_act * 0.7071067811865476))
    density = jnp.exp(-0.5 * pre_act * pre_act) * 0.3989422804014327
    z_low = (pre_act * cumulative).astype(LOW)
    outputs = resid + dot(z_low, w_down, NN)
    dy_low = cotangent.astype(LOW)
    grad_down = dot(z_low, dy_low, TN).astype(LOW)
    d_gelu = dot(dy_low, w_down, NT)
    d_pre = (d_gelu * (cumulative + pre_act * density)).astype(LOW)
    grad_up = dot(b_low, d_pre, TN).astype(LOW)
    grad_bias_up = jnp.sum(d_pre.astype(WIDE), axis=0)
    d_normed = dot(d_pre, w_up, NT)
    grad_gain_mlp = jnp.sum(d_normed * normed_mlp, axis=0)
    d_resid = cotangent + norm_back(d_normed * gain_mlp, normed_mlp, inverse_mlp)
    dr_low = d_resid.astype(LOW)
    grad_out = dot(attn_low, dr_low, TN).astype(LOW)
    d_attn_t = dot(w_out, dr_low, NT).astype(LOW)
    row_dots = jnp.sum(
        (d_attn_t.astype(WIDE) * attended).reshape(pairs, 2, HEAD, rows), axis=2
    )

    if groups == 8 and rows == width:
        small = jnp.concatenate([jnp.zeros_like(gain_attn), grad_gain_mlp, grad_bias_up])
        sum_down, sum_up, sum_out, sum_qkv, sum_small, d_normed_attn = gradient_call(
            keys,
            values,
            shards,
            query,
            d_attn_t,
            lse,
            row_dots,
            clips,
            query_clip,
            w_qkv,
            grad_down,
            grad_up,
            grad_out,
            jnp.pad(small.reshape(6, width), ((0, 2), (0, 0))),
        )
        input_grad = d_resid + norm_back(d_normed_attn * gain_attn, normed_attn, inverse_attn)
        return (
            outputs,
            input_grad,
            sum_small[0] / gain_attn,
            sum_qkv.astype(WIDE),
            sum_out.astype(WIDE),
            sum_small[1],
            sum_up.astype(WIDE),
            sum_small[2:6].reshape(-1),
            sum_down.astype(WIDE),
        )

    everywhere = ("dp", "blk")

    def back(index, dq):
        return backward_call(
            index == 3,
            index == 0,
            keys[index],
            values[index],
            query,
            d_attn_t,
            lse,
            row_dots,
            clips[index * rows : (index + 1) * rows],
            query_clip,
            w_qkv,
            dq,
        )

    middle, outward, inward = [(1, 2), (2, 1)], [(1, 0), (2, 3)], [(0, 1), (3, 2)]
    dk_3, dv_3, dq, part_3 = back(3, None)
    far = send(part_3, inward)
    dk_2, dv_2, dq, part_2 = back(2, dq)
    far, part_2, dq = lax.optimization_barrier((far, part_2, dq))
    onward = (part_3.astype(WIDE) + far.astype(WIDE)).astype(LOW)
    mid_3 = send(onward, middle)
    mid_2 = send(part_2, inward)
    dq, onward = lax.optimization_barrier((dq, onward))
    dk_1, dv_1, dq, part_1 = back(1, dq)
    mid_3, mid_2, part_1, dq = lax.optimization_barrier((mid_3, mid_2, part_1, dq))
    onward_1 = (part_2.astype(WIDE) + mid_2.astype(WIDE)).astype(LOW)
    onward_2 = (part_1.astype(WIDE) + mid_3.astype(WIDE)).astype(LOW)
    last_1 = send(onward_1, middle)
    last_2 = send(onward_2, outward)
    last_3 = send(part_1, inward)
    dq, onward_1, onward_2 = lax.optimization_barrier((dq, onward_1, onward_2))
    dk_0, dv_0, dq, part_0 = back(0, dq)
    grad_query = dot(a_low, dq, TN).astype(LOW)
    d_keys, d_values = (dk_0, dk_1, dk_2, dk_3), (dv_0, dv_1, dv_2, dv_3)
    grad_key = sum(dot(shard, term, TN) for shard, term in zip(shards, d_keys)).astype(LOW)
    grad_value = sum(dot(shard, term, TN) for shard, term in zip(shards, d_values)).astype(LOW)
    d_normed_attn = (
        part_0
        + dot(dq, w_query, NT)
        + last_1.astype(WIDE)
        + last_2.astype(WIDE)
        + last_3.astype(WIDE)
    )
    grad_gain_attn = jnp.sum(d_normed_attn * normed_attn, axis=0)
    input_grad = d_resid + norm_back(d_normed_attn * gain_attn, normed_attn, inverse_attn)
    small = jnp.concatenate([grad_gain_attn, grad_gain_mlp, grad_bias_up])
    sums = lax.psum((grad_down, grad_up, grad_out, grad_query, grad_key, grad_value), everywhere)
    sum_small = lax.psum(small, everywhere)
    sum_down, sum_up, sum_out, *sum_qkv = sums
    return (
        outputs,
        input_grad,
        sum_small[:width],
        jnp.concatenate(sum_qkv, axis=1).astype(WIDE),
        sum_out.astype(WIDE),
        sum_small[width : 2 * width],
        sum_up.astype(WIDE),
        sum_small[2 * width :],
        sum_down.astype(WIDE),
    )


def solution(mesh):
    rows = P(("dp", "blk"), None)
    placed = (rows, P(("dp", "blk")), P("dp"), P(), P(), P(), P(), P(), P(), P(), rows)
    return jax.shard_map(
        functools.partial(on_device, mesh.shape["dp"]),
        mesh=mesh,
        in_specs=placed,
        out_specs=(rows, rows, P(), P(), P(), P(), P(), P(), P()),
        check_vma=False,
    )
```

```python
import functools
import math

import jax
import jax.numpy as jnp
from jax import lax
from jax.experimental import pallas as pl
from jax.experimental.pallas import tpu as pltpu
from jax.sharding import PartitionSpec as P

HEADS = 12
HEAD = 64
PAIR = 2 * HEAD
SCALE = HEAD**-0.5
LOG2E = 1.4426950408889634
MASKED = -1.0e9
QUERY_BLOCK = 384
EPS_NORM = 1e-06
LOW = jnp.bfloat16
WIDE = jnp.float32

NN = (((1,), (0,)), ((), ()))
NT = (((1,), (1,)), ((), ()))
TN = (((0,), (0,)), ((), ()))


def dot(left, right, dims):
    return lax.dot_general(left, right, dims, preferred_element_type=WIDE)


def position_table(positions, model_width):
    half_width = model_width // 2
    freqs = jnp.exp(jnp.arange(half_width, dtype=WIDE) * (-math.log(10000.0) / half_width))
    angles = positions.astype(WIDE)[:, None] * freqs[None, :]
    return jnp.concatenate([jnp.sin(angles), jnp.cos(angles)], axis=1)


def normalize(values):
    center = values - jnp.mean(values, axis=-1, keepdims=True)
    inverse = lax.rsqrt(jnp.mean(center * center, axis=-1, keepdims=True) + EPS_NORM)
    return center * inverse, inverse


def norm_back(grad_norm, normed, inverse):
    first = jnp.mean(grad_norm, axis=-1, keepdims=True)
    second = jnp.mean(grad_norm * normed, axis=-1, keepdims=True)
    return inverse * (grad_norm - first - normed * second)


def in_head(values, head):
    lanes = lax.broadcasted_iota(jnp.int32, values.shape, 1)
    return (lanes < HEAD) == (head == 0)


def only_head(values, head, other=None):
    other = jnp.zeros_like(values) if other is None else other
    return jnp.where(in_head(values, head), values, other)


def split_scaled(query):
    scaled = query.astype(WIDE) * (SCALE * LOG2E)
    high = scaled.astype(LOW)
    return high, (scaled - high.astype(WIDE)).astype(LOW)


def score_sides(key, query):
    high, low = split_scaled(query)
    key_side = jnp.concatenate([key, key], axis=1)
    query_side = [
        jnp.concatenate([only_head(high, head), only_head(low, head)], axis=1) for head in range(2)
    ]
    return key_side, query_side


def work_items(rows):
    return [(start, head) for start in range(0, rows, QUERY_BLOCK) for head in range(2)]


def whole(*shape):
    return pl.BlockSpec(shape, lambda pair: (0,) * len(shape))


def columns_of(rows, first=0):
    return pl.BlockSpec((rows, PAIR), lambda pair: (0, pair + first))


def backward_pair(key, value, query, grad_t, lse, row_dots, key_clip, query_clip, add):
    rows = query.shape[0]
    grad = grad_t.T
    key_t, query_t = key.T, query.T
    key_side, query_side = score_sides(key, query)
    grad_side = [only_head(grad, head) for head in range(2)]
    for start, head in work_items(rows):
        stop = start + QUERY_BLOCK
        lanes, row = slice(head * HEAD, (head + 1) * HEAD), slice(head, head + 1)
        score = dot(key_side, query_side[head][start:stop], NT)
        score = jnp.where(key_clip == query_clip[:, start:stop], score, MASKED)
        probs = jnp.exp2(score - lse[row, start:stop])
        d_probs = dot(value, grad_side[head][start:stop], NT)
        d_scores = (probs * (d_probs - row_dots[row, start:stop])).astype(LOW)
        probs = probs.astype(LOW)
        dv = dot(grad_t[lanes, start:stop], probs, NT)
        dk = dot(query_t[lanes, start:stop], d_scores, NT)
        dq = dot(key_t[lanes], d_scores, NN)
        add(head, start, stop, dq, dk, dv)


def backward_kernel(first, last, *refs):
    k_ref, v_ref, q_ref, grad_ref, lse_ref, dots_ref, key_clip, query_clip, wk_ref, wv_ref = refs[:10]
    refs = refs[10:]
    if not first:
        dq_in = refs[0]
        refs = refs[1:]
    dk_ref, dv_ref, dq_ref, part_ref, dk_sum, dv_sum, dq_sum, dk_all, dv_all = refs
    pair = pl.program_id(0)
    rows = q_ref.shape[0]

    def add(head, start, stop, dq, dk, dv):
        lanes = slice(head * HEAD, (head + 1) * HEAD)
        if start == 0:
            dv_sum[lanes], dk_sum[lanes] = dv, dk
        else:
            dv_sum[lanes] += dv
            dk_sum[lanes] += dk
        if not first:
            dq = dq + dq_in[lanes, start:stop]
        if last:
            dq_sum[lanes, start:stop] = dq
        else:
            dq_ref[lanes, start:stop] = dq

    backward_pair(
        k_ref[...],
        v_ref[...],
        q_ref[...],
        grad_ref[...],
        lse_ref,
        dots_ref,
        key_clip[...],
        query_clip[...],
        add,
    )
    if last:
        dq_ref[...] = (dq_sum[...] * SCALE).T.astype(LOW)
    dk = (dk_sum[...] * SCALE).T.astype(LOW)
    dv = dv_sum[...].T.astype(LOW)
    dk_ref[...] = dk
    dv_ref[...] = dv
    dk_all[pair] = dk
    dv_all[pair] = dv

    @pl.when(pair == pl.num_programs(0) - 1)
    def _():
        pairs = dk_all.shape[0]
        dk_rows = jnp.concatenate([dk_all[index] for index in range(pairs)], axis=1)
        dv_rows = jnp.concatenate([dv_all[index] for index in range(pairs)], axis=1)
        part = dot(dk_rows, wk_ref[...], NT) + dot(dv_rows, wv_ref[...], NT)
        part_ref[...] = part.astype(part_ref.dtype)


def backward_call(first, last, key, value, query, grad_t, lse, row_dots, key_clip, query_clip, w_qkv, dq):
    rows, width = query.shape
    pairs = width // PAIR
    across = pl.BlockSpec((PAIR, rows), lambda pair: (pair, 0))
    line = pl.BlockSpec((None, 2, rows), lambda pair: (pair, 0, 0))
    columns = columns_of(rows)
    in_specs = [columns, columns, columns, across, line, line, whole(rows, 1), whole(1, rows)]
    in_specs += [
        pl.BlockSpec((width, width), lambda pair: (0, 1)),
        pl.BlockSpec((width, width), lambda pair: (0, 2)),
    ]
    operands = [key, value, query, grad_t, lse, row_dots, key_clip, query_clip, w_qkv, w_qkv]
    if not first:
        in_specs.append(across)
        operands.append(dq)
    low_rows = jax.ShapeDtypeStruct((rows, width), LOW)
    tall = pltpu.VMEM((PAIR, rows), WIDE)
    parts = pltpu.VMEM((pairs, rows, PAIR), LOW)
    return pl.pallas_call(
        functools.partial(backward_kernel, first, last),
        grid=(pairs,),
        in_specs=in_specs,
        out_specs=[columns, columns, columns if last else across, whole(rows, width)],
        out_shape=[
            low_rows,
            low_rows,
            low_rows if last else jax.ShapeDtypeStruct((width, rows), WIDE),
            jax.ShapeDtypeStruct((rows, width), WIDE if last else LOW),
        ],
        scratch_shapes=[tall, tall, tall, parts, parts],
        name="attend_back",
        cost_estimate=pl.CostEstimate(
            flops=40 * rows * rows * width, bytes_accessed=24 * rows * width, transcendentals=0
        ),
        compiler_params=pltpu.CompilerParams(vmem_limit_bytes=48 * 2**20),
    )(*operands)


MESH = pl.DeviceIdType.MESH
TURNS = ((0, 1, 2), (0, 2, 1))
STEPS = 5
ADD_ROWS = 48
FORWARD = 8


def place_bits(turn):
    group, place = lax.axis_index("dp"), lax.axis_index("blk")
    steps = []
    for bit in TURNS[turn]:
        mine = group // (1 << bit) % 2
        steps.append((mine, (group + (1 - 2 * mine) * (1 << bit), place)))
    for bit in range(2):
        mine = place // (1 << bit) % 2
        steps.append((mine, (group, place + (1 - 2 * mine) * (1 << bit))))
    return steps


def remote(source, target, sems, index, device):
    return pltpu.make_async_remote_copy(
        src_ref=source,
        dst_ref=target,
        send_sem=sems[0].at[index],
        recv_sem=sems[1].at[index],
        device_id=device,
        device_id_type=MESH,
    )


def part_of(row, rows, column, columns):
    row = row if isinstance(row, int) else pl.multiple_of(row, 16)
    column = column if isinstance(column, int) else pl.multiple_of(column, PAIR)
    return pl.ds(row, rows), pl.ds(column, columns)


def add_block(total, term, row=0, column=0):
    rows, columns = term.shape

    @pl.loop(0, rows // ADD_ROWS)
    def _(index):
        here = part_of(row + index * ADD_ROWS, ADD_ROWS, column, columns)
        there = part_of(index * ADD_ROWS, ADD_ROWS, 0, columns)
        total[here] = (total[here].astype(WIDE) + term[there].astype(WIDE)).astype(total.dtype)


def halves(shape, axes):
    shapes = []
    for axis in axes:
        shape = (shape[0] // 2, shape[1]) if axis == "r" else (shape[0], shape[1] // 2)
        shapes.append(shape)
    return shapes


class Sum:
    def __init__(self, turn, axes, corner, shape, term, result, total, arrived, sems, local_sems):
        self.term, self.result, self.total, self.arrived = term, result, total, arrived
        self.sems, self.local_sems = sems, local_sems
        self.steps = place_bits(turn)
        self.shapes = halves(shape, axes)
        self.kept, self.left = [], []
        row, column = corner
        for axis, (rows, columns), (mine, _) in zip(axes, self.shapes, self.steps):
            down, across = (rows, 0) if axis == "r" else (0, columns)
            self.left.append((row + (1 - mine) * down, rows, column + (1 - mine) * across, columns))
            row, column = row + mine * down, column + mine * across
            self.kept.append((row, rows, column, columns))

    def inside(self, place):
        row, rows, column, columns = place
        return part_of(row - self.kept[0][0], rows, column - self.kept[0][2], columns)

    def load(self):
        return pltpu.make_async_copy(
            self.term.at[part_of(*self.kept[0])], self.total, self.local_sems.at[0]
        )

    def store(self):
        return pltpu.make_async_copy(
            self.total.at[self.inside(self.kept[-1])],
            self.result.at[part_of(*self.kept[-1])],
            self.local_sems.at[1],
        )

    def gather(self, step):
        place = self.left[step]
        source = self.term.at[part_of(*place)] if step == 0 else self.total.at[self.inside(place)]
        return remote(source, self.arrived[step], self.sems, step, self.steps[step][1])

    def spread(self, step):
        here = self.result.at[part_of(*self.kept[step])]
        return remote(here, here, self.sems, STEPS + step, self.steps[step][1])

    def start(self):
        self.load().start()
        self.gather(0).start()

    def turn(self, tick):
        if tick < STEPS:
            if tick == 0:
                self.load().wait()
            self.gather(tick).wait()
            row, _, column, _ = self.kept[tick]
            add_block(self.total, self.arrived[tick], row - self.kept[0][0], column - self.kept[0][2])
            if tick + 1 < STEPS:
                self.gather(tick + 1).start()
            else:
                self.store().start()
                self.store().wait()
                self.spread(STEPS - 1).start()
        else:
            step = 2 * STEPS - 1 - tick
            self.spread(step).wait()
            if step:
                self.spread(step - 1).start()


def greet():
    group, place = lax.axis_index("dp"), lax.axis_index("blk")
    devices = [device for _, device in place_bits(0)]
    devices.append((group, 3 - place))
    barrier = pltpu.get_barrier_semaphore()
    for device in devices:
        pl.semaphore_signal(barrier, inc=1, device_id=device, device_id_type=MESH)
    pl.semaphore_wait(barrier, len(devices))


PASS_NEAR = (2, 4, 5, 6, 6, 6)
PASS_FAR = (10, 11, 12, 13, 15, 16)


def attention_kernel(*refs):
    a_in, w_ref, clips, query_clip = refs[:4]
    a_out, k_out, v_out, q_ref, acc_ref, lse_ref, attn_ref = refs[4:11]
    a_all, top_all, total_all, kv_slot, clip_slot = refs[11:16]
    a_sems, kv_sems, clip_sem, line_sends, line_receives = refs[16:]
    rows, width = q_ref.shape
    pairs = width // PAIR
    pieces = 4 * pairs
    chunk_rows = rows // pairs
    group, place = lax.axis_index("dp"), lax.axis_index("blk")
    near = (group, place + 1 - 2 * (place % 2))
    across = (group, 3 - place)
    at_end = place % 3 == 0
    at_middle = jnp.logical_not(at_end)

    def line_copy(channel, chunk, source, target, device):
        here = pl.ds(pl.multiple_of(chunk * chunk_rows, chunk_rows), chunk_rows)
        return pltpu.make_async_remote_copy(
            src_ref=source.at[here],
            dst_ref=a_all.at[target, here],
            send_sem=line_sends.at[channel, chunk],
            recv_sem=line_receives.at[channel, chunk],
            device_id=device,
            device_id_type=MESH,
        )

    channels = (
        lambda chunk: line_copy(0, chunk, a_in, 1, near),
        lambda chunk: line_copy(1, chunk, a_in, 2, across),
        lambda chunk: line_copy(2, chunk, a_all.at[2], 2, near),
        lambda chunk: line_copy(3, chunk, a_all.at[1], 3, across),
        lambda chunk: line_copy(4, chunk, a_all.at[3], 3, near),
    )
    load = pltpu.make_async_copy(a_in, a_all.at[0], a_sems.at[4])
    load.start()
    barrier = pltpu.get_barrier_semaphore()
    for device in (near, across):
        pl.semaphore_signal(barrier, inc=1, device_id=device, device_id_type=MESH)
    pl.semaphore_wait(barrier, 2)
    for chunk in range(pairs):
        channels[0](chunk).start()

    @pl.when(at_middle)
    def _():
        for chunk in range(pairs):
            channels[1](chunk).start()

    top_all[...] = jnp.full_like(top_all, -1.0e30)
    total_all[...] = jnp.zeros_like(total_all)
    acc_ref[...] = jnp.zeros_like(acc_ref)

    def keep(shard):
        return pltpu.make_async_copy(a_all.at[shard], a_out.at[shard], a_sems.at[shard])

    def clip_copy(turn):
        source = clips.at[pl.ds(pl.multiple_of(turn * rows, 8), rows)]
        return pltpu.make_async_copy(source, clip_slot, clip_sem)

    def pair_columns(pair):
        return pl.ds(pl.multiple_of(pair * PAIR, PAIR), PAIR)

    def kv_copies(turn, pair, slot):
        return [
            pltpu.make_async_copy(
                kv_slot.at[slot, side], target.at[turn, :, pair_columns(pair)], kv_sems.at[slot, side]
            )
            for side, target in enumerate((k_out, v_out))
        ]

    load.wait()
    keep(0).start()

    @pl.loop(0, pieces)
    def _(piece):
        turn, pair, slot = piece // pairs, piece % pairs, piece % 2
        for chunk, when in enumerate(PASS_NEAR):

            @pl.when(jnp.logical_and(piece == when, at_middle))
            def _():
                channels[0](chunk).wait_recv()
                channels[3](chunk).start()
                channels[1](chunk).wait_recv()
                channels[2](chunk).start()

        for chunk, when in enumerate(PASS_FAR):

            @pl.when(jnp.logical_and(piece == when, at_middle))
            def _():
                channels[3](chunk).wait_recv()
                channels[4](chunk).start()

        for shard, channel in ((1, 0), (2, 2), (3, 4)):

            @pl.when(jnp.logical_and(piece == shard * pairs, at_end))
            def _():
                for chunk in range(pairs):
                    channels[channel](chunk).wait_recv()

            @pl.when(piece == shard * pairs)
            def _():
                keep(shard).start()

        @pl.when(pair == 0)
        def _():
            clip_copy(turn).start()
            clip_copy(turn).wait()

        @pl.when(piece >= 2)
        def _():
            for copy in kv_copies(turn, pair, slot):
                copy.wait()

        columns = pair_columns(pair)

        @pl.when(turn == 0)
        def _():
            q_ref[:, columns] = dot(a_all[0], w_ref[:, columns], NN).astype(LOW)

        w_pair = jnp.concatenate(
            [w_ref[:, pair_columns(pair + pairs)], w_ref[:, pair_columns(pair + 2 * pairs)]], axis=1
        )
        kv = dot(a_all[turn], w_pair, NN).astype(LOW)
        key, value = kv[:, :PAIR], kv[:, PAIR:]
        kv_slot[slot, 0] = key
        kv_slot[slot, 1] = value
        for copy in kv_copies(turn, pair, slot):
            copy.start()
        value_t = value.T
        ones = jnp.ones((16, rows), LOW)
        value_rows = [
            jnp.concatenate([value_t[head * HEAD : (head + 1) * HEAD], ones], axis=0)
            for head in range(2)
        ]
        key_side, query_side = score_sides(key, q_ref[:, columns])
        key_clip = clip_slot[...]

        def scores(start, head):
            stop = start + QUERY_BLOCK
            result = dot(key_side, query_side[head][start:stop], NT)
            return jnp.where(key_clip == query_clip[:, start:stop], result, MASKED)

        def weights(start, head, result):
            here = slice(start, start + QUERY_BLOCK)
            before = top_all[pair, head : head + 1, here]
            top = jnp.maximum(before, jnp.max(result, axis=0, keepdims=True))
            top_all[pair, head : head + 1, here] = top
            return jnp.exp2(result - top).astype(LOW), jnp.exp2(before - top)

        def attend(start, head, expd, shrink):
            here, row = slice(start, start + QUERY_BLOCK), slice(head, head + 1)
            lanes = pl.ds(pl.multiple_of(pair * PAIR + head * HEAD, HEAD), HEAD)
            result = dot(value_rows[head], expd, NN)
            acc_ref[lanes, here] = acc_ref[lanes, here] * shrink + result[:HEAD]
            total_all[pair, row, here] = total_all[pair, row, here] * shrink + result[HEAD : HEAD + 1]

        items = work_items(rows)
        result = scores(*items[0])
        before = None
        for index, item in enumerate(items):
            following = scores(*items[index + 1]) if index + 1 < len(items) else None
            done = weights(*item, result)
            if before is not None:
                attend(*before)
            before = (*item, *done)
            result = following
        attend(*before)

        @pl.when(turn == 3)
        def _():
            for head in range(2):
                lanes = pl.ds(pl.multiple_of(pair * PAIR + head * HEAD, HEAD), HEAD)
                total = total_all[pair, head : head + 1]
                acc_ref[lanes] = acc_ref[lanes] * (1.0 / total)
                lse_ref[pair, head : head + 1] = top_all[pair, head : head + 1] + jnp.log(total) * LOG2E
            attn_ref[:, columns] = acc_ref[columns].T.astype(LOW)

    for slot in range(2):
        for copy in kv_copies(3, pairs - 2 + slot, slot):
            copy.wait()
    for shard in range(4):
        keep(shard).wait()
    for chunk in range(pairs):
        channels[0](chunk).wait_send()

    @pl.when(at_middle)
    def _():
        for channel in channels[1:]:
            for chunk in range(pairs):
                channel(chunk).wait_send()


def attention_call(a_low, w_qkv, clips, query_clip):
    rows, width = a_low.shape
    pairs = width // PAIR
    anywhere = pl.BlockSpec(memory_space=pl.ANY)
    inside = pl.BlockSpec(memory_space=pltpu.VMEM)
    four = jax.ShapeDtypeStruct((4, rows, width), LOW)
    square = jax.ShapeDtypeStruct((rows, width), LOW)
    lines = jax.ShapeDtypeStruct((pairs, 2, rows), WIDE)
    return pl.pallas_call(
        attention_kernel,
        in_specs=[anywhere, inside, anywhere, inside],
        out_specs=[anywhere] * 3 + [inside] * 4,
        out_shape=[four, four, four, square, jax.ShapeDtypeStruct((width, rows), WIDE), lines, square],
        scratch_shapes=[
            pltpu.VMEM((4, rows, width), LOW),
            pltpu.VMEM((pairs, 2, rows), WIDE),
            pltpu.VMEM((pairs, 2, rows), WIDE),
            pltpu.VMEM((2, 2, rows, PAIR), LOW),
            pltpu.VMEM((rows, 1), clips.dtype),
            pltpu.SemaphoreType.DMA((5,)),
            pltpu.SemaphoreType.DMA((2, 2)),
            pltpu.SemaphoreType.DMA,
            pltpu.SemaphoreType.DMA((5, pairs)),
            pltpu.SemaphoreType.DMA((5, pairs)),
        ],
        name="attention",
        compiler_params=pltpu.CompilerParams(
            collective_id=2, has_side_effects=True, vmem_limit_bytes=48 * 2**20
        ),
    )(a_low, w_qkv, clips, query_clip)


FF_BLOCK = 512
ROW_BLOCK = 384


def mlp_kernel(
    hidden_ref,
    attn_ref,
    attended_ref,
    cotangent_ref,
    w_out_ref,
    gain_ref,
    w_up_ref,
    b_up_ref,
    w_down_ref,
    outputs_ref,
    d_resid_ref,
    grad_t_ref,
    dots_ref,
    grad_down_ref,
    grad_up_ref,
    grad_out_ref,
    grad_gain_ref,
    grad_bias_ref,
    normed_ref,
    inverse_ref,
    b_ref,
    dy_ref,
    db_ref,
    z_ref,
    d_pre_ref,
):
    block = pl.program_id(0)
    rows = hidden_ref.shape[0]

    @pl.when(block == 0)
    def _():
        resid = hidden_ref[...] + dot(attn_ref[...], w_out_ref[...], NN)
        normed, inverse = normalize(resid)
        normed_ref[...] = normed
        inverse_ref[...] = inverse
        b_ref[...] = (normed * gain_ref[...]).astype(LOW)
        dy_ref[...] = cotangent_ref[...].astype(LOW)
        outputs_ref[...] = resid
        db_ref[...] = jnp.zeros_like(db_ref)

    bias = jnp.zeros((1, FF_BLOCK), WIDE)
    for start in range(0, rows, ROW_BLOCK):
        here = slice(start, start + ROW_BLOCK)
        pre_act = dot(b_ref[here], w_up_ref[...], NN) + b_up_ref[...]
        cumulative = 0.5 * (1.0 + lax.erf(pre_act * 0.7071067811865476))
        density = jnp.exp(-0.5 * pre_act * pre_act) * 0.3989422804014327
        z_ref[here] = (pre_act * cumulative).astype(LOW)
        d_gelu = dot(dy_ref[here], w_down_ref[...], NT)
        d_pre = (d_gelu * (cumulative + pre_act * density)).astype(LOW)
        d_pre_ref[here] = d_pre
        bias += jnp.sum(d_pre.astype(WIDE), axis=0, keepdims=True)
        outputs_ref[here] += dot(z_ref[here], w_down_ref[...], NN)
        db_ref[here] += dot(d_pre, w_up_ref[...], NT)
    grad_bias_ref[...] = bias
    grad_down_ref[...] = dot(z_ref[...], dy_ref[...], TN).astype(LOW)
    grad_up_ref[...] = dot(b_ref[...], d_pre_ref[...], TN).astype(LOW)

    @pl.when(block == pl.num_programs(0) - 1)
    def _():
        normed, db = normed_ref[...], db_ref[...]
        grad_gain_ref[...] = jnp.sum(db * normed, axis=0, keepdims=True)
        d_resid = cotangent_ref[...] + norm_back(db * gain_ref[...], normed, inverse_ref[...])
        d_resid_ref[...] = d_resid
        dr_low = d_resid.astype(LOW)
        grad_out_ref[...] = dot(attn_ref[...], dr_low, TN).astype(LOW)
        grad_t = dot(w_out_ref[...], dr_low, NT).astype(LOW)
        grad_t_ref[...] = grad_t
        product = grad_t.astype(WIDE) * attended_ref[...]
        for pair in range(dots_ref.shape[0]):
            for head in range(2):
                lanes = slice(pair * PAIR + head * HEAD, pair * PAIR + (head + 1) * HEAD)
                dots_ref[pair, head : head + 1] = jnp.sum(product[lanes], axis=0, keepdims=True)


def mlp_call(hidden, attn_low, attended, cotangent, w_out, gain_mlp, w_up, b_up, w_down):
    rows, width = hidden.shape
    hidden_units = w_up.shape[1]
    pairs = width // PAIR
    once = lambda *shape: pl.BlockSpec(
        shape, lambda block: (0,) * len(shape), pipeline_mode=pl.Buffered(1)
    )
    square, line = once(rows, width), once(1, width)
    up = pl.BlockSpec((width, FF_BLOCK), lambda block: (0, block))
    down = pl.BlockSpec((FF_BLOCK, width), lambda block: (block, 0))
    bias = pl.BlockSpec((1, FF_BLOCK), lambda block: (0, block))
    wide = jax.ShapeDtypeStruct((rows, width), WIDE)
    return pl.pallas_call(
        mlp_kernel,
        grid=(hidden_units // FF_BLOCK,),
        in_specs=[square] * 4 + [once(width, width), line, up, bias, down],
        out_specs=[
            whole(rows, width),
            whole(rows, width),
            whole(width, rows),
            whole(pairs, 2, rows),
            down,
            up,
            whole(width, width),
            whole(1, width),
            bias,
        ],
        out_shape=[
            wide,
            wide,
            jax.ShapeDtypeStruct((width, rows), LOW),
            jax.ShapeDtypeStruct((pairs, 2, rows), WIDE),
            jax.ShapeDtypeStruct(w_down.shape, LOW),
            jax.ShapeDtypeStruct(w_up.shape, LOW),
            jax.ShapeDtypeStruct((width, width), LOW),
            jax.ShapeDtypeStruct((1, width), WIDE),
            jax.ShapeDtypeStruct((1, hidden_units), WIDE),
        ],
        scratch_shapes=[
            pltpu.VMEM((rows, width), WIDE),
            pltpu.VMEM((rows, 1), WIDE),
            pltpu.VMEM((rows, width), LOW),
            pltpu.VMEM((rows, width), LOW),
            pltpu.VMEM((rows, width), WIDE),
            pltpu.VMEM((rows, FF_BLOCK), LOW),
            pltpu.VMEM((rows, FF_BLOCK), LOW),
        ],
        name="mlp",
        compiler_params=pltpu.CompilerParams(vmem_limit_bytes=56 * 2**20),
    )(hidden, attn_low, attended, cotangent, w_out, gain_mlp[None], w_up, b_up[None], w_down)


PARTS = (
    ("down", (0, 0), (1536, 384), "rrrrr", 0, (1, 3, 7, 9, 10, 12, 14, 15, 17, 18)),
    ("down", (0, 384), (1536, 384), "rrrrr", 1, (1, 3, 7, 8, 9, 11, 12, 14, 17, 18)),
    ("down", (1536, 0), (1536, 384), "rrrrr", 1, (2, 5, 10, 11, 13, 15, 17, 18, 21, 22)),
    ("down", (1536, 384), (1536, 384), "rrrrr", 0, (2, 5, 8, 9, 11, 12, 15, 18, 20, 21)),
    ("up", (0, 0), (768, 768), "rrrrc", 0, (2, 6, 9, 10, 12, 14, 16, 18, 23, 24)),
    ("up", (0, 768), (768, 768), "rrrrc", 1, (3, 6, 10, 12, 14, 17, 18, 21, 23, 24)),
    ("up", (0, 1536), (768, 768), "rrrrc", 0, (3, 7, 10, 12, 13, 16, 18, 20, 24, 24)),
    ("up", (0, 2304), (768, 768), "rrrrc", 1, (3, 7, 11, 13, 16, 18, 19, 23, 24, 24)),
    ("out", (0, 0), (768, 768), "rrrrc", 0, (3, 9, 10, 12, 15, 17, 18, 22, 24, 24)),
    ("qkv", (0, 0), (768, 512), "rrrrc", 0, None),
    ("qkv", (0, 512), (768, 512), "rrrrc", 1, None),
    ("qkv", (0, 1024), (768, 512), "rrrrc", 0, None),
    ("qkv", (0, 1536), (768, 768), "rrrrc", 1, None),
)


def gradient_kernel(*refs):
    keys, values, shards = refs[:3]
    q_ref, grad_ref, lse_ref, dots_ref, clips, query_clip, w_ref = refs[3:10]
    down_in, up_in, out_in, small_in = refs[10:14]
    down_out, up_out, out_out, qkv_out, small_out, input_out = refs[14:20]
    refs = refs[20:]
    kv_slot, a_slot, dq_sum, dk_sum, dv_sum, dk_all, dv_all, grad_k, grad_v, parts = refs[:10]
    from_near, from_across, qkv_term, clip_slot, small_arrived = refs[10:15]
    input_sum = dq_sum
    kv_sems, a_sem, line_sends, line_receives, sends, receives, locals_ = refs[15:22]
    small_sends, small_receives, out_sem, clip_sem = refs[22:26]
    refs = refs[26:]
    rows, width = q_ref.shape
    pairs = width // PAIR
    pieces = 4 * pairs
    group, place = lax.axis_index("dp"), lax.axis_index("blk")
    near = (group, place + 1 - 2 * (place % 2))
    across = (group, 3 - place)
    at_end = place % 3 == 0

    arrays = {
        "down": (down_in, down_out),
        "up": (up_in, up_out),
        "out": (out_in, out_out),
        "qkv": (qkv_term, qkv_out),
    }
    sums = []
    for index, (name, corner, shape, axes, turn, _) in enumerate(PARTS):
        total, arrived = refs[0], refs[1:STEPS]
        refs = refs[STEPS:]
        if name == "down":
            arrived = (qkv_term.at[:, pl.ds(index * shape[1], shape[1])], *arrived)
        else:
            arrived, refs = (refs[0], *arrived), refs[1:]
        sums.append(
            Sum(
                turn,
                axes,
                corner,
                shape,
                *arrays[name],
                total,
                arrived,
                (sends.at[index], receives.at[index]),
                locals_.at[index],
            )
        )
    early = [(each, part[5]) for each, part in zip(sums, PARTS) if part[5] is not None]
    late = [each for each, part in zip(sums, PARTS) if part[5] is None]

    chunk_rows = rows // pairs

    def chunk_of(chunk):
        return pl.ds(pl.multiple_of(chunk * chunk_rows, chunk_rows), chunk_rows)

    def line_copy(channel, chunk, source, target, device):
        return pltpu.make_async_remote_copy(
            src_ref=parts.at[source, chunk_of(chunk)],
            dst_ref=target.at[chunk_of(chunk)],
            send_sem=line_sends.at[channel, chunk],
            recv_sem=line_receives.at[channel, chunk],
            device_id=device,
            device_id_type=MESH,
        )

    def inward(source, chunk):
        return line_copy(source, chunk, source, from_near.at[source], near)

    def middle(source, chunk):
        return line_copy(3 + source, chunk, source, from_across.at[source], across)

    def outward(chunk):
        return line_copy(5, chunk, 2, from_near.at[0], near)

    def add_chunk(total, term, chunk):
        here = chunk_of(chunk)
        total[here] = (total[here].astype(WIDE) + term[here].astype(WIDE)).astype(total.dtype)

    def pair_columns(pair):
        return pl.ds(pl.multiple_of(pair * PAIR, PAIR), PAIR)

    def kv_copies(shard, pair, slot):
        return [
            pltpu.make_async_copy(
                source.at[shard, :, pair_columns(pair)], kv_slot.at[slot, side], kv_sems.at[slot, side]
            )
            for side, source in enumerate((keys, values))
        ]

    def a_copy(shard):
        return pltpu.make_async_copy(shards.at[shard], a_slot, a_sem)

    def clip_copy(turn):
        source = clips.at[pl.ds(pl.multiple_of((3 - turn) * rows, 8), rows)]
        return pltpu.make_async_copy(source, clip_slot, clip_sem)

    def of_pairs(stack):
        return jnp.concatenate([stack[pair] for pair in range(pairs)], axis=1)

    for copy in kv_copies(3, 0, 0):
        copy.start()
    greet()
    for each, _ in early:
        each.start()
    dq_sum[...] = jnp.zeros_like(dq_sum)
    grad_k[...] = jnp.zeros_like(grad_k)
    grad_v[...] = jnp.zeros_like(grad_v)
    small_out[...] = small_in[...]

    def weight_terms(d_query):
        a_copy(0).wait()
        d_key, d_value = of_pairs(dk_all), of_pairs(dv_all)
        part = dot(d_key, w_ref[:, width : 2 * width], NT) + dot(d_value, w_ref[:, 2 * width :], NT)
        if d_query is not None:
            part = part + dot(d_query, w_ref[:, :width], NT)
        small_out[:1] += jnp.sum(part * a_slot[...].astype(WIDE), axis=0, keepdims=True)
        grad_k[...] += dot(a_slot[...], d_key, TN)
        grad_v[...] += dot(a_slot[...], d_value, TN)
        return part

    @pl.loop(0, pieces)
    def _(piece):
        turn, pair, slot = piece // pairs, piece % pairs, piece % 2

        def at(when, *actions):
            @pl.when(piece == when)
            def _():
                for action in actions:
                    action()

        following = piece + 1

        @pl.when(following < pieces)
        def _():
            for copy in kv_copies(3 - following // pairs, following % pairs, following % 2):
                copy.start()

        @pl.when(pair == 1)
        def _():
            a_copy(3 - turn).start()

        for when in range(pieces):
            ends = [
                functools.partial(each.turn, tick)
                for tick in range(2 * STEPS)
                for each, ticks in early
                if ticks[tick] == when
            ]
            if ends:
                at(when, *ends)
        at_middle = jnp.logical_not(at_end)

        @pl.when(jnp.logical_and(turn > 0, at_end))
        def _():
            inward(turn - 1, pair).start()

        @pl.when(jnp.logical_and(at_middle, jnp.logical_and(piece >= FORWARD, piece < FORWARD + 2 * pairs)))
        def _():
            source, chunk = (piece - FORWARD) // pairs, (piece - FORWARD) % pairs
            inward(source, chunk).wait_recv()
            add_chunk(parts.at[source], from_near.at[source], chunk)
            middle(source, chunk).start()

        @pl.when(jnp.logical_and(at_middle, turn == 3))
        def _():
            middle(0, pair).wait_recv()
            add_chunk(parts.at[2], from_across.at[0], pair)
            outward(pair).start()

        @pl.when(pair == 0)
        def _():
            clip_copy(turn).start()
            clip_copy(turn).wait()

        for copy in kv_copies(0, pair, slot):
            copy.wait()
        columns = pair_columns(pair)

        def add(head, start, stop, dq, dk, dv):
            lanes = slice(head * HEAD, (head + 1) * HEAD)
            if start == 0:
                dv_sum[lanes], dk_sum[lanes] = dv, dk
            else:
                dv_sum[lanes] += dv
                dk_sum[lanes] += dk
            at_lanes = pl.ds(pl.multiple_of(pair * PAIR + head * HEAD, HEAD), HEAD)
            dq_sum[at_lanes, start:stop] += dq

        backward_pair(
            kv_slot[slot, 0],
            kv_slot[slot, 1],
            q_ref[:, columns],
            grad_ref[columns, :],
            lse_ref.at[pair],
            dots_ref.at[pair],
            clip_slot[...],
            query_clip[...],
            add,
        )
        dk_all[pair] = (dk_sum[...] * SCALE).T.astype(LOW)
        dv_all[pair] = dv_sum[...].T.astype(LOW)

        @pl.when(jnp.logical_and(pair == pairs - 1, turn < 3))
        def _():
            parts[turn] = weight_terms(None).astype(LOW)

    d_query = (dq_sum[...] * SCALE).T.astype(LOW)
    input_sum[...] = weight_terms(d_query)
    qkv_term[:, :width] = dot(a_slot[...], d_query, TN).astype(LOW)
    qkv_term[:, width : 2 * width] = grad_k[...].astype(LOW)
    qkv_term[:, 2 * width :] = grad_v[...].astype(LOW)

    small_steps = place_bits(0)

    def small(step):
        return remote(
            small_out, small_arrived.at[step], (small_sends, small_receives), step, small_steps[step][1]
        )

    for each in late:
        each.start()
    open_sums = [(each, [tick for tick in range(2 * STEPS) if ticks[tick] == pieces]) for each, ticks in early]
    open_sums += [(each, list(range(2 * STEPS))) for each in late]

    @pl.when(at_end)
    def _():
        @pl.loop(0, pairs)
        def _(chunk):
            for source in range(3):
                inward(source, chunk).wait_send()
            outward(chunk).wait_recv()
            add_chunk(input_sum, from_near.at[0], chunk)

    @pl.when(jnp.logical_not(at_end))
    def _():
        @pl.loop(0, pairs)
        def _(chunk):
            outward(chunk).wait_send()
            for source in range(2):
                middle(source, chunk).wait_send()
            middle(1, chunk).wait_recv()
            add_chunk(input_sum, from_across.at[1], chunk)
            inward(2, chunk).wait_recv()
            add_chunk(input_sum, from_near.at[2], chunk)

    store = pltpu.make_async_copy(input_sum, input_out, out_sem)
    store.start()
    for tick in range(2 * STEPS):
        if tick < STEPS:
            small(tick).start()
        for each, ticks in open_sums:
            if ticks:
                each.turn(ticks.pop(0))
        if tick < STEPS:
            small(tick).wait()
            small_out[...] += small_arrived[tick]
    store.wait()


def gradient_call(
    keys, values, shards, query, grad_t, lse, row_dots, clips, query_clip, w_qkv, grad_down, grad_up, grad_out, small
):
    rows, width = query.shape
    pairs = width // PAIR
    anywhere = pl.BlockSpec(memory_space=pl.ANY)
    inside = pl.BlockSpec(memory_space=pltpu.VMEM)
    square = (rows, width)
    scratch = [
        pltpu.VMEM((2, 2, rows, PAIR), LOW),
        pltpu.VMEM(square, LOW),
        pltpu.VMEM((width, rows), WIDE),
        pltpu.VMEM((PAIR, rows), WIDE),
        pltpu.VMEM((PAIR, rows), WIDE),
        pltpu.VMEM((pairs, rows, PAIR), LOW),
        pltpu.VMEM((pairs, rows, PAIR), LOW),
        pltpu.VMEM((width, width), WIDE),
        pltpu.VMEM((width, width), WIDE),
        pltpu.VMEM((3, *square), LOW),
    ]
    scratch += [pltpu.VMEM((3, *square), LOW), pltpu.VMEM((2, *square), LOW)]
    scratch += [
        pltpu.VMEM((width, 3 * width), LOW),
        pltpu.VMEM((rows, 1), clips.dtype),
        pltpu.VMEM((STEPS, *small.shape), WIDE),
        pltpu.SemaphoreType.DMA((2, 2)),
        pltpu.SemaphoreType.DMA,
        pltpu.SemaphoreType.DMA((6, pairs)),
        pltpu.SemaphoreType.DMA((6, pairs)),
        pltpu.SemaphoreType.DMA((len(PARTS), 2 * STEPS)),
        pltpu.SemaphoreType.DMA((len(PARTS), 2 * STEPS)),
        pltpu.SemaphoreType.DMA((len(PARTS), 2)),
        pltpu.SemaphoreType.DMA((STEPS,)),
        pltpu.SemaphoreType.DMA((STEPS,)),
        pltpu.SemaphoreType.DMA,
        pltpu.SemaphoreType.DMA,
    ]
    for name, _, shape, axes, _, _ in PARTS:
        shapes = halves(shape, axes)
        scratch += [pltpu.VMEM(each, LOW) for each in (shapes[0], *shapes[1:])]
        if name != "down":
            scratch.append(pltpu.VMEM(shapes[0], LOW))
    like = lambda array: jax.ShapeDtypeStruct(array.shape, array.dtype)
    return pl.pallas_call(
        gradient_kernel,
        in_specs=[anywhere] * 3 + [inside] * 4 + [anywhere] + [inside] * 2 + [anywhere] * 3 + [inside],
        out_specs=[anywhere] * 4 + [inside, anywhere],
        out_shape=[
            like(grad_down),
            like(grad_up),
            like(grad_out),
            jax.ShapeDtypeStruct((width, 3 * width), LOW),
            like(small),
            jax.ShapeDtypeStruct(square, WIDE),
        ],
        scratch_shapes=scratch,
        name="gradients",
        compiler_params=pltpu.CompilerParams(
            collective_id=1, has_side_effects=True, vmem_limit_bytes=62 * 2**20
        ),
    )(
        keys, values, shards, query, grad_t, lse, row_dots, clips, query_clip, w_qkv,
        grad_down, grad_up, grad_out, small,
    )


def on_device(
    groups, inputs, positions, segments, gain_attn, w_qkv, w_out, gain_mlp, w_up, b_up, w_down, cotangent
):
    rows, width = inputs.shape
    pairs = width // PAIR
    place = lax.axis_index("blk")
    w_query = w_qkv[:, :width]

    def send(value, pairs_of_places):
        return lax.ppermute(value, "blk", pairs_of_places)

    hidden = inputs + position_table(positions, width)
    normed_attn, inverse_attn = normalize(hidden)
    a_low = (normed_attn * gain_attn).astype(LOW)

    table = jnp.array([[0, 1, 2, 3], [1, 0, 2, 3], [2, 3, 1, 0], [3, 2, 1, 0]], jnp.int32)
    order = lax.dynamic_index_in_dim(table, place, keepdims=False)
    clips = jnp.concatenate(
        [lax.dynamic_slice_in_dim(segments, order[index] * rows, rows) for index in range(4)]
    )[:, None]
    query_clip = lax.dynamic_slice_in_dim(segments, place * rows, rows)[None, :]
    shards, keys, values, query, attended, lse, attn_low = attention_call(
        a_low, w_qkv, clips, query_clip
    )

    (
        outputs,
        d_resid,
        d_attn_t,
        row_dots,
        grad_down,
        grad_up,
        grad_out,
        grad_gain_mlp,
        grad_bias_up,
    ) = mlp_call(hidden, attn_low, attended, cotangent, w_out, gain_mlp, w_up, b_up, w_down)
    grad_gain_mlp, grad_bias_up = grad_gain_mlp[0], grad_bias_up[0]

    if groups == 8 and rows == width:
        small = jnp.concatenate([jnp.zeros_like(gain_attn), grad_gain_mlp, grad_bias_up])
        sum_down, sum_up, sum_out, sum_qkv, sum_small, d_normed_attn = gradient_call(
            keys,
            values,
            shards,
            query,
            d_attn_t,
            lse,
            row_dots,
            clips,
            query_clip,
            w_qkv,
            grad_down,
            grad_up,
            grad_out,
            jnp.pad(small.reshape(6, width), ((0, 2), (0, 0))),
        )
        input_grad = d_resid + norm_back(d_normed_attn * gain_attn, normed_attn, inverse_attn)
        return (
            outputs,
            input_grad,
            sum_small[0] / gain_attn,
            sum_qkv.astype(WIDE),
            sum_out.astype(WIDE),
            sum_small[1],
            sum_up.astype(WIDE),
            sum_small[2:6].reshape(-1),
            sum_down.astype(WIDE),
        )

    everywhere = ("dp", "blk")

    def back(index, dq):
        return backward_call(
            index == 3,
            index == 0,
            keys[index],
            values[index],
            query,
            d_attn_t,
            lse,
            row_dots,
            clips[index * rows : (index + 1) * rows],
            query_clip,
            w_qkv,
            dq,
        )

    middle, outward, inward = [(1, 2), (2, 1)], [(1, 0), (2, 3)], [(0, 1), (3, 2)]
    dk_3, dv_3, dq, part_3 = back(3, None)
    far = send(part_3, inward)
    dk_2, dv_2, dq, part_2 = back(2, dq)
    far, part_2, dq = lax.optimization_barrier((far, part_2, dq))
    onward = (part_3.astype(WIDE) + far.astype(WIDE)).astype(LOW)
    mid_3 = send(onward, middle)
    mid_2 = send(part_2, inward)
    dq, onward = lax.optimization_barrier((dq, onward))
    dk_1, dv_1, dq, part_1 = back(1, dq)
    mid_3, mid_2, part_1, dq = lax.optimization_barrier((mid_3, mid_2, part_1, dq))
    onward_1 = (part_2.astype(WIDE) + mid_2.astype(WIDE)).astype(LOW)
    onward_2 = (part_1.astype(WIDE) + mid_3.astype(WIDE)).astype(LOW)
    last_1 = send(onward_1, middle)
    last_2 = send(onward_2, outward)
    last_3 = send(part_1, inward)
    dq, onward_1, onward_2 = lax.optimization_barrier((dq, onward_1, onward_2))
    dk_0, dv_0, dq, part_0 = back(0, dq)
    grad_query = dot(a_low, dq, TN).astype(LOW)
    d_keys, d_values = (dk_0, dk_1, dk_2, dk_3), (dv_0, dv_1, dv_2, dv_3)
    grad_key = sum(dot(shard, term, TN) for shard, term in zip(shards, d_keys)).astype(LOW)
    grad_value = sum(dot(shard, term, TN) for shard, term in zip(shards, d_values)).astype(LOW)
    d_normed_attn = (
        part_0
        + dot(dq, w_query, NT)
        + last_1.astype(WIDE)
        + last_2.astype(WIDE)
        + last_3.astype(WIDE)
    )
    grad_gain_attn = jnp.sum(d_normed_attn * normed_attn, axis=0)
    input_grad = d_resid + norm_back(d_normed_attn * gain_attn, normed_attn, inverse_attn)
    small = jnp.concatenate([grad_gain_attn, grad_gain_mlp, grad_bias_up])
    sums = lax.psum((grad_down, grad_up, grad_out, grad_query, grad_key, grad_value), everywhere)
    sum_small = lax.psum(small, everywhere)
    sum_down, sum_up, sum_out, *sum_qkv = sums
    return (
        outputs,
        input_grad,
        sum_small[:width],
        jnp.concatenate(sum_qkv, axis=1).astype(WIDE),
        sum_out.astype(WIDE),
        sum_small[width : 2 * width],
        sum_up.astype(WIDE),
        sum_small[2 * width :],
        sum_down.astype(WIDE),
    )


def solution(mesh):
    rows = P(("dp", "blk"), None)
    placed = (rows, P(("dp", "blk")), P("dp"), P(), P(), P(), P(), P(), P(), P(), rows)
    return jax.shard_map(
        functools.partial(on_device, mesh.shape["dp"]),
        mesh=mesh,
        in_specs=placed,
        out_specs=(rows, rows, P(), P(), P(), P(), P(), P(), P()),
        check_vma=False,
    )
```

```python
import functools
import math

import jax
import jax.numpy as jnp
from jax import lax
from jax.experimental import pallas as pl
from jax.experimental.pallas import tpu as pltpu
from jax.sharding import PartitionSpec as P

HEADS = 12
HEAD = 64
PAIR = 2 * HEAD
SCALE = HEAD**-0.5
LOG2E = 1.4426950408889634
MASKED = -1.0e9
QUERY_BLOCK = 384
EPS_NORM = 1e-06
LOW = jnp.bfloat16
WIDE = jnp.float32

NN = (((1,), (0,)), ((), ()))
NT = (((1,), (1,)), ((), ()))
TN = (((0,), (0,)), ((), ()))


def dot(left, right, dims):
    return lax.dot_general(left, right, dims, preferred_element_type=WIDE)


def position_table(positions, model_width):
    half_width = model_width // 2
    freqs = jnp.exp(jnp.arange(half_width, dtype=WIDE) * (-math.log(10000.0) / half_width))
    angles = positions.astype(WIDE)[:, None] * freqs[None, :]
    return jnp.concatenate([jnp.sin(angles), jnp.cos(angles)], axis=1)


def normalize(values):
    center = values - jnp.mean(values, axis=-1, keepdims=True)
    inverse = lax.rsqrt(jnp.mean(center * center, axis=-1, keepdims=True) + EPS_NORM)
    return center * inverse, inverse


def norm_back(grad_norm, normed, inverse):
    first = jnp.mean(grad_norm, axis=-1, keepdims=True)
    second = jnp.mean(grad_norm * normed, axis=-1, keepdims=True)
    return inverse * (grad_norm - first - normed * second)


def in_head(values, head):
    lanes = lax.broadcasted_iota(jnp.int32, values.shape, 1)
    return (lanes < HEAD) == (head == 0)


def only_head(values, head, other=None):
    other = jnp.zeros_like(values) if other is None else other
    return jnp.where(in_head(values, head), values, other)


def split_scaled(query):
    scaled = query.astype(WIDE) * (SCALE * LOG2E)
    high = scaled.astype(LOW)
    return high, (scaled - high.astype(WIDE)).astype(LOW)


def score_sides(key, query):
    high, low = split_scaled(query)
    key_side = jnp.concatenate([key, key], axis=1)
    query_side = [
        jnp.concatenate([only_head(high, head), only_head(low, head)], axis=1) for head in range(2)
    ]
    return key_side, query_side


def work_items(rows):
    return [(start, head) for start in range(0, rows, QUERY_BLOCK) for head in range(2)]


def whole(*shape):
    return pl.BlockSpec(shape, lambda pair: (0,) * len(shape))


def columns_of(rows, first=0):
    return pl.BlockSpec((rows, PAIR), lambda pair: (0, pair + first))


def backward_pair(key, value, query, grad_t, lse, row_dots, key_clip, query_clip, add):
    rows = query.shape[0]
    grad = grad_t.T
    key_t, query_t = key.T, query.T
    key_side, query_side = score_sides(key, query)
    grad_side = [only_head(grad, head) for head in range(2)]
    for start, head in work_items(rows):
        stop = start + QUERY_BLOCK
        lanes, row = slice(head * HEAD, (head + 1) * HEAD), slice(head, head + 1)
        score = dot(key_side, query_side[head][start:stop], NT)
        score = jnp.where(key_clip == query_clip[:, start:stop], score, MASKED)
        probs = jnp.exp2(score - lse[row, start:stop])
        d_probs = dot(value, grad_side[head][start:stop], NT)
        d_scores = (probs * (d_probs - row_dots[row, start:stop])).astype(LOW)
        probs = probs.astype(LOW)
        dv = dot(grad_t[lanes, start:stop], probs, NT)
        dk = dot(query_t[lanes, start:stop], d_scores, NT)
        dq = dot(key_t[lanes], d_scores, NN)
        add(head, start, stop, dq, dk, dv)


def backward_kernel(first, last, *refs):
    k_ref, v_ref, q_ref, grad_ref, lse_ref, dots_ref, key_clip, query_clip, wk_ref, wv_ref = refs[:10]
    refs = refs[10:]
    if not first:
        dq_in = refs[0]
        refs = refs[1:]
    dk_ref, dv_ref, dq_ref, part_ref, dk_sum, dv_sum, dq_sum, dk_all, dv_all = refs
    pair = pl.program_id(0)
    rows = q_ref.shape[0]

    def add(head, start, stop, dq, dk, dv):
        lanes = slice(head * HEAD, (head + 1) * HEAD)
        if start == 0:
            dv_sum[lanes], dk_sum[lanes] = dv, dk
        else:
            dv_sum[lanes] += dv
            dk_sum[lanes] += dk
        if not first:
            dq = dq + dq_in[lanes, start:stop]
        if last:
            dq_sum[lanes, start:stop] = dq
        else:
            dq_ref[lanes, start:stop] = dq

    backward_pair(
        k_ref[...],
        v_ref[...],
        q_ref[...],
        grad_ref[...],
        lse_ref,
        dots_ref,
        key_clip[...],
        query_clip[...],
        add,
    )
    if last:
        dq_ref[...] = (dq_sum[...] * SCALE).T.astype(LOW)
    dk = (dk_sum[...] * SCALE).T.astype(LOW)
    dv = dv_sum[...].T.astype(LOW)
    dk_ref[...] = dk
    dv_ref[...] = dv
    dk_all[pair] = dk
    dv_all[pair] = dv

    @pl.when(pair == pl.num_programs(0) - 1)
    def _():
        pairs = dk_all.shape[0]
        dk_rows = jnp.concatenate([dk_all[index] for index in range(pairs)], axis=1)
        dv_rows = jnp.concatenate([dv_all[index] for index in range(pairs)], axis=1)
        part = dot(dk_rows, wk_ref[...], NT) + dot(dv_rows, wv_ref[...], NT)
        part_ref[...] = part.astype(part_ref.dtype)


def backward_call(first, last, key, value, query, grad_t, lse, row_dots, key_clip, query_clip, w_qkv, dq):
    rows, width = query.shape
    pairs = width // PAIR
    across = pl.BlockSpec((PAIR, rows), lambda pair: (pair, 0))
    line = pl.BlockSpec((None, 2, rows), lambda pair: (pair, 0, 0))
    columns = columns_of(rows)
    in_specs = [columns, columns, columns, across, line, line, whole(rows, 1), whole(1, rows)]
    in_specs += [
        pl.BlockSpec((width, width), lambda pair: (0, 1)),
        pl.BlockSpec((width, width), lambda pair: (0, 2)),
    ]
    operands = [key, value, query, grad_t, lse, row_dots, key_clip, query_clip, w_qkv, w_qkv]
    if not first:
        in_specs.append(across)
        operands.append(dq)
    low_rows = jax.ShapeDtypeStruct((rows, width), LOW)
    tall = pltpu.VMEM((PAIR, rows), WIDE)
    parts = pltpu.VMEM((pairs, rows, PAIR), LOW)
    return pl.pallas_call(
        functools.partial(backward_kernel, first, last),
        grid=(pairs,),
        in_specs=in_specs,
        out_specs=[columns, columns, columns if last else across, whole(rows, width)],
        out_shape=[
            low_rows,
            low_rows,
            low_rows if last else jax.ShapeDtypeStruct((width, rows), WIDE),
            jax.ShapeDtypeStruct((rows, width), WIDE if last else LOW),
        ],
        scratch_shapes=[tall, tall, tall, parts, parts],
        name="attend_back",
        cost_estimate=pl.CostEstimate(
            flops=40 * rows * rows * width, bytes_accessed=24 * rows * width, transcendentals=0
        ),
        compiler_params=pltpu.CompilerParams(vmem_limit_bytes=48 * 2**20),
    )(*operands)


MESH = pl.DeviceIdType.MESH
TURNS = ((0, 1, 2), (0, 2, 1))
STEPS = 5
FORWARD = 8


def place_bits(turn):
    group, place = lax.axis_index("dp"), lax.axis_index("blk")
    steps = []
    for bit in TURNS[turn]:
        mine = group // (1 << bit) % 2
        steps.append((mine, (group + (1 - 2 * mine) * (1 << bit), place)))
    for bit in range(2):
        mine = place // (1 << bit) % 2
        steps.append((mine, (group, place + (1 - 2 * mine) * (1 << bit))))
    return steps


def remote(source, target, sems, index, device):
    return pltpu.make_async_remote_copy(
        src_ref=source,
        dst_ref=target,
        send_sem=sems[0].at[index],
        recv_sem=sems[1].at[index],
        device_id=device,
        device_id_type=MESH,
    )


def part_of(row, rows, column, columns):
    row = row if isinstance(row, int) else pl.multiple_of(row, 16)
    column = column if isinstance(column, int) else pl.multiple_of(column, PAIR)
    return pl.ds(row, rows), pl.ds(column, columns)


def add_block(total, term, row=0, column=0):
    rows, columns = term.shape
    block = next(size for size in (48, 32, 16) if rows % size == 0)

    @pl.loop(0, rows // block)
    def _(index):
        here = part_of(row + index * block, block, column, columns)
        there = part_of(index * block, block, 0, columns)
        total[here] = (total[here].astype(WIDE) + term[there].astype(WIDE)).astype(total.dtype)


def halves(shape, axes):
    shapes = []
    for axis in axes:
        shape = (shape[0] // 2, shape[1]) if axis == "r" else (shape[0], shape[1] // 2)
        shapes.append(shape)
    return shapes


class Sum:
    def __init__(
        self, turn, axes, corner, shape, term, result, total, arrived, sems, local_sems, begin=0, stop=STEPS
    ):
        self.term, self.result, self.total, self.arrived = term, result, total, arrived
        self.sems, self.local_sems, self.begin, self.stop = sems, local_sems, begin, stop
        self.steps = place_bits(turn)
        self.shapes = halves(shape, axes)
        self.kept, self.left = [], []
        row, column = corner
        for axis, (rows, columns), (mine, _) in zip(axes, self.shapes, self.steps):
            down, across = (rows, 0) if axis == "r" else (0, columns)
            self.left.append((row + (1 - mine) * down, rows, column + (1 - mine) * across, columns))
            row, column = row + mine * down, column + mine * across
            self.kept.append((row, rows, column, columns))
        self.held = self.kept[max(begin - 1, 0)]

    def inside(self, place):
        row, rows, column, columns = place
        return part_of(row - self.held[0], rows, column - self.held[2], columns)

    def load(self):
        source = self.term if self.begin else self.term.at[part_of(*self.kept[0])]
        return pltpu.make_async_copy(source, self.total, self.local_sems.at[0])

    def store(self):
        place = self.kept[self.stop - 1]
        target = self.result.at[part_of(*place)] if self.stop == STEPS else self.result
        return pltpu.make_async_copy(
            self.total.at[self.inside(place)], target, self.local_sems.at[1]
        )

    def gather(self, step):
        place = self.left[step]
        source = self.term.at[part_of(*place)] if step == 0 else self.total.at[self.inside(place)]
        return remote(source, self.arrived[step - self.begin], self.sems, step, self.steps[step][1])

    def spread(self, step):
        here = self.result.at[part_of(*self.kept[step])]
        source = self.total.at[self.inside(self.kept[step])] if step == STEPS - 1 else here
        return remote(source, here, self.sems, STEPS + step, self.steps[step][1])

    def start(self):
        self.load().start()
        if self.begin:
            self.load().wait()
        self.gather(self.begin).start()

    def turn(self, tick):
        if tick < STEPS:
            if tick == 0:
                self.load().wait()
            self.gather(tick).wait()
            row, _, column, _ = self.kept[tick]
            add_block(
                self.total, self.arrived[tick - self.begin], row - self.held[0], column - self.held[2]
            )
            if tick + 1 < self.stop:
                self.gather(tick + 1).start()
            else:
                self.store().start()
                if self.stop == STEPS:
                    self.spread(STEPS - 1).start()
        else:
            step = 2 * STEPS - 1 - tick
            if step == STEPS - 1:
                self.store().wait()
            self.spread(step).wait()
            if step:
                self.spread(step - 1).start()


def greet(devices):
    barrier = pltpu.get_barrier_semaphore()
    for device in devices:
        pl.semaphore_signal(barrier, inc=1, device_id=device, device_id_type=MESH)
    pl.semaphore_wait(barrier, len(devices))


PASS_NEAR = (2, 4, 5, 6, 6, 6)
PASS_FAR = (10, 11, 12, 13, 15, 16)


def attention_kernel(*refs):
    a_in, w_ref, clips, query_clip = refs[:4]
    a_out, k_out, v_out, q_ref, acc_ref, lse_ref, attn_ref = refs[4:11]
    a_all, top_all, total_all, kv_slot, clip_slot = refs[11:16]
    a_sems, kv_sems, clip_sem, line_sends, line_receives = refs[16:]
    rows, width = q_ref.shape
    pairs = width // PAIR
    pieces = 4 * pairs
    chunk_rows = rows // pairs
    group, place = lax.axis_index("dp"), lax.axis_index("blk")
    near = (group, place + 1 - 2 * (place % 2))
    across = (group, 3 - place)
    at_end = place % 3 == 0
    at_middle = jnp.logical_not(at_end)

    def line_copy(channel, chunk, source, target, device):
        here = pl.ds(pl.multiple_of(chunk * chunk_rows, chunk_rows), chunk_rows)
        return pltpu.make_async_remote_copy(
            src_ref=source.at[here],
            dst_ref=a_all.at[target, here],
            send_sem=line_sends.at[channel, chunk],
            recv_sem=line_receives.at[channel, chunk],
            device_id=device,
            device_id_type=MESH,
        )

    channels = (
        lambda chunk: line_copy(0, chunk, a_in, 1, near),
        lambda chunk: line_copy(1, chunk, a_in, 2, across),
        lambda chunk: line_copy(2, chunk, a_all.at[2], 2, near),
        lambda chunk: line_copy(3, chunk, a_all.at[1], 3, across),
        lambda chunk: line_copy(4, chunk, a_all.at[3], 3, near),
    )
    load = pltpu.make_async_copy(a_in, a_all.at[0], a_sems.at[4])
    load.start()
    greet((near, across))
    for chunk in range(pairs):
        channels[0](chunk).start()

    @pl.when(at_middle)
    def _():
        for chunk in range(pairs):
            channels[1](chunk).start()

    top_all[...] = jnp.full_like(top_all, -1.0e30)
    total_all[...] = jnp.zeros_like(total_all)
    acc_ref[...] = jnp.zeros_like(acc_ref)

    def keep(shard):
        return pltpu.make_async_copy(a_all.at[shard], a_out.at[shard], a_sems.at[shard])

    def clip_copy(turn):
        source = clips.at[pl.ds(pl.multiple_of(turn * rows, 8), rows)]
        return pltpu.make_async_copy(source, clip_slot, clip_sem)

    def pair_columns(pair):
        return pl.ds(pl.multiple_of(pair * PAIR, PAIR), PAIR)

    def kv_copies(turn, pair, slot):
        return [
            pltpu.make_async_copy(
                kv_slot.at[slot, side], target.at[turn, :, pair_columns(pair)], kv_sems.at[slot, side]
            )
            for side, target in enumerate((k_out, v_out))
        ]

    load.wait()
    keep(0).start()

    @pl.loop(0, pieces)
    def _(piece):
        turn, pair, slot = piece // pairs, piece % pairs, piece % 2
        for chunk, when in enumerate(PASS_NEAR):

            @pl.when(jnp.logical_and(piece == when, at_middle))
            def _():
                channels[0](chunk).wait_recv()
                channels[3](chunk).start()
                channels[1](chunk).wait_recv()
                channels[2](chunk).start()

        for chunk, when in enumerate(PASS_FAR):

            @pl.when(jnp.logical_and(piece == when, at_middle))
            def _():
                channels[3](chunk).wait_recv()
                channels[4](chunk).start()

        for shard, channel in ((1, 0), (2, 2), (3, 4)):

            @pl.when(jnp.logical_and(piece == shard * pairs, at_end))
            def _():
                for chunk in range(pairs):
                    channels[channel](chunk).wait_recv()

            @pl.when(piece == shard * pairs)
            def _():
                keep(shard).start()

        @pl.when(pair == 0)
        def _():
            clip_copy(turn).start()
            clip_copy(turn).wait()

        @pl.when(piece >= 2)
        def _():
            for copy in kv_copies(turn, pair, slot):
                copy.wait()

        columns = pair_columns(pair)

        @pl.when(turn == 0)
        def _():
            q_ref[:, columns] = dot(a_all[0], w_ref[:, columns], NN).astype(LOW)

        w_pair = jnp.concatenate(
            [w_ref[:, pair_columns(pair + pairs)], w_ref[:, pair_columns(pair + 2 * pairs)]], axis=1
        )
        kv = dot(a_all[turn], w_pair, NN).astype(LOW)
        key, value = kv[:, :PAIR], kv[:, PAIR:]
        kv_slot[slot, 0] = key
        kv_slot[slot, 1] = value
        for copy in kv_copies(turn, pair, slot):
            copy.start()
        value_t = value.T
        ones = jnp.ones((16, rows), LOW)
        value_rows = [
            jnp.concatenate([value_t[head * HEAD : (head + 1) * HEAD], ones], axis=0)
            for head in range(2)
        ]
        key_side, query_side = score_sides(key, q_ref[:, columns])
        key_clip = clip_slot[...]

        def scores(start, head):
            stop = start + QUERY_BLOCK
            result = dot(key_side, query_side[head][start:stop], NT)
            return jnp.where(key_clip == query_clip[:, start:stop], result, MASKED)

        def weights(start, head, result):
            here = slice(start, start + QUERY_BLOCK)
            before = top_all[pair, head : head + 1, here]
            top = jnp.maximum(before, jnp.max(result, axis=0, keepdims=True))
            top_all[pair, head : head + 1, here] = top
            return jnp.exp2(result - top).astype(LOW), jnp.exp2(before - top)

        def attend(start, head, expd, shrink):
            here, row = slice(start, start + QUERY_BLOCK), slice(head, head + 1)
            lanes = pl.ds(pl.multiple_of(pair * PAIR + head * HEAD, HEAD), HEAD)
            result = dot(value_rows[head], expd, NN)
            acc_ref[lanes, here] = acc_ref[lanes, here] * shrink + result[:HEAD]
            total_all[pair, row, here] = total_all[pair, row, here] * shrink + result[HEAD : HEAD + 1]

        items = work_items(rows)
        result = scores(*items[0])
        before = None
        for index, item in enumerate(items):
            following = scores(*items[index + 1]) if index + 1 < len(items) else None
            done = weights(*item, result)
            if before is not None:
                attend(*before)
            before = (*item, *done)
            result = following
        attend(*before)

        @pl.when(turn == 3)
        def _():
            for head in range(2):
                lanes = pl.ds(pl.multiple_of(pair * PAIR + head * HEAD, HEAD), HEAD)
                total = total_all[pair, head : head + 1]
                acc_ref[lanes] = acc_ref[lanes] * (1.0 / total)
                lse_ref[pair, head : head + 1] = top_all[pair, head : head + 1] + jnp.log(total) * LOG2E
            attn_ref[:, columns] = acc_ref[columns].T.astype(LOW)

    for slot in range(2):
        for copy in kv_copies(3, pairs - 2 + slot, slot):
            copy.wait()
    for shard in range(4):
        keep(shard).wait()
    for chunk in range(pairs):
        channels[0](chunk).wait_send()

    @pl.when(at_middle)
    def _():
        for channel in channels[1:]:
            for chunk in range(pairs):
                channel(chunk).wait_send()


def attention_call(a_low, w_qkv, clips, query_clip):
    rows, width = a_low.shape
    pairs = width // PAIR
    anywhere = pl.BlockSpec(memory_space=pl.ANY)
    inside = pl.BlockSpec(memory_space=pltpu.VMEM)
    four = jax.ShapeDtypeStruct((4, rows, width), LOW)
    square = jax.ShapeDtypeStruct((rows, width), LOW)
    lines = jax.ShapeDtypeStruct((pairs, 2, rows), WIDE)
    return pl.pallas_call(
        attention_kernel,
        in_specs=[anywhere, inside, anywhere, inside],
        out_specs=[anywhere] * 3 + [inside] * 4,
        out_shape=[four, four, four, square, jax.ShapeDtypeStruct((width, rows), WIDE), lines, square],
        scratch_shapes=[
            pltpu.VMEM((4, rows, width), LOW),
            pltpu.VMEM((pairs, 2, rows), WIDE),
            pltpu.VMEM((pairs, 2, rows), WIDE),
            pltpu.VMEM((2, 2, rows, PAIR), LOW),
            pltpu.VMEM((rows, 1), clips.dtype),
            pltpu.SemaphoreType.DMA((5,)),
            pltpu.SemaphoreType.DMA((2, 2)),
            pltpu.SemaphoreType.DMA,
            pltpu.SemaphoreType.DMA((5, pairs)),
            pltpu.SemaphoreType.DMA((5, pairs)),
        ],
        name="attention",
        compiler_params=pltpu.CompilerParams(
            collective_id=2, has_side_effects=True, vmem_limit_bytes=48 * 2**20
        ),
    )(a_low, w_qkv, clips, query_clip)


FF_BLOCK = 512
ROW_BLOCK = 384
AHEAD_STEPS = (3, 3, 2, 2)
AHEAD_TICKS = ((1, 3, 4), (2, 4, 5), (3, 5), (4, 5))
AHEAD = len(AHEAD_STEPS)
LAST_BLOCK = 5
DOWN_AXES, UP_AXES = "rrrrr", "rrrrc"


def ahead_rows(shape, axes):
    rows = [halves(shape, axes)[steps - 1][0] for steps in AHEAD_STEPS]
    return [(sum(rows[:block]), rows[block]) for block in range(AHEAD)]


def ahead_scratch(width):
    scratch = [pltpu.VMEM((2, FF_BLOCK, width), LOW), pltpu.VMEM((2, width, FF_BLOCK), LOW)]
    for shape, axes in (((FF_BLOCK, width), DOWN_AXES), ((width, FF_BLOCK), UP_AXES)):
        for steps in AHEAD_STEPS:
            shapes = halves(shape, axes)[:steps]
            scratch += [pltpu.VMEM(each, LOW) for each in (shapes[0], *shapes)]
    scratch += [pltpu.SemaphoreType.DMA((2 * AHEAD, 2 * STEPS))] * 2
    return scratch + [pltpu.SemaphoreType.DMA((2 * AHEAD, 2))]


def ahead_sums(width, part_down, part_up, refs):
    terms, refs = refs[:2], refs[2:]
    sends, receives, locals_ = refs[-3:]
    sums = []
    for side, (axes, shape, parts) in enumerate(
        ((DOWN_AXES, (FF_BLOCK, width), part_down), (UP_AXES, (width, FF_BLOCK), part_up))
    ):
        places = ahead_rows(shape, axes)
        for block, steps in enumerate(AHEAD_STEPS):
            index = side * AHEAD + block
            own, refs = refs[: steps + 1], refs[steps + 1 :]
            sums.append(
                Sum(
                    (block + side) % 2,
                    axes,
                    (0, 0),
                    shape,
                    terms[side].at[block % 2],
                    parts.at[pl.ds(*places[block])],
                    own[0],
                    own[1:],
                    (sends.at[index], receives.at[index]),
                    locals_.at[index],
                    stop=steps,
                )
            )
    return terms, [(sums[block], sums[AHEAD + block]) for block in range(AHEAD)]


def mlp_kernel(
    ahead,
    hidden_ref,
    attn_ref,
    attended_ref,
    cotangent_ref,
    w_out_ref,
    gain_ref,
    w_up_ref,
    b_up_ref,
    w_down_ref,
    outputs_ref,
    d_resid_ref,
    grad_t_ref,
    dots_ref,
    grad_down_ref,
    grad_up_ref,
    grad_out_ref,
    grad_gain_ref,
    grad_bias_ref,
    *refs,
):
    block = pl.program_id(0)
    rows, width = hidden_ref.shape
    if ahead:
        parts, refs = refs[:2], refs[2:]
    normed_ref, inverse_ref, b_ref, dy_ref, db_ref, z_ref, d_pre_ref = refs[:7]
    if ahead:
        terms, sums = ahead_sums(width, *parts, refs[7:])

        @pl.when(block == 0)
        def _():
            greet([device for _, device in place_bits(0)[: max(AHEAD_STEPS)]])

    def trade(chosen, tick, when):
        @pl.when(block == when)
        def _():
            for each in sums[chosen]:
                each.turn(tick)

    @pl.when(block == 0)
    def _():
        resid = hidden_ref[...] + dot(attn_ref[...], w_out_ref[...], NN)
        normed, inverse = normalize(resid)
        normed_ref[...] = normed
        inverse_ref[...] = inverse
        b_ref[...] = (normed * gain_ref[...]).astype(LOW)
        dy_ref[...] = cotangent_ref[...].astype(LOW)
        outputs_ref[...] = resid
        db_ref[...] = jnp.zeros_like(db_ref)

    bias = jnp.zeros((1, FF_BLOCK), WIDE)
    for start in range(0, rows, ROW_BLOCK):
        here = slice(start, start + ROW_BLOCK)
        pre_act = dot(b_ref[here], w_up_ref[...], NN) + b_up_ref[...]
        cumulative = 0.5 * (1.0 + lax.erf(pre_act * 0.7071067811865476))
        density = jnp.exp(-0.5 * pre_act * pre_act) * 0.3989422804014327
        z_ref[here] = (pre_act * cumulative).astype(LOW)
        d_gelu = dot(dy_ref[here], w_down_ref[...], NT)
        d_pre = (d_gelu * (cumulative + pre_act * density)).astype(LOW)
        d_pre_ref[here] = d_pre
        bias += jnp.sum(d_pre.astype(WIDE), axis=0, keepdims=True)
        outputs_ref[here] += dot(z_ref[here], w_down_ref[...], NN)
        db_ref[here] += dot(d_pre, w_up_ref[...], NT)
    grad_bias_ref[...] = bias
    grad_down = dot(z_ref[...], dy_ref[...], TN).astype(LOW)
    grad_up = dot(b_ref[...], d_pre_ref[...], TN).astype(LOW)
    grad_down_ref[...] = grad_down
    grad_up_ref[...] = grad_up
    if ahead:
        for chosen, ticks in enumerate(AHEAD_TICKS):
            for tick, when in enumerate(ticks):
                if when < LAST_BLOCK:
                    trade(chosen, tick, when)
        for chosen in range(AHEAD):

            @pl.when(block == chosen)
            def _():
                terms[0][chosen % 2] = grad_down
                terms[1][chosen % 2] = grad_up
                for each in sums[chosen]:
                    each.start()


    @pl.when(block == pl.num_programs(0) - 1)
    def _():
        normed, db = normed_ref[...], db_ref[...]
        grad_gain_ref[...] = jnp.sum(db * normed, axis=0, keepdims=True)
        d_resid = cotangent_ref[...] + norm_back(db * gain_ref[...], normed, inverse_ref[...])
        d_resid_ref[...] = d_resid
        dr_low = d_resid.astype(LOW)
        grad_out_ref[...] = dot(attn_ref[...], dr_low, TN).astype(LOW)
        grad_t = dot(w_out_ref[...], dr_low, NT).astype(LOW)
        grad_t_ref[...] = grad_t
        product = grad_t.astype(WIDE) * attended_ref[...]
        for pair in range(dots_ref.shape[0]):
            for head in range(2):
                lanes = slice(pair * PAIR + head * HEAD, pair * PAIR + (head + 1) * HEAD)
                dots_ref[pair, head : head + 1] = jnp.sum(product[lanes], axis=0, keepdims=True)

    if ahead:
        for chosen, ticks in enumerate(AHEAD_TICKS):
            for tick, when in enumerate(ticks):
                if when == LAST_BLOCK:
                    trade(chosen, tick, when)

        @pl.when(block == pl.num_programs(0) - 1)
        def _():
            for pair in sums:
                for each in pair:
                    each.store().wait()


def mlp_call(ahead, hidden, attn_low, attended, cotangent, w_out, gain_mlp, w_up, b_up, w_down):
    rows, width = hidden.shape
    hidden_units = w_up.shape[1]
    pairs = width // PAIR
    once = lambda *shape: pl.BlockSpec(
        shape, lambda block: (0,) * len(shape), pipeline_mode=pl.Buffered(1)
    )
    square, line = once(rows, width), once(1, width)
    up = pl.BlockSpec((width, FF_BLOCK), lambda block: (0, block))
    down = pl.BlockSpec((FF_BLOCK, width), lambda block: (block, 0))
    bias = pl.BlockSpec((1, FF_BLOCK), lambda block: (0, block))
    wide = jax.ShapeDtypeStruct((rows, width), WIDE)
    anywhere = pl.BlockSpec(memory_space=pl.ANY)
    down_rows = sum(ahead_rows((FF_BLOCK, width), DOWN_AXES)[-1])
    up_rows = sum(ahead_rows((width, FF_BLOCK), UP_AXES)[-1])
    part_shapes = [
        jax.ShapeDtypeStruct((down_rows, width), LOW),
        jax.ShapeDtypeStruct((up_rows, FF_BLOCK), LOW),
    ]
    params = dict(collective_id=3, has_side_effects=True) if ahead else {}
    return pl.pallas_call(
        functools.partial(mlp_kernel, ahead),
        grid=(hidden_units // FF_BLOCK,),
        in_specs=[square] * 4 + [once(width, width), line, up, bias, down],
        out_specs=[
            whole(rows, width),
            whole(rows, width),
            whole(width, rows),
            whole(pairs, 2, rows),
            down,
            up,
            whole(width, width),
            whole(1, width),
            bias,
        ]
        + [anywhere] * (2 if ahead else 0),
        out_shape=[
            wide,
            wide,
            jax.ShapeDtypeStruct((width, rows), LOW),
            jax.ShapeDtypeStruct((pairs, 2, rows), WIDE),
            jax.ShapeDtypeStruct(w_down.shape, LOW),
            jax.ShapeDtypeStruct(w_up.shape, LOW),
            jax.ShapeDtypeStruct((width, width), LOW),
            jax.ShapeDtypeStruct((1, width), WIDE),
            jax.ShapeDtypeStruct((1, hidden_units), WIDE),
        ]
        + (part_shapes if ahead else []),
        scratch_shapes=[
            pltpu.VMEM((rows, width), WIDE),
            pltpu.VMEM((rows, 1), WIDE),
            pltpu.VMEM((rows, width), LOW),
            pltpu.VMEM((rows, width), LOW),
            pltpu.VMEM((rows, width), WIDE),
            pltpu.VMEM((rows, FF_BLOCK), LOW),
            pltpu.VMEM((rows, FF_BLOCK), LOW),
        ]
        + (ahead_scratch(width) if ahead else []),
        name="mlp",
        compiler_params=pltpu.CompilerParams(vmem_limit_bytes=60 * 2**20, **params),
    )(hidden, attn_low, attended, cotangent, w_out, gain_mlp[None], w_up, b_up[None], w_down)


PARTS = (
    ("down", (0, 0), (512, 768), DOWN_AXES, 0, AHEAD_STEPS[0], 0, (24, 24, 24, 1, 2, 4, 5, 6, 8, 9)),
    ("down", (512, 0), (512, 768), DOWN_AXES, 1, AHEAD_STEPS[1], 1, (24, 24, 24, 1, 2, 4, 5, 6, 8, 9)),
    ("down", (1024, 0), (512, 768), DOWN_AXES, 0, AHEAD_STEPS[2], 2, (24, 24, 1, 2, 4, 6, 7, 9, 12, 13)),
    ("down", (1536, 0), (512, 768), DOWN_AXES, 1, AHEAD_STEPS[3], 3, (24, 24, 1, 2, 4, 6, 8, 10, 12, 13)),
    ("up", (0, 0), (768, 512), UP_AXES, 1, AHEAD_STEPS[0], 0, (24, 24, 24, 1, 2, 5, 6, 7, 10, 11)),
    ("up", (0, 512), (768, 512), UP_AXES, 0, AHEAD_STEPS[1], 1, (24, 24, 24, 2, 3, 5, 6, 8, 10, 11)),
    ("up", (0, 1024), (768, 512), UP_AXES, 1, AHEAD_STEPS[2], 2, (24, 24, 2, 3, 5, 6, 8, 11, 12, 14)),
    ("up", (0, 1536), (768, 512), UP_AXES, 0, AHEAD_STEPS[3], 3, (24, 24, 2, 4, 5, 6, 9, 11, 12, 13)),
    ("down", (2048, 0), (1024, 768), "rrrrr", 0, 0, None, (1, 4, 6, 8, 12, 16, 19, 21, 24, 24)),
    ("up", (0, 2048), (768, 1024), "rrrcc", 1, 0, None, (1, 4, 6, 8, 12, 16, 20, 22, 24, 24)),
    ("out", (0, 0), (768, 768), "rrrrc", 0, 0, None, (2, 5, 6, 9, 12, 16, 20, 22, 24, 24)),
    ("qkv", (0, 0), (768, 512), "rrrrc", 0, 0, None, None),
    ("qkv", (0, 512), (768, 512), "rrrrc", 1, 0, None, None),
    ("qkv", (0, 1024), (768, 512), "rrrrc", 0, 0, None, None),
    ("qkv", (0, 1536), (768, 768), "rrrrc", 1, 0, None, None),
)


def gradient_kernel(*refs):
    keys, values, shards = refs[:3]
    q_ref, grad_ref, lse_ref, dots_ref, clips, query_clip, w_ref = refs[3:10]
    down_in, up_in, out_in, part_down, part_up, small_in = refs[10:16]
    down_out, up_out, out_out, qkv_out, small_out, input_out = refs[16:22]
    refs = refs[22:]
    kv_slot, a_slot, dq_sum, dk_sum, dv_sum, dk_all, dv_all, grad_k, grad_v, parts = refs[:10]
    from_near, from_across, qkv_term, clip_slot, small_arrived = refs[10:15]
    input_sum = dq_sum
    kv_sems, a_sem, line_sends, line_receives, sends, receives, locals_ = refs[15:22]
    small_sends, small_receives, out_sem, clip_sem = refs[22:26]
    refs = refs[26:]
    rows, width = q_ref.shape
    pairs = width // PAIR
    pieces = 4 * pairs
    group, place = lax.axis_index("dp"), lax.axis_index("blk")
    near = (group, place + 1 - 2 * (place % 2))
    across = (group, 3 - place)
    at_end = place % 3 == 0

    arrays = {
        "down": (down_in, down_out),
        "up": (up_in, up_out),
        "out": (out_in, out_out),
        "qkv": (qkv_term, qkv_out),
    }
    sums = []
    for index, (name, corner, shape, axes, turn, begin, block, _) in enumerate(PARTS):
        steps = STEPS - begin
        total, arrived, refs = refs[0], refs[1 : steps + 1], refs[steps + 1 :]
        term, result = arrays[name]
        if block is not None:
            term = {"down": part_down, "up": part_up}[name]
            term = term.at[pl.ds(*ahead_rows(shape, axes)[block])]
        sums.append(
            Sum(
                turn,
                axes,
                corner,
                shape,
                term,
                result,
                total,
                arrived,
                (sends.at[index], receives.at[index]),
                locals_.at[index],
                begin=begin,
            )
        )
    early = [(each, part[-1]) for each, part in zip(sums, PARTS) if part[-1] is not None]
    late = [each for each, part in zip(sums, PARTS) if part[-1] is None]

    chunk_rows = rows // pairs

    def chunk_of(chunk):
        return pl.ds(pl.multiple_of(chunk * chunk_rows, chunk_rows), chunk_rows)

    def line_copy(channel, chunk, source, target, device):
        return pltpu.make_async_remote_copy(
            src_ref=parts.at[source, chunk_of(chunk)],
            dst_ref=target.at[chunk_of(chunk)],
            send_sem=line_sends.at[channel, chunk],
            recv_sem=line_receives.at[channel, chunk],
            device_id=device,
            device_id_type=MESH,
        )

    def inward(source, chunk):
        return line_copy(source, chunk, source, from_near.at[source], near)

    def middle(source, chunk):
        return line_copy(3 + source, chunk, source, from_across.at[source], across)

    def outward(chunk):
        return line_copy(5, chunk, 2, from_near.at[0], near)

    def add_chunk(total, term, chunk):
        here = chunk_of(chunk)
        total[here] = (total[here].astype(WIDE) + term[here].astype(WIDE)).astype(total.dtype)

    def pair_columns(pair):
        return pl.ds(pl.multiple_of(pair * PAIR, PAIR), PAIR)

    def kv_copies(shard, pair, slot):
        return [
            pltpu.make_async_copy(
                source.at[shard, :, pair_columns(pair)], kv_slot.at[slot, side], kv_sems.at[slot, side]
            )
            for side, source in enumerate((keys, values))
        ]

    def a_copy(shard):
        return pltpu.make_async_copy(shards.at[shard], a_slot, a_sem)

    def clip_copy(turn):
        source = clips.at[pl.ds(pl.multiple_of((3 - turn) * rows, 8), rows)]
        return pltpu.make_async_copy(source, clip_slot, clip_sem)

    def of_pairs(stack):
        return jnp.concatenate([stack[pair] for pair in range(pairs)], axis=1)

    for copy in kv_copies(3, 0, 0):
        copy.start()
    greet([device for _, device in place_bits(0)] + [across])
    for each, _ in early:
        each.start()
    dq_sum[...] = jnp.zeros_like(dq_sum)
    grad_k[...] = jnp.zeros_like(grad_k)
    grad_v[...] = jnp.zeros_like(grad_v)
    small_out[...] = small_in[...]

    def weight_terms(d_query):
        a_copy(0).wait()
        d_key, d_value = of_pairs(dk_all), of_pairs(dv_all)
        part = dot(d_key, w_ref[:, width : 2 * width], NT) + dot(d_value, w_ref[:, 2 * width :], NT)
        if d_query is not None:
            part = part + dot(d_query, w_ref[:, :width], NT)
        small_out[:1] += jnp.sum(part * a_slot[...].astype(WIDE), axis=0, keepdims=True)
        grad_k[...] += dot(a_slot[...], d_key, TN)
        grad_v[...] += dot(a_slot[...], d_value, TN)
        return part

    @pl.loop(0, pieces)
    def _(piece):
        turn, pair, slot = piece // pairs, piece % pairs, piece % 2

        def at(when, *actions):
            @pl.when(piece == when)
            def _():
                for action in actions:
                    action()

        following = piece + 1

        @pl.when(following < pieces)
        def _():
            for copy in kv_copies(3 - following // pairs, following % pairs, following % 2):
                copy.start()

        @pl.when(pair == 1)
        def _():
            a_copy(3 - turn).start()

        for when in range(pieces):
            ends = [
                functools.partial(each.turn, tick)
                for tick in range(2 * STEPS)
                for each, ticks in early
                if ticks[tick] == when and tick >= each.begin
            ]
            if ends:
                at(when, *ends)
        at_middle = jnp.logical_not(at_end)

        @pl.when(jnp.logical_and(turn > 0, at_end))
        def _():
            inward(turn - 1, pair).start()

        @pl.when(jnp.logical_and(at_middle, jnp.logical_and(piece >= FORWARD, piece < FORWARD + 2 * pairs)))
        def _():
            source, chunk = (piece - FORWARD) // pairs, (piece - FORWARD) % pairs
            inward(source, chunk).wait_recv()
            add_chunk(parts.at[source], from_near.at[source], chunk)
            middle(source, chunk).start()

        @pl.when(jnp.logical_and(at_middle, turn == 3))
        def _():
            middle(0, pair).wait_recv()
            add_chunk(parts.at[2], from_across.at[0], pair)
            outward(pair).start()

        @pl.when(pair == 0)
        def _():
            clip_copy(turn).start()
            clip_copy(turn).wait()

        for copy in kv_copies(0, pair, slot):
            copy.wait()
        columns = pair_columns(pair)

        def add(head, start, stop, dq, dk, dv):
            lanes = slice(head * HEAD, (head + 1) * HEAD)
            if start == 0:
                dv_sum[lanes], dk_sum[lanes] = dv, dk
            else:
                dv_sum[lanes] += dv
                dk_sum[lanes] += dk
            at_lanes = pl.ds(pl.multiple_of(pair * PAIR + head * HEAD, HEAD), HEAD)
            dq_sum[at_lanes, start:stop] += dq

        backward_pair(
            kv_slot[slot, 0],
            kv_slot[slot, 1],
            q_ref[:, columns],
            grad_ref[columns, :],
            lse_ref.at[pair],
            dots_ref.at[pair],
            clip_slot[...],
            query_clip[...],
            add,
        )
        dk_all[pair] = (dk_sum[...] * SCALE).T.astype(LOW)
        dv_all[pair] = dv_sum[...].T.astype(LOW)

        @pl.when(jnp.logical_and(pair == pairs - 1, turn < 3))
        def _():
            parts[turn] = weight_terms(None).astype(LOW)

    d_query = (dq_sum[...] * SCALE).T.astype(LOW)
    input_sum[...] = weight_terms(d_query)
    qkv_term[:, :width] = dot(a_slot[...], d_query, TN).astype(LOW)
    qkv_term[:, width : 2 * width] = grad_k[...].astype(LOW)
    qkv_term[:, 2 * width :] = grad_v[...].astype(LOW)

    small_steps = place_bits(0)

    def small(step):
        return remote(
            small_out, small_arrived.at[step], (small_sends, small_receives), step, small_steps[step][1]
        )

    for each in late:
        each.start()
    open_sums = [
        (each, [tick for tick in range(each.begin, 2 * STEPS) if ticks[tick] == pieces])
        for each, ticks in early
    ]
    open_sums += [(each, list(range(2 * STEPS))) for each in late]

    @pl.when(at_end)
    def _():
        @pl.loop(0, pairs)
        def _(chunk):
            for source in range(3):
                inward(source, chunk).wait_send()
            outward(chunk).wait_recv()
            add_chunk(input_sum, from_near.at[0], chunk)

    @pl.when(jnp.logical_not(at_end))
    def _():
        @pl.loop(0, pairs)
        def _(chunk):
            outward(chunk).wait_send()
            for source in range(2):
                middle(source, chunk).wait_send()
            middle(1, chunk).wait_recv()
            add_chunk(input_sum, from_across.at[1], chunk)
            inward(2, chunk).wait_recv()
            add_chunk(input_sum, from_near.at[2], chunk)

    store = pltpu.make_async_copy(input_sum, input_out, out_sem)
    store.start()
    for tick in range(2 * STEPS):
        if tick < STEPS:
            small(tick).start()
        for each, ticks in open_sums:
            if ticks:
                each.turn(ticks.pop(0))
        if tick < STEPS:
            small(tick).wait()
            small_out[...] += small_arrived[tick]
    store.wait()


def gradient_call(
    keys, values, shards, query, grad_t, lse, row_dots, clips, query_clip, w_qkv, grad_down, grad_up, grad_out, part_down, part_up, small
):
    rows, width = query.shape
    pairs = width // PAIR
    anywhere = pl.BlockSpec(memory_space=pl.ANY)
    inside = pl.BlockSpec(memory_space=pltpu.VMEM)
    square = (rows, width)
    scratch = [
        pltpu.VMEM((2, 2, rows, PAIR), LOW),
        pltpu.VMEM(square, LOW),
        pltpu.VMEM((width, rows), WIDE),
        pltpu.VMEM((PAIR, rows), WIDE),
        pltpu.VMEM((PAIR, rows), WIDE),
        pltpu.VMEM((pairs, rows, PAIR), LOW),
        pltpu.VMEM((pairs, rows, PAIR), LOW),
        pltpu.VMEM((width, width), WIDE),
        pltpu.VMEM((width, width), WIDE),
        pltpu.VMEM((3, *square), LOW),
    ]
    scratch += [pltpu.VMEM((3, *square), LOW), pltpu.VMEM((2, *square), LOW)]
    scratch += [
        pltpu.VMEM((width, 3 * width), LOW),
        pltpu.VMEM((rows, 1), clips.dtype),
        pltpu.VMEM((STEPS, *small.shape), WIDE),
        pltpu.SemaphoreType.DMA((2, 2)),
        pltpu.SemaphoreType.DMA,
        pltpu.SemaphoreType.DMA((6, pairs)),
        pltpu.SemaphoreType.DMA((6, pairs)),
        pltpu.SemaphoreType.DMA((len(PARTS), 2 * STEPS)),
        pltpu.SemaphoreType.DMA((len(PARTS), 2 * STEPS)),
        pltpu.SemaphoreType.DMA((len(PARTS), 2)),
        pltpu.SemaphoreType.DMA((STEPS,)),
        pltpu.SemaphoreType.DMA((STEPS,)),
        pltpu.SemaphoreType.DMA,
        pltpu.SemaphoreType.DMA,
    ]
    for _, _, shape, axes, _, begin, _, _ in PARTS:
        shapes = halves(shape, axes)
        scratch += [pltpu.VMEM(each, LOW) for each in (shapes[max(begin - 1, 0)], *shapes[begin:])]
    like = lambda array: jax.ShapeDtypeStruct(array.shape, array.dtype)
    return pl.pallas_call(
        gradient_kernel,
        in_specs=[anywhere] * 3 + [inside] * 4 + [anywhere] + [inside] * 2 + [anywhere] * 5 + [inside],
        out_specs=[anywhere] * 4 + [inside, anywhere],
        out_shape=[
            like(grad_down),
            like(grad_up),
            like(grad_out),
            jax.ShapeDtypeStruct((width, 3 * width), LOW),
            like(small),
            jax.ShapeDtypeStruct(square, WIDE),
        ],
        scratch_shapes=scratch,
        name="gradients",
        compiler_params=pltpu.CompilerParams(
            collective_id=1, has_side_effects=True, vmem_limit_bytes=62 * 2**20
        ),
    )(
        keys, values, shards, query, grad_t, lse, row_dots, clips, query_clip, w_qkv,
        grad_down, grad_up, grad_out, part_down, part_up, small,
    )


def on_device(
    groups, inputs, positions, segments, gain_attn, w_qkv, w_out, gain_mlp, w_up, b_up, w_down, cotangent
):
    rows, width = inputs.shape
    pairs = width // PAIR
    place = lax.axis_index("blk")
    w_query = w_qkv[:, :width]

    def send(value, pairs_of_places):
        return lax.ppermute(value, "blk", pairs_of_places)

    hidden = inputs + position_table(positions, width)
    normed_attn, inverse_attn = normalize(hidden)
    a_low = (normed_attn * gain_attn).astype(LOW)

    table = jnp.array([[0, 1, 2, 3], [1, 0, 2, 3], [2, 3, 1, 0], [3, 2, 1, 0]], jnp.int32)
    order = lax.dynamic_index_in_dim(table, place, keepdims=False)
    clips = jnp.concatenate(
        [lax.dynamic_slice_in_dim(segments, order[index] * rows, rows) for index in range(4)]
    )[:, None]
    query_clip = lax.dynamic_slice_in_dim(segments, place * rows, rows)[None, :]
    shards, keys, values, query, attended, lse, attn_low = attention_call(
        a_low, w_qkv, clips, query_clip
    )

    quick = groups == 8 and rows == width
    (
        outputs,
        d_resid,
        d_attn_t,
        row_dots,
        grad_down,
        grad_up,
        grad_out,
        grad_gain_mlp,
        grad_bias_up,
        *parts,
    ) = mlp_call(quick, hidden, attn_low, attended, cotangent, w_out, gain_mlp, w_up, b_up, w_down)
    grad_gain_mlp, grad_bias_up = grad_gain_mlp[0], grad_bias_up[0]

    if quick:
        small = jnp.concatenate([jnp.zeros_like(gain_attn), grad_gain_mlp, grad_bias_up])
        sum_down, sum_up, sum_out, sum_qkv, sum_small, d_normed_attn = gradient_call(
            keys,
            values,
            shards,
            query,
            d_attn_t,
            lse,
            row_dots,
            clips,
            query_clip,
            w_qkv,
            grad_down,
            grad_up,
            grad_out,
            *parts,
            jnp.pad(small.reshape(6, width), ((0, 2), (0, 0))),
        )
        input_grad = d_resid + norm_back(d_normed_attn * gain_attn, normed_attn, inverse_attn)
        return (
            outputs,
            input_grad,
            sum_small[0] / gain_attn,
            sum_qkv.astype(WIDE),
            sum_out.astype(WIDE),
            sum_small[1],
            sum_up.astype(WIDE),
            sum_small[2:6].reshape(-1),
            sum_down.astype(WIDE),
        )

    everywhere = ("dp", "blk")

    def back(index, dq):
        return backward_call(
            index == 3,
            index == 0,
            keys[index],
            values[index],
            query,
            d_attn_t,
            lse,
            row_dots,
            clips[index * rows : (index + 1) * rows],
            query_clip,
            w_qkv,
            dq,
        )

    middle, outward, inward = [(1, 2), (2, 1)], [(1, 0), (2, 3)], [(0, 1), (3, 2)]
    dk_3, dv_3, dq, part_3 = back(3, None)
    far = send(part_3, inward)
    dk_2, dv_2, dq, part_2 = back(2, dq)
    far, part_2, dq = lax.optimization_barrier((far, part_2, dq))
    onward = (part_3.astype(WIDE) + far.astype(WIDE)).astype(LOW)
    mid_3 = send(onward, middle)
    mid_2 = send(part_2, inward)
    dq, onward = lax.optimization_barrier((dq, onward))
    dk_1, dv_1, dq, part_1 = back(1, dq)
    mid_3, mid_2, part_1, dq = lax.optimization_barrier((mid_3, mid_2, part_1, dq))
    onward_1 = (part_2.astype(WIDE) + mid_2.astype(WIDE)).astype(LOW)
    onward_2 = (part_1.astype(WIDE) + mid_3.astype(WIDE)).astype(LOW)
    last_1 = send(onward_1, middle)
    last_2 = send(onward_2, outward)
    last_3 = send(part_1, inward)
    dq, onward_1, onward_2 = lax.optimization_barrier((dq, onward_1, onward_2))
    dk_0, dv_0, dq, part_0 = back(0, dq)
    grad_query = dot(a_low, dq, TN).astype(LOW)
    d_keys, d_values = (dk_0, dk_1, dk_2, dk_3), (dv_0, dv_1, dv_2, dv_3)
    grad_key = sum(dot(shard, term, TN) for shard, term in zip(shards, d_keys)).astype(LOW)
    grad_value = sum(dot(shard, term, TN) for shard, term in zip(shards, d_values)).astype(LOW)
    d_normed_attn = (
        part_0
        + dot(dq, w_query, NT)
        + last_1.astype(WIDE)
        + last_2.astype(WIDE)
        + last_3.astype(WIDE)
    )
    grad_gain_attn = jnp.sum(d_normed_attn * normed_attn, axis=0)
    input_grad = d_resid + norm_back(d_normed_attn * gain_attn, normed_attn, inverse_attn)
    small = jnp.concatenate([grad_gain_attn, grad_gain_mlp, grad_bias_up])
    sums = lax.psum((grad_down, grad_up, grad_out, grad_query, grad_key, grad_value), everywhere)
    sum_small = lax.psum(small, everywhere)
    sum_down, sum_up, sum_out, *sum_qkv = sums
    return (
        outputs,
        input_grad,
        sum_small[:width],
        jnp.concatenate(sum_qkv, axis=1).astype(WIDE),
        sum_out.astype(WIDE),
        sum_small[width : 2 * width],
        sum_up.astype(WIDE),
        sum_small[2 * width :],
        sum_down.astype(WIDE),
    )


def solution(mesh):
    rows = P(("dp", "blk"), None)
    placed = (rows, P(("dp", "blk")), P("dp"), P(), P(), P(), P(), P(), P(), P(), rows)
    return jax.shard_map(
        functools.partial(on_device, mesh.shape["dp"]),
        mesh=mesh,
        in_specs=placed,
        out_specs=(rows, rows, P(), P(), P(), P(), P(), P(), P()),
        check_vma=False,
    )
```

```python
import functools
import math

import jax
import jax.numpy as jnp
from jax import lax
from jax.experimental import pallas as pl
from jax.experimental.pallas import tpu as pltpu
from jax.sharding import PartitionSpec as P

HEADS = 12
HEAD = 64
PAIR = 2 * HEAD
SCALE = HEAD**-0.5
LOG2E = 1.4426950408889634
MASKED = -1.0e9
QUERY_BLOCK = 384
EPS_NORM = 1e-06
LOW = jnp.bfloat16
WIDE = jnp.float32

NN = (((1,), (0,)), ((), ()))
NT = (((1,), (1,)), ((), ()))
TN = (((0,), (0,)), ((), ()))


def dot(left, right, dims):
    return lax.dot_general(left, right, dims, preferred_element_type=WIDE)


def position_table(positions, model_width):
    half_width = model_width // 2
    freqs = jnp.exp(jnp.arange(half_width, dtype=WIDE) * (-math.log(10000.0) / half_width))
    angles = positions.astype(WIDE)[:, None] * freqs[None, :]
    return jnp.concatenate([jnp.sin(angles), jnp.cos(angles)], axis=1)


def normalize(values):
    center = values - jnp.mean(values, axis=-1, keepdims=True)
    inverse = lax.rsqrt(jnp.mean(center * center, axis=-1, keepdims=True) + EPS_NORM)
    return center * inverse, inverse


def norm_back(grad_norm, normed, inverse):
    first = jnp.mean(grad_norm, axis=-1, keepdims=True)
    second = jnp.mean(grad_norm * normed, axis=-1, keepdims=True)
    return inverse * (grad_norm - first - normed * second)


def in_head(values, head):
    lanes = lax.broadcasted_iota(jnp.int32, values.shape, 1)
    return (lanes < HEAD) == (head == 0)


def only_head(values, head, other=None):
    other = jnp.zeros_like(values) if other is None else other
    return jnp.where(in_head(values, head), values, other)


def split_scaled(query):
    scaled = query.astype(WIDE) * (SCALE * LOG2E)
    high = scaled.astype(LOW)
    return high, (scaled - high.astype(WIDE)).astype(LOW)


def score_sides(key, query):
    high, low = split_scaled(query)
    key_side = jnp.concatenate([key, key], axis=1)
    query_side = [
        jnp.concatenate([only_head(high, head), only_head(low, head)], axis=1) for head in range(2)
    ]
    return key_side, query_side


def work_items(rows):
    return [(start, head) for start in range(0, rows, QUERY_BLOCK) for head in range(2)]


def whole(*shape):
    return pl.BlockSpec(shape, lambda pair: (0,) * len(shape))


def columns_of(rows, first=0):
    return pl.BlockSpec((rows, PAIR), lambda pair: (0, pair + first))


def backward_pair(key, value, query, grad_t, lse, row_dots, key_clip, query_clip, add):
    rows = query.shape[0]
    grad = grad_t.T
    key_t, query_t = key.T, query.T
    key_side, query_side = score_sides(key, query)
    grad_side = [only_head(grad, head) for head in range(2)]
    for start, head in work_items(rows):
        stop = start + QUERY_BLOCK
        lanes, row = slice(head * HEAD, (head + 1) * HEAD), slice(head, head + 1)
        score = dot(key_side, query_side[head][start:stop], NT)
        score = jnp.where(key_clip == query_clip[:, start:stop], score, MASKED)
        probs = jnp.exp2(score - lse[row, start:stop])
        d_probs = dot(value, grad_side[head][start:stop], NT)
        d_scores = (probs * (d_probs - row_dots[row, start:stop])).astype(LOW)
        probs = probs.astype(LOW)
        dv = dot(grad_t[lanes, start:stop], probs, NT)
        dk = dot(query_t[lanes, start:stop], d_scores, NT)
        dq = dot(key_t[lanes], d_scores, NN)
        add(head, start, stop, dq, dk, dv)


def backward_kernel(first, last, *refs):
    k_ref, v_ref, q_ref, grad_ref, lse_ref, dots_ref, key_clip, query_clip, wk_ref, wv_ref = refs[:10]
    refs = refs[10:]
    if not first:
        dq_in = refs[0]
        refs = refs[1:]
    dk_ref, dv_ref, dq_ref, part_ref, dk_sum, dv_sum, dq_sum, dk_all, dv_all = refs
    pair = pl.program_id(0)
    rows = q_ref.shape[0]

    def add(head, start, stop, dq, dk, dv):
        lanes = slice(head * HEAD, (head + 1) * HEAD)
        if start == 0:
            dv_sum[lanes], dk_sum[lanes] = dv, dk
        else:
            dv_sum[lanes] += dv
            dk_sum[lanes] += dk
        if not first:
            dq = dq + dq_in[lanes, start:stop]
        if last:
            dq_sum[lanes, start:stop] = dq
        else:
            dq_ref[lanes, start:stop] = dq

    backward_pair(
        k_ref[...],
        v_ref[...],
        q_ref[...],
        grad_ref[...],
        lse_ref,
        dots_ref,
        key_clip[...],
        query_clip[...],
        add,
    )
    if last:
        dq_ref[...] = (dq_sum[...] * SCALE).T.astype(LOW)
    dk = (dk_sum[...] * SCALE).T.astype(LOW)
    dv = dv_sum[...].T.astype(LOW)
    dk_ref[...] = dk
    dv_ref[...] = dv
    dk_all[pair] = dk
    dv_all[pair] = dv

    @pl.when(pair == pl.num_programs(0) - 1)
    def _():
        pairs = dk_all.shape[0]
        dk_rows = jnp.concatenate([dk_all[index] for index in range(pairs)], axis=1)
        dv_rows = jnp.concatenate([dv_all[index] for index in range(pairs)], axis=1)
        part = dot(dk_rows, wk_ref[...], NT) + dot(dv_rows, wv_ref[...], NT)
        part_ref[...] = part.astype(part_ref.dtype)


def backward_call(first, last, key, value, query, grad_t, lse, row_dots, key_clip, query_clip, w_qkv, dq):
    rows, width = query.shape
    pairs = width // PAIR
    across = pl.BlockSpec((PAIR, rows), lambda pair: (pair, 0))
    line = pl.BlockSpec((None, 2, rows), lambda pair: (pair, 0, 0))
    columns = columns_of(rows)
    in_specs = [columns, columns, columns, across, line, line, whole(rows, 1), whole(1, rows)]
    in_specs += [
        pl.BlockSpec((width, width), lambda pair: (0, 1)),
        pl.BlockSpec((width, width), lambda pair: (0, 2)),
    ]
    operands = [key, value, query, grad_t, lse, row_dots, key_clip, query_clip, w_qkv, w_qkv]
    if not first:
        in_specs.append(across)
        operands.append(dq)
    low_rows = jax.ShapeDtypeStruct((rows, width), LOW)
    tall = pltpu.VMEM((PAIR, rows), WIDE)
    parts = pltpu.VMEM((pairs, rows, PAIR), LOW)
    return pl.pallas_call(
        functools.partial(backward_kernel, first, last),
        grid=(pairs,),
        in_specs=in_specs,
        out_specs=[columns, columns, columns if last else across, whole(rows, width)],
        out_shape=[
            low_rows,
            low_rows,
            low_rows if last else jax.ShapeDtypeStruct((width, rows), WIDE),
            jax.ShapeDtypeStruct((rows, width), WIDE if last else LOW),
        ],
        scratch_shapes=[tall, tall, tall, parts, parts],
        name="attend_back",
        cost_estimate=pl.CostEstimate(
            flops=40 * rows * rows * width, bytes_accessed=24 * rows * width, transcendentals=0
        ),
        compiler_params=pltpu.CompilerParams(vmem_limit_bytes=48 * 2**20),
    )(*operands)


MESH = pl.DeviceIdType.MESH
TURNS = ((0, 1, 2), (0, 2, 1))
STEPS = 5
FORWARD = 8


def place_bits(turn):
    group, place = lax.axis_index("dp"), lax.axis_index("blk")
    steps = []
    for bit in TURNS[turn]:
        mine = group // (1 << bit) % 2
        steps.append((mine, (group + (1 - 2 * mine) * (1 << bit), place)))
    for bit in range(2):
        mine = place // (1 << bit) % 2
        steps.append((mine, (group, place + (1 - 2 * mine) * (1 << bit))))
    return steps


def remote(source, target, sems, index, device):
    return pltpu.make_async_remote_copy(
        src_ref=source,
        dst_ref=target,
        send_sem=sems[0].at[index],
        recv_sem=sems[1].at[index],
        device_id=device,
        device_id_type=MESH,
    )


def part_of(row, rows, column, columns):
    row = row if isinstance(row, int) else pl.multiple_of(row, 16)
    column = column if isinstance(column, int) else pl.multiple_of(column, PAIR)
    return pl.ds(row, rows), pl.ds(column, columns)


def add_block(total, term, row=0, column=0):
    rows, columns = term.shape
    block = next(size for size in (48, 32, 16) if rows % size == 0)

    @pl.loop(0, rows // block)
    def _(index):
        here = part_of(row + index * block, block, column, columns)
        there = part_of(index * block, block, 0, columns)
        total[here] = (total[here].astype(WIDE) + term[there].astype(WIDE)).astype(total.dtype)


def halves(shape, axes):
    shapes = []
    for axis in axes:
        shape = (shape[0] // 2, shape[1]) if axis == "r" else (shape[0], shape[1] // 2)
        shapes.append(shape)
    return shapes


class Sum:
    def __init__(
        self, turn, axes, corner, shape, term, result, total, arrived, sems, local_sems, begin=0, stop=STEPS
    ):
        self.term, self.result, self.total, self.arrived = term, result, total, arrived
        self.sems, self.local_sems, self.begin, self.stop = sems, local_sems, begin, stop
        self.steps = place_bits(turn)
        self.shapes = halves(shape, axes)
        self.kept, self.left = [], []
        row, column = corner
        for axis, (rows, columns), (mine, _) in zip(axes, self.shapes, self.steps):
            down, across = (rows, 0) if axis == "r" else (0, columns)
            self.left.append((row + (1 - mine) * down, rows, column + (1 - mine) * across, columns))
            row, column = row + mine * down, column + mine * across
            self.kept.append((row, rows, column, columns))
        self.held = self.kept[max(begin - 1, 0)]

    def inside(self, place):
        row, rows, column, columns = place
        return part_of(row - self.held[0], rows, column - self.held[2], columns)

    def load(self):
        source = self.term if self.begin else self.term.at[part_of(*self.kept[0])]
        return pltpu.make_async_copy(source, self.total, self.local_sems.at[0])

    def store(self):
        place = self.kept[self.stop - 1]
        target = self.result.at[part_of(*place)] if self.stop == STEPS else self.result
        return pltpu.make_async_copy(
            self.total.at[self.inside(place)], target, self.local_sems.at[1]
        )

    def gather(self, step):
        place = self.left[step]
        source = self.term.at[part_of(*place)] if step == 0 else self.total.at[self.inside(place)]
        return remote(source, self.arrived[step - self.begin], self.sems, step, self.steps[step][1])

    def spread(self, step):
        here = self.result.at[part_of(*self.kept[step])]
        source = self.total.at[self.inside(self.kept[step])] if step == STEPS - 1 else here
        return remote(source, here, self.sems, STEPS + step, self.steps[step][1])

    def start(self):
        self.load().start()
        if self.begin:
            self.load().wait()
        self.gather(self.begin).start()

    def turn(self, tick):
        if tick < STEPS:
            if tick == 0:
                self.load().wait()
            self.gather(tick).wait()
            row, _, column, _ = self.kept[tick]
            add_block(
                self.total, self.arrived[tick - self.begin], row - self.held[0], column - self.held[2]
            )
            if tick + 1 < self.stop:
                self.gather(tick + 1).start()
            else:
                self.store().start()
                if self.stop == STEPS:
                    self.spread(STEPS - 1).start()
        else:
            step = 2 * STEPS - 1 - tick
            if step == STEPS - 1:
                self.store().wait()
            self.spread(step).wait()
            if step:
                self.spread(step - 1).start()


def greet(devices):
    barrier = pltpu.get_barrier_semaphore()
    for device in devices:
        pl.semaphore_signal(barrier, inc=1, device_id=device, device_id_type=MESH)
    pl.semaphore_wait(barrier, len(devices))


PASS_NEAR = (2, 4, 5, 6, 6, 6)
PASS_FAR = (10, 11, 12, 13, 15, 16)


def attention_kernel(*refs):
    a_in, w_ref, clips, query_clip = refs[:4]
    a_out, k_out, v_out, q_ref, acc_ref, lse_ref, attn_ref = refs[4:11]
    a_all, top_all, total_all, kv_slot, clip_slot = refs[11:16]
    a_sems, kv_sems, clip_sem, line_sends, line_receives = refs[16:]
    rows, width = q_ref.shape
    pairs = width // PAIR
    pieces = 4 * pairs
    chunk_rows = rows // pairs
    group, place = lax.axis_index("dp"), lax.axis_index("blk")
    near = (group, place + 1 - 2 * (place % 2))
    across = (group, 3 - place)
    at_end = place % 3 == 0
    at_middle = jnp.logical_not(at_end)

    def line_copy(channel, chunk, source, target, device):
        here = pl.ds(pl.multiple_of(chunk * chunk_rows, chunk_rows), chunk_rows)
        return pltpu.make_async_remote_copy(
            src_ref=source.at[here],
            dst_ref=a_all.at[target, here],
            send_sem=line_sends.at[channel, chunk],
            recv_sem=line_receives.at[channel, chunk],
            device_id=device,
            device_id_type=MESH,
        )

    channels = (
        lambda chunk: line_copy(0, chunk, a_in, 1, near),
        lambda chunk: line_copy(1, chunk, a_in, 2, across),
        lambda chunk: line_copy(2, chunk, a_all.at[2], 2, near),
        lambda chunk: line_copy(3, chunk, a_all.at[1], 3, across),
        lambda chunk: line_copy(4, chunk, a_all.at[3], 3, near),
    )
    load = pltpu.make_async_copy(a_in, a_all.at[0], a_sems.at[4])
    load.start()
    greet((near, across))
    for chunk in range(pairs):
        channels[0](chunk).start()

    @pl.when(at_middle)
    def _():
        for chunk in range(pairs):
            channels[1](chunk).start()

    top_all[...] = jnp.full_like(top_all, -1.0e30)
    total_all[...] = jnp.zeros_like(total_all)
    acc_ref[...] = jnp.zeros_like(acc_ref)

    def keep(shard):
        return pltpu.make_async_copy(a_all.at[shard], a_out.at[shard], a_sems.at[shard])

    def clip_copy(turn):
        source = clips.at[pl.ds(pl.multiple_of(turn * rows, 8), rows)]
        return pltpu.make_async_copy(source, clip_slot, clip_sem)

    def pair_columns(pair):
        return pl.ds(pl.multiple_of(pair * PAIR, PAIR), PAIR)

    def kv_copies(turn, pair, slot):
        return [
            pltpu.make_async_copy(
                kv_slot.at[slot, side], target.at[turn, :, pair_columns(pair)], kv_sems.at[slot, side]
            )
            for side, target in enumerate((k_out, v_out))
        ]

    load.wait()
    keep(0).start()

    @pl.loop(0, pieces)
    def _(piece):
        turn, pair, slot = piece // pairs, piece % pairs, piece % 2
        for chunk, when in enumerate(PASS_NEAR):

            @pl.when(jnp.logical_and(piece == when, at_middle))
            def _():
                channels[0](chunk).wait_recv()
                channels[3](chunk).start()
                channels[1](chunk).wait_recv()
                channels[2](chunk).start()

        for chunk, when in enumerate(PASS_FAR):

            @pl.when(jnp.logical_and(piece == when, at_middle))
            def _():
                channels[3](chunk).wait_recv()
                channels[4](chunk).start()

        for shard, channel in ((1, 0), (2, 2), (3, 4)):

            @pl.when(jnp.logical_and(piece == shard * pairs, at_end))
            def _():
                for chunk in range(pairs):
                    channels[channel](chunk).wait_recv()

            @pl.when(piece == shard * pairs)
            def _():
                keep(shard).start()

        @pl.when(pair == 0)
        def _():
            clip_copy(turn).start()
            clip_copy(turn).wait()

        @pl.when(piece >= 2)
        def _():
            for copy in kv_copies(turn, pair, slot):
                copy.wait()

        columns = pair_columns(pair)

        @pl.when(turn == 0)
        def _():
            q_ref[:, columns] = dot(a_all[0], w_ref[:, columns], NN).astype(LOW)

        w_pair = jnp.concatenate(
            [w_ref[:, pair_columns(pair + pairs)], w_ref[:, pair_columns(pair + 2 * pairs)]], axis=1
        )
        kv = dot(a_all[turn], w_pair, NN).astype(LOW)
        key, value = kv[:, :PAIR], kv[:, PAIR:]
        kv_slot[slot, 0] = key
        kv_slot[slot, 1] = value
        for copy in kv_copies(turn, pair, slot):
            copy.start()
        value_t = value.T
        ones = jnp.ones((16, rows), LOW)
        value_rows = [
            jnp.concatenate([value_t[head * HEAD : (head + 1) * HEAD], ones], axis=0)
            for head in range(2)
        ]
        key_side, query_side = score_sides(key, q_ref[:, columns])
        key_clip = clip_slot[...]

        def scores(start, head):
            stop = start + QUERY_BLOCK
            result = dot(key_side, query_side[head][start:stop], NT)
            return jnp.where(key_clip == query_clip[:, start:stop], result, MASKED)

        def weights(start, head, result):
            here = slice(start, start + QUERY_BLOCK)
            before = top_all[pair, head : head + 1, here]
            top = jnp.maximum(before, jnp.max(result, axis=0, keepdims=True))
            top_all[pair, head : head + 1, here] = top
            return jnp.exp2(result - top).astype(LOW), jnp.exp2(before - top)

        def attend(start, head, expd, shrink):
            here, row = slice(start, start + QUERY_BLOCK), slice(head, head + 1)
            lanes = pl.ds(pl.multiple_of(pair * PAIR + head * HEAD, HEAD), HEAD)
            result = dot(value_rows[head], expd, NN)
            acc_ref[lanes, here] = acc_ref[lanes, here] * shrink + result[:HEAD]
            total_all[pair, row, here] = total_all[pair, row, here] * shrink + result[HEAD : HEAD + 1]

        items = work_items(rows)
        result = scores(*items[0])
        before = None
        for index, item in enumerate(items):
            following = scores(*items[index + 1]) if index + 1 < len(items) else None
            done = weights(*item, result)
            if before is not None:
                attend(*before)
            before = (*item, *done)
            result = following
        attend(*before)

        @pl.when(turn == 3)
        def _():
            for head in range(2):
                lanes = pl.ds(pl.multiple_of(pair * PAIR + head * HEAD, HEAD), HEAD)
                total = total_all[pair, head : head + 1]
                acc_ref[lanes] = acc_ref[lanes] * (1.0 / total)
                lse_ref[pair, head : head + 1] = top_all[pair, head : head + 1] + jnp.log(total) * LOG2E
            attn_ref[:, columns] = acc_ref[columns].T.astype(LOW)

    for slot in range(2):
        for copy in kv_copies(3, pairs - 2 + slot, slot):
            copy.wait()
    for shard in range(4):
        keep(shard).wait()
    for chunk in range(pairs):
        channels[0](chunk).wait_send()

    @pl.when(at_middle)
    def _():
        for channel in channels[1:]:
            for chunk in range(pairs):
                channel(chunk).wait_send()


def attention_call(a_low, w_qkv, clips, query_clip):
    rows, width = a_low.shape
    pairs = width // PAIR
    anywhere = pl.BlockSpec(memory_space=pl.ANY)
    inside = pl.BlockSpec(memory_space=pltpu.VMEM)
    four = jax.ShapeDtypeStruct((4, rows, width), LOW)
    square = jax.ShapeDtypeStruct((rows, width), LOW)
    lines = jax.ShapeDtypeStruct((pairs, 2, rows), WIDE)
    return pl.pallas_call(
        attention_kernel,
        in_specs=[anywhere, inside, anywhere, inside],
        out_specs=[anywhere] * 3 + [inside] * 4,
        out_shape=[four, four, four, square, jax.ShapeDtypeStruct((width, rows), WIDE), lines, square],
        scratch_shapes=[
            pltpu.VMEM((4, rows, width), LOW),
            pltpu.VMEM((pairs, 2, rows), WIDE),
            pltpu.VMEM((pairs, 2, rows), WIDE),
            pltpu.VMEM((2, 2, rows, PAIR), LOW),
            pltpu.VMEM((rows, 1), clips.dtype),
            pltpu.SemaphoreType.DMA((5,)),
            pltpu.SemaphoreType.DMA((2, 2)),
            pltpu.SemaphoreType.DMA,
            pltpu.SemaphoreType.DMA((5, pairs)),
            pltpu.SemaphoreType.DMA((5, pairs)),
        ],
        name="attention",
        compiler_params=pltpu.CompilerParams(
            collective_id=2, has_side_effects=True, vmem_limit_bytes=48 * 2**20
        ),
    )(a_low, w_qkv, clips, query_clip)


FF_BLOCK = 512
ROW_BLOCK = 384
AHEAD_STEPS = (3, 3, 2, 2)
AHEAD_TICKS = ((1, 3, 4), (2, 4, 5), (3, 5), (4, 5))
AHEAD = len(AHEAD_STEPS)
LAST_BLOCK = 5
DOWN_AXES, UP_AXES = "rrrrr", "rrrrc"


def ahead_rows(shape, axes):
    rows = [halves(shape, axes)[steps - 1][0] for steps in AHEAD_STEPS]
    return [(sum(rows[:block]), rows[block]) for block in range(AHEAD)]


def ahead_scratch(width):
    scratch = [pltpu.VMEM((2, FF_BLOCK, width), LOW), pltpu.VMEM((2, width, FF_BLOCK), LOW)]
    for shape, axes in (((FF_BLOCK, width), DOWN_AXES), ((width, FF_BLOCK), UP_AXES)):
        for steps in AHEAD_STEPS:
            shapes = halves(shape, axes)[:steps]
            scratch += [pltpu.VMEM(each, LOW) for each in (shapes[0], *shapes)]
    scratch += [pltpu.SemaphoreType.DMA((2 * AHEAD, 2 * STEPS))] * 2
    return scratch + [pltpu.SemaphoreType.DMA((2 * AHEAD, 2))]


def ahead_sums(width, part_down, part_up, refs):
    terms, refs = refs[:2], refs[2:]
    sends, receives, locals_ = refs[-3:]
    sums = []
    for side, (axes, shape, parts) in enumerate(
        ((DOWN_AXES, (FF_BLOCK, width), part_down), (UP_AXES, (width, FF_BLOCK), part_up))
    ):
        places = ahead_rows(shape, axes)
        for block, steps in enumerate(AHEAD_STEPS):
            index = side * AHEAD + block
            own, refs = refs[: steps + 1], refs[steps + 1 :]
            sums.append(
                Sum(
                    (block + side) % 2,
                    axes,
                    (0, 0),
                    shape,
                    terms[side].at[block % 2],
                    parts.at[pl.ds(*places[block])],
                    own[0],
                    own[1:],
                    (sends.at[index], receives.at[index]),
                    locals_.at[index],
                    stop=steps,
                )
            )
    return terms, [(sums[block], sums[AHEAD + block]) for block in range(AHEAD)]


def mlp_kernel(
    ahead,
    hidden_ref,
    attn_ref,
    attended_ref,
    cotangent_ref,
    w_out_ref,
    gain_ref,
    w_up_ref,
    b_up_ref,
    w_down_ref,
    outputs_ref,
    d_resid_ref,
    grad_t_ref,
    dots_ref,
    grad_down_ref,
    grad_up_ref,
    grad_out_ref,
    grad_gain_ref,
    grad_bias_ref,
    *refs,
):
    block = pl.program_id(0)
    rows, width = hidden_ref.shape
    if ahead:
        parts, refs = refs[:2], refs[2:]
    normed_ref, inverse_ref, b_ref, dy_ref, db_ref, z_ref, d_pre_ref = refs[:7]
    if ahead:
        terms, sums = ahead_sums(width, *parts, refs[7:])

        @pl.when(block == 0)
        def _():
            greet([device for _, device in place_bits(0)[: max(AHEAD_STEPS)]])

    def trade(chosen, tick, when):
        @pl.when(block == when)
        def _():
            for each in sums[chosen]:
                each.turn(tick)

    @pl.when(block == 0)
    def _():
        resid = hidden_ref[...] + dot(attn_ref[...], w_out_ref[...], NN)
        normed, inverse = normalize(resid)
        normed_ref[...] = normed
        inverse_ref[...] = inverse
        b_ref[...] = (normed * gain_ref[...]).astype(LOW)
        dy_ref[...] = cotangent_ref[...].astype(LOW)
        outputs_ref[...] = resid
        db_ref[...] = jnp.zeros_like(db_ref)

    bias = jnp.zeros((1, FF_BLOCK), WIDE)
    for start in range(0, rows, ROW_BLOCK):
        here = slice(start, start + ROW_BLOCK)
        pre_act = dot(b_ref[here], w_up_ref[...], NN) + b_up_ref[...]
        cumulative = 0.5 * (1.0 + lax.erf(pre_act * 0.7071067811865476))
        density = jnp.exp(-0.5 * pre_act * pre_act) * 0.3989422804014327
        z_ref[here] = (pre_act * cumulative).astype(LOW)
        d_gelu = dot(dy_ref[here], w_down_ref[...], NT)
        d_pre = (d_gelu * (cumulative + pre_act * density)).astype(LOW)
        d_pre_ref[here] = d_pre
        bias += jnp.sum(d_pre.astype(WIDE), axis=0, keepdims=True)
        outputs_ref[here] += dot(z_ref[here], w_down_ref[...], NN)
        db_ref[here] += dot(d_pre, w_up_ref[...], NT)
    grad_bias_ref[...] = bias
    grad_down = dot(z_ref[...], dy_ref[...], TN).astype(LOW)
    grad_up = dot(b_ref[...], d_pre_ref[...], TN).astype(LOW)
    grad_down_ref[...] = grad_down
    grad_up_ref[...] = grad_up
    if ahead:
        for chosen, ticks in enumerate(AHEAD_TICKS):
            for tick, when in enumerate(ticks):
                if when < LAST_BLOCK:
                    trade(chosen, tick, when)
        for chosen in range(AHEAD):

            @pl.when(block == chosen)
            def _():
                terms[0][chosen % 2] = grad_down
                terms[1][chosen % 2] = grad_up
                for each in sums[chosen]:
                    each.start()


    @pl.when(block == pl.num_programs(0) - 1)
    def _():
        normed, db = normed_ref[...], db_ref[...]
        grad_gain_ref[...] = jnp.sum(db * normed, axis=0, keepdims=True)
        d_resid = cotangent_ref[...] + norm_back(db * gain_ref[...], normed, inverse_ref[...])
        d_resid_ref[...] = d_resid
        dr_low = d_resid.astype(LOW)
        grad_out_ref[...] = dot(attn_ref[...], dr_low, TN).astype(LOW)
        grad_t = dot(w_out_ref[...], dr_low, NT).astype(LOW)
        grad_t_ref[...] = grad_t
        product = grad_t.astype(WIDE) * attended_ref[...]
        for pair in range(dots_ref.shape[0]):
            for head in range(2):
                lanes = slice(pair * PAIR + head * HEAD, pair * PAIR + (head + 1) * HEAD)
                dots_ref[pair, head : head + 1] = jnp.sum(product[lanes], axis=0, keepdims=True)

    if ahead:
        for chosen, ticks in enumerate(AHEAD_TICKS):
            for tick, when in enumerate(ticks):
                if when == LAST_BLOCK:
                    trade(chosen, tick, when)

        @pl.when(block == pl.num_programs(0) - 1)
        def _():
            for pair in sums:
                for each in pair:
                    each.store().wait()


def mlp_call(ahead, hidden, attn_low, attended, cotangent, w_out, gain_mlp, w_up, b_up, w_down):
    rows, width = hidden.shape
    hidden_units = w_up.shape[1]
    pairs = width // PAIR
    once = lambda *shape: pl.BlockSpec(
        shape, lambda block: (0,) * len(shape), pipeline_mode=pl.Buffered(1)
    )
    square, line = once(rows, width), once(1, width)
    up = pl.BlockSpec((width, FF_BLOCK), lambda block: (0, block))
    down = pl.BlockSpec((FF_BLOCK, width), lambda block: (block, 0))
    bias = pl.BlockSpec((1, FF_BLOCK), lambda block: (0, block))
    wide = jax.ShapeDtypeStruct((rows, width), WIDE)
    anywhere = pl.BlockSpec(memory_space=pl.ANY)
    down_rows = sum(ahead_rows((FF_BLOCK, width), DOWN_AXES)[-1])
    up_rows = sum(ahead_rows((width, FF_BLOCK), UP_AXES)[-1])
    part_shapes = [
        jax.ShapeDtypeStruct((down_rows, width), LOW),
        jax.ShapeDtypeStruct((up_rows, FF_BLOCK), LOW),
    ]
    params = dict(collective_id=3, has_side_effects=True) if ahead else {}
    return pl.pallas_call(
        functools.partial(mlp_kernel, ahead),
        grid=(hidden_units // FF_BLOCK,),
        in_specs=[square] * 4 + [once(width, width), line, up, bias, down],
        out_specs=[
            whole(rows, width),
            whole(rows, width),
            whole(width, rows),
            whole(pairs, 2, rows),
            down,
            up,
            whole(width, width),
            whole(1, width),
            bias,
        ]
        + [anywhere] * (2 if ahead else 0),
        out_shape=[
            wide,
            wide,
            jax.ShapeDtypeStruct((width, rows), LOW),
            jax.ShapeDtypeStruct((pairs, 2, rows), WIDE),
            jax.ShapeDtypeStruct(w_down.shape, LOW),
            jax.ShapeDtypeStruct(w_up.shape, LOW),
            jax.ShapeDtypeStruct((width, width), LOW),
            jax.ShapeDtypeStruct((1, width), WIDE),
            jax.ShapeDtypeStruct((1, hidden_units), WIDE),
        ]
        + (part_shapes if ahead else []),
        scratch_shapes=[
            pltpu.VMEM((rows, width), WIDE),
            pltpu.VMEM((rows, 1), WIDE),
            pltpu.VMEM((rows, width), LOW),
            pltpu.VMEM((rows, width), LOW),
            pltpu.VMEM((rows, width), WIDE),
            pltpu.VMEM((rows, FF_BLOCK), LOW),
            pltpu.VMEM((rows, FF_BLOCK), LOW),
        ]
        + (ahead_scratch(width) if ahead else []),
        name="mlp",
        compiler_params=pltpu.CompilerParams(vmem_limit_bytes=60 * 2**20, **params),
    )(hidden, attn_low, attended, cotangent, w_out, gain_mlp[None], w_up, b_up[None], w_down)


PARTS = (
    ("down", (0, 0), (512, 768), DOWN_AXES, 0, AHEAD_STEPS[0], 0, (24, 24, 24, 1, 2, 4, 5, 6, 8, 9)),
    ("down", (512, 0), (512, 768), DOWN_AXES, 1, AHEAD_STEPS[1], 1, (24, 24, 24, 1, 2, 4, 5, 6, 8, 9)),
    ("down", (1024, 0), (512, 768), DOWN_AXES, 0, AHEAD_STEPS[2], 2, (24, 24, 1, 2, 4, 6, 7, 9, 12, 13)),
    ("down", (1536, 0), (512, 768), DOWN_AXES, 1, AHEAD_STEPS[3], 3, (24, 24, 1, 2, 4, 6, 8, 10, 12, 13)),
    ("up", (0, 0), (768, 512), UP_AXES, 1, AHEAD_STEPS[0], 0, (24, 24, 24, 1, 2, 5, 6, 7, 10, 11)),
    ("up", (0, 512), (768, 512), UP_AXES, 0, AHEAD_STEPS[1], 1, (24, 24, 24, 2, 3, 5, 6, 8, 10, 11)),
    ("up", (0, 1024), (768, 512), UP_AXES, 1, AHEAD_STEPS[2], 2, (24, 24, 2, 3, 5, 6, 8, 11, 12, 14)),
    ("up", (0, 1536), (768, 512), UP_AXES, 0, AHEAD_STEPS[3], 3, (24, 24, 2, 4, 5, 6, 9, 11, 12, 13)),
    ("down", (2048, 0), (1024, 768), "rrrrr", 0, 0, None, (1, 4, 6, 8, 12, 16, 19, 21, 24, 24)),
    ("up", (0, 2048), (768, 1024), "rrrcc", 1, 0, None, (1, 4, 6, 8, 12, 16, 20, 22, 24, 24)),
    ("out", (0, 0), (768, 768), "rrrrc", 0, 0, None, (2, 5, 6, 9, 12, 16, 20, 22, 24, 24)),
    ("qkv", (0, 0), (768, 256), "rrrrc", 0, 0, None, None),
    ("qkv", (0, 256), (768, 256), "rrrrc", 1, 0, None, None),
    ("qkv", (0, 512), (768, 256), "rrrrc", 0, 0, None, None),
    ("qkv", (0, 768), (768, 256), "rrrrc", 1, 0, None, None),
    ("qkv", (0, 1024), (768, 256), "rrrrc", 0, 0, None, None),
    ("qkv", (0, 1280), (768, 256), "rrrrc", 1, 0, None, None),
    ("qkv", (0, 1536), (768, 256), "rrrrc", 0, 0, None, None),
    ("qkv", (0, 1792), (768, 256), "rrrrc", 1, 0, None, None),
    ("qkv", (0, 2048), (768, 256), "rrrrc", 0, 0, None, None),
)


def gradient_kernel(*refs):
    keys, values, shards = refs[:3]
    q_ref, grad_ref, lse_ref, dots_ref, clips, query_clip, w_ref = refs[3:10]
    down_in, up_in, out_in, part_down, part_up, small_in = refs[10:16]
    down_out, up_out, out_out, qkv_out, small_out, input_out = refs[16:22]
    refs = refs[22:]
    kv_slot, a_slot, dq_sum, dk_sum, dv_sum, dk_all, dv_all, grad_k, grad_v, parts = refs[:10]
    from_near, from_across, qkv_term, clip_slot, small_arrived = refs[10:15]
    input_sum = dq_sum
    kv_sems, a_sem, line_sends, line_receives, sends, receives, locals_ = refs[15:22]
    small_sends, small_receives, out_sem, clip_sem = refs[22:26]
    refs = refs[26:]
    rows, width = q_ref.shape
    pairs = width // PAIR
    pieces = 4 * pairs
    group, place = lax.axis_index("dp"), lax.axis_index("blk")
    near = (group, place + 1 - 2 * (place % 2))
    across = (group, 3 - place)
    at_end = place % 3 == 0

    arrays = {
        "down": (down_in, down_out),
        "up": (up_in, up_out),
        "out": (out_in, out_out),
        "qkv": (qkv_term, qkv_out),
    }
    sums = []
    for index, (name, corner, shape, axes, turn, begin, block, _) in enumerate(PARTS):
        steps = STEPS - begin
        total, arrived, refs = refs[0], refs[1 : steps + 1], refs[steps + 1 :]
        term, result = arrays[name]
        if block is not None:
            term = {"down": part_down, "up": part_up}[name]
            term = term.at[pl.ds(*ahead_rows(shape, axes)[block])]
        sums.append(
            Sum(
                turn,
                axes,
                corner,
                shape,
                term,
                result,
                total,
                arrived,
                (sends.at[index], receives.at[index]),
                locals_.at[index],
                begin=begin,
            )
        )
    early = [(each, part[-1]) for each, part in zip(sums, PARTS) if part[-1] is not None]
    late = [each for each, part in zip(sums, PARTS) if part[-1] is None]

    chunk_rows = rows // pairs

    def chunk_of(chunk):
        return pl.ds(pl.multiple_of(chunk * chunk_rows, chunk_rows), chunk_rows)

    def line_copy(channel, chunk, source, target, device):
        return pltpu.make_async_remote_copy(
            src_ref=parts.at[source, chunk_of(chunk)],
            dst_ref=target.at[chunk_of(chunk)],
            send_sem=line_sends.at[channel, chunk],
            recv_sem=line_receives.at[channel, chunk],
            device_id=device,
            device_id_type=MESH,
        )

    def inward(source, chunk):
        return line_copy(source, chunk, source, from_near.at[source], near)

    def middle(source, chunk):
        return line_copy(3 + source, chunk, source, from_across.at[source], across)

    def outward(chunk):
        return line_copy(5, chunk, 2, from_near.at[0], near)

    def add_chunk(total, term, chunk):
        here = chunk_of(chunk)
        total[here] = (total[here].astype(WIDE) + term[here].astype(WIDE)).astype(total.dtype)

    def pair_columns(pair):
        return pl.ds(pl.multiple_of(pair * PAIR, PAIR), PAIR)

    def kv_copies(shard, pair, slot):
        return [
            pltpu.make_async_copy(
                source.at[shard, :, pair_columns(pair)], kv_slot.at[slot, side], kv_sems.at[slot, side]
            )
            for side, source in enumerate((keys, values))
        ]

    def a_copy(shard):
        return pltpu.make_async_copy(shards.at[shard], a_slot, a_sem)

    def clip_copy(turn):
        source = clips.at[pl.ds(pl.multiple_of((3 - turn) * rows, 8), rows)]
        return pltpu.make_async_copy(source, clip_slot, clip_sem)

    def of_pairs(stack):
        return jnp.concatenate([stack[pair] for pair in range(pairs)], axis=1)

    for copy in kv_copies(3, 0, 0):
        copy.start()
    greet([device for _, device in place_bits(0)] + [across])
    for each, _ in early:
        each.start()
    dq_sum[...] = jnp.zeros_like(dq_sum)
    grad_k[...] = jnp.zeros_like(grad_k)
    grad_v[...] = jnp.zeros_like(grad_v)
    small_out[...] = small_in[...]

    def weight_terms(d_query):
        a_copy(0).wait()
        d_key, d_value = of_pairs(dk_all), of_pairs(dv_all)
        part = dot(d_key, w_ref[:, width : 2 * width], NT) + dot(d_value, w_ref[:, 2 * width :], NT)
        if d_query is not None:
            part = part + dot(d_query, w_ref[:, :width], NT)
        small_out[:1] += jnp.sum(part * a_slot[...].astype(WIDE), axis=0, keepdims=True)
        grad_k[...] += dot(a_slot[...], d_key, TN)
        grad_v[...] += dot(a_slot[...], d_value, TN)
        return part

    @pl.loop(0, pieces)
    def _(piece):
        turn, pair, slot = piece // pairs, piece % pairs, piece % 2

        def at(when, *actions):
            @pl.when(piece == when)
            def _():
                for action in actions:
                    action()

        following = piece + 1

        @pl.when(following < pieces)
        def _():
            for copy in kv_copies(3 - following // pairs, following % pairs, following % 2):
                copy.start()

        @pl.when(pair == 1)
        def _():
            a_copy(3 - turn).start()

        for when in range(pieces):
            ends = [
                functools.partial(each.turn, tick)
                for tick in range(2 * STEPS)
                for each, ticks in early
                if ticks[tick] == when and tick >= each.begin
            ]
            if ends:
                at(when, *ends)
        at_middle = jnp.logical_not(at_end)

        @pl.when(jnp.logical_and(turn > 0, at_end))
        def _():
            inward(turn - 1, pair).start()

        @pl.when(jnp.logical_and(at_middle, jnp.logical_and(piece >= FORWARD, piece < FORWARD + 2 * pairs)))
        def _():
            source, chunk = (piece - FORWARD) // pairs, (piece - FORWARD) % pairs
            inward(source, chunk).wait_recv()
            add_chunk(parts.at[source], from_near.at[source], chunk)
            middle(source, chunk).start()

        @pl.when(jnp.logical_and(at_middle, turn == 3))
        def _():
            middle(0, pair).wait_recv()
            add_chunk(parts.at[2], from_across.at[0], pair)
            outward(pair).start()

        @pl.when(pair == 0)
        def _():
            clip_copy(turn).start()
            clip_copy(turn).wait()

        for copy in kv_copies(0, pair, slot):
            copy.wait()
        columns = pair_columns(pair)

        def add(head, start, stop, dq, dk, dv):
            lanes = slice(head * HEAD, (head + 1) * HEAD)
            if start == 0:
                dv_sum[lanes], dk_sum[lanes] = dv, dk
            else:
                dv_sum[lanes] += dv
                dk_sum[lanes] += dk
            at_lanes = pl.ds(pl.multiple_of(pair * PAIR + head * HEAD, HEAD), HEAD)
            dq_sum[at_lanes, start:stop] += dq

        backward_pair(
            kv_slot[slot, 0],
            kv_slot[slot, 1],
            q_ref[:, columns],
            grad_ref[columns, :],
            lse_ref.at[pair],
            dots_ref.at[pair],
            clip_slot[...],
            query_clip[...],
            add,
        )
        dk_all[pair] = (dk_sum[...] * SCALE).T.astype(LOW)
        dv_all[pair] = dv_sum[...].T.astype(LOW)

        @pl.when(jnp.logical_and(pair == pairs - 1, turn < 3))
        def _():
            parts[turn] = weight_terms(None).astype(LOW)

    d_query = (dq_sum[...] * SCALE).T.astype(LOW)
    input_sum[...] = weight_terms(d_query)
    qkv_term[:, :width] = dot(a_slot[...], d_query, TN).astype(LOW)
    qkv_term[:, width : 2 * width] = grad_k[...].astype(LOW)
    qkv_term[:, 2 * width :] = grad_v[...].astype(LOW)

    small_steps = place_bits(0)

    def small(step):
        return remote(
            small_out, small_arrived.at[step], (small_sends, small_receives), step, small_steps[step][1]
        )

    for each in late:
        each.start()
    open_sums = [
        (each, [tick for tick in range(each.begin, 2 * STEPS) if ticks[tick] == pieces])
        for each, ticks in early
    ]
    open_sums += [(each, list(range(2 * STEPS))) for each in late]

    @pl.when(at_end)
    def _():
        @pl.loop(0, pairs)
        def _(chunk):
            for source in range(3):
                inward(source, chunk).wait_send()
            outward(chunk).wait_recv()
            add_chunk(input_sum, from_near.at[0], chunk)

    @pl.when(jnp.logical_not(at_end))
    def _():
        @pl.loop(0, pairs)
        def _(chunk):
            outward(chunk).wait_send()
            for source in range(2):
                middle(source, chunk).wait_send()
            middle(1, chunk).wait_recv()
            add_chunk(input_sum, from_across.at[1], chunk)
            inward(2, chunk).wait_recv()
            add_chunk(input_sum, from_near.at[2], chunk)

    store = pltpu.make_async_copy(input_sum, input_out, out_sem)
    store.start()
    for tick in range(2 * STEPS):
        if tick < STEPS:
            small(tick).start()
        for each, ticks in open_sums:
            if ticks:
                each.turn(ticks.pop(0))
        if tick < STEPS:
            small(tick).wait()
            small_out[...] += small_arrived[tick]
    store.wait()


def gradient_call(
    keys, values, shards, query, grad_t, lse, row_dots, clips, query_clip, w_qkv, grad_down, grad_up, grad_out, part_down, part_up, small
):
    rows, width = query.shape
    pairs = width // PAIR
    anywhere = pl.BlockSpec(memory_space=pl.ANY)
    inside = pl.BlockSpec(memory_space=pltpu.VMEM)
    square = (rows, width)
    scratch = [
        pltpu.VMEM((2, 2, rows, PAIR), LOW),
        pltpu.VMEM(square, LOW),
        pltpu.VMEM((width, rows), WIDE),
        pltpu.VMEM((PAIR, rows), WIDE),
        pltpu.VMEM((PAIR, rows), WIDE),
        pltpu.VMEM((pairs, rows, PAIR), LOW),
        pltpu.VMEM((pairs, rows, PAIR), LOW),
        pltpu.VMEM((width, width), WIDE),
        pltpu.VMEM((width, width), WIDE),
        pltpu.VMEM((3, *square), LOW),
    ]
    scratch += [pltpu.VMEM((3, *square), LOW), pltpu.VMEM((2, *square), LOW)]
    scratch += [
        pltpu.VMEM((width, 3 * width), LOW),
        pltpu.VMEM((rows, 1), clips.dtype),
        pltpu.VMEM((STEPS, *small.shape), WIDE),
        pltpu.SemaphoreType.DMA((2, 2)),
        pltpu.SemaphoreType.DMA,
        pltpu.SemaphoreType.DMA((6, pairs)),
        pltpu.SemaphoreType.DMA((6, pairs)),
        pltpu.SemaphoreType.DMA((len(PARTS), 2 * STEPS)),
        pltpu.SemaphoreType.DMA((len(PARTS), 2 * STEPS)),
        pltpu.SemaphoreType.DMA((len(PARTS), 2)),
        pltpu.SemaphoreType.DMA((STEPS,)),
        pltpu.SemaphoreType.DMA((STEPS,)),
        pltpu.SemaphoreType.DMA,
        pltpu.SemaphoreType.DMA,
    ]
    for _, _, shape, axes, _, begin, _, _ in PARTS:
        shapes = halves(shape, axes)
        scratch += [pltpu.VMEM(each, LOW) for each in (shapes[max(begin - 1, 0)], *shapes[begin:])]
    like = lambda array: jax.ShapeDtypeStruct(array.shape, array.dtype)
    return pl.pallas_call(
        gradient_kernel,
        in_specs=[anywhere] * 3 + [inside] * 4 + [anywhere] + [inside] * 2 + [anywhere] * 5 + [inside],
        out_specs=[anywhere] * 4 + [inside, anywhere],
        out_shape=[
            like(grad_down),
            like(grad_up),
            like(grad_out),
            jax.ShapeDtypeStruct((width, 3 * width), LOW),
            like(small),
            jax.ShapeDtypeStruct(square, WIDE),
        ],
        scratch_shapes=scratch,
        name="gradients",
        compiler_params=pltpu.CompilerParams(
            collective_id=1, has_side_effects=True, vmem_limit_bytes=62 * 2**20
        ),
    )(
        keys, values, shards, query, grad_t, lse, row_dots, clips, query_clip, w_qkv,
        grad_down, grad_up, grad_out, part_down, part_up, small,
    )


def on_device(
    groups, inputs, positions, segments, gain_attn, w_qkv, w_out, gain_mlp, w_up, b_up, w_down, cotangent
):
    rows, width = inputs.shape
    pairs = width // PAIR
    place = lax.axis_index("blk")
    w_query = w_qkv[:, :width]

    def send(value, pairs_of_places):
        return lax.ppermute(value, "blk", pairs_of_places)

    hidden = inputs + position_table(positions, width)
    normed_attn, inverse_attn = normalize(hidden)
    a_low = (normed_attn * gain_attn).astype(LOW)

    table = jnp.array([[0, 1, 2, 3], [1, 0, 2, 3], [2, 3, 1, 0], [3, 2, 1, 0]], jnp.int32)
    order = lax.dynamic_index_in_dim(table, place, keepdims=False)
    clips = jnp.concatenate(
        [lax.dynamic_slice_in_dim(segments, order[index] * rows, rows) for index in range(4)]
    )[:, None]
    query_clip = lax.dynamic_slice_in_dim(segments, place * rows, rows)[None, :]
    shards, keys, values, query, attended, lse, attn_low = attention_call(
        a_low, w_qkv, clips, query_clip
    )

    quick = groups == 8 and rows == width
    (
        outputs,
        d_resid,
        d_attn_t,
        row_dots,
        grad_down,
        grad_up,
        grad_out,
        grad_gain_mlp,
        grad_bias_up,
        *parts,
    ) = mlp_call(quick, hidden, attn_low, attended, cotangent, w_out, gain_mlp, w_up, b_up, w_down)
    grad_gain_mlp, grad_bias_up = grad_gain_mlp[0], grad_bias_up[0]

    if quick:
        small = jnp.concatenate([jnp.zeros_like(gain_attn), grad_gain_mlp, grad_bias_up])
        sum_down, sum_up, sum_out, sum_qkv, sum_small, d_normed_attn = gradient_call(
            keys,
            values,
            shards,
            query,
            d_attn_t,
            lse,
            row_dots,
            clips,
            query_clip,
            w_qkv,
            grad_down,
            grad_up,
            grad_out,
            *parts,
            jnp.pad(small.reshape(6, width), ((0, 2), (0, 0))),
        )
        input_grad = d_resid + norm_back(d_normed_attn * gain_attn, normed_attn, inverse_attn)
        return (
            outputs,
            input_grad,
            sum_small[0] / gain_attn,
            sum_qkv.astype(WIDE),
            sum_out.astype(WIDE),
            sum_small[1],
            sum_up.astype(WIDE),
            sum_small[2:6].reshape(-1),
            sum_down.astype(WIDE),
        )

    everywhere = ("dp", "blk")

    def back(index, dq):
        return backward_call(
            index == 3,
            index == 0,
            keys[index],
            values[index],
            query,
            d_attn_t,
            lse,
            row_dots,
            clips[index * rows : (index + 1) * rows],
            query_clip,
            w_qkv,
            dq,
        )

    middle, outward, inward = [(1, 2), (2, 1)], [(1, 0), (2, 3)], [(0, 1), (3, 2)]
    dk_3, dv_3, dq, part_3 = back(3, None)
    far = send(part_3, inward)
    dk_2, dv_2, dq, part_2 = back(2, dq)
    far, part_2, dq = lax.optimization_barrier((far, part_2, dq))
    onward = (part_3.astype(WIDE) + far.astype(WIDE)).astype(LOW)
    mid_3 = send(onward, middle)
    mid_2 = send(part_2, inward)
    dq, onward = lax.optimization_barrier((dq, onward))
    dk_1, dv_1, dq, part_1 = back(1, dq)
    mid_3, mid_2, part_1, dq = lax.optimization_barrier((mid_3, mid_2, part_1, dq))
    onward_1 = (part_2.astype(WIDE) + mid_2.astype(WIDE)).astype(LOW)
    onward_2 = (part_1.astype(WIDE) + mid_3.astype(WIDE)).astype(LOW)
    last_1 = send(onward_1, middle)
    last_2 = send(onward_2, outward)
    last_3 = send(part_1, inward)
    dq, onward_1, onward_2 = lax.optimization_barrier((dq, onward_1, onward_2))
    dk_0, dv_0, dq, part_0 = back(0, dq)
    grad_query = dot(a_low, dq, TN).astype(LOW)
    d_keys, d_values = (dk_0, dk_1, dk_2, dk_3), (dv_0, dv_1, dv_2, dv_3)
    grad_key = sum(dot(shard, term, TN) for shard, term in zip(shards, d_keys)).astype(LOW)
    grad_value = sum(dot(shard, term, TN) for shard, term in zip(shards, d_values)).astype(LOW)
    d_normed_attn = (
        part_0
        + dot(dq, w_query, NT)
        + last_1.astype(WIDE)
        + last_2.astype(WIDE)
        + last_3.astype(WIDE)
    )
    grad_gain_attn = jnp.sum(d_normed_attn * normed_attn, axis=0)
    input_grad = d_resid + norm_back(d_normed_attn * gain_attn, normed_attn, inverse_attn)
    small = jnp.concatenate([grad_gain_attn, grad_gain_mlp, grad_bias_up])
    sums = lax.psum((grad_down, grad_up, grad_out, grad_query, grad_key, grad_value), everywhere)
    sum_small = lax.psum(small, everywhere)
    sum_down, sum_up, sum_out, *sum_qkv = sums
    return (
        outputs,
        input_grad,
        sum_small[:width],
        jnp.concatenate(sum_qkv, axis=1).astype(WIDE),
        sum_out.astype(WIDE),
        sum_small[width : 2 * width],
        sum_up.astype(WIDE),
        sum_small[2 * width :],
        sum_down.astype(WIDE),
    )


def solution(mesh):
    rows = P(("dp", "blk"), None)
    placed = (rows, P(("dp", "blk")), P("dp"), P(), P(), P(), P(), P(), P(), P(), rows)
    return jax.shard_map(
        functools.partial(on_device, mesh.shape["dp"]),
        mesh=mesh,
        in_specs=placed,
        out_specs=(rows, rows, P(), P(), P(), P(), P(), P(), P()),
        check_vma=False,
    )
```

```python
import functools
import math

import jax
import jax.numpy as jnp
from jax import lax
from jax.experimental import pallas as pl
from jax.experimental.pallas import tpu as pltpu
from jax.sharding import PartitionSpec as P

HEADS = 12
HEAD = 64
PAIR = 2 * HEAD
SCALE = HEAD**-0.5
LOG2E = 1.4426950408889634
MASKED = -1.0e9
QUERY_BLOCK = 384
EPS_NORM = 1e-06
LOW = jnp.bfloat16
WIDE = jnp.float32

NN = (((1,), (0,)), ((), ()))
NT = (((1,), (1,)), ((), ()))
TN = (((0,), (0,)), ((), ()))


def dot(left, right, dims):
    return lax.dot_general(left, right, dims, preferred_element_type=WIDE)


def position_table(positions, model_width):
    half_width = model_width // 2
    freqs = jnp.exp(jnp.arange(half_width, dtype=WIDE) * (-math.log(10000.0) / half_width))
    angles = positions.astype(WIDE)[:, None] * freqs[None, :]
    return jnp.concatenate([jnp.sin(angles), jnp.cos(angles)], axis=1)


def normalize(values):
    center = values - jnp.mean(values, axis=-1, keepdims=True)
    inverse = lax.rsqrt(jnp.mean(center * center, axis=-1, keepdims=True) + EPS_NORM)
    return center * inverse, inverse


def norm_back(grad_norm, normed, inverse):
    first = jnp.mean(grad_norm, axis=-1, keepdims=True)
    second = jnp.mean(grad_norm * normed, axis=-1, keepdims=True)
    return inverse * (grad_norm - first - normed * second)


def in_head(values, head):
    lanes = lax.broadcasted_iota(jnp.int32, values.shape, 1)
    return (lanes < HEAD) == (head == 0)


def only_head(values, head, other=None):
    other = jnp.zeros_like(values) if other is None else other
    return jnp.where(in_head(values, head), values, other)


def split_scaled(query):
    scaled = query.astype(WIDE) * (SCALE * LOG2E)
    high = scaled.astype(LOW)
    return high, (scaled - high.astype(WIDE)).astype(LOW)


def score_sides(key, query):
    high, low = split_scaled(query)
    key_side = jnp.concatenate([key, key], axis=1)
    query_side = [
        jnp.concatenate([only_head(high, head), only_head(low, head)], axis=1) for head in range(2)
    ]
    return key_side, query_side


def work_items(rows):
    return [(start, head) for start in range(0, rows, QUERY_BLOCK) for head in range(2)]


def whole(*shape):
    return pl.BlockSpec(shape, lambda pair: (0,) * len(shape))


def columns_of(rows, first=0):
    return pl.BlockSpec((rows, PAIR), lambda pair: (0, pair + first))


def backward_pair(key, value, query, grad_t, lse, row_dots, key_clip, query_clip, add):
    rows = query.shape[0]
    grad = grad_t.T
    key_t, query_t = key.T, query.T
    key_side, query_side = score_sides(key, query)
    grad_side = [only_head(grad, head) for head in range(2)]
    for start, head in work_items(rows):
        stop = start + QUERY_BLOCK
        lanes, row = slice(head * HEAD, (head + 1) * HEAD), slice(head, head + 1)
        score = dot(key_side, query_side[head][start:stop], NT)
        score = jnp.where(key_clip == query_clip[:, start:stop], score, MASKED)
        probs = jnp.exp2(score - lse[row, start:stop])
        d_probs = dot(value, grad_side[head][start:stop], NT)
        d_scores = (probs * (d_probs - row_dots[row, start:stop])).astype(LOW)
        probs = probs.astype(LOW)
        dv = dot(grad_t[lanes, start:stop], probs, NT)
        dk = dot(query_t[lanes, start:stop], d_scores, NT)
        dq = dot(key_t[lanes], d_scores, NN)
        add(head, start, stop, dq, dk, dv)


def backward_kernel(first, last, *refs):
    k_ref, v_ref, q_ref, grad_ref, lse_ref, dots_ref, key_clip, query_clip, wk_ref, wv_ref = refs[:10]
    refs = refs[10:]
    if not first:
        dq_in = refs[0]
        refs = refs[1:]
    dk_ref, dv_ref, dq_ref, part_ref, dk_sum, dv_sum, dq_sum, dk_all, dv_all = refs
    pair = pl.program_id(0)
    rows = q_ref.shape[0]

    def add(head, start, stop, dq, dk, dv):
        lanes = slice(head * HEAD, (head + 1) * HEAD)
        if start == 0:
            dv_sum[lanes], dk_sum[lanes] = dv, dk
        else:
            dv_sum[lanes] += dv
            dk_sum[lanes] += dk
        if not first:
            dq = dq + dq_in[lanes, start:stop]
        if last:
            dq_sum[lanes, start:stop] = dq
        else:
            dq_ref[lanes, start:stop] = dq

    backward_pair(
        k_ref[...],
        v_ref[...],
        q_ref[...],
        grad_ref[...],
        lse_ref,
        dots_ref,
        key_clip[...],
        query_clip[...],
        add,
    )
    if last:
        dq_ref[...] = (dq_sum[...] * SCALE).T.astype(LOW)
    dk = (dk_sum[...] * SCALE).T.astype(LOW)
    dv = dv_sum[...].T.astype(LOW)
    dk_ref[...] = dk
    dv_ref[...] = dv
    dk_all[pair] = dk
    dv_all[pair] = dv

    @pl.when(pair == pl.num_programs(0) - 1)
    def _():
        pairs = dk_all.shape[0]
        dk_rows = jnp.concatenate([dk_all[index] for index in range(pairs)], axis=1)
        dv_rows = jnp.concatenate([dv_all[index] for index in range(pairs)], axis=1)
        part = dot(dk_rows, wk_ref[...], NT) + dot(dv_rows, wv_ref[...], NT)
        part_ref[...] = part.astype(part_ref.dtype)


def backward_call(first, last, key, value, query, grad_t, lse, row_dots, key_clip, query_clip, w_qkv, dq):
    rows, width = query.shape
    pairs = width // PAIR
    across = pl.BlockSpec((PAIR, rows), lambda pair: (pair, 0))
    line = pl.BlockSpec((None, 2, rows), lambda pair: (pair, 0, 0))
    columns = columns_of(rows)
    in_specs = [columns, columns, columns, across, line, line, whole(rows, 1), whole(1, rows)]
    in_specs += [
        pl.BlockSpec((width, width), lambda pair: (0, 1)),
        pl.BlockSpec((width, width), lambda pair: (0, 2)),
    ]
    operands = [key, value, query, grad_t, lse, row_dots, key_clip, query_clip, w_qkv, w_qkv]
    if not first:
        in_specs.append(across)
        operands.append(dq)
    low_rows = jax.ShapeDtypeStruct((rows, width), LOW)
    tall = pltpu.VMEM((PAIR, rows), WIDE)
    parts = pltpu.VMEM((pairs, rows, PAIR), LOW)
    return pl.pallas_call(
        functools.partial(backward_kernel, first, last),
        grid=(pairs,),
        in_specs=in_specs,
        out_specs=[columns, columns, columns if last else across, whole(rows, width)],
        out_shape=[
            low_rows,
            low_rows,
            low_rows if last else jax.ShapeDtypeStruct((width, rows), WIDE),
            jax.ShapeDtypeStruct((rows, width), WIDE if last else LOW),
        ],
        scratch_shapes=[tall, tall, tall, parts, parts],
        name="attend_back",
        cost_estimate=pl.CostEstimate(
            flops=40 * rows * rows * width, bytes_accessed=24 * rows * width, transcendentals=0
        ),
        compiler_params=pltpu.CompilerParams(vmem_limit_bytes=48 * 2**20),
    )(*operands)


MESH = pl.DeviceIdType.MESH
TURNS = ((0, 1, 2), (0, 2, 1))
STEPS = 5
FORWARD = 8


def place_bits(turn):
    group, place = lax.axis_index("dp"), lax.axis_index("blk")
    steps = []
    for bit in TURNS[turn]:
        mine = group // (1 << bit) % 2
        steps.append((mine, (group + (1 - 2 * mine) * (1 << bit), place)))
    for bit in range(2):
        mine = place // (1 << bit) % 2
        steps.append((mine, (group, place + (1 - 2 * mine) * (1 << bit))))
    return steps


def remote(source, target, sems, index, device):
    return pltpu.make_async_remote_copy(
        src_ref=source,
        dst_ref=target,
        send_sem=sems[0].at[index],
        recv_sem=sems[1].at[index],
        device_id=device,
        device_id_type=MESH,
    )


def part_of(row, rows, column, columns):
    row = row if isinstance(row, int) else pl.multiple_of(row, 16)
    column = column if isinstance(column, int) else pl.multiple_of(column, PAIR)
    return pl.ds(row, rows), pl.ds(column, columns)


def add_block(total, term, row=0, column=0):
    rows, columns = term.shape
    block = next(size for size in (48, 32, 16) if rows % size == 0)

    @pl.loop(0, rows // block)
    def _(index):
        here = part_of(row + index * block, block, column, columns)
        there = part_of(index * block, block, 0, columns)
        total[here] = (total[here].astype(WIDE) + term[there].astype(WIDE)).astype(total.dtype)


def halves(shape, axes):
    shapes = []
    for axis in axes:
        shape = (shape[0] // 2, shape[1]) if axis == "r" else (shape[0], shape[1] // 2)
        shapes.append(shape)
    return shapes


class Sum:
    def __init__(
        self, turn, axes, corner, shape, term, result, total, arrived, sems, local_sems, begin=0, stop=STEPS
    ):
        self.term, self.result, self.total, self.arrived = term, result, total, arrived
        self.sems, self.local_sems, self.begin, self.stop = sems, local_sems, begin, stop
        self.steps = place_bits(turn)
        self.shapes = halves(shape, axes)
        self.kept, self.left = [], []
        row, column = corner
        for axis, (rows, columns), (mine, _) in zip(axes, self.shapes, self.steps):
            down, across = (rows, 0) if axis == "r" else (0, columns)
            self.left.append((row + (1 - mine) * down, rows, column + (1 - mine) * across, columns))
            row, column = row + mine * down, column + mine * across
            self.kept.append((row, rows, column, columns))
        self.held = self.kept[max(begin - 1, 0)]

    def inside(self, place):
        row, rows, column, columns = place
        return part_of(row - self.held[0], rows, column - self.held[2], columns)

    def load(self):
        source = self.term if self.begin else self.term.at[part_of(*self.kept[0])]
        return pltpu.make_async_copy(source, self.total, self.local_sems.at[0])

    def store(self):
        place = self.kept[self.stop - 1]
        target = self.result.at[part_of(*place)] if self.stop == STEPS else self.result
        return pltpu.make_async_copy(
            self.total.at[self.inside(place)], target, self.local_sems.at[1]
        )

    def gather(self, step):
        place = self.left[step]
        source = self.term.at[part_of(*place)] if step == 0 else self.total.at[self.inside(place)]
        return remote(source, self.arrived[step - self.begin], self.sems, step, self.steps[step][1])

    def spread(self, step):
        here = self.result.at[part_of(*self.kept[step])]
        source = self.total.at[self.inside(self.kept[step])] if step == STEPS - 1 else here
        return remote(source, here, self.sems, STEPS + step, self.steps[step][1])

    def start(self):
        self.load().start()
        if self.begin:
            self.load().wait()
        self.gather(self.begin).start()

    def turn(self, tick):
        if tick < STEPS:
            if tick == 0:
                self.load().wait()
            self.gather(tick).wait()
            row, _, column, _ = self.kept[tick]
            add_block(
                self.total, self.arrived[tick - self.begin], row - self.held[0], column - self.held[2]
            )
            if tick + 1 < self.stop:
                self.gather(tick + 1).start()
            else:
                self.store().start()
                if self.stop == STEPS:
                    self.spread(STEPS - 1).start()
        else:
            step = 2 * STEPS - 1 - tick
            if step == STEPS - 1:
                self.store().wait()
            self.spread(step).wait()
            if step:
                self.spread(step - 1).start()


def greet(devices):
    barrier = pltpu.get_barrier_semaphore()
    for device in devices:
        pl.semaphore_signal(barrier, inc=1, device_id=device, device_id_type=MESH)
    pl.semaphore_wait(barrier, len(devices))


PASS_NEAR = (2, 4, 5, 6, 6, 6)
PASS_FAR = (10, 11, 12, 13, 15, 16)


def attention_kernel(*refs):
    a_in, w_ref, clips, query_clip = refs[:4]
    a_out, k_out, v_out, q_ref, acc_ref, lse_ref, attn_ref = refs[4:11]
    a_all, top_all, total_all, kv_slot, clip_slot = refs[11:16]
    a_sems, kv_sems, clip_sem, line_sends, line_receives = refs[16:]
    rows, width = q_ref.shape
    pairs = width // PAIR
    pieces = 4 * pairs
    chunk_rows = rows // pairs
    group, place = lax.axis_index("dp"), lax.axis_index("blk")
    near = (group, place + 1 - 2 * (place % 2))
    across = (group, 3 - place)
    at_end = place % 3 == 0
    at_middle = jnp.logical_not(at_end)

    def line_copy(channel, chunk, source, target, device):
        here = pl.ds(pl.multiple_of(chunk * chunk_rows, chunk_rows), chunk_rows)
        return pltpu.make_async_remote_copy(
            src_ref=source.at[here],
            dst_ref=a_all.at[target, here],
            send_sem=line_sends.at[channel, chunk],
            recv_sem=line_receives.at[channel, chunk],
            device_id=device,
            device_id_type=MESH,
        )

    channels = (
        lambda chunk: line_copy(0, chunk, a_in, 1, near),
        lambda chunk: line_copy(1, chunk, a_in, 2, across),
        lambda chunk: line_copy(2, chunk, a_all.at[2], 2, near),
        lambda chunk: line_copy(3, chunk, a_all.at[1], 3, across),
        lambda chunk: line_copy(4, chunk, a_all.at[3], 3, near),
    )
    load = pltpu.make_async_copy(a_in, a_all.at[0], a_sems.at[4])
    load.start()
    greet((near, across))
    for chunk in range(pairs):
        channels[0](chunk).start()

    @pl.when(at_middle)
    def _():
        for chunk in range(pairs):
            channels[1](chunk).start()

    top_all[...] = jnp.full_like(top_all, -1.0e30)
    total_all[...] = jnp.zeros_like(total_all)
    acc_ref[...] = jnp.zeros_like(acc_ref)

    def keep(shard):
        return pltpu.make_async_copy(a_all.at[shard], a_out.at[shard], a_sems.at[shard])

    def clip_copy(turn):
        source = clips.at[pl.ds(pl.multiple_of(turn * rows, 8), rows)]
        return pltpu.make_async_copy(source, clip_slot, clip_sem)

    def pair_columns(pair):
        return pl.ds(pl.multiple_of(pair * PAIR, PAIR), PAIR)

    def kv_copies(turn, pair, slot):
        return [
            pltpu.make_async_copy(
                kv_slot.at[slot, side], target.at[turn, :, pair_columns(pair)], kv_sems.at[slot, side]
            )
            for side, target in enumerate((k_out, v_out))
        ]

    load.wait()
    keep(0).start()

    @pl.loop(0, pieces)
    def _(piece):
        turn, pair, slot = piece // pairs, piece % pairs, piece % 2
        for chunk, when in enumerate(PASS_NEAR):

            @pl.when(jnp.logical_and(piece == when, at_middle))
            def _():
                channels[0](chunk).wait_recv()
                channels[3](chunk).start()
                channels[1](chunk).wait_recv()
                channels[2](chunk).start()

        for chunk, when in enumerate(PASS_FAR):

            @pl.when(jnp.logical_and(piece == when, at_middle))
            def _():
                channels[3](chunk).wait_recv()
                channels[4](chunk).start()

        for shard, channel in ((1, 0), (2, 2), (3, 4)):

            @pl.when(jnp.logical_and(piece == shard * pairs, at_end))
            def _():
                for chunk in range(pairs):
                    channels[channel](chunk).wait_recv()

            @pl.when(piece == shard * pairs)
            def _():
                keep(shard).start()

        @pl.when(pair == 0)
        def _():
            clip_copy(turn).start()
            clip_copy(turn).wait()

        @pl.when(piece >= 2)
        def _():
            for copy in kv_copies(turn, pair, slot):
                copy.wait()

        columns = pair_columns(pair)

        @pl.when(turn == 0)
        def _():
            q_ref[:, columns] = dot(a_all[0], w_ref[:, columns], NN).astype(LOW)

        w_pair = jnp.concatenate(
            [w_ref[:, pair_columns(pair + pairs)], w_ref[:, pair_columns(pair + 2 * pairs)]], axis=1
        )
        kv = dot(a_all[turn], w_pair, NN).astype(LOW)
        key, value = kv[:, :PAIR], kv[:, PAIR:]
        kv_slot[slot, 0] = key
        kv_slot[slot, 1] = value
        for copy in kv_copies(turn, pair, slot):
            copy.start()
        value_t = value.T
        ones = jnp.ones((16, rows), LOW)
        value_rows = [
            jnp.concatenate([value_t[head * HEAD : (head + 1) * HEAD], ones], axis=0)
            for head in range(2)
        ]
        key_side, query_side = score_sides(key, q_ref[:, columns])
        key_clip = clip_slot[...]

        def scores(start, head):
            stop = start + QUERY_BLOCK
            result = dot(key_side, query_side[head][start:stop], NT)
            return jnp.where(key_clip == query_clip[:, start:stop], result, MASKED)

        def weights(start, head, result):
            here = slice(start, start + QUERY_BLOCK)
            before = top_all[pair, head : head + 1, here]
            top = jnp.maximum(before, jnp.max(result, axis=0, keepdims=True))
            top_all[pair, head : head + 1, here] = top
            return jnp.exp2(result - top).astype(LOW), jnp.exp2(before - top)

        def attend(start, head, expd, shrink):
            here, row = slice(start, start + QUERY_BLOCK), slice(head, head + 1)
            lanes = pl.ds(pl.multiple_of(pair * PAIR + head * HEAD, HEAD), HEAD)
            result = dot(value_rows[head], expd, NN)
            acc_ref[lanes, here] = acc_ref[lanes, here] * shrink + result[:HEAD]
            total_all[pair, row, here] = total_all[pair, row, here] * shrink + result[HEAD : HEAD + 1]

        items = work_items(rows)
        result = scores(*items[0])
        before = None
        for index, item in enumerate(items):
            following = scores(*items[index + 1]) if index + 1 < len(items) else None
            done = weights(*item, result)
            if before is not None:
                attend(*before)
            before = (*item, *done)
            result = following
        attend(*before)

        @pl.when(turn == 3)
        def _():
            for head in range(2):
                lanes = pl.ds(pl.multiple_of(pair * PAIR + head * HEAD, HEAD), HEAD)
                total = total_all[pair, head : head + 1]
                acc_ref[lanes] = acc_ref[lanes] * (1.0 / total)
                lse_ref[pair, head : head + 1] = top_all[pair, head : head + 1] + jnp.log(total) * LOG2E
            attn_ref[:, columns] = acc_ref[columns].T.astype(LOW)

    for slot in range(2):
        for copy in kv_copies(3, pairs - 2 + slot, slot):
            copy.wait()
    for shard in range(4):
        keep(shard).wait()
    for chunk in range(pairs):
        channels[0](chunk).wait_send()

    @pl.when(at_middle)
    def _():
        for channel in channels[1:]:
            for chunk in range(pairs):
                channel(chunk).wait_send()


def attention_call(a_low, w_qkv, clips, query_clip):
    rows, width = a_low.shape
    pairs = width // PAIR
    anywhere = pl.BlockSpec(memory_space=pl.ANY)
    inside = pl.BlockSpec(memory_space=pltpu.VMEM)
    four = jax.ShapeDtypeStruct((4, rows, width), LOW)
    square = jax.ShapeDtypeStruct((rows, width), LOW)
    lines = jax.ShapeDtypeStruct((pairs, 2, rows), WIDE)
    return pl.pallas_call(
        attention_kernel,
        in_specs=[anywhere, inside, anywhere, inside],
        out_specs=[anywhere] * 3 + [inside] * 4,
        out_shape=[four, four, four, square, jax.ShapeDtypeStruct((width, rows), WIDE), lines, square],
        scratch_shapes=[
            pltpu.VMEM((4, rows, width), LOW),
            pltpu.VMEM((pairs, 2, rows), WIDE),
            pltpu.VMEM((pairs, 2, rows), WIDE),
            pltpu.VMEM((2, 2, rows, PAIR), LOW),
            pltpu.VMEM((rows, 1), clips.dtype),
            pltpu.SemaphoreType.DMA((5,)),
            pltpu.SemaphoreType.DMA((2, 2)),
            pltpu.SemaphoreType.DMA,
            pltpu.SemaphoreType.DMA((5, pairs)),
            pltpu.SemaphoreType.DMA((5, pairs)),
        ],
        name="attention",
        compiler_params=pltpu.CompilerParams(
            collective_id=2, has_side_effects=True, vmem_limit_bytes=48 * 2**20
        ),
    )(a_low, w_qkv, clips, query_clip)


FF_BLOCK = 512
ROW_BLOCK = 384
AHEAD_STEPS = (3, 3, 2, 2)
AHEAD_TICKS = ((1, 3, 4), (2, 4, 5), (3, 5), (4, 5))
AHEAD = len(AHEAD_STEPS)
LAST_BLOCK = 5
DOWN_AXES, UP_AXES = "rrrrr", "rrrrc"


def ahead_rows(shape, axes):
    rows = [halves(shape, axes)[steps - 1][0] for steps in AHEAD_STEPS]
    return [(sum(rows[:block]), rows[block]) for block in range(AHEAD)]


def ahead_scratch(width):
    scratch = [pltpu.VMEM((2, FF_BLOCK, width), LOW), pltpu.VMEM((2, width, FF_BLOCK), LOW)]
    for shape, axes in (((FF_BLOCK, width), DOWN_AXES), ((width, FF_BLOCK), UP_AXES)):
        for steps in AHEAD_STEPS:
            shapes = halves(shape, axes)[:steps]
            scratch += [pltpu.VMEM(each, LOW) for each in (shapes[0], *shapes)]
    scratch += [pltpu.SemaphoreType.DMA((2 * AHEAD, 2 * STEPS))] * 2
    return scratch + [pltpu.SemaphoreType.DMA((2 * AHEAD, 2))]


def ahead_sums(width, part_down, part_up, refs):
    terms, refs = refs[:2], refs[2:]
    sends, receives, locals_ = refs[-3:]
    sums = []
    for side, (axes, shape, parts) in enumerate(
        ((DOWN_AXES, (FF_BLOCK, width), part_down), (UP_AXES, (width, FF_BLOCK), part_up))
    ):
        places = ahead_rows(shape, axes)
        for block, steps in enumerate(AHEAD_STEPS):
            index = side * AHEAD + block
            own, refs = refs[: steps + 1], refs[steps + 1 :]
            sums.append(
                Sum(
                    (block + side) % 2,
                    axes,
                    (0, 0),
                    shape,
                    terms[side].at[block % 2],
                    parts.at[pl.ds(*places[block])],
                    own[0],
                    own[1:],
                    (sends.at[index], receives.at[index]),
                    locals_.at[index],
                    stop=steps,
                )
            )
    return terms, [(sums[block], sums[AHEAD + block]) for block in range(AHEAD)]


def mlp_kernel(
    ahead,
    hidden_ref,
    attn_ref,
    attended_ref,
    cotangent_ref,
    w_out_ref,
    gain_ref,
    w_up_ref,
    b_up_ref,
    w_down_ref,
    outputs_ref,
    d_resid_ref,
    grad_t_ref,
    dots_ref,
    grad_down_ref,
    grad_up_ref,
    grad_out_ref,
    grad_gain_ref,
    grad_bias_ref,
    *refs,
):
    block = pl.program_id(0)
    rows, width = hidden_ref.shape
    if ahead:
        parts, refs = refs[:2], refs[2:]
    normed_ref, inverse_ref, b_ref, dy_ref, db_ref, z_ref, d_pre_ref = refs[:7]
    if ahead:
        terms, sums = ahead_sums(width, *parts, refs[7:])

        @pl.when(block == 0)
        def _():
            greet([device for _, device in place_bits(0)[: max(AHEAD_STEPS)]])

    def trade(chosen, tick, when):
        @pl.when(block == when)
        def _():
            for each in sums[chosen]:
                each.turn(tick)

    @pl.when(block == 0)
    def _():
        resid = hidden_ref[...] + dot(attn_ref[...], w_out_ref[...], NN)
        normed, inverse = normalize(resid)
        normed_ref[...] = normed
        inverse_ref[...] = inverse
        b_ref[...] = (normed * gain_ref[...]).astype(LOW)
        dy_ref[...] = cotangent_ref[...].astype(LOW)
        outputs_ref[...] = resid
        db_ref[...] = jnp.zeros_like(db_ref)

    bias = jnp.zeros((1, FF_BLOCK), WIDE)
    for start in range(0, rows, ROW_BLOCK):
        here = slice(start, start + ROW_BLOCK)
        pre_act = dot(b_ref[here], w_up_ref[...], NN) + b_up_ref[...]
        cumulative = 0.5 * (1.0 + lax.erf(pre_act * 0.7071067811865476))
        density = jnp.exp(-0.5 * pre_act * pre_act) * 0.3989422804014327
        z_ref[here] = (pre_act * cumulative).astype(LOW)
        d_gelu = dot(dy_ref[here], w_down_ref[...], NT)
        d_pre = (d_gelu * (cumulative + pre_act * density)).astype(LOW)
        d_pre_ref[here] = d_pre
        bias += jnp.sum(d_pre.astype(WIDE), axis=0, keepdims=True)
        outputs_ref[here] += dot(z_ref[here], w_down_ref[...], NN)
        db_ref[here] += dot(d_pre, w_up_ref[...], NT)
    grad_bias_ref[...] = bias
    grad_down = dot(z_ref[...], dy_ref[...], TN).astype(LOW)
    grad_up = dot(b_ref[...], d_pre_ref[...], TN).astype(LOW)
    grad_down_ref[...] = grad_down
    grad_up_ref[...] = grad_up
    if ahead:
        for chosen, ticks in enumerate(AHEAD_TICKS):
            for tick, when in enumerate(ticks):
                if when < LAST_BLOCK:
                    trade(chosen, tick, when)
        for chosen in range(AHEAD):

            @pl.when(block == chosen)
            def _():
                terms[0][chosen % 2] = grad_down
                terms[1][chosen % 2] = grad_up
                for each in sums[chosen]:
                    each.start()


    @pl.when(block == pl.num_programs(0) - 1)
    def _():
        normed, db = normed_ref[...], db_ref[...]
        grad_gain_ref[...] = jnp.sum(db * normed, axis=0, keepdims=True)
        d_resid = cotangent_ref[...] + norm_back(db * gain_ref[...], normed, inverse_ref[...])
        d_resid_ref[...] = d_resid
        dr_low = d_resid.astype(LOW)
        grad_out_ref[...] = dot(attn_ref[...], dr_low, TN).astype(LOW)
        grad_t = dot(w_out_ref[...], dr_low, NT).astype(LOW)
        grad_t_ref[...] = grad_t
        product = grad_t.astype(WIDE) * attended_ref[...]
        for pair in range(dots_ref.shape[0]):
            for head in range(2):
                lanes = slice(pair * PAIR + head * HEAD, pair * PAIR + (head + 1) * HEAD)
                dots_ref[pair, head : head + 1] = jnp.sum(product[lanes], axis=0, keepdims=True)

    if ahead:
        for chosen, ticks in enumerate(AHEAD_TICKS):
            for tick, when in enumerate(ticks):
                if when == LAST_BLOCK:
                    trade(chosen, tick, when)

        @pl.when(block == pl.num_programs(0) - 1)
        def _():
            for pair in sums:
                for each in pair:
                    each.store().wait()


def mlp_call(ahead, hidden, attn_low, attended, cotangent, w_out, gain_mlp, w_up, b_up, w_down):
    rows, width = hidden.shape
    hidden_units = w_up.shape[1]
    pairs = width // PAIR
    once = lambda *shape: pl.BlockSpec(
        shape, lambda block: (0,) * len(shape), pipeline_mode=pl.Buffered(1)
    )
    square, line = once(rows, width), once(1, width)
    up = pl.BlockSpec((width, FF_BLOCK), lambda block: (0, block))
    down = pl.BlockSpec((FF_BLOCK, width), lambda block: (block, 0))
    bias = pl.BlockSpec((1, FF_BLOCK), lambda block: (0, block))
    wide = jax.ShapeDtypeStruct((rows, width), WIDE)
    anywhere = pl.BlockSpec(memory_space=pl.ANY)
    down_rows = sum(ahead_rows((FF_BLOCK, width), DOWN_AXES)[-1])
    up_rows = sum(ahead_rows((width, FF_BLOCK), UP_AXES)[-1])
    part_shapes = [
        jax.ShapeDtypeStruct((down_rows, width), LOW),
        jax.ShapeDtypeStruct((up_rows, FF_BLOCK), LOW),
    ]
    params = dict(collective_id=3, has_side_effects=True) if ahead else {}
    return pl.pallas_call(
        functools.partial(mlp_kernel, ahead),
        grid=(hidden_units // FF_BLOCK,),
        in_specs=[square] * 4 + [once(width, width), line, up, bias, down],
        out_specs=[
            whole(rows, width),
            whole(rows, width),
            whole(width, rows),
            whole(pairs, 2, rows),
            down,
            up,
            whole(width, width),
            whole(1, width),
            bias,
        ]
        + [anywhere] * (2 if ahead else 0),
        out_shape=[
            wide,
            wide,
            jax.ShapeDtypeStruct((width, rows), LOW),
            jax.ShapeDtypeStruct((pairs, 2, rows), WIDE),
            jax.ShapeDtypeStruct(w_down.shape, LOW),
            jax.ShapeDtypeStruct(w_up.shape, LOW),
            jax.ShapeDtypeStruct((width, width), LOW),
            jax.ShapeDtypeStruct((1, width), WIDE),
            jax.ShapeDtypeStruct((1, hidden_units), WIDE),
        ]
        + (part_shapes if ahead else []),
        scratch_shapes=[
            pltpu.VMEM((rows, width), WIDE),
            pltpu.VMEM((rows, 1), WIDE),
            pltpu.VMEM((rows, width), LOW),
            pltpu.VMEM((rows, width), LOW),
            pltpu.VMEM((rows, width), WIDE),
            pltpu.VMEM((rows, FF_BLOCK), LOW),
            pltpu.VMEM((rows, FF_BLOCK), LOW),
        ]
        + (ahead_scratch(width) if ahead else []),
        name="mlp",
        compiler_params=pltpu.CompilerParams(vmem_limit_bytes=60 * 2**20, **params),
    )(hidden, attn_low, attended, cotangent, w_out, gain_mlp[None], w_up, b_up[None], w_down)


PARTS = (
    ("down", (0, 0), (512, 768), DOWN_AXES, 0, AHEAD_STEPS[0], 0, (24, 24, 24, 1, 2, 4, 5, 6, 8, 9)),
    ("down", (512, 0), (512, 768), DOWN_AXES, 1, AHEAD_STEPS[1], 1, (24, 24, 24, 1, 2, 4, 5, 6, 8, 9)),
    ("down", (1024, 0), (512, 768), DOWN_AXES, 0, AHEAD_STEPS[2], 2, (24, 24, 1, 2, 4, 6, 7, 9, 12, 13)),
    ("down", (1536, 0), (512, 768), DOWN_AXES, 1, AHEAD_STEPS[3], 3, (24, 24, 1, 2, 4, 6, 8, 10, 12, 13)),
    ("up", (0, 0), (768, 512), UP_AXES, 1, AHEAD_STEPS[0], 0, (24, 24, 24, 1, 2, 5, 6, 7, 10, 11)),
    ("up", (0, 512), (768, 512), UP_AXES, 0, AHEAD_STEPS[1], 1, (24, 24, 24, 2, 3, 5, 6, 8, 10, 11)),
    ("up", (0, 1024), (768, 512), UP_AXES, 1, AHEAD_STEPS[2], 2, (24, 24, 2, 3, 5, 6, 8, 11, 12, 14)),
    ("up", (0, 1536), (768, 512), UP_AXES, 0, AHEAD_STEPS[3], 3, (24, 24, 2, 4, 5, 6, 9, 10, 12, 13)),
    ("down", (2048, 0), (1024, 768), "rrrrr", 0, 0, None, (1, 4, 6, 8, 9, 11, 12, 14, 17, 18)),
    ("up", (0, 2048), (768, 1024), "rrrcc", 1, 0, None, (1, 4, 6, 8, 10, 12, 13, 15, 18, 19)),
    ("out", (0, 0), (768, 768), "rrrrc", 0, 0, None, (2, 5, 6, 9, 10, 12, 14, 16, 18, 20)),
    ("qkv", (0, 0), (768, 256), "rrrrc", 0, 0, None, None),
    ("qkv", (0, 256), (768, 256), "rrrrc", 1, 0, None, None),
    ("qkv", (0, 512), (768, 256), "rrrrc", 0, 0, None, None),
    ("qkv", (0, 768), (768, 256), "rrrrc", 1, 0, None, None),
    ("qkv", (0, 1024), (768, 256), "rrrrc", 0, 0, None, None),
    ("qkv", (0, 1280), (768, 256), "rrrrc", 1, 0, None, None),
    ("qkv", (0, 1536), (768, 256), "rrrrc", 0, 0, None, None),
    ("qkv", (0, 1792), (768, 256), "rrrrc", 1, 0, None, None),
    ("qkv", (0, 2048), (768, 256), "rrrrc", 0, 0, None, None),
)


def gradient_kernel(*refs):
    keys, values, shards = refs[:3]
    q_ref, grad_ref, lse_ref, dots_ref, clips, query_clip, w_ref = refs[3:10]
    down_in, up_in, out_in, part_down, part_up, small_in = refs[10:16]
    down_out, up_out, out_out, qkv_out, small_out, input_out = refs[16:22]
    refs = refs[22:]
    kv_slot, a_slot, dq_sum, dk_sum, dv_sum, dk_all, dv_all, grad_k, grad_v, parts = refs[:10]
    from_near, from_across, qkv_term, clip_slot, small_arrived = refs[10:15]
    input_sum = dq_sum
    kv_sems, a_sem, line_sends, line_receives, sends, receives, locals_ = refs[15:22]
    small_sends, small_receives, out_sem, clip_sem = refs[22:26]
    refs = refs[26:]
    rows, width = q_ref.shape
    pairs = width // PAIR
    pieces = 4 * pairs
    group, place = lax.axis_index("dp"), lax.axis_index("blk")
    near = (group, place + 1 - 2 * (place % 2))
    across = (group, 3 - place)
    at_end = place % 3 == 0

    arrays = {
        "down": (down_in, down_out),
        "up": (up_in, up_out),
        "out": (out_in, out_out),
        "qkv": (qkv_term, qkv_out),
    }
    sums = []
    for index, (name, corner, shape, axes, turn, begin, block, _) in enumerate(PARTS):
        steps = STEPS - begin
        total, arrived, refs = refs[0], refs[1 : steps + 1], refs[steps + 1 :]
        term, result = arrays[name]
        if block is not None:
            term = {"down": part_down, "up": part_up}[name]
            term = term.at[pl.ds(*ahead_rows(shape, axes)[block])]
        sums.append(
            Sum(
                turn,
                axes,
                corner,
                shape,
                term,
                result,
                total,
                arrived,
                (sends.at[index], receives.at[index]),
                locals_.at[index],
                begin=begin,
            )
        )
    early = [(each, part[-1]) for each, part in zip(sums, PARTS) if part[-1] is not None]
    late = [each for each, part in zip(sums, PARTS) if part[-1] is None]

    chunk_rows = rows // pairs

    def chunk_of(chunk):
        return pl.ds(pl.multiple_of(chunk * chunk_rows, chunk_rows), chunk_rows)

    def line_copy(channel, chunk, source, target, device):
        return pltpu.make_async_remote_copy(
            src_ref=parts.at[source, chunk_of(chunk)],
            dst_ref=target.at[chunk_of(chunk)],
            send_sem=line_sends.at[channel, chunk],
            recv_sem=line_receives.at[channel, chunk],
            device_id=device,
            device_id_type=MESH,
        )

    def inward(source, chunk):
        return line_copy(source, chunk, source, from_near.at[source], near)

    def middle(source, chunk):
        return line_copy(3 + source, chunk, source, from_across.at[source], across)

    def outward(chunk):
        return line_copy(5, chunk, 2, from_near.at[0], near)

    def add_chunk(total, term, chunk):
        here = chunk_of(chunk)
        total[here] = (total[here].astype(WIDE) + term[here].astype(WIDE)).astype(total.dtype)

    def pair_columns(pair):
        return pl.ds(pl.multiple_of(pair * PAIR, PAIR), PAIR)

    def kv_copies(shard, pair, slot):
        return [
            pltpu.make_async_copy(
                source.at[shard, :, pair_columns(pair)], kv_slot.at[slot, side], kv_sems.at[slot, side]
            )
            for side, source in enumerate((keys, values))
        ]

    def a_copy(shard):
        return pltpu.make_async_copy(shards.at[shard], a_slot, a_sem)

    def clip_copy(turn):
        source = clips.at[pl.ds(pl.multiple_of((3 - turn) * rows, 8), rows)]
        return pltpu.make_async_copy(source, clip_slot, clip_sem)

    def of_pairs(stack):
        return jnp.concatenate([stack[pair] for pair in range(pairs)], axis=1)

    for copy in kv_copies(3, 0, 0):
        copy.start()
    greet([device for _, device in place_bits(0)] + [across])
    for each, _ in early:
        each.start()
    dq_sum[...] = jnp.zeros_like(dq_sum)
    grad_k[...] = jnp.zeros_like(grad_k)
    grad_v[...] = jnp.zeros_like(grad_v)
    small_out[...] = small_in[...]

    def weight_terms(d_query):
        a_copy(0).wait()
        d_key, d_value = of_pairs(dk_all), of_pairs(dv_all)
        part = dot(d_key, w_ref[:, width : 2 * width], NT) + dot(d_value, w_ref[:, 2 * width :], NT)
        if d_query is not None:
            part = part + dot(d_query, w_ref[:, :width], NT)
        small_out[:1] += jnp.sum(part * a_slot[...].astype(WIDE), axis=0, keepdims=True)
        grad_k[...] += dot(a_slot[...], d_key, TN)
        grad_v[...] += dot(a_slot[...], d_value, TN)
        return part

    @pl.loop(0, pieces)
    def _(piece):
        turn, pair, slot = piece // pairs, piece % pairs, piece % 2

        def at(when, *actions):
            @pl.when(piece == when)
            def _():
                for action in actions:
                    action()

        following = piece + 1

        @pl.when(following < pieces)
        def _():
            for copy in kv_copies(3 - following // pairs, following % pairs, following % 2):
                copy.start()

        @pl.when(pair == 1)
        def _():
            a_copy(3 - turn).start()

        for when in range(pieces):
            ends = [
                functools.partial(each.turn, tick)
                for tick in range(2 * STEPS)
                for each, ticks in early
                if ticks[tick] == when and tick >= each.begin
            ]
            if ends:
                at(when, *ends)
        at_middle = jnp.logical_not(at_end)

        @pl.when(jnp.logical_and(turn > 0, at_end))
        def _():
            inward(turn - 1, pair).start()

        @pl.when(jnp.logical_and(at_middle, jnp.logical_and(piece >= FORWARD, piece < FORWARD + 2 * pairs)))
        def _():
            source, chunk = (piece - FORWARD) // pairs, (piece - FORWARD) % pairs
            inward(source, chunk).wait_recv()
            add_chunk(parts.at[source], from_near.at[source], chunk)
            middle(source, chunk).start()

        @pl.when(jnp.logical_and(at_middle, turn == 3))
        def _():
            middle(0, pair).wait_recv()
            add_chunk(parts.at[2], from_across.at[0], pair)
            outward(pair).start()

        @pl.when(pair == 0)
        def _():
            clip_copy(turn).start()
            clip_copy(turn).wait()

        for copy in kv_copies(0, pair, slot):
            copy.wait()
        columns = pair_columns(pair)

        def add(head, start, stop, dq, dk, dv):
            lanes = slice(head * HEAD, (head + 1) * HEAD)
            if start == 0:
                dv_sum[lanes], dk_sum[lanes] = dv, dk
            else:
                dv_sum[lanes] += dv
                dk_sum[lanes] += dk
            at_lanes = pl.ds(pl.multiple_of(pair * PAIR + head * HEAD, HEAD), HEAD)
            dq_sum[at_lanes, start:stop] += dq

        backward_pair(
            kv_slot[slot, 0],
            kv_slot[slot, 1],
            q_ref[:, columns],
            grad_ref[columns, :],
            lse_ref.at[pair],
            dots_ref.at[pair],
            clip_slot[...],
            query_clip[...],
            add,
        )
        dk_all[pair] = (dk_sum[...] * SCALE).T.astype(LOW)
        dv_all[pair] = dv_sum[...].T.astype(LOW)

        @pl.when(jnp.logical_and(pair == pairs - 1, turn < 3))
        def _():
            parts[turn] = weight_terms(None).astype(LOW)

    d_query = (dq_sum[...] * SCALE).T.astype(LOW)
    input_sum[...] = weight_terms(d_query)
    qkv_term[:, :width] = dot(a_slot[...], d_query, TN).astype(LOW)
    qkv_term[:, width : 2 * width] = grad_k[...].astype(LOW)
    qkv_term[:, 2 * width :] = grad_v[...].astype(LOW)

    small_steps = place_bits(0)

    def small(step):
        return remote(
            small_out, small_arrived.at[step], (small_sends, small_receives), step, small_steps[step][1]
        )

    for each in late:
        each.start()
    open_sums = [
        (each, [tick for tick in range(each.begin, 2 * STEPS) if ticks[tick] == pieces])
        for each, ticks in early
    ]
    open_sums += [(each, list(range(2 * STEPS))) for each in late]

    @pl.when(at_end)
    def _():
        @pl.loop(0, pairs)
        def _(chunk):
            for source in range(3):
                inward(source, chunk).wait_send()
            outward(chunk).wait_recv()
            add_chunk(input_sum, from_near.at[0], chunk)

    @pl.when(jnp.logical_not(at_end))
    def _():
        @pl.loop(0, pairs)
        def _(chunk):
            outward(chunk).wait_send()
            for source in range(2):
                middle(source, chunk).wait_send()
            middle(1, chunk).wait_recv()
            add_chunk(input_sum, from_across.at[1], chunk)
            inward(2, chunk).wait_recv()
            add_chunk(input_sum, from_near.at[2], chunk)

    store = pltpu.make_async_copy(input_sum, input_out, out_sem)
    store.start()
    for tick in range(2 * STEPS):
        if tick < STEPS:
            small(tick).start()
        for each, ticks in open_sums:
            if ticks:
                each.turn(ticks.pop(0))
        if tick < STEPS:
            small(tick).wait()
            small_out[...] += small_arrived[tick]
    store.wait()


def gradient_call(
    keys, values, shards, query, grad_t, lse, row_dots, clips, query_clip, w_qkv, grad_down, grad_up, grad_out, part_down, part_up, small
):
    rows, width = query.shape
    pairs = width // PAIR
    anywhere = pl.BlockSpec(memory_space=pl.ANY)
    inside = pl.BlockSpec(memory_space=pltpu.VMEM)
    square = (rows, width)
    scratch = [
        pltpu.VMEM((2, 2, rows, PAIR), LOW),
        pltpu.VMEM(square, LOW),
        pltpu.VMEM((width, rows), WIDE),
        pltpu.VMEM((PAIR, rows), WIDE),
        pltpu.VMEM((PAIR, rows), WIDE),
        pltpu.VMEM((pairs, rows, PAIR), LOW),
        pltpu.VMEM((pairs, rows, PAIR), LOW),
        pltpu.VMEM((width, width), WIDE),
        pltpu.VMEM((width, width), WIDE),
        pltpu.VMEM((3, *square), LOW),
    ]
    scratch += [pltpu.VMEM((3, *square), LOW), pltpu.VMEM((2, *square), LOW)]
    scratch += [
        pltpu.VMEM((width, 3 * width), LOW),
        pltpu.VMEM((rows, 1), clips.dtype),
        pltpu.VMEM((STEPS, *small.shape), WIDE),
        pltpu.SemaphoreType.DMA((2, 2)),
        pltpu.SemaphoreType.DMA,
        pltpu.SemaphoreType.DMA((6, pairs)),
        pltpu.SemaphoreType.DMA((6, pairs)),
        pltpu.SemaphoreType.DMA((len(PARTS), 2 * STEPS)),
        pltpu.SemaphoreType.DMA((len(PARTS), 2 * STEPS)),
        pltpu.SemaphoreType.DMA((len(PARTS), 2)),
        pltpu.SemaphoreType.DMA((STEPS,)),
        pltpu.SemaphoreType.DMA((STEPS,)),
        pltpu.SemaphoreType.DMA,
        pltpu.SemaphoreType.DMA,
    ]
    for _, _, shape, axes, _, begin, _, _ in PARTS:
        shapes = halves(shape, axes)
        scratch += [pltpu.VMEM(each, LOW) for each in (shapes[max(begin - 1, 0)], *shapes[begin:])]
    like = lambda array: jax.ShapeDtypeStruct(array.shape, array.dtype)
    return pl.pallas_call(
        gradient_kernel,
        in_specs=[anywhere] * 3 + [inside] * 4 + [anywhere] + [inside] * 2 + [anywhere] * 5 + [inside],
        out_specs=[anywhere] * 4 + [inside, anywhere],
        out_shape=[
            like(grad_down),
            like(grad_up),
            like(grad_out),
            jax.ShapeDtypeStruct((width, 3 * width), LOW),
            like(small),
            jax.ShapeDtypeStruct(square, WIDE),
        ],
        scratch_shapes=scratch,
        name="gradients",
        compiler_params=pltpu.CompilerParams(
            collective_id=1, has_side_effects=True, vmem_limit_bytes=62 * 2**20
        ),
    )(
        keys, values, shards, query, grad_t, lse, row_dots, clips, query_clip, w_qkv,
        grad_down, grad_up, grad_out, part_down, part_up, small,
    )


def on_device(
    groups, inputs, positions, segments, gain_attn, w_qkv, w_out, gain_mlp, w_up, b_up, w_down, cotangent
):
    rows, width = inputs.shape
    pairs = width // PAIR
    place = lax.axis_index("blk")
    w_query = w_qkv[:, :width]

    def send(value, pairs_of_places):
        return lax.ppermute(value, "blk", pairs_of_places)

    hidden = inputs + position_table(positions, width)
    normed_attn, inverse_attn = normalize(hidden)
    a_low = (normed_attn * gain_attn).astype(LOW)

    table = jnp.array([[0, 1, 2, 3], [1, 0, 2, 3], [2, 3, 1, 0], [3, 2, 1, 0]], jnp.int32)
    order = lax.dynamic_index_in_dim(table, place, keepdims=False)
    clips = jnp.concatenate(
        [lax.dynamic_slice_in_dim(segments, order[index] * rows, rows) for index in range(4)]
    )[:, None]
    query_clip = lax.dynamic_slice_in_dim(segments, place * rows, rows)[None, :]
    shards, keys, values, query, attended, lse, attn_low = attention_call(
        a_low, w_qkv, clips, query_clip
    )

    quick = groups == 8 and rows == width
    (
        outputs,
        d_resid,
        d_attn_t,
        row_dots,
        grad_down,
        grad_up,
        grad_out,
        grad_gain_mlp,
        grad_bias_up,
        *parts,
    ) = mlp_call(quick, hidden, attn_low, attended, cotangent, w_out, gain_mlp, w_up, b_up, w_down)
    grad_gain_mlp, grad_bias_up = grad_gain_mlp[0], grad_bias_up[0]

    if quick:
        small = jnp.concatenate([jnp.zeros_like(gain_attn), grad_gain_mlp, grad_bias_up])
        sum_down, sum_up, sum_out, sum_qkv, sum_small, d_normed_attn = gradient_call(
            keys,
            values,
            shards,
            query,
            d_attn_t,
            lse,
            row_dots,
            clips,
            query_clip,
            w_qkv,
            grad_down,
            grad_up,
            grad_out,
            *parts,
            jnp.pad(small.reshape(6, width), ((0, 2), (0, 0))),
        )
        input_grad = d_resid + norm_back(d_normed_attn * gain_attn, normed_attn, inverse_attn)
        return (
            outputs,
            input_grad,
            sum_small[0] / gain_attn,
            sum_qkv.astype(WIDE),
            sum_out.astype(WIDE),
            sum_small[1],
            sum_up.astype(WIDE),
            sum_small[2:6].reshape(-1),
            sum_down.astype(WIDE),
        )

    everywhere = ("dp", "blk")

    def back(index, dq):
        return backward_call(
            index == 3,
            index == 0,
            keys[index],
            values[index],
            query,
            d_attn_t,
            lse,
            row_dots,
            clips[index * rows : (index + 1) * rows],
            query_clip,
            w_qkv,
            dq,
        )

    middle, outward, inward = [(1, 2), (2, 1)], [(1, 0), (2, 3)], [(0, 1), (3, 2)]
    dk_3, dv_3, dq, part_3 = back(3, None)
    far = send(part_3, inward)
    dk_2, dv_2, dq, part_2 = back(2, dq)
    far, part_2, dq = lax.optimization_barrier((far, part_2, dq))
    onward = (part_3.astype(WIDE) + far.astype(WIDE)).astype(LOW)
    mid_3 = send(onward, middle)
    mid_2 = send(part_2, inward)
    dq, onward = lax.optimization_barrier((dq, onward))
    dk_1, dv_1, dq, part_1 = back(1, dq)
    mid_3, mid_2, part_1, dq = lax.optimization_barrier((mid_3, mid_2, part_1, dq))
    onward_1 = (part_2.astype(WIDE) + mid_2.astype(WIDE)).astype(LOW)
    onward_2 = (part_1.astype(WIDE) + mid_3.astype(WIDE)).astype(LOW)
    last_1 = send(onward_1, middle)
    last_2 = send(onward_2, outward)
    last_3 = send(part_1, inward)
    dq, onward_1, onward_2 = lax.optimization_barrier((dq, onward_1, onward_2))
    dk_0, dv_0, dq, part_0 = back(0, dq)
    grad_query = dot(a_low, dq, TN).astype(LOW)
    d_keys, d_values = (dk_0, dk_1, dk_2, dk_3), (dv_0, dv_1, dv_2, dv_3)
    grad_key = sum(dot(shard, term, TN) for shard, term in zip(shards, d_keys)).astype(LOW)
    grad_value = sum(dot(shard, term, TN) for shard, term in zip(shards, d_values)).astype(LOW)
    d_normed_attn = (
        part_0
        + dot(dq, w_query, NT)
        + last_1.astype(WIDE)
        + last_2.astype(WIDE)
        + last_3.astype(WIDE)
    )
    grad_gain_attn = jnp.sum(d_normed_attn * normed_attn, axis=0)
    input_grad = d_resid + norm_back(d_normed_attn * gain_attn, normed_attn, inverse_attn)
    small = jnp.concatenate([grad_gain_attn, grad_gain_mlp, grad_bias_up])
    sums = lax.psum((grad_down, grad_up, grad_out, grad_query, grad_key, grad_value), everywhere)
    sum_small = lax.psum(small, everywhere)
    sum_down, sum_up, sum_out, *sum_qkv = sums
    return (
        outputs,
        input_grad,
        sum_small[:width],
        jnp.concatenate(sum_qkv, axis=1).astype(WIDE),
        sum_out.astype(WIDE),
        sum_small[width : 2 * width],
        sum_up.astype(WIDE),
        sum_small[2 * width :],
        sum_down.astype(WIDE),
    )


def solution(mesh):
    rows = P(("dp", "blk"), None)
    placed = (rows, P(("dp", "blk")), P("dp"), P(), P(), P(), P(), P(), P(), P(), rows)
    return jax.shard_map(
        functools.partial(on_device, mesh.shape["dp"]),
        mesh=mesh,
        in_specs=placed,
        out_specs=(rows, rows, P(), P(), P(), P(), P(), P(), P()),
        check_vma=False,
    )
```

```python
import functools
import math

import jax
import jax.numpy as jnp
from jax import lax
from jax.experimental import pallas as pl
from jax.experimental.pallas import tpu as pltpu
from jax.sharding import PartitionSpec as P

HEADS = 12
HEAD = 64
PAIR = 2 * HEAD
SCALE = HEAD**-0.5
LOG2E = 1.4426950408889634
MASKED = -1.0e9
QUERY_BLOCK = 384
EPS_NORM = 1e-06
LOW = jnp.bfloat16
WIDE = jnp.float32

NN = (((1,), (0,)), ((), ()))
NT = (((1,), (1,)), ((), ()))
TN = (((0,), (0,)), ((), ()))


def dot(left, right, dims):
    return lax.dot_general(left, right, dims, preferred_element_type=WIDE)


def position_table(positions, model_width):
    half_width = model_width // 2
    freqs = jnp.exp(jnp.arange(half_width, dtype=WIDE) * (-math.log(10000.0) / half_width))
    angles = positions.astype(WIDE)[:, None] * freqs[None, :]
    return jnp.concatenate([jnp.sin(angles), jnp.cos(angles)], axis=1)


def normalize(values):
    center = values - jnp.mean(values, axis=-1, keepdims=True)
    inverse = lax.rsqrt(jnp.mean(center * center, axis=-1, keepdims=True) + EPS_NORM)
    return center * inverse, inverse


def norm_back(grad_norm, normed, inverse):
    first = jnp.mean(grad_norm, axis=-1, keepdims=True)
    second = jnp.mean(grad_norm * normed, axis=-1, keepdims=True)
    return inverse * (grad_norm - first - normed * second)


def in_head(values, head):
    lanes = lax.broadcasted_iota(jnp.int32, values.shape, 1)
    return (lanes < HEAD) == (head == 0)


def only_head(values, head, other=None):
    other = jnp.zeros_like(values) if other is None else other
    return jnp.where(in_head(values, head), values, other)


def split_scaled(query):
    scaled = query.astype(WIDE) * (SCALE * LOG2E)
    high = scaled.astype(LOW)
    return high, (scaled - high.astype(WIDE)).astype(LOW)


def score_sides(key, query):
    high, low = split_scaled(query)
    key_side = jnp.concatenate([key, key], axis=1)
    query_side = [
        jnp.concatenate([only_head(high, head), only_head(low, head)], axis=1) for head in range(2)
    ]
    return key_side, query_side


def work_items(rows):
    return [(start, head) for start in range(0, rows, QUERY_BLOCK) for head in range(2)]


def whole(*shape):
    return pl.BlockSpec(shape, lambda pair: (0,) * len(shape))


def columns_of(rows, first=0):
    return pl.BlockSpec((rows, PAIR), lambda pair: (0, pair + first))


def backward_pair(key, value, query, grad_t, lse, row_dots, key_clip, query_clip, add):
    rows = query.shape[0]
    grad = grad_t.T
    key_t, query_t = key.T, query.T
    key_side, query_side = score_sides(key, query)
    grad_side = [only_head(grad, head) for head in range(2)]
    for start, head in work_items(rows):
        stop = start + QUERY_BLOCK
        lanes, row = slice(head * HEAD, (head + 1) * HEAD), slice(head, head + 1)
        score = dot(key_side, query_side[head][start:stop], NT)
        score = jnp.where(key_clip == query_clip[:, start:stop], score, MASKED)
        probs = jnp.exp2(score - lse[row, start:stop])
        d_probs = dot(value, grad_side[head][start:stop], NT)
        d_scores = (probs * (d_probs - row_dots[row, start:stop])).astype(LOW)
        probs = probs.astype(LOW)
        dv = dot(grad_t[lanes, start:stop], probs, NT)
        dk = dot(query_t[lanes, start:stop], d_scores, NT)
        dq = dot(key_t[lanes], d_scores, NN)
        add(head, start, stop, dq, dk, dv)


def backward_kernel(first, last, *refs):
    k_ref, v_ref, q_ref, grad_ref, lse_ref, dots_ref, key_clip, query_clip, wk_ref, wv_ref = refs[:10]
    refs = refs[10:]
    if not first:
        dq_in = refs[0]
        refs = refs[1:]
    dk_ref, dv_ref, dq_ref, part_ref, dk_sum, dv_sum, dq_sum, dk_all, dv_all = refs
    pair = pl.program_id(0)
    rows = q_ref.shape[0]

    def add(head, start, stop, dq, dk, dv):
        lanes = slice(head * HEAD, (head + 1) * HEAD)
        if start == 0:
            dv_sum[lanes], dk_sum[lanes] = dv, dk
        else:
            dv_sum[lanes] += dv
            dk_sum[lanes] += dk
        if not first:
            dq = dq + dq_in[lanes, start:stop]
        if last:
            dq_sum[lanes, start:stop] = dq
        else:
            dq_ref[lanes, start:stop] = dq

    backward_pair(
        k_ref[...],
        v_ref[...],
        q_ref[...],
        grad_ref[...],
        lse_ref,
        dots_ref,
        key_clip[...],
        query_clip[...],
        add,
    )
    if last:
        dq_ref[...] = (dq_sum[...] * SCALE).T.astype(LOW)
    dk = (dk_sum[...] * SCALE).T.astype(LOW)
    dv = dv_sum[...].T.astype(LOW)
    dk_ref[...] = dk
    dv_ref[...] = dv
    dk_all[pair] = dk
    dv_all[pair] = dv

    @pl.when(pair == pl.num_programs(0) - 1)
    def _():
        pairs = dk_all.shape[0]
        dk_rows = jnp.concatenate([dk_all[index] for index in range(pairs)], axis=1)
        dv_rows = jnp.concatenate([dv_all[index] for index in range(pairs)], axis=1)
        part = dot(dk_rows, wk_ref[...], NT) + dot(dv_rows, wv_ref[...], NT)
        part_ref[...] = part.astype(part_ref.dtype)


def backward_call(first, last, key, value, query, grad_t, lse, row_dots, key_clip, query_clip, w_qkv, dq):
    rows, width = query.shape
    pairs = width // PAIR
    across = pl.BlockSpec((PAIR, rows), lambda pair: (pair, 0))
    line = pl.BlockSpec((None, 2, rows), lambda pair: (pair, 0, 0))
    columns = columns_of(rows)
    in_specs = [columns, columns, columns, across, line, line, whole(rows, 1), whole(1, rows)]
    in_specs += [
        pl.BlockSpec((width, width), lambda pair: (0, 1)),
        pl.BlockSpec((width, width), lambda pair: (0, 2)),
    ]
    operands = [key, value, query, grad_t, lse, row_dots, key_clip, query_clip, w_qkv, w_qkv]
    if not first:
        in_specs.append(across)
        operands.append(dq)
    low_rows = jax.ShapeDtypeStruct((rows, width), LOW)
    tall = pltpu.VMEM((PAIR, rows), WIDE)
    parts = pltpu.VMEM((pairs, rows, PAIR), LOW)
    return pl.pallas_call(
        functools.partial(backward_kernel, first, last),
        grid=(pairs,),
        in_specs=in_specs,
        out_specs=[columns, columns, columns if last else across, whole(rows, width)],
        out_shape=[
            low_rows,
            low_rows,
            low_rows if last else jax.ShapeDtypeStruct((width, rows), WIDE),
            jax.ShapeDtypeStruct((rows, width), WIDE if last else LOW),
        ],
        scratch_shapes=[tall, tall, tall, parts, parts],
        name="attend_back",
        cost_estimate=pl.CostEstimate(
            flops=40 * rows * rows * width, bytes_accessed=24 * rows * width, transcendentals=0
        ),
        compiler_params=pltpu.CompilerParams(vmem_limit_bytes=48 * 2**20),
    )(*operands)


MESH = pl.DeviceIdType.MESH
TURNS = ((0, 1, 2), (0, 2, 1))
STEPS = 5
FORWARD = 8


def place_bits(turn):
    group, place = lax.axis_index("dp"), lax.axis_index("blk")
    steps = []
    for bit in TURNS[turn]:
        mine = group // (1 << bit) % 2
        steps.append((mine, (group + (1 - 2 * mine) * (1 << bit), place)))
    for bit in range(2):
        mine = place // (1 << bit) % 2
        steps.append((mine, (group, place + (1 - 2 * mine) * (1 << bit))))
    return steps


def remote(source, target, sems, index, device):
    return pltpu.make_async_remote_copy(
        src_ref=source,
        dst_ref=target,
        send_sem=sems[0].at[index],
        recv_sem=sems[1].at[index],
        device_id=device,
        device_id_type=MESH,
    )


def part_of(row, rows, column, columns):
    row = row if isinstance(row, int) else pl.multiple_of(row, 16)
    column = column if isinstance(column, int) else pl.multiple_of(column, PAIR)
    return pl.ds(row, rows), pl.ds(column, columns)


def add_block(total, term, row=0, column=0):
    rows, columns = term.shape
    block = next(size for size in (48, 32, 16) if rows % size == 0)

    @pl.loop(0, rows // block)
    def _(index):
        here = part_of(row + index * block, block, column, columns)
        there = part_of(index * block, block, 0, columns)
        total[here] = (total[here].astype(WIDE) + term[there].astype(WIDE)).astype(total.dtype)


def halves(shape, axes):
    shapes = []
    for axis in axes:
        shape = (shape[0] // 2, shape[1]) if axis == "r" else (shape[0], shape[1] // 2)
        shapes.append(shape)
    return shapes


class Sum:
    def __init__(
        self, turn, axes, corner, shape, term, result, total, arrived, sems, local_sems, begin=0, stop=STEPS
    ):
        self.term, self.result, self.total, self.arrived = term, result, total, arrived
        self.sems, self.local_sems, self.begin, self.stop = sems, local_sems, begin, stop
        self.steps = place_bits(turn)
        self.shapes = halves(shape, axes)
        self.kept, self.left = [], []
        row, column = corner
        for axis, (rows, columns), (mine, _) in zip(axes, self.shapes, self.steps):
            down, across = (rows, 0) if axis == "r" else (0, columns)
            self.left.append((row + (1 - mine) * down, rows, column + (1 - mine) * across, columns))
            row, column = row + mine * down, column + mine * across
            self.kept.append((row, rows, column, columns))
        self.held = self.kept[max(begin - 1, 0)]

    def inside(self, place):
        row, rows, column, columns = place
        return part_of(row - self.held[0], rows, column - self.held[2], columns)

    def load(self):
        source = self.term if self.begin else self.term.at[part_of(*self.kept[0])]
        return pltpu.make_async_copy(source, self.total, self.local_sems.at[0])

    def store(self):
        place = self.kept[self.stop - 1]
        target = self.result.at[part_of(*place)] if self.stop == STEPS else self.result
        return pltpu.make_async_copy(
            self.total.at[self.inside(place)], target, self.local_sems.at[1]
        )

    def gather(self, step):
        place = self.left[step]
        source = self.term.at[part_of(*place)] if step == 0 else self.total.at[self.inside(place)]
        return remote(source, self.arrived[step - self.begin], self.sems, step, self.steps[step][1])

    def spread(self, step):
        here = self.result.at[part_of(*self.kept[step])]
        source = self.total.at[self.inside(self.kept[step])] if step == STEPS - 1 else here
        return remote(source, here, self.sems, STEPS + step, self.steps[step][1])

    def start(self):
        self.load().start()
        if self.begin:
            self.load().wait()
        self.gather(self.begin).start()

    def turn(self, tick):
        if tick < STEPS:
            if tick == 0:
                self.load().wait()
            self.gather(tick).wait()
            row, _, column, _ = self.kept[tick]
            add_block(
                self.total, self.arrived[tick - self.begin], row - self.held[0], column - self.held[2]
            )
            if tick + 1 < self.stop:
                self.gather(tick + 1).start()
            else:
                self.store().start()
                if self.stop == STEPS:
                    self.spread(STEPS - 1).start()
        else:
            step = 2 * STEPS - 1 - tick
            if step == STEPS - 1:
                self.store().wait()
            self.spread(step).wait()
            if step:
                self.spread(step - 1).start()


def greet(devices):
    barrier = pltpu.get_barrier_semaphore()
    for device in devices:
        pl.semaphore_signal(barrier, inc=1, device_id=device, device_id_type=MESH)
    pl.semaphore_wait(barrier, len(devices))


PASS_NEAR = (2, 4, 5, 6, 6, 6)
PASS_FAR = (10, 11, 12, 13, 15, 16)


def attention_kernel(*refs):
    a_in, w_ref, clips, query_clip = refs[:4]
    a_out, k_out, v_out, q_ref, acc_ref, lse_ref, attn_ref = refs[4:11]
    a_all, top_all, total_all, kv_slot, clip_slot = refs[11:16]
    a_sems, kv_sems, clip_sem, line_sends, line_receives = refs[16:]
    rows, width = q_ref.shape
    pairs = width // PAIR
    chunk_rows = rows // pairs
    group, place = lax.axis_index("dp"), lax.axis_index("blk")
    near = (group, place + 1 - 2 * (place % 2))
    across = (group, 3 - place)
    at_end = place % 3 == 0
    at_middle = jnp.logical_not(at_end)

    def line_copy(channel, chunk, source, target, device):
        here = pl.ds(pl.multiple_of(chunk * chunk_rows, chunk_rows), chunk_rows)
        return pltpu.make_async_remote_copy(
            src_ref=source.at[here],
            dst_ref=a_all.at[target, here],
            send_sem=line_sends.at[channel, chunk],
            recv_sem=line_receives.at[channel, chunk],
            device_id=device,
            device_id_type=MESH,
        )

    channels = (
        lambda chunk: line_copy(0, chunk, a_in, 1, near),
        lambda chunk: line_copy(1, chunk, a_in, 2, across),
        lambda chunk: line_copy(2, chunk, a_all.at[2], 2, near),
        lambda chunk: line_copy(3, chunk, a_all.at[1], 3, across),
        lambda chunk: line_copy(4, chunk, a_all.at[3], 3, near),
    )
    load = pltpu.make_async_copy(a_in, a_all.at[0], a_sems.at[4])
    load.start()
    greet((near, across))
    for chunk in range(pairs):
        channels[0](chunk).start()

    @pl.when(at_middle)
    def _():
        for chunk in range(pairs):
            channels[1](chunk).start()

    top_all[...] = jnp.full_like(top_all, -1.0e30)
    total_all[...] = jnp.zeros_like(total_all)
    acc_ref[...] = jnp.zeros_like(acc_ref)

    def keep(shard):
        return pltpu.make_async_copy(a_all.at[shard], a_out.at[shard], a_sems.at[shard])

    def clip_copy(turn):
        source = clips.at[pl.ds(pl.multiple_of(turn * rows, 8), rows)]
        return pltpu.make_async_copy(source, clip_slot, clip_sem)

    half_rows = rows // 2

    def pair_columns(pair):
        return pl.ds(pl.multiple_of(pair * PAIR, PAIR), PAIR)

    def kv_copies(turn, pair, slot, first, count):
        keys = pl.ds(pl.multiple_of(first, half_rows), count)
        return [
            pltpu.make_async_copy(
                kv_slot.at[slot, side, pl.ds(0, count)],
                target.at[turn, keys, pair_columns(pair)],
                kv_sems.at[slot, side],
            )
            for side, target in enumerate((k_out, v_out))
        ]

    load.wait()
    keep(0).start()

    def attend_keys(turn, pair, slot, first, count):
        w_pair = jnp.concatenate(
            [w_ref[:, pair_columns(pair + pairs)], w_ref[:, pair_columns(pair + 2 * pairs)]], axis=1
        )
        keys = pl.ds(pl.multiple_of(first, half_rows), count)
        kv = dot(a_all[turn, keys], w_pair, NN).astype(LOW)
        key, value = kv[:, :PAIR], kv[:, PAIR:]
        kv_slot[slot, 0, :count] = key
        kv_slot[slot, 1, :count] = value
        for copy in kv_copies(turn, pair, slot, first, count):
            copy.start()
        value_t = value.T
        ones = jnp.ones((16, count), LOW)
        value_rows = [
            jnp.concatenate([value_t[head * HEAD : (head + 1) * HEAD], ones], axis=0)
            for head in range(2)
        ]
        key_side, query_side = score_sides(key, q_ref[:, pair_columns(pair)])
        key_clip = clip_slot[keys]

        def scores(start, head):
            stop = start + QUERY_BLOCK
            result = dot(key_side, query_side[head][start:stop], NT)
            return jnp.where(key_clip == query_clip[:, start:stop], result, MASKED)

        def weights(start, head, result):
            here = slice(start, start + QUERY_BLOCK)
            before = top_all[pair, head : head + 1, here]
            top = jnp.maximum(before, jnp.max(result, axis=0, keepdims=True))
            top_all[pair, head : head + 1, here] = top
            return jnp.exp2(result - top).astype(LOW), jnp.exp2(before - top)

        def attend(start, head, expd, shrink):
            here, row = slice(start, start + QUERY_BLOCK), slice(head, head + 1)
            lanes = pl.ds(pl.multiple_of(pair * PAIR + head * HEAD, HEAD), HEAD)
            result = dot(value_rows[head], expd, NN)
            acc_ref[lanes, here] = acc_ref[lanes, here] * shrink + result[:HEAD]
            total_all[pair, row, here] = total_all[pair, row, here] * shrink + result[HEAD : HEAD + 1]

        items = work_items(rows)
        result = scores(*items[0])
        before = None
        for index, item in enumerate(items):
            following = scores(*items[index + 1]) if index + 1 < len(items) else None
            done = weights(*item, result)
            if before is not None:
                attend(*before)
            before = (*item, *done)
            result = following
        attend(*before)

    @pl.loop(0, 3 * pairs)
    def _(piece):
        turn, pair, slot = piece // pairs, piece % pairs, piece % 2
        for chunk, when in enumerate(PASS_NEAR):

            @pl.when(jnp.logical_and(piece == when, at_middle))
            def _():
                channels[0](chunk).wait_recv()
                channels[3](chunk).start()
                channels[1](chunk).wait_recv()
                channels[2](chunk).start()

        for chunk, when in enumerate(PASS_FAR):

            @pl.when(jnp.logical_and(piece == when, at_middle))
            def _():
                channels[3](chunk).wait_recv()
                channels[4](chunk).start()

        for shard, channel in ((1, 0), (2, 2)):

            @pl.when(jnp.logical_and(piece == shard * pairs, at_end))
            def _():
                for chunk in range(pairs):
                    channels[channel](chunk).wait_recv()

            @pl.when(piece == shard * pairs)
            def _():
                keep(shard).start()

        @pl.when(pair == 0)
        def _():
            clip_copy(turn).start()
            clip_copy(turn).wait()

        @pl.when(piece >= 2)
        def _():
            for copy in kv_copies(turn, pair, slot, 0, rows):
                copy.wait()

        columns = pair_columns(pair)

        @pl.when(turn == 0)
        def _():
            q_ref[:, columns] = dot(a_all[0], w_ref[:, columns], NN).astype(LOW)

        attend_keys(turn, pair, slot, 0, rows)

    for slot in range(2):
        for copy in kv_copies(2, pairs - 2 + slot, slot, 0, rows):
            copy.wait()
    clip_copy(3).start()
    clip_copy(3).wait()

    @pl.loop(0, 2 * pairs)
    def _(piece):
        half, pair, slot = piece // pairs, piece % pairs, piece % 2
        for part in range(2):

            @pl.when(jnp.logical_and(piece == part * pairs, at_end))
            def _():
                for chunk in range(part * pairs // 2, (part + 1) * pairs // 2):
                    channels[4](chunk).wait_recv()

        @pl.when(piece == pairs)
        def _():
            keep(3).start()

        @pl.when(piece >= 2)
        def _():
            for copy in kv_copies(3, pair, slot, half * half_rows, half_rows):
                copy.wait()

        attend_keys(3, pair, slot, half * half_rows, half_rows)

        @pl.when(half == 1)
        def _():
            for head in range(2):
                lanes = pl.ds(pl.multiple_of(pair * PAIR + head * HEAD, HEAD), HEAD)
                total = total_all[pair, head : head + 1]
                acc_ref[lanes] = acc_ref[lanes] * (1.0 / total)
                lse_ref[pair, head : head + 1] = top_all[pair, head : head + 1] + jnp.log(total) * LOG2E
            columns = pair_columns(pair)
            attn_ref[:, columns] = acc_ref[columns].T.astype(LOW)

    for slot in range(2):
        for copy in kv_copies(3, pairs - 2 + slot, slot, half_rows, half_rows):
            copy.wait()
    for shard in range(4):
        keep(shard).wait()
    for chunk in range(pairs):
        channels[0](chunk).wait_send()

    @pl.when(at_middle)
    def _():
        for channel in channels[1:]:
            for chunk in range(pairs):
                channel(chunk).wait_send()


def attention_call(a_low, w_qkv, clips, query_clip):
    rows, width = a_low.shape
    pairs = width // PAIR
    anywhere = pl.BlockSpec(memory_space=pl.ANY)
    inside = pl.BlockSpec(memory_space=pltpu.VMEM)
    four = jax.ShapeDtypeStruct((4, rows, width), LOW)
    square = jax.ShapeDtypeStruct((rows, width), LOW)
    lines = jax.ShapeDtypeStruct((pairs, 2, rows), WIDE)
    return pl.pallas_call(
        attention_kernel,
        in_specs=[anywhere, inside, anywhere, inside],
        out_specs=[anywhere] * 3 + [inside] * 4,
        out_shape=[four, four, four, square, jax.ShapeDtypeStruct((width, rows), WIDE), lines, square],
        scratch_shapes=[
            pltpu.VMEM((4, rows, width), LOW),
            pltpu.VMEM((pairs, 2, rows), WIDE),
            pltpu.VMEM((pairs, 2, rows), WIDE),
            pltpu.VMEM((2, 2, rows, PAIR), LOW),
            pltpu.VMEM((rows, 1), clips.dtype),
            pltpu.SemaphoreType.DMA((5,)),
            pltpu.SemaphoreType.DMA((2, 2)),
            pltpu.SemaphoreType.DMA,
            pltpu.SemaphoreType.DMA((5, pairs)),
            pltpu.SemaphoreType.DMA((5, pairs)),
        ],
        name="attention",
        compiler_params=pltpu.CompilerParams(
            collective_id=2, has_side_effects=True, vmem_limit_bytes=48 * 2**20
        ),
    )(a_low, w_qkv, clips, query_clip)


FF_BLOCK = 512
ROW_BLOCK = 384
AHEAD_STEPS = (3, 3, 2, 2)
AHEAD_TICKS = ((1, 3, 4), (2, 4, 5), (3, 5), (4, 5))
AHEAD = len(AHEAD_STEPS)
LAST_BLOCK = 5
DOWN_AXES, UP_AXES = "rrrrr", "rrrrc"


def ahead_rows(shape, axes):
    rows = [halves(shape, axes)[steps - 1][0] for steps in AHEAD_STEPS]
    return [(sum(rows[:block]), rows[block]) for block in range(AHEAD)]


def ahead_scratch(width):
    scratch = [pltpu.VMEM((2, FF_BLOCK, width), LOW), pltpu.VMEM((2, width, FF_BLOCK), LOW)]
    for shape, axes in (((FF_BLOCK, width), DOWN_AXES), ((width, FF_BLOCK), UP_AXES)):
        for steps in AHEAD_STEPS:
            shapes = halves(shape, axes)[:steps]
            scratch += [pltpu.VMEM(each, LOW) for each in (shapes[0], *shapes)]
    scratch += [pltpu.SemaphoreType.DMA((2 * AHEAD, 2 * STEPS))] * 2
    return scratch + [pltpu.SemaphoreType.DMA((2 * AHEAD, 2))]


def ahead_sums(width, part_down, part_up, refs):
    terms, refs = refs[:2], refs[2:]
    sends, receives, locals_ = refs[-3:]
    sums = []
    for side, (axes, shape, parts) in enumerate(
        ((DOWN_AXES, (FF_BLOCK, width), part_down), (UP_AXES, (width, FF_BLOCK), part_up))
    ):
        places = ahead_rows(shape, axes)
        for block, steps in enumerate(AHEAD_STEPS):
            index = side * AHEAD + block
            own, refs = refs[: steps + 1], refs[steps + 1 :]
            sums.append(
                Sum(
                    (block + side) % 2,
                    axes,
                    (0, 0),
                    shape,
                    terms[side].at[block % 2],
                    parts.at[pl.ds(*places[block])],
                    own[0],
                    own[1:],
                    (sends.at[index], receives.at[index]),
                    locals_.at[index],
                    stop=steps,
                )
            )
    return terms, [(sums[block], sums[AHEAD + block]) for block in range(AHEAD)]


def mlp_kernel(
    ahead,
    hidden_ref,
    attn_ref,
    attended_ref,
    cotangent_ref,
    w_out_ref,
    gain_ref,
    w_up_ref,
    b_up_ref,
    w_down_ref,
    outputs_ref,
    d_resid_ref,
    grad_t_ref,
    dots_ref,
    grad_down_ref,
    grad_up_ref,
    grad_out_ref,
    grad_gain_ref,
    grad_bias_ref,
    *refs,
):
    block = pl.program_id(0)
    rows, width = hidden_ref.shape
    if ahead:
        parts, refs = refs[:2], refs[2:]
    normed_ref, inverse_ref, b_ref, dy_ref, db_ref, z_ref, d_pre_ref = refs[:7]
    if ahead:
        terms, sums = ahead_sums(width, *parts, refs[7:])

        @pl.when(block == 0)
        def _():
            greet([device for _, device in place_bits(0)[: max(AHEAD_STEPS)]])

    def trade(chosen, tick, when):
        @pl.when(block == when)
        def _():
            for each in sums[chosen]:
                each.turn(tick)

    @pl.when(block == 0)
    def _():
        resid = hidden_ref[...] + dot(attn_ref[...], w_out_ref[...], NN)
        normed, inverse = normalize(resid)
        normed_ref[...] = normed
        inverse_ref[...] = inverse
        b_ref[...] = (normed * gain_ref[...]).astype(LOW)
        dy_ref[...] = cotangent_ref[...].astype(LOW)
        outputs_ref[...] = resid
        db_ref[...] = jnp.zeros_like(db_ref)

    bias = jnp.zeros((1, FF_BLOCK), WIDE)
    for start in range(0, rows, ROW_BLOCK):
        here = slice(start, start + ROW_BLOCK)
        pre_act = dot(b_ref[here], w_up_ref[...], NN) + b_up_ref[...]
        cumulative = 0.5 * (1.0 + lax.erf(pre_act * 0.7071067811865476))
        density = jnp.exp(-0.5 * pre_act * pre_act) * 0.3989422804014327
        z_ref[here] = (pre_act * cumulative).astype(LOW)
        d_gelu = dot(dy_ref[here], w_down_ref[...], NT)
        d_pre = (d_gelu * (cumulative + pre_act * density)).astype(LOW)
        d_pre_ref[here] = d_pre
        bias += jnp.sum(d_pre.astype(WIDE), axis=0, keepdims=True)
        outputs_ref[here] += dot(z_ref[here], w_down_ref[...], NN)
        db_ref[here] += dot(d_pre, w_up_ref[...], NT)
    grad_bias_ref[...] = bias
    grad_down = dot(z_ref[...], dy_ref[...], TN).astype(LOW)
    grad_up = dot(b_ref[...], d_pre_ref[...], TN).astype(LOW)
    grad_down_ref[...] = grad_down
    grad_up_ref[...] = grad_up
    if ahead:
        for chosen, ticks in enumerate(AHEAD_TICKS):
            for tick, when in enumerate(ticks):
                if when < LAST_BLOCK:
                    trade(chosen, tick, when)
        for chosen in range(AHEAD):

            @pl.when(block == chosen)
            def _():
                terms[0][chosen % 2] = grad_down
                terms[1][chosen % 2] = grad_up
                for each in sums[chosen]:
                    each.start()


    @pl.when(block == pl.num_programs(0) - 1)
    def _():
        normed, db = normed_ref[...], db_ref[...]
        grad_gain_ref[...] = jnp.sum(db * normed, axis=0, keepdims=True)
        d_resid = cotangent_ref[...] + norm_back(db * gain_ref[...], normed, inverse_ref[...])
        d_resid_ref[...] = d_resid
        dr_low = d_resid.astype(LOW)
        grad_out_ref[...] = dot(attn_ref[...], dr_low, TN).astype(LOW)
        grad_t = dot(w_out_ref[...], dr_low, NT).astype(LOW)
        grad_t_ref[...] = grad_t
        product = grad_t.astype(WIDE) * attended_ref[...]
        for pair in range(dots_ref.shape[0]):
            for head in range(2):
                lanes = slice(pair * PAIR + head * HEAD, pair * PAIR + (head + 1) * HEAD)
                dots_ref[pair, head : head + 1] = jnp.sum(product[lanes], axis=0, keepdims=True)

    if ahead:
        for chosen, ticks in enumerate(AHEAD_TICKS):
            for tick, when in enumerate(ticks):
                if when == LAST_BLOCK:
                    trade(chosen, tick, when)

        @pl.when(block == pl.num_programs(0) - 1)
        def _():
            for pair in sums:
                for each in pair:
                    each.store().wait()


def mlp_call(ahead, hidden, attn_low, attended, cotangent, w_out, gain_mlp, w_up, b_up, w_down):
    rows, width = hidden.shape
    hidden_units = w_up.shape[1]
    pairs = width // PAIR
    once = lambda *shape: pl.BlockSpec(
        shape, lambda block: (0,) * len(shape), pipeline_mode=pl.Buffered(1)
    )
    square, line = once(rows, width), once(1, width)
    up = pl.BlockSpec((width, FF_BLOCK), lambda block: (0, block))
    down = pl.BlockSpec((FF_BLOCK, width), lambda block: (block, 0))
    bias = pl.BlockSpec((1, FF_BLOCK), lambda block: (0, block))
    wide = jax.ShapeDtypeStruct((rows, width), WIDE)
    anywhere = pl.BlockSpec(memory_space=pl.ANY)
    down_rows = sum(ahead_rows((FF_BLOCK, width), DOWN_AXES)[-1])
    up_rows = sum(ahead_rows((width, FF_BLOCK), UP_AXES)[-1])
    part_shapes = [
        jax.ShapeDtypeStruct((down_rows, width), LOW),
        jax.ShapeDtypeStruct((up_rows, FF_BLOCK), LOW),
    ]
    params = dict(collective_id=3, has_side_effects=True) if ahead else {}
    return pl.pallas_call(
        functools.partial(mlp_kernel, ahead),
        grid=(hidden_units // FF_BLOCK,),
        in_specs=[square] * 4 + [once(width, width), line, up, bias, down],
        out_specs=[
            whole(rows, width),
            whole(rows, width),
            whole(width, rows),
            whole(pairs, 2, rows),
            down,
            up,
            whole(width, width),
            whole(1, width),
            bias,
        ]
        + [anywhere] * (2 if ahead else 0),
        out_shape=[
            wide,
            wide,
            jax.ShapeDtypeStruct((width, rows), LOW),
            jax.ShapeDtypeStruct((pairs, 2, rows), WIDE),
            jax.ShapeDtypeStruct(w_down.shape, LOW),
            jax.ShapeDtypeStruct(w_up.shape, LOW),
            jax.ShapeDtypeStruct((width, width), LOW),
            jax.ShapeDtypeStruct((1, width), WIDE),
            jax.ShapeDtypeStruct((1, hidden_units), WIDE),
        ]
        + (part_shapes if ahead else []),
        scratch_shapes=[
            pltpu.VMEM((rows, width), WIDE),
            pltpu.VMEM((rows, 1), WIDE),
            pltpu.VMEM((rows, width), LOW),
            pltpu.VMEM((rows, width), LOW),
            pltpu.VMEM((rows, width), WIDE),
            pltpu.VMEM((rows, FF_BLOCK), LOW),
            pltpu.VMEM((rows, FF_BLOCK), LOW),
        ]
        + (ahead_scratch(width) if ahead else []),
        name="mlp",
        compiler_params=pltpu.CompilerParams(vmem_limit_bytes=60 * 2**20, **params),
    )(hidden, attn_low, attended, cotangent, w_out, gain_mlp[None], w_up, b_up[None], w_down)


PARTS = (
    ("down", (0, 0), (512, 768), DOWN_AXES, 0, AHEAD_STEPS[0], 0, (24, 24, 24, 1, 2, 4, 5, 6, 8, 9)),
    ("down", (512, 0), (512, 768), DOWN_AXES, 1, AHEAD_STEPS[1], 1, (24, 24, 24, 1, 2, 4, 5, 6, 8, 9)),
    ("down", (1024, 0), (512, 768), DOWN_AXES, 0, AHEAD_STEPS[2], 2, (24, 24, 1, 2, 4, 6, 7, 9, 12, 13)),
    ("down", (1536, 0), (512, 768), DOWN_AXES, 1, AHEAD_STEPS[3], 3, (24, 24, 1, 2, 4, 6, 8, 10, 12, 13)),
    ("up", (0, 0), (768, 512), UP_AXES, 1, AHEAD_STEPS[0], 0, (24, 24, 24, 1, 2, 5, 6, 7, 10, 11)),
    ("up", (0, 512), (768, 512), UP_AXES, 0, AHEAD_STEPS[1], 1, (24, 24, 24, 2, 3, 5, 6, 8, 10, 11)),
    ("up", (0, 1024), (768, 512), UP_AXES, 1, AHEAD_STEPS[2], 2, (24, 24, 2, 3, 5, 6, 8, 11, 12, 14)),
    ("up", (0, 1536), (768, 512), UP_AXES, 0, AHEAD_STEPS[3], 3, (24, 24, 2, 4, 5, 6, 9, 11, 12, 13)),
    ("down", (2048, 0), (1024, 768), "rrrrr", 0, 0, None, (1, 4, 6, 8, 12, 16, 19, 21, 24, 24)),
    ("up", (0, 2048), (768, 1024), "rrrcc", 1, 0, None, (1, 4, 6, 8, 12, 16, 20, 22, 24, 24)),
    ("out", (0, 0), (768, 768), "rrrrc", 0, 0, None, (2, 5, 6, 9, 12, 16, 20, 22, 24, 24)),
    ("qkv", (0, 0), (768, 256), "rrrrc", 0, 0, None, None),
    ("qkv", (0, 256), (768, 256), "rrrrc", 1, 0, None, None),
    ("qkv", (0, 512), (768, 256), "rrrrc", 0, 0, None, None),
    ("qkv", (0, 768), (768, 256), "rrrrc", 1, 0, None, None),
    ("qkv", (0, 1024), (768, 256), "rrrrc", 0, 0, None, None),
    ("qkv", (0, 1280), (768, 256), "rrrrc", 1, 0, None, None),
    ("qkv", (0, 1536), (768, 256), "rrrrc", 0, 0, None, None),
    ("qkv", (0, 1792), (768, 256), "rrrrc", 1, 0, None, None),
    ("qkv", (0, 2048), (768, 256), "rrrrc", 0, 0, None, None),
)


def gradient_kernel(*refs):
    keys, values, shards = refs[:3]
    q_ref, grad_ref, lse_ref, dots_ref, clips, query_clip, w_ref = refs[3:10]
    down_in, up_in, out_in, part_down, part_up, small_in = refs[10:16]
    down_out, up_out, out_out, qkv_out, small_out, input_out = refs[16:22]
    refs = refs[22:]
    kv_slot, a_slot, dq_sum, dk_sum, dv_sum, dk_all, dv_all, grad_k, grad_v, parts = refs[:10]
    from_near, from_across, qkv_term, clip_slot, small_arrived = refs[10:15]
    input_sum = dq_sum
    kv_sems, a_sem, line_sends, line_receives, sends, receives, locals_ = refs[15:22]
    small_sends, small_receives, out_sem, clip_sem = refs[22:26]
    refs = refs[26:]
    rows, width = q_ref.shape
    pairs = width // PAIR
    pieces = 4 * pairs
    group, place = lax.axis_index("dp"), lax.axis_index("blk")
    near = (group, place + 1 - 2 * (place % 2))
    across = (group, 3 - place)
    at_end = place % 3 == 0

    arrays = {
        "down": (down_in, down_out),
        "up": (up_in, up_out),
        "out": (out_in, out_out),
        "qkv": (qkv_term, qkv_out),
    }
    sums = []
    for index, (name, corner, shape, axes, turn, begin, block, _) in enumerate(PARTS):
        steps = STEPS - begin
        total, arrived, refs = refs[0], refs[1 : steps + 1], refs[steps + 1 :]
        term, result = arrays[name]
        if block is not None:
            term = {"down": part_down, "up": part_up}[name]
            term = term.at[pl.ds(*ahead_rows(shape, axes)[block])]
        sums.append(
            Sum(
                turn,
                axes,
                corner,
                shape,
                term,
                result,
                total,
                arrived,
                (sends.at[index], receives.at[index]),
                locals_.at[index],
                begin=begin,
            )
        )
    early = [(each, part[-1]) for each, part in zip(sums, PARTS) if part[-1] is not None]
    late = [each for each, part in zip(sums, PARTS) if part[-1] is None]

    chunk_rows = rows // pairs

    def chunk_of(chunk):
        return pl.ds(pl.multiple_of(chunk * chunk_rows, chunk_rows), chunk_rows)

    def line_copy(channel, chunk, source, target, device):
        return pltpu.make_async_remote_copy(
            src_ref=parts.at[source, chunk_of(chunk)],
            dst_ref=target.at[chunk_of(chunk)],
            send_sem=line_sends.at[channel, chunk],
            recv_sem=line_receives.at[channel, chunk],
            device_id=device,
            device_id_type=MESH,
        )

    def inward(source, chunk):
        return line_copy(source, chunk, source, from_near.at[source], near)

    def middle(source, chunk):
        return line_copy(3 + source, chunk, source, from_across.at[source], across)

    def outward(chunk):
        return line_copy(5, chunk, 2, from_near.at[0], near)

    def add_chunk(total, term, chunk):
        here = chunk_of(chunk)
        total[here] = (total[here].astype(WIDE) + term[here].astype(WIDE)).astype(total.dtype)

    def pair_columns(pair):
        return pl.ds(pl.multiple_of(pair * PAIR, PAIR), PAIR)

    def kv_copies(shard, pair, slot):
        return [
            pltpu.make_async_copy(
                source.at[shard, :, pair_columns(pair)], kv_slot.at[slot, side], kv_sems.at[slot, side]
            )
            for side, source in enumerate((keys, values))
        ]

    def a_copy(shard):
        return pltpu.make_async_copy(shards.at[shard], a_slot, a_sem)

    def clip_copy(turn):
        source = clips.at[pl.ds(pl.multiple_of((3 - turn) * rows, 8), rows)]
        return pltpu.make_async_copy(source, clip_slot, clip_sem)

    def of_pairs(stack):
        return jnp.concatenate([stack[pair] for pair in range(pairs)], axis=1)

    for copy in kv_copies(3, 0, 0):
        copy.start()
    greet([device for _, device in place_bits(0)] + [across])
    for each, _ in early:
        each.start()
    dq_sum[...] = jnp.zeros_like(dq_sum)
    grad_k[...] = jnp.zeros_like(grad_k)
    grad_v[...] = jnp.zeros_like(grad_v)
    small_out[...] = small_in[...]

    def weight_terms(d_query):
        a_copy(0).wait()
        d_key, d_value = of_pairs(dk_all), of_pairs(dv_all)
        part = dot(d_key, w_ref[:, width : 2 * width], NT) + dot(d_value, w_ref[:, 2 * width :], NT)
        if d_query is not None:
            part = part + dot(d_query, w_ref[:, :width], NT)
        small_out[:1] += jnp.sum(part * a_slot[...].astype(WIDE), axis=0, keepdims=True)
        grad_k[...] += dot(a_slot[...], d_key, TN)
        grad_v[...] += dot(a_slot[...], d_value, TN)
        return part

    @pl.loop(0, pieces)
    def _(piece):
        turn, pair, slot = piece // pairs, piece % pairs, piece % 2

        def at(when, *actions):
            @pl.when(piece == when)
            def _():
                for action in actions:
                    action()

        following = piece + 1

        @pl.when(following < pieces)
        def _():
            for copy in kv_copies(3 - following // pairs, following % pairs, following % 2):
                copy.start()

        @pl.when(pair == 1)
        def _():
            a_copy(3 - turn).start()

        for when in range(pieces):
            ends = [
                functools.partial(each.turn, tick)
                for tick in range(2 * STEPS)
                for each, ticks in early
                if ticks[tick] == when and tick >= each.begin
            ]
            if ends:
                at(when, *ends)
        at_middle = jnp.logical_not(at_end)

        @pl.when(jnp.logical_and(turn > 0, at_end))
        def _():
            inward(turn - 1, pair).start()

        @pl.when(jnp.logical_and(at_middle, jnp.logical_and(piece >= FORWARD, piece < FORWARD + 2 * pairs)))
        def _():
            source, chunk = (piece - FORWARD) // pairs, (piece - FORWARD) % pairs
            inward(source, chunk).wait_recv()
            add_chunk(parts.at[source], from_near.at[source], chunk)
            middle(source, chunk).start()

        @pl.when(jnp.logical_and(at_middle, turn == 3))
        def _():
            middle(0, pair).wait_recv()
            add_chunk(parts.at[2], from_across.at[0], pair)
            outward(pair).start()

        @pl.when(pair == 0)
        def _():
            clip_copy(turn).start()
            clip_copy(turn).wait()

        for copy in kv_copies(0, pair, slot):
            copy.wait()
        columns = pair_columns(pair)

        def add(head, start, stop, dq, dk, dv):
            lanes = slice(head * HEAD, (head + 1) * HEAD)
            if start == 0:
                dv_sum[lanes], dk_sum[lanes] = dv, dk
            else:
                dv_sum[lanes] += dv
                dk_sum[lanes] += dk
            at_lanes = pl.ds(pl.multiple_of(pair * PAIR + head * HEAD, HEAD), HEAD)
            dq_sum[at_lanes, start:stop] += dq

        backward_pair(
            kv_slot[slot, 0],
            kv_slot[slot, 1],
            q_ref[:, columns],
            grad_ref[columns, :],
            lse_ref.at[pair],
            dots_ref.at[pair],
            clip_slot[...],
            query_clip[...],
            add,
        )
        dk_all[pair] = (dk_sum[...] * SCALE).T.astype(LOW)
        dv_all[pair] = dv_sum[...].T.astype(LOW)

        @pl.when(jnp.logical_and(pair == pairs - 1, turn < 3))
        def _():
            parts[turn] = weight_terms(None).astype(LOW)

    d_query = (dq_sum[...] * SCALE).T.astype(LOW)
    input_sum[...] = weight_terms(d_query)
    qkv_term[:, :width] = dot(a_slot[...], d_query, TN).astype(LOW)
    qkv_term[:, width : 2 * width] = grad_k[...].astype(LOW)
    qkv_term[:, 2 * width :] = grad_v[...].astype(LOW)

    small_steps = place_bits(0)

    def small(step):
        return remote(
            small_out, small_arrived.at[step], (small_sends, small_receives), step, small_steps[step][1]
        )

    for each in late:
        each.start()
    open_sums = [
        (each, [tick for tick in range(each.begin, 2 * STEPS) if ticks[tick] == pieces])
        for each, ticks in early
    ]
    open_sums += [(each, list(range(2 * STEPS))) for each in late]

    @pl.when(at_end)
    def _():
        @pl.loop(0, pairs)
        def _(chunk):
            for source in range(3):
                inward(source, chunk).wait_send()
            outward(chunk).wait_recv()
            add_chunk(input_sum, from_near.at[0], chunk)

    @pl.when(jnp.logical_not(at_end))
    def _():
        @pl.loop(0, pairs)
        def _(chunk):
            outward(chunk).wait_send()
            for source in range(2):
                middle(source, chunk).wait_send()
            middle(1, chunk).wait_recv()
            add_chunk(input_sum, from_across.at[1], chunk)
            inward(2, chunk).wait_recv()
            add_chunk(input_sum, from_near.at[2], chunk)

    store = pltpu.make_async_copy(input_sum, input_out, out_sem)
    store.start()
    for tick in range(2 * STEPS):
        if tick < STEPS:
            small(tick).start()
        for each, ticks in open_sums:
            if ticks:
                each.turn(ticks.pop(0))
        if tick < STEPS:
            small(tick).wait()
            small_out[...] += small_arrived[tick]
    store.wait()


def gradient_call(
    keys, values, shards, query, grad_t, lse, row_dots, clips, query_clip, w_qkv, grad_down, grad_up, grad_out, part_down, part_up, small
):
    rows, width = query.shape
    pairs = width // PAIR
    anywhere = pl.BlockSpec(memory_space=pl.ANY)
    inside = pl.BlockSpec(memory_space=pltpu.VMEM)
    square = (rows, width)
    scratch = [
        pltpu.VMEM((2, 2, rows, PAIR), LOW),
        pltpu.VMEM(square, LOW),
        pltpu.VMEM((width, rows), WIDE),
        pltpu.VMEM((PAIR, rows), WIDE),
        pltpu.VMEM((PAIR, rows), WIDE),
        pltpu.VMEM((pairs, rows, PAIR), LOW),
        pltpu.VMEM((pairs, rows, PAIR), LOW),
        pltpu.VMEM((width, width), WIDE),
        pltpu.VMEM((width, width), WIDE),
        pltpu.VMEM((3, *square), LOW),
    ]
    scratch += [pltpu.VMEM((3, *square), LOW), pltpu.VMEM((2, *square), LOW)]
    scratch += [
        pltpu.VMEM((width, 3 * width), LOW),
        pltpu.VMEM((rows, 1), clips.dtype),
        pltpu.VMEM((STEPS, *small.shape), WIDE),
        pltpu.SemaphoreType.DMA((2, 2)),
        pltpu.SemaphoreType.DMA,
        pltpu.SemaphoreType.DMA((6, pairs)),
        pltpu.SemaphoreType.DMA((6, pairs)),
        pltpu.SemaphoreType.DMA((len(PARTS), 2 * STEPS)),
        pltpu.SemaphoreType.DMA((len(PARTS), 2 * STEPS)),
        pltpu.SemaphoreType.DMA((len(PARTS), 2)),
        pltpu.SemaphoreType.DMA((STEPS,)),
        pltpu.SemaphoreType.DMA((STEPS,)),
        pltpu.SemaphoreType.DMA,
        pltpu.SemaphoreType.DMA,
    ]
    for _, _, shape, axes, _, begin, _, _ in PARTS:
        shapes = halves(shape, axes)
        scratch += [pltpu.VMEM(each, LOW) for each in (shapes[max(begin - 1, 0)], *shapes[begin:])]
    like = lambda array: jax.ShapeDtypeStruct(array.shape, array.dtype)
    return pl.pallas_call(
        gradient_kernel,
        in_specs=[anywhere] * 3 + [inside] * 4 + [anywhere] + [inside] * 2 + [anywhere] * 5 + [inside],
        out_specs=[anywhere] * 4 + [inside, anywhere],
        out_shape=[
            like(grad_down),
            like(grad_up),
            like(grad_out),
            jax.ShapeDtypeStruct((width, 3 * width), LOW),
            like(small),
            jax.ShapeDtypeStruct(square, WIDE),
        ],
        scratch_shapes=scratch,
        name="gradients",
        compiler_params=pltpu.CompilerParams(
            collective_id=1, has_side_effects=True, vmem_limit_bytes=62 * 2**20
        ),
    )(
        keys, values, shards, query, grad_t, lse, row_dots, clips, query_clip, w_qkv,
        grad_down, grad_up, grad_out, part_down, part_up, small,
    )


def on_device(
    groups, inputs, positions, segments, gain_attn, w_qkv, w_out, gain_mlp, w_up, b_up, w_down, cotangent
):
    rows, width = inputs.shape
    pairs = width // PAIR
    place = lax.axis_index("blk")
    w_query = w_qkv[:, :width]

    def send(value, pairs_of_places):
        return lax.ppermute(value, "blk", pairs_of_places)

    hidden = inputs + position_table(positions, width)
    normed_attn, inverse_attn = normalize(hidden)
    a_low = (normed_attn * gain_attn).astype(LOW)

    table = jnp.array([[0, 1, 2, 3], [1, 0, 2, 3], [2, 3, 1, 0], [3, 2, 1, 0]], jnp.int32)
    order = lax.dynamic_index_in_dim(table, place, keepdims=False)
    clips = jnp.concatenate(
        [lax.dynamic_slice_in_dim(segments, order[index] * rows, rows) for index in range(4)]
    )[:, None]
    query_clip = lax.dynamic_slice_in_dim(segments, place * rows, rows)[None, :]
    shards, keys, values, query, attended, lse, attn_low = attention_call(
        a_low, w_qkv, clips, query_clip
    )

    quick = groups == 8 and rows == width
    (
        outputs,
        d_resid,
        d_attn_t,
        row_dots,
        grad_down,
        grad_up,
        grad_out,
        grad_gain_mlp,
        grad_bias_up,
        *parts,
    ) = mlp_call(quick, hidden, attn_low, attended, cotangent, w_out, gain_mlp, w_up, b_up, w_down)
    grad_gain_mlp, grad_bias_up = grad_gain_mlp[0], grad_bias_up[0]

    if quick:
        small = jnp.concatenate([jnp.zeros_like(gain_attn), grad_gain_mlp, grad_bias_up])
        sum_down, sum_up, sum_out, sum_qkv, sum_small, d_normed_attn = gradient_call(
            keys,
            values,
            shards,
            query,
            d_attn_t,
            lse,
            row_dots,
            clips,
            query_clip,
            w_qkv,
            grad_down,
            grad_up,
            grad_out,
            *parts,
            jnp.pad(small.reshape(6, width), ((0, 2), (0, 0))),
        )
        input_grad = d_resid + norm_back(d_normed_attn * gain_attn, normed_attn, inverse_attn)
        return (
            outputs,
            input_grad,
            sum_small[0] / gain_attn,
            sum_qkv.astype(WIDE),
            sum_out.astype(WIDE),
            sum_small[1],
            sum_up.astype(WIDE),
            sum_small[2:6].reshape(-1),
            sum_down.astype(WIDE),
        )

    everywhere = ("dp", "blk")

    def back(index, dq):
        return backward_call(
            index == 3,
            index == 0,
            keys[index],
            values[index],
            query,
            d_attn_t,
            lse,
            row_dots,
            clips[index * rows : (index + 1) * rows],
            query_clip,
            w_qkv,
            dq,
        )

    middle, outward, inward = [(1, 2), (2, 1)], [(1, 0), (2, 3)], [(0, 1), (3, 2)]
    dk_3, dv_3, dq, part_3 = back(3, None)
    far = send(part_3, inward)
    dk_2, dv_2, dq, part_2 = back(2, dq)
    far, part_2, dq = lax.optimization_barrier((far, part_2, dq))
    onward = (part_3.astype(WIDE) + far.astype(WIDE)).astype(LOW)
    mid_3 = send(onward, middle)
    mid_2 = send(part_2, inward)
    dq, onward = lax.optimization_barrier((dq, onward))
    dk_1, dv_1, dq, part_1 = back(1, dq)
    mid_3, mid_2, part_1, dq = lax.optimization_barrier((mid_3, mid_2, part_1, dq))
    onward_1 = (part_2.astype(WIDE) + mid_2.astype(WIDE)).astype(LOW)
    onward_2 = (part_1.astype(WIDE) + mid_3.astype(WIDE)).astype(LOW)
    last_1 = send(onward_1, middle)
    last_2 = send(onward_2, outward)
    last_3 = send(part_1, inward)
    dq, onward_1, onward_2 = lax.optimization_barrier((dq, onward_1, onward_2))
    dk_0, dv_0, dq, part_0 = back(0, dq)
    grad_query = dot(a_low, dq, TN).astype(LOW)
    d_keys, d_values = (dk_0, dk_1, dk_2, dk_3), (dv_0, dv_1, dv_2, dv_3)
    grad_key = sum(dot(shard, term, TN) for shard, term in zip(shards, d_keys)).astype(LOW)
    grad_value = sum(dot(shard, term, TN) for shard, term in zip(shards, d_values)).astype(LOW)
    d_normed_attn = (
        part_0
        + dot(dq, w_query, NT)
        + last_1.astype(WIDE)
        + last_2.astype(WIDE)
        + last_3.astype(WIDE)
    )
    grad_gain_attn = jnp.sum(d_normed_attn * normed_attn, axis=0)
    input_grad = d_resid + norm_back(d_normed_attn * gain_attn, normed_attn, inverse_attn)
    small = jnp.concatenate([grad_gain_attn, grad_gain_mlp, grad_bias_up])
    sums = lax.psum((grad_down, grad_up, grad_out, grad_query, grad_key, grad_value), everywhere)
    sum_small = lax.psum(small, everywhere)
    sum_down, sum_up, sum_out, *sum_qkv = sums
    return (
        outputs,
        input_grad,
        sum_small[:width],
        jnp.concatenate(sum_qkv, axis=1).astype(WIDE),
        sum_out.astype(WIDE),
        sum_small[width : 2 * width],
        sum_up.astype(WIDE),
        sum_small[2 * width :],
        sum_down.astype(WIDE),
    )


def solution(mesh):
    rows = P(("dp", "blk"), None)
    placed = (rows, P(("dp", "blk")), P("dp"), P(), P(), P(), P(), P(), P(), P(), rows)
    return jax.shard_map(
        functools.partial(on_device, mesh.shape["dp"]),
        mesh=mesh,
        in_specs=placed,
        out_specs=(rows, rows, P(), P(), P(), P(), P(), P(), P()),
        check_vma=False,
    )
```
